32 devices in a mesh: dp: 4 (over y, x), seq: 8 (over z, core).
Axes of the slice: x: 2, y: 2, z: 4, core: 2. Of those that a mesh axis runs over, the one named last changes fastest.
Arguments:
- tokens: bfloat16 [4, 1024, 2048], P('dp', 'seq'), may hold values from -6 to 6
- segments: int32 [4, 1024], P('dp', 'seq'), may hold values from 0 to 2, as said below
- norm_one: bfloat16 [2048], P(('dp', 'seq')), may hold values from 0.5 to 1.5
- w_qkv: bfloat16 [2048, 6144], P(('dp', 'seq')), may hold values from -0.125 to 0.125
- w_lr: bfloat16 [2048, 32], P(('dp', 'seq')), may hold values from -0.125 to 0.125
- lr_bias: bfloat16 [32], replicated, may hold values from -3 to 3
- w_gate: bfloat16 [2048, 2048], P(('dp', 'seq')), may hold values from -0.125 to 0.125
- w_out: bfloat16 [2048, 2048], P(('dp', 'seq')), may hold values from -0.125 to 0.125
- w_init: bfloat16 [2048, 64], P(('dp', 'seq')), may hold values from -0.75 to 0.75
- b_init: bfloat16 [2048], P(('dp', 'seq')), may hold values from -3 to 3
- tnorm_w: bfloat16 [2048], P(('dp', 'seq')), may hold values from 0.25 to 1.75
- tnorm_b: bfloat16 [2048], P(('dp', 'seq')), may hold values from -2 to 2
- post_w: bfloat16 [2048], P(('dp', 'seq')), may hold values from 0.5 to 1.5
- post_b: bfloat16 [2048], P(('dp', 'seq')), may hold values from -2 to 2
- norm_two: bfloat16 [2048], P(('dp', 'seq')), may hold values from 0.5 to 1.5
- w_gate_up: bfloat16 [2048, 11008], P(('dp', 'seq')), may hold values from -0.125 to 0.125
- w_down: bfloat16 [5504, 2048], P(('dp', 'seq')), may hold values from -0.078125 to 0.078125
- grad_out: bfloat16 [4, 1024, 2048], P('dp', 'seq'), may hold values from -6 to 6
Outputs:
- block_out: bfloat16 [4, 1024, 2048], P('dp', 'seq')
- d_tokens: bfloat16 [4, 1024, 2048], P('dp', 'seq')
- g_norm_one: float32 [2048], P(('dp', 'seq'))
- g_qkv: float32 [2048, 6144], P(('dp', 'seq'))
- g_lr: float32 [2048, 32], P(('dp', 'seq'))
- g_lr_bias: float32 [32], replicated
- g_gate: float32 [2048, 2048], P(('dp', 'seq'))
- g_out: float32 [2048, 2048], P(('dp', 'seq'))
- g_init_w: float32 [2048, 64], P(('dp', 'seq'))
- g_init_b: float32 [2048], P(('dp', 'seq'))
- g_tnorm_w: float32 [2048], P(('dp', 'seq'))
- g_tnorm_b: float32 [2048], P(('dp', 'seq'))
- g_post_w: float32 [2048], P(('dp', 'seq'))
- g_post_b: float32 [2048], P(('dp', 'seq'))
- g_norm_two: float32 [2048], P(('dp', 'seq'))
- g_gate_up: float32 [2048, 11008], P(('dp', 'seq'))
- g_down: float32 [5504, 2048], P(('dp', 'seq'))
The draws below stay inside these ranges and needn't reach their ends.
Inputs may be any that keep to these rules, and one draw needn't show every extreme that they name: `segments`: in each pack the document numbers are 0, 1, 2 in order and constant on each aligned block of 16 tokens; document 1 begins within the pack's first 128 tokens and ends within its last 128 tokens; documents 0 and 2 are never empty.
All inputs are finite; a program needn't handle non-finite values.
Results may differ from the reference program's by a relative error of at most 0.0095.
Values may be sent and summed in bfloat16 or wider, within the bound.
A program may use at most 576 MiB of HBM per device.

```python
import jax
import jax.numpy as jnp
from jax import lax

D = 2048
H = 32
HD = 64
FF = 5504
MB = 16
SPAN = 128
LENGTH = 1024
PACKS = 4


def draw_segments(key, part):
    key = jax.random.fold_in(key, 7)
    first_key, last_key = jax.random.split(key)
    per_span = SPAN // MB
    blocks = LENGTH // MB
    opening = jax.random.randint(first_key, (PACKS, 1), 1, per_span)
    finish = blocks - per_span + jax.random.randint(last_key, (PACKS, 1), 1, per_span)
    positions = jnp.arange(blocks)[None, :]
    labels = (positions >= opening).astype(jnp.int32) + (positions >= finish).astype(jnp.int32)
    return jnp.repeat(labels, MB, axis=1)


def block_levels(stream_key, dims, cuts, low, high):
    factor_of, own = 1.0, jax.random.fold_in(stream_key, 6)
    for position, parts in cuts:
        steps = jnp.exp(jax.random.uniform(jax.random.fold_in(own, position), (parts,), jnp.float32, low / len(cuts), high / len(cuts)))
        factor_of = factor_of * jnp.repeat(steps, dims[position] // parts).reshape([-1 if axis == position else 1 for axis in range(len(dims))])
    return factor_of


def scatter_about(stream_key, shape, spread, most, cuts=(), held_as=jnp.bfloat16):
    level = block_levels(stream_key, shape, cuts, -0.22, 0.18) if cuts else 1.0
    values = jax.random.normal(stream_key, shape, jnp.float32) * spread * level
    return jnp.minimum(jnp.maximum(values, -most), most).astype(held_as)


def setup_inputs(seed: int = 0) -> dict:
    key_list = jax.random.split(jax.random.key(seed), 19)
    tokens = scatter_about(key_list[0], (PACKS, LENGTH, D), 1.0, 6.0, ((0, 4), (1, 8)))
    segments = draw_segments(jax.random.fold_in(key_list[18], 71), 0)
    norm_one = jnp.clip(1.0 + 0.1 * jax.random.normal(key_list[2], (D,), jnp.float32), 0.5, 1.5).astype(jnp.bfloat16)
    w_qkv = scatter_about(key_list[3], (D, 3 * D), D ** -0.5, 0.125, ((0, 32),))
    w_lr = scatter_about(key_list[4], (D, H), D ** -0.5, 0.125, ((0, 32),))
    lr_bias = scatter_about(key_list[5], (H,), 1.0, 3.0)
    w_gate = scatter_about(key_list[6], (D, D), D ** -0.5, 0.125, ((0, 32),))
    w_out = scatter_about(key_list[7], (D, D), D ** -0.5, 0.125, ((0, 32),))
    w_init = scatter_about(key_list[8], (D, HD), HD ** -0.5, 0.75, ((0, 32),))
    b_init = scatter_about(key_list[9], (D,), 0.5, 3.0, ((0, 32),))
    tnorm_w = jnp.clip(1.0 + 0.15 * jax.random.normal(key_list[10], (D,), jnp.float32), 0.25, 1.75).astype(jnp.bfloat16)
    tnorm_b = scatter_about(key_list[11], (D,), 0.3, 2.0, ((0, 32),))
    post_w = jnp.clip(1.0 + 0.1 * jax.random.normal(key_list[12], (D,), jnp.float32), 0.5, 1.5).astype(jnp.bfloat16)
    post_b = scatter_about(key_list[13], (D,), 0.3, 2.0, ((0, 32),))
    norm_two = jnp.clip(1.0 + 0.1 * jax.random.normal(key_list[14], (D,), jnp.float32), 0.5, 1.5).astype(jnp.bfloat16)
    w_gate_up = scatter_about(key_list[15], (D, 2 * FF), D ** -0.5, 0.125, ((0, 32),))
    w_down = scatter_about(key_list[16], (FF, D), FF ** -0.5, 0.078125, ((0, 32),))
    grad_out = scatter_about(key_list[17], (PACKS, LENGTH, D), 1.0, 6.0, ((0, 4), (1, 8)))
    return dict(tokens=tokens, segments=segments, norm_one=norm_one, w_qkv=w_qkv, w_lr=w_lr, lr_bias=lr_bias, w_gate=w_gate, w_out=w_out, w_init=w_init, b_init=b_init, tnorm_w=tnorm_w, tnorm_b=tnorm_b, post_w=post_w, post_b=post_b, norm_two=norm_two, w_gate_up=w_gate_up, w_down=w_down, grad_out=grad_out)


EPSILON = 1e-06
BASE_RATE = 1.0
PRECISE = lax.Precision.HIGHEST

@jax.custom_vjp
def low(v):
    return lax.optimization_barrier(v.astype(jnp.bfloat16)).astype(jnp.float32)

@jax.custom_vjp
def low_back(v):
    return v

def low_keep(v):
    return (low(v), None)

def low_pass(kept, grad):
    return (grad,)

def back_keep(v):
    return (v, None)

def back_low(kept, grad):
    return (low(grad),)
low.defvjp(low_keep, low_pass)
low_back.defvjp(back_keep, back_low)

def matmul_hi(left_side, right_side):
    return jnp.dot(left_side, right_side, precision=PRECISE, preferred_element_type=jnp.float32)

def normalize(values):
    center = values - lax.optimization_barrier(jnp.mean(values, -1, keepdims=True))
    scale_inv = lax.rsqrt(lax.optimization_barrier(jnp.mean(center * center, -1, keepdims=True)) + EPSILON)
    return (center * scale_inv, scale_inv)

def rms_scale(values):
    return lax.rsqrt(lax.optimization_barrier(jnp.mean(values * values, -1, keepdims=True)) + EPSILON)

def inner_step(w_mat, b_vec, q_rows, k_rows, v_rows, lr_rows, norm_gain, norm_shift):
    z_one = jnp.einsum('hti,hij->htj', k_rows, w_mat, precision=PRECISE) + b_vec[:, None, :]
    target = v_rows - k_rows
    x_hat, scale_inv = normalize(z_one)
    gain_rows = norm_gain[:, None, :]
    shift_rows = norm_shift[:, None, :]
    error_rows = gain_rows * x_hat + shift_rows - target
    g_hat = error_rows * gain_rows
    slope = scale_inv * (g_hat - lax.optimization_barrier(jnp.mean(g_hat, -1, keepdims=True)) - x_hat * lax.optimization_barrier(jnp.mean(g_hat * x_hat, -1, keepdims=True)))
    places = jnp.arange(q_rows.shape[1])
    causal = places[:, None] >= places[None, :]
    divisor = (places[:, None] + 1).astype(jnp.float32)
    step_size = jnp.where(causal[None, :, :], lr_rows[:, None, :] / divisor[None, :, :], 0.0)
    scores = jnp.einsum('hti,hsi->hts', q_rows, k_rows, precision=PRECISE)
    z_bar = jnp.einsum('hti,hij->htj', q_rows, w_mat, precision=PRECISE) + b_vec[:, None, :] - jnp.einsum('hts,hsj->htj', step_size * (scores + 1.0), slope, precision=PRECISE)
    last_row = step_size[:, -1, :]
    w_next = w_mat - jnp.einsum('hsi,hsj->hij', k_rows * last_row[:, :, None], slope, precision=PRECISE)
    b_next = b_vec - lax.optimization_barrier(jnp.sum(last_row[:, :, None] * slope, axis=1))
    bar_hat, _ = normalize(z_bar)
    return (w_next, b_next, q_rows + gain_rows * bar_hat + shift_rows)

def pack_forward(inputs, seg_ids, params):
    norm_one, w_qkv, w_lr, lr_bias, w_gate, w_out, w_init, b_init, tnorm_w, tnorm_b, post_w, post_b, norm_two, w_gate_up, w_down = params
    length = inputs.shape[0]
    blocks = length // MB
    normed_in = inputs * rms_scale(inputs)
    x_one = low(normed_in * norm_one)
    qkv_rows = low_back(matmul_hi(x_one, w_qkv))
    lr_logit = low_back(matmul_hi(x_one, w_lr) + lr_bias)
    gate_pre = low_back(matmul_hi(x_one, w_gate))
    lr_rate = BASE_RATE * jax.nn.sigmoid(lr_logit) / HD

    def split_heads(tensor):
        return tensor.reshape(blocks, MB, H, HD).transpose(0, 2, 1, 3)
    q_heads = split_heads(qkv_rows[:, :D])
    k_heads = split_heads(qkv_rows[:, D:2 * D])
    v_heads = split_heads(qkv_rows[:, 2 * D:])
    lr_heads = lr_rate.reshape(blocks, MB, H).transpose(0, 2, 1)
    block_tags = seg_ids.reshape(blocks, MB)[:, 0]
    init_w = w_init.reshape(H, HD, HD)
    init_b = b_init.reshape(H, HD)
    norm_gain = tnorm_w.reshape(H, HD)
    norm_shift = tnorm_b.reshape(H, HD)

    def advance(state_in, block_in):
        w_mat, b_vec, last_tag = state_in
        q_rows, k_rows, v_rows, lr_rows, blk_tag = block_in
        is_fresh = blk_tag != last_tag
        w_mat = jnp.where(is_fresh, init_w, w_mat)
        b_vec = jnp.where(is_fresh, init_b, b_vec)
        w_next, b_next, out_rows = inner_step(w_mat, b_vec, q_rows, k_rows, v_rows, lr_rows, norm_gain, norm_shift)
        return ((w_next, b_next, blk_tag), out_rows)
    start_state = (jnp.zeros((H, HD, HD), jnp.float32), jnp.zeros((H, HD), jnp.float32), jnp.array(-1, jnp.int32))
    _, block_outs = lax.scan(jax.checkpoint(advance), start_state, (q_heads, k_heads, v_heads, lr_heads, block_tags))
    ttt_mixed = block_outs.transpose(0, 2, 1, 3).reshape(length, D)
    out_hat, _ = normalize(ttt_mixed)
    normed_out = out_hat * post_w + post_b
    gated_unit = low(jax.nn.gelu(gate_pre) * normed_out)
    residual = inputs + low_back(matmul_hi(gated_unit, w_out))
    x_two = low(residual * rms_scale(residual) * norm_two)
    gate_up = low_back(matmul_hi(x_two, w_gate_up))
    hidden = low(jax.nn.silu(gate_up[:, :FF]) * gate_up[:, FF:])
    return residual + low_back(matmul_hi(hidden, w_down))

def reference(tokens, segments, norm_one, w_qkv, w_lr, lr_bias, w_gate, w_out, w_init, b_init, tnorm_w, tnorm_b, post_w, post_b, norm_two, w_gate_up, w_down, grad_out):
    params = tuple((weight_in.astype(jnp.float32) for weight_in in (norm_one, w_qkv, w_lr, lr_bias, w_gate, w_out, w_init, b_init, tnorm_w, tnorm_b, post_w, post_b, norm_two, w_gate_up, w_down)))
    inputs = tokens.astype(jnp.float32)

    def forward(all_inputs, all_params):

        def one_pack(packed):
            return pack_forward(packed[0], packed[1], all_params)
        return lax.map(jax.checkpoint(one_pack), (all_inputs, segments))
    outputs, pullback = jax.vjp(forward, inputs, params)
    d_inputs, d_params = pullback(grad_out.astype(jnp.float32))
    return (outputs.astype(jnp.bfloat16), d_inputs.astype(jnp.bfloat16), d_params[0], d_params[1], d_params[2], d_params[3], d_params[4], d_params[5], d_params[6], d_params[7], d_params[8], d_params[9], d_params[10], d_params[11], d_params[12], d_params[13], d_params[14])
```

```python
import functools
import jax
import jax.numpy as jnp
from jax import lax
from jax.experimental import pallas as pl
from jax.experimental.pallas import tpu as pltpu
from jax.sharding import PartitionSpec as P

HD = 64
MB = 16
PER = 8
EPSILON = 1e-06


def nn(left, right):
    return lax.dot_general(left, right, (((1,), (0,)), ((), ())), preferred_element_type=jnp.float32)


def nt(left, right):
    return lax.dot_general(left, right, (((1,), (1,)), ((), ())), preferred_element_type=jnp.float32)


def tn(left, right):
    return lax.dot_general(left, right, (((0,), (0,)), ((), ())), preferred_element_type=jnp.float32)


def halves(value):
    high = value.astype(jnp.bfloat16)
    return high, (value - high.astype(jnp.float32)).astype(jnp.bfloat16)


def head_masks(heads):
    ht, hi = heads * MB, heads * HD

    def iota(shape, axis):
        return lax.broadcasted_iota(jnp.int32, shape, axis)

    own = (iota((ht, hi), 0) // MB == iota((ht, hi), 1) // HD).astype(jnp.float32)
    unit = (iota((HD, hi), 0) == iota((HD, hi), 1) % HD).astype(jnp.bfloat16)
    row, col = iota((ht, ht), 0), iota((ht, ht), 1)
    same = (row // MB == col // MB).astype(jnp.bfloat16)
    ts, tt = row % MB, col % MB
    later = jnp.where((row // MB == col // MB) & (ts <= tt), MB / (tt + 1).astype(jnp.float32), 0.0)
    earlier = jnp.where((row // MB == col // MB) & (tt <= ts), MB / (ts + 1).astype(jnp.float32), 0.0)
    return own, unit, same, later, earlier


def spread(rows, own, heads):
    return (jnp.concatenate([rows] * heads, axis=0) * own).astype(jnp.bfloat16)


def fold(values, heads):
    total = values[:MB]
    for h in range(1, heads):
        total = total + values[h * MB : (h + 1) * MB]
    return total


def turned(rows, own, unit, heads):
    wide = jnp.concatenate([rows] * heads, axis=0) * own
    high, low = halves(wide)
    return nt(unit, high) + nt(unit, low)


def mean0(value):
    return jnp.sum(value, axis=0, keepdims=True) * (1.0 / HD)


def forward_kernel(heads, per, fresh_ref, qkv_ref, e_ref, w0_ref, c0_ref, gain_ref, shift_ref,
                   mixed_ref, wsave_ref, hat_ref, slope_ref, gap_ref, bar_ref, rows_ref, w_ref, c_ref):
    hi = heads * HD
    own, unit, same, later, _ = head_masks(heads)
    gain, shift, w0, c0 = gain_ref[...], shift_ref[...], w0_ref[...], c0_ref[...]
    gain2 = gain * gain

    @pl.when(pl.program_id(0) == 0)
    def _():
        w_ref[...] = jnp.zeros_like(w_ref)
        c_ref[...] = jnp.zeros_like(c_ref)

    w, c = w_ref[...], c_ref[...]
    for b in range(per):
        is_fresh = fresh_ref[pl.program_id(0) * per + b] != 0
        lines = slice(b * MB, (b + 1) * MB)
        q, k, v = qkv_ref[lines, :hi], qkv_ref[lines, hi : 2 * hi], qkv_ref[lines, 2 * hi :]
        e = e_ref[b]
        kb, qb = spread(k, own, heads), spread(q, own, heads)
        gap = shift - turned(v - k, own, unit, heads)
        base = gain * gap
        w = jnp.where(is_fresh, w0, w)
        c = jnp.where(is_fresh, c0, c)
        wb = w.astype(jnp.bfloat16)
        wsave_ref[b] = wb
        z = nt(wb, kb) + c
        gz = gain2 * z
        s = lax.rsqrt(mean0(z * z) + EPSILON)
        mean_g = s * mean0(gz) + mean0(base)
        mean_gx = s * (s * mean0(gz * z) + mean0(base * z))
        hat = s * z
        slope = s * (gain2 * hat + base - mean_g - hat * mean_gx)
        eb = (e * slope).astype(jnp.bfloat16)
        mix = (later * (nt(kb, qb) + 1.0)).astype(jnp.bfloat16)
        zbar = nt(wb, qb) + c - nn(eb, mix)
        w = w - nn(eb, kb)
        c = c - nn(eb, same)
        sbar = lax.rsqrt(mean0(zbar * zbar) + EPSILON)
        bar = zbar * sbar
        high, low = halves(gain * bar + shift)
        mixed_ref[lines, :] = q + fold((tn(high, unit) + tn(low, unit)) * own, heads)
        hat_ref[b] = hat
        slope_ref[b] = slope
        gap_ref[b] = gap
        bar_ref[b] = bar
        rows_ref[b] = jnp.concatenate([s, sbar, mean_g, mean_gx], axis=0)
    w_ref[...] = w
    c_ref[...] = c


def inner_forward(fresh, qkv, e_rows, w0, c0, gain, shift):
    tokens, heads = qkv.shape[0], qkv.shape[1] // (3 * HD)
    ht, hi = heads * MB, heads * HD
    blocks = tokens // MB
    per = PER
    f32 = jnp.float32
    whole = lambda shape: pl.BlockSpec(shape, lambda i: (0, 0))
    save = pl.BlockSpec((per, HD, ht), lambda i: (i, 0, 0))
    return pl.pallas_call(
        functools.partial(forward_kernel, heads, per),
        grid=(blocks // per,),
        in_specs=[
            pl.BlockSpec(memory_space=pltpu.SMEM),
            pl.BlockSpec((per * MB, 3 * hi), lambda i: (i, 0)),
            pl.BlockSpec((per, 1, ht), lambda i: (i, 0, 0)),
            whole((HD, hi)), whole((HD, ht)), whole((HD, ht)), whole((HD, ht)),
        ],
        out_specs=[
            pl.BlockSpec((per * MB, hi), lambda i: (i, 0)),
            pl.BlockSpec((per, HD, hi), lambda i: (i, 0, 0)),
            save, save, save, save,
            pl.BlockSpec((per, 4, ht), lambda i: (i, 0, 0)),
        ],
        out_shape=[
            jax.ShapeDtypeStruct((tokens, hi), f32),
            jax.ShapeDtypeStruct((blocks, HD, hi), jnp.bfloat16),
        ] + [jax.ShapeDtypeStruct((blocks, HD, ht), f32)] * 4 + [jax.ShapeDtypeStruct((blocks, 4, ht), f32)],
        scratch_shapes=[pltpu.VMEM((HD, hi), f32), pltpu.VMEM((HD, ht), f32)],
        compiler_params=pltpu.CompilerParams(vmem_limit_bytes=48 * 1024 * 1024),
        name="inner_forward",
    )(fresh, qkv, e_rows, w0, c0, gain, shift)


def backward_kernel(heads, per, fresh_ref, qkv_ref, e_ref, dmix_ref, wsave_ref, hat_ref, slope_ref, gap_ref,
                    bar_ref, rows_ref, gain_ref, shift_ref,
                    dqkv_ref, drate_ref, dw0_ref, dc0_ref, dgain_ref, dshift_ref, a_ref, ac_ref):
    hi, ht = heads * HD, heads * MB
    own, unit, same, later, earlier = head_masks(heads)
    gain = gain_ref[...]
    gain2 = gain * gain
    step = pl.program_id(0)

    @pl.when(step == 0)
    def _():
        for ref in (a_ref, ac_ref, dw0_ref, dc0_ref, dgain_ref, dshift_ref):
            ref[...] = jnp.zeros_like(ref)

    a, ac = a_ref[...], ac_ref[...]
    dw0, dc0, dgain, dshift = dw0_ref[...], dc0_ref[...], dgain_ref[...], dshift_ref[...]
    for b in reversed(range(per)):
        is_fresh = fresh_ref[(pl.num_programs(0) - 1 - step) * per + b] != 0
        lines = slice(b * MB, (b + 1) * MB)
        q, k = qkv_ref[lines, :hi], qkv_ref[lines, hi : 2 * hi]
        e = e_ref[b]
        wb, hat, slope, gap, bar = wsave_ref[b], hat_ref[b], slope_ref[b], gap_ref[b], bar_ref[b]
        s, sbar, mean_g, mean_gx = (rows_ref[b][i : i + 1] for i in range(4))
        kb, qb = spread(k, own, heads), spread(q, own, heads)
        dout = dmix_ref[lines, :]
        dturn = turned(dout, own, unit, heads)
        head = gain * dturn
        dbar = sbar * (head - mean0(head) - bar * mean0(head * bar))
        dbarb = dbar.astype(jnp.bfloat16)
        scores = nt(qb, kb) + 1.0
        mix = earlier * scores
        s2 = s * s
        gh = gain2 * hat
        alpha = s2 * (gain2 - mean_gx)
        kappa = s2 * (gain2 * hat + gap * gain + gh)
        kappa1 = mean_g + mean0(gh)
        kappa2 = 2.0 * mean_gx + mean0(gh * hat)
        ab = a.astype(jnp.bfloat16)
        ka = nt(ab, kb) + ac
        u = -e * (ka + nn(dbarb, mix.astype(jnp.bfloat16)))
        ug = gain2 * u
        r2 = mean0(u * hat)
        r3 = mean0(ug)
        r4 = mean0(ug * hat)
        r5 = mean0(u * slope)
        row1 = s2 * (r3 - r2 * kappa1)
        row2 = s2 * (r4 - r2 * kappa2) + s * r5
        dz = alpha * u - r2 * kappa - row1 - hat * row2
        dzb = dz.astype(jnp.bfloat16)
        dg = s * (u - hat * r2)
        a_next = a + nn(dbarb, qb) + nn(dzb, kb)
        ac_next = ac + nn(dbarb, same) + nn(dzb, same)
        dm = -tn(dbarb, slope.astype(jnp.bfloat16))
        ds = (earlier * e * dm).astype(jnp.bfloat16)
        drate_ref[b] = (jnp.sum(mix * dm, axis=0, keepdims=True) - jnp.sum(ka * slope, axis=0, keepdims=True)) * (1.0 / MB)
        dgb = (gain * dg)
        ndg = fold(tn(dgb.astype(jnp.bfloat16), unit) * own, heads)
        dq = dout + fold(tn(dbarb, wb) * own + nn(ds, kb), heads)
        dk = ndg + fold((tn(dzb, wb) - tn((e * slope).astype(jnp.bfloat16), ab)) * own + tn(ds, qb), heads)
        dqkv_ref[lines, :hi] = dq.astype(jnp.bfloat16)
        dqkv_ref[lines, hi : 2 * hi] = dk.astype(jnp.bfloat16)
        dqkv_ref[lines, 2 * hi :] = (-ndg).astype(jnp.bfloat16)
        dgain = dgain + dturn * bar + dg * (2.0 * gain * hat + gap)
        dshift = dshift + dturn + dgb
        dw0 = dw0 + jnp.where(is_fresh, a_next, 0.0)
        dc0 = dc0 + jnp.where(is_fresh, ac_next, 0.0)
        a = jnp.where(is_fresh, 0.0, a_next)
        ac = jnp.where(is_fresh, 0.0, ac_next)
    a_ref[...] = a
    ac_ref[...] = ac
    dw0_ref[...] = dw0
    dc0_ref[...] = dc0
    dgain_ref[...] = dgain
    dshift_ref[...] = dshift


def inner_backward(fresh, qkv, e_rows, dmix, saved, gain, shift):
    tokens, heads = qkv.shape[0], qkv.shape[1] // (3 * HD)
    ht, hi = heads * MB, heads * HD
    blocks = tokens // MB
    per = PER
    last = blocks // per - 1
    f32 = jnp.float32
    whole = lambda shape: pl.BlockSpec(shape, lambda i: (0, 0))
    three = lambda shape: pl.BlockSpec(shape, lambda i: (last - i, 0, 0))
    two = lambda shape: pl.BlockSpec(shape, lambda i: (last - i, 0))
    save = three((per, HD, ht))
    return pl.pallas_call(
        functools.partial(backward_kernel, heads, per),
        grid=(blocks // per,),
        in_specs=[
            pl.BlockSpec(memory_space=pltpu.SMEM),
            two((per * MB, 3 * hi)), three((per, 1, ht)), two((per * MB, hi)),
            three((per, HD, hi)), save, save, save, save, three((per, 4, ht)),
            whole((HD, ht)), whole((HD, ht)),
        ],
        out_specs=[
            two((per * MB, 3 * hi)), three((per, 1, ht)),
            whole((HD, hi)), whole((HD, ht)), whole((HD, ht)), whole((HD, ht)),
        ],
        out_shape=[
            jax.ShapeDtypeStruct((tokens, 3 * hi), jnp.bfloat16),
            jax.ShapeDtypeStruct((blocks, 1, ht), f32),
            jax.ShapeDtypeStruct((HD, hi), f32),
        ] + [jax.ShapeDtypeStruct((HD, ht), f32)] * 3,
        scratch_shapes=[pltpu.VMEM((HD, hi), f32), pltpu.VMEM((HD, ht), f32)],
        compiler_params=pltpu.CompilerParams(vmem_limit_bytes=48 * 1024 * 1024),
        name="inner_backward",
    )(fresh, qkv, e_rows, dmix, *saved, gain, shift)


def cross_rows(left_side, right_side):
    return lax.dot_general(left_side, right_side, (((0,), (0,)), ((), ())), preferred_element_type=jnp.float32)


def cross_cols(left_side, right_side):
    return lax.dot_general(left_side, right_side, (((1,), (1,)), ((), ())), preferred_element_type=jnp.float32)


def dot(left_side, right_side):
    return jnp.dot(left_side, right_side, preferred_element_type=jnp.float32)


def on_device(
    tokens,
    segments,
    norm_one,
    w_qkv,
    w_lr,
    lr_bias,
    w_gate,
    w_out,
    w_init,
    b_init,
    tnorm_w,
    tnorm_b,
    post_w,
    post_b,
    norm_two,
    w_gate_up,
    w_down,
    grad_out,
):
    floats = jnp.float32
    bf16 = jnp.bfloat16
    both = ("dp", "seq")
    packs, per_seq = lax.axis_size("dp"), lax.axis_size("seq")
    devices = packs * per_seq
    place = lax.axis_index("seq")
    span, width = tokens.shape[1], tokens.shape[2]
    rows = norm_one.shape[0]
    heads_all = lr_bias.shape[0]
    units = w_down.shape[0]
    length = span * per_seq
    blocks = length // MB
    heads = heads_all // per_seq
    aligned = rows % HD == 0
    outer = packs if aligned else 1
    inner = width // (outer * per_seq)
    mine = outer * inner

    def own_rows(array):
        cut = array.reshape((outer, per_seq, inner) + array.shape[1:])
        cut = lax.dynamic_index_in_dim(cut, place, 1, keepdims=False)
        return cut.reshape((mine,) + array.shape[1:])

    def put_rows(array):
        full = jnp.zeros((outer, per_seq, inner) + array.shape[1:], array.dtype)
        part = array.reshape((outer, 1, inner) + array.shape[1:])
        at = (0, place) + (0,) * (part.ndim - 2)
        return lax.dynamic_update_slice(full, part, at).reshape((width,) + array.shape[1:])

    def by_place(weight, parts, out, last):
        depth = weight.shape[0]
        cut = weight.reshape(depth, parts, out, per_seq, last).transpose(3, 0, 1, 2, 4)
        cut = cut.reshape(per_seq, depth, parts * out * last)
        return cut

    def gather_columns(cut):
        got = lax.all_to_all(cut, "seq", 0, 0, tiled=True)
        got = got.reshape(-1, cut.shape[-1])
        return lax.all_gather(got, "dp", axis=0, tiled=True)

    def return_columns(grad):
        got = lax.psum_scatter(grad, "dp", scatter_dimension=0, tiled=True)
        got = got.reshape(per_seq, -1, grad.shape[1])
        return lax.all_to_all(got, "seq", 0, 0, tiled=True)

    def columns_back(got, parts, out, last):
        depth = got.shape[1]
        got = got.reshape(per_seq, depth, parts, out, last).transpose(1, 2, 3, 0, 4)
        return got.reshape(depth, parts * out * per_seq * last)

    inputs = tokens[0].astype(floats)
    lanes = max(HD, heads_all)
    pad = lambda array: jnp.pad(array, ((0, 0), (0, lanes - array.shape[1])))
    tags = segments[0].reshape(span // MB, MB)[:, 0].astype(bf16)
    vectors = jnp.stack([norm_one, norm_two, b_init, tnorm_w, tnorm_b, post_w, post_b], axis=1)
    small = jnp.concatenate([pad(w_init), pad(w_lr), pad(vectors), pad(jnp.broadcast_to(tags[None], (8, span // MB)))], axis=0)
    small = lax.all_gather(small, both, axis=0)
    init_all = small[:, :rows, :HD].reshape(width, HD)
    lr_all = small[:, rows : 2 * rows, :heads_all].reshape(width, heads_all)
    vec_all = small[:, 2 * rows : 3 * rows, :7].reshape(width, 7)
    pack_tags = lax.dynamic_index_in_dim(
        small[:, 3 * rows, : span // MB].reshape(packs, blocks), lax.axis_index("dp"), 0, keepdims=False
    )
    fresh = jnp.concatenate([jnp.ones((1,), jnp.int32), (pack_tags[1:] != pack_tags[:-1]).astype(jnp.int32)])
    gain_one, gain_two = vec_all[:, 0].astype(floats), vec_all[:, 1].astype(floats)
    vec_own = own_rows(vec_all).astype(floats)
    post_gain, post_shift = vec_own[:, 5], vec_own[:, 6]
    lr_cols = lr_all.reshape(width, outer, per_seq, heads // outer)
    lr_own = lax.dynamic_index_in_dim(lr_cols, place, 2, keepdims=False).reshape(width, heads)
    bias_own = lax.dynamic_index_in_dim(lr_bias.reshape(outer, per_seq, heads // outer), place, 1, keepdims=False)
    bias_own = bias_own.reshape(heads).astype(floats)

    w_mix = gather_columns(
        jnp.concatenate([by_place(w_qkv, 3, outer, inner), by_place(w_gate, 1, outer, inner)], axis=2)
    )
    w_gu = gather_columns(by_place(w_gate_up, 2, packs, units))
    if aligned:
        w_o = lax.all_gather(w_out, "dp", axis=0, tiled=True)
    else:
        w_o = own_rows(lax.all_gather(w_out, both, axis=0, tiled=True))
    w_d = lax.all_gather(w_down, "dp", axis=0, tiled=True)
    d_top = lax.all_gather(grad_out[0], "seq", axis=0, tiled=True)

    scale_one = lax.rsqrt(jnp.mean(inputs * inputs, -1, keepdims=True) + EPSILON)
    normed_in = inputs * scale_one
    x_one = lax.all_gather((normed_in * gain_one).astype(bf16), "seq", axis=0, tiled=True)
    qkv = dot(x_one, w_mix[:, : 3 * mine])
    gate_pre = dot(x_one, w_mix[:, 3 * mine :])
    lr_sigm = jax.nn.sigmoid(dot(x_one, lr_own) + bias_own)
    e_rows = (lr_sigm * (1.0 / (HD * MB))).reshape(blocks, MB, heads).transpose(0, 2, 1).reshape(blocks, 1, heads * MB)

    def by_token(vector):
        return jnp.repeat(vector.reshape(heads, HD).T, MB, axis=1)

    init_w = own_rows(init_all).astype(floats).reshape(heads, HD, HD)
    init_w = (init_w - jnp.mean(init_w, -1, keepdims=True)).transpose(2, 0, 1).reshape(HD, heads * HD)
    init_b = vec_own[:, 2].reshape(heads, HD)
    init_b = (init_b - jnp.mean(init_b, -1, keepdims=True)).reshape(-1)
    gain_t, shift_t = by_token(vec_own[:, 3]), by_token(vec_own[:, 4])
    mixed, *saved = inner_forward(fresh, qkv, e_rows, init_w, by_token(init_b), gain_t, shift_t)

    mean_own = jnp.mean(mixed, -1)
    spread_own = jnp.sum((mixed - mean_own[:, None]) ** 2, -1)
    stats = lax.all_gather(jnp.stack([mean_own, spread_own]), "seq", axis=0)
    mean_all = jnp.mean(stats[:, 0], 0)
    var_all = (jnp.sum(stats[:, 1], 0) + mine * jnp.sum((stats[:, 0] - mean_all) ** 2, 0)) * (1.0 / width)
    out_scale = lax.rsqrt(var_all + EPSILON)[:, None]
    out_hat = (mixed - mean_all[:, None]) * out_scale
    normed_out = out_hat * post_gain + post_shift
    gelu_gate, gelu_pull = jax.vjp(jax.nn.gelu, gate_pre)
    gated_unit = (gelu_gate * normed_out).astype(bf16)
    branch = lax.psum_scatter(dot(gated_unit, w_o), "seq", scatter_dimension=0, tiled=True)
    residual = inputs + branch
    scale_two = lax.rsqrt(jnp.mean(residual * residual, -1, keepdims=True) + EPSILON)
    normed_mid = residual * scale_two
    x_two = lax.all_gather((normed_mid * gain_two).astype(bf16), "seq", axis=0, tiled=True)
    hidden_units = packs * units
    gate_up = dot(x_two, w_gu)
    gate_part, up_part = gate_up[:, :hidden_units], gate_up[:, hidden_units:]
    silu_sig = jax.nn.sigmoid(gate_part)
    silu_val = gate_part * silu_sig
    hidden = (silu_val * up_part).astype(bf16)
    down = lax.psum_scatter(dot(hidden, w_d), "seq", scatter_dimension=0, tiled=True)
    result = residual + down

    g_down = lax.psum_scatter(cross_rows(hidden, d_top), "dp", scatter_dimension=0, tiled=True)
    d_hidden = cross_cols(d_top, w_d)
    d_gate = d_hidden * up_part * silu_sig * (1.0 + gate_part * (1.0 - silu_sig))
    d_up = d_hidden * silu_val
    d_gate_up = jnp.concatenate([d_gate, d_up], axis=1).astype(bf16)
    d_xtwo = lax.psum_scatter(cross_cols(d_gate_up, w_gu), "seq", scatter_dimension=0, tiled=True)
    g_gate_up = return_columns(cross_rows(x_two, d_gate_up))
    g_gate_up = columns_back(g_gate_up, 2, packs, units)
    g_two = jnp.sum(d_xtwo * normed_mid, axis=0)
    d_mid = d_xtwo * gain_two
    d_residual = grad_out[0].astype(floats) + scale_two * (
        d_mid - normed_mid * jnp.mean(d_mid * normed_mid, -1, keepdims=True)
    )
    d_branch = lax.all_gather(d_residual.astype(bf16), "seq", axis=0, tiled=True)
    g_out = cross_rows(gated_unit, d_branch)
    if aligned:
        g_out = lax.psum_scatter(g_out, "dp", scatter_dimension=0, tiled=True)
    else:
        g_out = lax.psum_scatter(put_rows(g_out), both, scatter_dimension=0, tiled=True)
    d_unit = cross_cols(d_branch, w_o)
    d_normed = d_unit * gelu_gate
    g_post_w = jnp.sum(d_normed * out_hat, axis=0)
    g_post_b = jnp.sum(d_normed, axis=0)
    d_hat = d_normed * post_gain
    sums = lax.psum(jnp.stack([jnp.sum(d_hat, -1), jnp.sum(d_hat * out_hat, -1)]), "seq") * (1.0 / width)
    d_mixed = out_scale * (d_hat - sums[0][:, None] - out_hat * sums[1][:, None])
    d_gate_pre = gelu_pull(d_unit * normed_out)[0].astype(bf16)
    d_qkv, d_rate, d_w0, d_c0, d_gain, d_shift = inner_backward(fresh, qkv, e_rows, d_mixed, saved, gain_t, shift_t)
    d_rate = d_rate.reshape(blocks, heads, MB).transpose(0, 2, 1).reshape(length, heads)
    d_logit = (d_rate * (1.0 / HD) * lr_sigm * (1.0 - lr_sigm)).astype(bf16)
    d_mix = jnp.concatenate([d_qkv, d_gate_pre], axis=1)
    g_mix = return_columns(cross_rows(x_one, d_mix))
    g_qkv = columns_back(g_mix[:, :, : 3 * mine], 3, outer, inner)
    g_gate = columns_back(g_mix[:, :, 3 * mine :], 1, outer, inner)
    d_xone = lax.psum_scatter(
        cross_cols(d_mix, w_mix) + cross_cols(d_logit, lr_own), "seq", scatter_dimension=0, tiled=True
    )
    g_one = jnp.sum(d_xone * normed_in, axis=0)
    d_inner = d_xone * gain_one
    d_tokens = d_residual + scale_one * (
        d_inner - normed_in * jnp.mean(d_inner * normed_in, -1, keepdims=True)
    )

    def from_token(array):
        return jnp.sum(array.reshape(HD, heads, MB), -1).T.reshape(mine)

    g_vec = jnp.stack(
        [d_c0.reshape(HD, heads, MB)[:, :, 0].T.reshape(mine), from_token(d_gain), from_token(d_shift), g_post_w, g_post_b],
        axis=1,
    )
    g_vec = jnp.concatenate([jnp.stack([g_one, g_two], axis=1), put_rows(g_vec)], axis=1)
    g_init = put_rows(d_w0.reshape(HD, heads, HD).transpose(1, 2, 0).reshape(mine, HD))
    g_lr = cross_rows(x_one, d_logit).reshape(width, outer, 1, heads // outer)
    g_lr = lax.dynamic_update_slice(
        jnp.zeros((width, outer, per_seq, heads // outer), floats), g_lr, (0, 0, place, 0)
    ).reshape(width, heads_all)
    g_bias = jnp.sum(d_logit.astype(floats), axis=0).reshape(outer, 1, heads // outer)
    g_bias = lax.dynamic_update_slice(
        jnp.zeros((outer, per_seq, heads // outer), floats), g_bias, (0, place, 0)
    ).reshape(heads_all)
    wide = HD + heads_all + 7
    g_small = jnp.concatenate([g_init, g_lr, g_vec], axis=1).reshape(devices, rows, wide)
    g_last = jnp.broadcast_to(jnp.pad(g_bias, (0, wide - heads_all)), (devices, 8, wide))
    g_small = jnp.concatenate([g_small, g_last], axis=1)
    g_small = lax.psum_scatter(g_small, both, scatter_dimension=0, tiled=True)[0]
    g_vec = g_small[:rows, HD + heads_all :]
    return (
        result.astype(bf16)[None],
        d_tokens.astype(bf16)[None],
        g_vec[:, 0],
        g_qkv,
        g_small[:rows, HD : HD + heads_all],
        g_small[rows, :heads_all],
        g_gate,
        g_out,
        g_small[:rows, :HD],
        g_vec[:, 2],
        g_vec[:, 3],
        g_vec[:, 4],
        g_vec[:, 5],
        g_vec[:, 6],
        g_vec[:, 1],
        g_gate_up,
        g_down,
    )


def solution(mesh):
    placed = (
        P("dp", "seq", None),
        P("dp", "seq"),
        P(("dp", "seq")),
        P(("dp", "seq"), None),
        P(("dp", "seq"), None),
        P(),
        P(("dp", "seq"), None),
        P(("dp", "seq"), None),
        P(("dp", "seq"), None),
        P(("dp", "seq")),
        P(("dp", "seq")),
        P(("dp", "seq")),
        P(("dp", "seq")),
        P(("dp", "seq")),
        P(("dp", "seq")),
        P(("dp", "seq"), None),
        P(("dp", "seq"), None),
        P("dp", "seq", None),
    )
    return jax.shard_map(
        on_device,
        mesh=mesh,
        in_specs=placed,
        out_specs=(
            P("dp", "seq", None),
            P("dp", "seq", None),
            P(("dp", "seq")),
            P(("dp", "seq"), None),
            P(("dp", "seq"), None),
            P(),
            P(("dp", "seq"), None),
            P(("dp", "seq"), None),
            P(("dp", "seq"), None),
            P(("dp", "seq")),
            P(("dp", "seq")),
            P(("dp", "seq")),
            P(("dp", "seq")),
            P(("dp", "seq")),
            P(("dp", "seq")),
            P(("dp", "seq"), None),
            P(("dp", "seq"), None),
        ),
        check_vma=False,
    )
```

```python
import functools
import jax
import jax.numpy as jnp
from jax import lax
from jax.experimental import pallas as pl
from jax.experimental.pallas import tpu as pltpu
from jax.sharding import PartitionSpec as P

HD = 64
MB = 16
PER = 8
EPSILON = 1e-06


def nn(left, right):
    return lax.dot_general(left, right, (((1,), (0,)), ((), ())), preferred_element_type=jnp.float32)


def nt(left, right):
    return lax.dot_general(left, right, (((1,), (1,)), ((), ())), preferred_element_type=jnp.float32)


def tn(left, right):
    return lax.dot_general(left, right, (((0,), (0,)), ((), ())), preferred_element_type=jnp.float32)


def halves(value):
    high = value.astype(jnp.bfloat16)
    return high, (value - high.astype(jnp.float32)).astype(jnp.bfloat16)


def head_masks(heads):
    ht, hi = heads * MB, heads * HD

    def iota(shape, axis):
        return lax.broadcasted_iota(jnp.int32, shape, axis)

    own = (iota((ht, hi), 0) // MB == iota((ht, hi), 1) // HD).astype(jnp.float32)
    unit = (iota((HD, hi), 0) == iota((HD, hi), 1) % HD).astype(jnp.bfloat16)
    row, col = iota((ht, ht), 0), iota((ht, ht), 1)
    same = (row // MB == col // MB).astype(jnp.bfloat16)
    ts, tt = row % MB, col % MB
    later = jnp.where((row // MB == col // MB) & (ts <= tt), MB / (tt + 1).astype(jnp.float32), 0.0)
    earlier = jnp.where((row // MB == col // MB) & (tt <= ts), MB / (ts + 1).astype(jnp.float32), 0.0)
    return own, unit, same, later, earlier


def spread(rows, own, heads):
    return (jnp.concatenate([rows] * heads, axis=0) * own).astype(jnp.bfloat16)


def fold(values, heads):
    total = values[:MB]
    for h in range(1, heads):
        total = total + values[h * MB : (h + 1) * MB]
    return total


def turned(rows, own, unit, heads):
    wide = jnp.concatenate([rows] * heads, axis=0) * own
    high, low = halves(wide)
    return nt(unit, high) + nt(unit, low)


def mean0(value):
    return jnp.sum(value, axis=0, keepdims=True) * (1.0 / HD)


def forward_kernel(heads, per, fresh_ref, qkv_ref, e_ref, w0_ref, c0_ref, gain_ref, shift_ref,
                   mixed_ref, wsave_ref, hat_ref, slope_ref, gap_ref, bar_ref, rows_ref, w_ref, c_ref):
    hi = heads * HD
    own, unit, same, later, _ = head_masks(heads)
    gain, shift, w0, c0 = gain_ref[...], shift_ref[...], w0_ref[...], c0_ref[...]
    gain2 = gain * gain

    @pl.when(pl.program_id(0) == 0)
    def _():
        w_ref[...] = jnp.zeros_like(w_ref)
        c_ref[...] = jnp.zeros_like(c_ref)

    w, c = w_ref[...], c_ref[...]
    for b in range(per):
        is_fresh = fresh_ref[pl.program_id(0) * per + b] != 0
        lines = slice(b * MB, (b + 1) * MB)
        q, k, v = qkv_ref[lines, :hi], qkv_ref[lines, hi : 2 * hi], qkv_ref[lines, 2 * hi :]
        e = e_ref[b]
        kb, qb = spread(k, own, heads), spread(q, own, heads)
        gap = shift - turned(v - k, own, unit, heads)
        base = gain * gap
        w = jnp.where(is_fresh, w0, w)
        c = jnp.where(is_fresh, c0, c)
        wb = w.astype(jnp.bfloat16)
        wsave_ref[b] = wb
        z = nt(wb, kb) + c
        gz = gain2 * z
        s = lax.rsqrt(mean0(z * z) + EPSILON)
        mean_g = s * mean0(gz) + mean0(base)
        mean_gx = s * (s * mean0(gz * z) + mean0(base * z))
        hat = s * z
        slope = s * (gain2 * hat + base - mean_g - hat * mean_gx)
        eb = (e * slope).astype(jnp.bfloat16)
        mix = (later * (nt(kb, qb) + 1.0)).astype(jnp.bfloat16)
        zbar = nt(wb, qb) + c - nn(eb, mix)
        w = w - nn(eb, kb)
        c = c - nn(eb, same)
        sbar = lax.rsqrt(mean0(zbar * zbar) + EPSILON)
        bar = zbar * sbar
        high, low = halves(gain * bar + shift)
        mixed_ref[lines, :] = q + fold((tn(high, unit) + tn(low, unit)) * own, heads)
        hat_ref[b] = hat
        slope_ref[b] = slope
        gap_ref[b] = gap
        bar_ref[b] = bar
        rows_ref[b] = jnp.concatenate([s, sbar, mean_g, mean_gx], axis=0)
    w_ref[...] = w
    c_ref[...] = c


def inner_forward(fresh, qkv, e_rows, w0, c0, gain, shift):
    tokens, heads = qkv.shape[0], qkv.shape[1] // (3 * HD)
    ht, hi = heads * MB, heads * HD
    blocks = tokens // MB
    per = PER
    f32 = jnp.float32
    whole = lambda shape: pl.BlockSpec(shape, lambda i: (0, 0))
    save = pl.BlockSpec((per, HD, ht), lambda i: (i, 0, 0))
    return pl.pallas_call(
        functools.partial(forward_kernel, heads, per),
        grid=(blocks // per,),
        in_specs=[
            pl.BlockSpec(memory_space=pltpu.SMEM),
            pl.BlockSpec((per * MB, 3 * hi), lambda i: (i, 0)),
            pl.BlockSpec((per, 1, ht), lambda i: (i, 0, 0)),
            whole((HD, hi)), whole((HD, ht)), whole((HD, ht)), whole((HD, ht)),
        ],
        out_specs=[
            pl.BlockSpec((per * MB, hi), lambda i: (i, 0)),
            pl.BlockSpec((per, HD, hi), lambda i: (i, 0, 0)),
            save, save, save, save,
            pl.BlockSpec((per, 4, ht), lambda i: (i, 0, 0)),
        ],
        out_shape=[
            jax.ShapeDtypeStruct((tokens, hi), f32),
            jax.ShapeDtypeStruct((blocks, HD, hi), jnp.bfloat16),
        ] + [jax.ShapeDtypeStruct((blocks, HD, ht), f32)] * 4 + [jax.ShapeDtypeStruct((blocks, 4, ht), f32)],
        scratch_shapes=[pltpu.VMEM((HD, hi), f32), pltpu.VMEM((HD, ht), f32)],
        compiler_params=pltpu.CompilerParams(vmem_limit_bytes=48 * 1024 * 1024),
        name="inner_forward",
    )(fresh, qkv, e_rows, w0, c0, gain, shift)


def backward_kernel(heads, per, fresh_ref, qkv_ref, e_ref, dmix_ref, wsave_ref, hat_ref, slope_ref, gap_ref,
                    bar_ref, rows_ref, gain_ref, shift_ref,
                    dqkv_ref, drate_ref, dw0_ref, dc0_ref, dgain_ref, dshift_ref, a_ref, ac_ref):
    hi, ht = heads * HD, heads * MB
    own, unit, same, later, earlier = head_masks(heads)
    gain = gain_ref[...]
    gain2 = gain * gain
    step = pl.program_id(0)

    @pl.when(step == 0)
    def _():
        for ref in (a_ref, ac_ref, dw0_ref, dc0_ref, dgain_ref, dshift_ref):
            ref[...] = jnp.zeros_like(ref)

    a, ac = a_ref[...], ac_ref[...]
    dw0, dc0, dgain, dshift = dw0_ref[...], dc0_ref[...], dgain_ref[...], dshift_ref[...]
    for b in reversed(range(per)):
        is_fresh = fresh_ref[(pl.num_programs(0) - 1 - step) * per + b] != 0
        lines = slice(b * MB, (b + 1) * MB)
        q, k = qkv_ref[lines, :hi], qkv_ref[lines, hi : 2 * hi]
        e = e_ref[b]
        wb, hat, slope, gap, bar = wsave_ref[b], hat_ref[b], slope_ref[b], gap_ref[b], bar_ref[b]
        s, sbar, mean_g, mean_gx = (rows_ref[b][i : i + 1] for i in range(4))
        kb, qb = spread(k, own, heads), spread(q, own, heads)
        dout = dmix_ref[lines, :]
        dturn = turned(dout, own, unit, heads)
        head = gain * dturn
        dbar = sbar * (head - mean0(head) - bar * mean0(head * bar))
        dbarb = dbar.astype(jnp.bfloat16)
        scores = nt(qb, kb) + 1.0
        mix = earlier * scores
        s2 = s * s
        gh = gain2 * hat
        alpha = s2 * (gain2 - mean_gx)
        kappa = s2 * (gain2 * hat + gap * gain + gh)
        kappa1 = mean_g + mean0(gh)
        kappa2 = 2.0 * mean_gx + mean0(gh * hat)
        ab = a.astype(jnp.bfloat16)
        ka = nt(ab, kb) + ac
        u = -e * (ka + nn(dbarb, mix.astype(jnp.bfloat16)))
        ug = gain2 * u
        r2 = mean0(u * hat)
        r3 = mean0(ug)
        r4 = mean0(ug * hat)
        r5 = mean0(u * slope)
        row1 = s2 * (r3 - r2 * kappa1)
        row2 = s2 * (r4 - r2 * kappa2) + s * r5
        dz = alpha * u - r2 * kappa - row1 - hat * row2
        dzb = dz.astype(jnp.bfloat16)
        dg = s * (u - hat * r2)
        a_next = a + nn(dbarb, qb) + nn(dzb, kb)
        ac_next = ac + nn(dbarb, same) + nn(dzb, same)
        dm = -tn(dbarb, slope.astype(jnp.bfloat16))
        ds = (earlier * e * dm).astype(jnp.bfloat16)
        drate_ref[b] = (jnp.sum(mix * dm, axis=0, keepdims=True) - jnp.sum(ka * slope, axis=0, keepdims=True)) * (1.0 / MB)
        dgb = (gain * dg)
        ndg = fold(tn(dgb.astype(jnp.bfloat16), unit) * own, heads)
        dq = dout + fold(tn(dbarb, wb) * own + nn(ds, kb), heads)
        dk = ndg + fold((tn(dzb, wb) - tn((e * slope).astype(jnp.bfloat16), ab)) * own + tn(ds, qb), heads)
        dqkv_ref[lines, :hi] = dq.astype(jnp.bfloat16)
        dqkv_ref[lines, hi : 2 * hi] = dk.astype(jnp.bfloat16)
        dqkv_ref[lines, 2 * hi :] = (-ndg).astype(jnp.bfloat16)
        dgain = dgain + dturn * bar + dg * (2.0 * gain * hat + gap)
        dshift = dshift + dturn + dgb
        dw0 = dw0 + jnp.where(is_fresh, a_next, 0.0)
        dc0 = dc0 + jnp.where(is_fresh, ac_next, 0.0)
        a = jnp.where(is_fresh, 0.0, a_next)
        ac = jnp.where(is_fresh, 0.0, ac_next)
    a_ref[...] = a
    ac_ref[...] = ac
    dw0_ref[...] = dw0
    dc0_ref[...] = dc0
    dgain_ref[...] = dgain
    dshift_ref[...] = dshift


def inner_backward(fresh, qkv, e_rows, dmix, saved, gain, shift):
    tokens, heads = qkv.shape[0], qkv.shape[1] // (3 * HD)
    ht, hi = heads * MB, heads * HD
    blocks = tokens // MB
    per = PER
    last = blocks // per - 1
    f32 = jnp.float32
    whole = lambda shape: pl.BlockSpec(shape, lambda i: (0, 0))
    three = lambda shape: pl.BlockSpec(shape, lambda i: (last - i, 0, 0))
    two = lambda shape: pl.BlockSpec(shape, lambda i: (last - i, 0))
    save = three((per, HD, ht))
    return pl.pallas_call(
        functools.partial(backward_kernel, heads, per),
        grid=(blocks // per,),
        in_specs=[
            pl.BlockSpec(memory_space=pltpu.SMEM),
            two((per * MB, 3 * hi)), three((per, 1, ht)), two((per * MB, hi)),
            three((per, HD, hi)), save, save, save, save, three((per, 4, ht)),
            whole((HD, ht)), whole((HD, ht)),
        ],
        out_specs=[
            two((per * MB, 3 * hi)), three((per, 1, ht)),
            whole((HD, hi)), whole((HD, ht)), whole((HD, ht)), whole((HD, ht)),
        ],
        out_shape=[
            jax.ShapeDtypeStruct((tokens, 3 * hi), jnp.bfloat16),
            jax.ShapeDtypeStruct((blocks, 1, ht), f32),
            jax.ShapeDtypeStruct((HD, hi), f32),
        ] + [jax.ShapeDtypeStruct((HD, ht), f32)] * 3,
        scratch_shapes=[pltpu.VMEM((HD, hi), f32), pltpu.VMEM((HD, ht), f32)],
        compiler_params=pltpu.CompilerParams(vmem_limit_bytes=48 * 1024 * 1024),
        name="inner_backward",
    )(fresh, qkv, e_rows, dmix, *saved, gain, shift)

MESH = pl.DeviceIdType.MESH


class Wires:
    def __init__(self, send_sems, recv_sems):
        self.send_sems, self.recv_sems, self.used = send_sems, recv_sems, 0

    def copy(self, source, target, device):
        at = self.number()
        return self.numbered(at, source, target, device)

    def number(self):
        self.used += 1
        return self.used - 1

    def numbered(self, at, source, target, device):
        return pltpu.make_async_remote_copy(
            src_ref=source,
            dst_ref=target,
            send_sem=self.send_sems.at[at],
            recv_sem=self.recv_sems.at[at],
            device_id=device,
            device_id_type=MESH,
        )

    def keep(self, source, target):
        at = self.number()
        return pltpu.make_async_copy(source, target, self.send_sems.at[at])


def on_line(step):
    return {"seq": lax.axis_index("seq") + step}


def sibling():
    me = lax.axis_index("seq")
    return {"seq": me + 1 - 2 * lax.rem(me, 2)}


def pack_peer(step):
    packs = lax.axis_size("dp")
    return {"dp": lax.rem(lax.axis_index("dp") + step, packs)}


def seq_peer(step):
    count = lax.axis_size("seq")
    return {"seq": lax.rem(lax.axis_index("seq") + step, count)}


def meet(groups):
    barrier = pltpu.get_barrier_semaphore()
    me, count = lax.axis_index("seq"), lax.axis_size("seq")

    def greet(device):
        pl.semaphore_signal(barrier, inc=1, device_id=device, device_id_type=MESH)

    peers = 0
    if "dp" in groups:
        for step in range(1, lax.axis_size("dp")):
            greet(pack_peer(step))
        peers += lax.axis_size("dp") - 1
    if "seq" in groups:
        for step in range(1, count):
            greet(seq_peer(step))
        peers += count - 1
    elif "line" in groups:
        greet(sibling())

        @pl.when(me >= 2)
        def _():
            greet(on_line(-2))

        @pl.when(me < count - 2)
        def _():
            greet(on_line(2))

        peers += 1 + jnp.minimum(me // 2, 1) + jnp.minimum((count - 1 - me) // 2, 1)
    pl.semaphore_wait(barrier, peers)


def gather_line(wires, source, out, cut):
    me, count = lax.axis_index("seq"), lax.axis_size("seq")
    chips, chip = count // 2, me // 2
    step = source.shape[0] // cut
    other = me + 1 - 2 * lax.rem(me, 2)

    def piece(slot, part):
        return out.at[slot, pl.ds(part * step, step)]

    own = wires.keep(source, out.at[me])
    own.start()
    numbers = {(way, i, part): wires.number() for way in "rlRL" for i in range(chips) for part in range(cut)}

    def copy(way, i, part):
        slot = me - 2 * i if way in "rR" else me + 2 * i
        start = source.at[pl.ds(part * step, step)] if i == 0 else piece(slot, part)
        device = {"r": on_line(2), "l": on_line(-2), "R": sibling(), "L": sibling()}[way]
        return wires.numbered(numbers[way, i, part], start, piece(slot, part), device)

    def arrived(way, i, part):
        if way in "rl":
            slot = me - 2 * (i + 1) if way == "r" else me + 2 * (i + 1)
        else:
            slot = other - 2 * i if way == "R" else other + 2 * i
        there = piece(slot, part)
        wires.numbered(numbers[way, i, part], there, there, sibling()).wait_recv()

    @pl.when(chip < chips - 1)
    def _():
        for part in range(cut):
            copy("r", 0, part).start()

    @pl.when(chip > 0)
    def _():
        for part in range(cut):
            copy("l", 0, part).start()

    for part in range(cut):
        copy("R", 0, part).start()
    for i in range(1, chips):
        for part in range(cut):
            yield

            @pl.when(chip >= i)
            def _():
                arrived("r", i - 1, part)

                @pl.when(chip < chips - 1)
                def _():
                    copy("r", i, part).start()

                copy("R", i, part).start()

            @pl.when(chip + i <= chips - 1)
            def _():
                arrived("l", i - 1, part)

                @pl.when(chip > 0)
                def _():
                    copy("l", i, part).start()

                copy("L", i, part).start()

    yield
    own.wait()
    for i in range(chips):
        for part in range(cut):
            if i == 0:
                arrived("R", 0, part)
                copy("R", 0, part).wait_send()
            else:

                @pl.when(chip >= i)
                def _():
                    arrived("R", i, part)
                    copy("R", i, part).wait_send()

                @pl.when(chip + i <= chips - 1)
                def _():
                    arrived("L", i, part)
                    copy("L", i, part).wait_send()

            @pl.when((chip >= i) & (chip < chips - 1))
            def _():
                copy("r", i, part).wait_send()

            @pl.when((chip + i <= chips - 1) & (chip > 0))
            def _():
                copy("l", i, part).wait_send()


def add_into(out, parts, rows=16):
    def body(i, _):
        lines = pl.ds(pl.multiple_of(i * rows, rows), rows)
        total = parts[0][lines, :].astype(jnp.float32)
        for part in parts[1:]:
            total = total + part[lines, :].astype(jnp.float32)
        out[lines, :] = total.astype(out.dtype)
        return 0

    lax.fori_loop(0, out.shape[0] // rows, body, 0)


def scatter_line(wires, source, out, near, from_left, from_right, to_right, to_left, cut):
    me, count = lax.axis_index("seq"), lax.axis_size("seq")
    chips, chip, core = count // 2, me // 2, lax.rem(me, 2)
    step = source.shape[1] // cut

    def lines(part):
        return pl.ds(part * step, step)

    order = []
    for i in range(chips // 2):
        order += [chips - 1 - i, i]
    order += [chips // 2] if chips % 2 else []
    across = {}
    for dest in order:
        for part in range(cut):
            across[dest, part] = wires.copy(
                source.at[2 * dest + 1 - core, lines(part)], near.at[dest, lines(part)], sibling()
            )
            across[dest, part].start()
    right, left = {}, {}
    for dest in range(chips):
        for part in range(cut):
            right[dest, part] = wires.copy(to_right.at[dest, lines(part)], from_left.at[dest, lines(part)], on_line(2))
            left[dest, part] = wires.copy(to_left.at[dest, lines(part)], from_right.at[dest, lines(part)], on_line(-2))
    for i in range(chips - 1):
        for part in range(cut):
            yield
            for dest, table, inbox, outbox, ahead, first in (
                (chips - 1 - i, right, from_left, to_right, chip < chips - 1 - i, chip == 0),
                (i, left, from_right, to_left, chip > i, chip == chips - 1),
            ):
                terms = [source.at[2 * dest + core, lines(part)], near.at[dest, lines(part)]]

                @pl.when(ahead)
                def _():
                    across[dest, part].wait_recv()

                    @pl.when(first)
                    def _():
                        add_into(outbox.at[dest, lines(part)], terms)

                    @pl.when(jnp.logical_not(first))
                    def _():
                        table[dest, part].wait_recv()
                        add_into(outbox.at[dest, lines(part)], terms + [inbox.at[dest, lines(part)]])

                    table[dest, part].start()

    for part in range(cut):
        yield
        for dest in range(chips):

            @pl.when(chip == dest)
            def _():
                across[dest, part].wait_recv()
                terms = [source.at[2 * dest + core, lines(part)], near.at[dest, lines(part)]]
                if dest > 0:
                    right[dest, part].wait_recv()
                    terms = terms + [from_left.at[dest, lines(part)]]
                if dest < chips - 1:
                    left[dest, part].wait_recv()
                    terms = terms + [from_right.at[dest, lines(part)]]
                add_into(out.at[lines(part)], terms)

    for dest in range(chips):
        for part in range(cut):
            across[dest, part].wait_send()

            @pl.when(chip < dest)
            def _():
                right[dest, part].wait_send()

            @pl.when(chip > dest)
            def _():
                left[dest, part].wait_send()


def swap_seq(wires, source, out):
    me, count = lax.axis_index("seq"), lax.axis_size("seq")
    own = wires.keep(source.at[me], out.at[me])
    own.start()
    sent = []
    for step in range(1, count):
        peer = lax.rem(me + step, count)
        sent.append(wires.copy(source.at[peer], out.at[me], seq_peer(step)))
        sent[-1].start()
    yield
    own.wait()
    for copy in sent:
        copy.wait()


def spread_seq(wires, source, out):
    me, count = lax.axis_index("seq"), lax.axis_size("seq")
    own = wires.keep(source, out.at[me])
    own.start()
    sent = []
    for step in range(1, count):
        sent.append(wires.copy(source, out.at[me], seq_peer(step)))
        sent[-1].start()
    yield
    own.wait()
    for copy in sent:
        copy.wait()


def swap_dp(wires, source, out):
    me, count = lax.axis_index("dp"), lax.axis_size("dp")
    own = wires.keep(source.at[me], out.at[me])
    own.start()
    sent = []
    for step in range(1, count):
        sent.append(wires.copy(source.at[lax.rem(me + step, count)], out.at[me], pack_peer(step)))
        sent[-1].start()
    yield
    own.wait()
    for copy in sent:
        copy.wait()


def spread_dp(wires, source, out):
    me, count = lax.axis_index("dp"), lax.axis_size("dp")
    own = wires.keep(source, out.at[me])
    own.start()
    sent = []
    for step in range(1, count):
        sent.append(wires.copy(source, out.at[me], pack_peer(step)))
        sent[-1].start()
    yield
    own.wait()
    for copy in sent:
        copy.wait()


def run_all(jobs):
    jobs = list(jobs)
    while jobs:
        for job in list(jobs):
            try:
                next(job)
            except StopIteration:
                jobs.remove(job)


def talk(name, cid, groups, operands, outs, plan, copies, in_vmem=(), out_vmem=(), scratch=()):
    n_in, n_out = len(operands), len(outs)

    def kernel(*refs):
        ins, results = refs[:n_in], refs[n_in : n_in + n_out]
        buffers, (send_sems, recv_sems) = refs[n_in + n_out : -2], refs[-2:]
        meet(groups)
        wires = Wires(send_sems, recv_sems)
        run_all(plan(wires, ins, results, buffers))
        assert wires.used <= copies, wires.used

    def where(i, chosen):
        return pl.BlockSpec(memory_space=pltpu.VMEM if i in chosen else pl.ANY)

    return pl.pallas_call(
        kernel,
        out_shape=outs,
        in_specs=[where(i, in_vmem) for i in range(n_in)],
        out_specs=[where(i, out_vmem) for i in range(n_out)],
        scratch_shapes=list(scratch) + [pltpu.SemaphoreType.DMA((copies,)), pltpu.SemaphoreType.DMA((copies,))],
        compiler_params=pltpu.CompilerParams(
            collective_id=cid, has_side_effects=True, vmem_limit_bytes=48 * 1024 * 1024
        ),
        name=name,
    )(*operands)


def all_gather_line(name, cid, block, cut=2):
    count = lax.axis_size("seq")
    out = jax.ShapeDtypeStruct((count,) + block.shape, block.dtype)
    (got,) = talk(
        name, cid, ("line",), (block,), [out],
        lambda wires, ins, outs, _: [gather_line(wires, ins[0], outs[0], cut)],
        1 + 4 * (count // 2) * cut,
    )
    return got.reshape((-1,) + block.shape[1:])


def reduce_scatter_line(name, cid, terms, cut=2):
    count = lax.axis_size("seq")
    rows, width = terms.shape[0] // count, terms.shape[1]
    box = pltpu.VMEM((count // 2, rows, width), terms.dtype)
    (got,) = talk(
        name, cid, ("line",), (terms.reshape(count, rows, width),), [jax.ShapeDtypeStruct((rows, width), jnp.float32)],
        lambda wires, ins, outs, boxes: [scatter_line(wires, ins[0], outs[0], *boxes, cut)],
        3 * (count // 2) * cut, in_vmem=(0,), out_vmem=(0,), scratch=(box,) * 5,
    )
    return got


def columns_out(wires, source, out):
    mine, me, count, packs = lax.axis_index("dp"), lax.axis_index("seq"), lax.axis_size("seq"), lax.axis_size("dp")
    own = wires.keep(source.at[me], out.at[mine, me])
    own.start()
    sent, onward = [], []
    for step in range(1, count):
        sent.append(wires.copy(source.at[lax.rem(me + step, count)], out.at[mine, me], seq_peer(step)))
        sent[-1].start()
    for step in range(1, packs):
        onward.append(wires.copy(source.at[me], out.at[mine, me], pack_peer(step)))
        onward[-1].start()
    for step in range(1, count):
        yield
        sent[step - 1].wait_recv()
        came = out.at[mine, lax.rem(me + count - step, count)]
        for other in range(1, packs):
            onward.append(wires.copy(came, came, pack_peer(other)))
            onward[-1].start()
    yield
    own.wait()
    for copy in sent:
        copy.wait_send()
    for copy in onward:
        copy.wait()


def spread_all(wires, source, out):
    mine, me, count, packs = lax.axis_index("dp"), lax.axis_index("seq"), lax.axis_size("seq"), lax.axis_size("dp")
    own = wires.keep(source, out.at[mine, me])
    own.start()
    sent, onward = [], []
    for step in range(1, packs):
        sent.append(wires.copy(source, out.at[mine, me], pack_peer(step)))
        sent[-1].start()
    for step in range(1, count):
        onward.append(wires.copy(source, out.at[mine, me], seq_peer(step)))
        onward[-1].start()
    for other in range(1, packs):
        yield
        sent[other - 1].wait_recv()
        came = out.at[lax.rem(mine + packs - other, packs), me]
        for step in range(1, count):
            onward.append(wires.copy(came, came, seq_peer(step)))
            onward[-1].start()
    yield
    own.wait()
    for copy in sent:
        copy.wait_send()
    for copy in onward:
        copy.wait()


def shape_of(shape, dtype):
    return jax.ShapeDtypeStruct(tuple(shape), dtype)


def first_exchange(small, mix, wide, block):
    packs, count = lax.axis_size("dp"), lax.axis_size("seq")
    outs = [
        shape_of((packs, count) + small.shape, small.dtype),
        shape_of((packs,) + mix.shape, mix.dtype),
        shape_of(wide.shape, wide.dtype),
        shape_of((count,) + block.shape, block.dtype),
    ]
    cut = 2

    def plan(wires, ins, results, _):
        return [
            columns_out(wires, ins[1], results[1]),
            spread_all(wires, ins[0], results[0]),
            gather_line(wires, ins[3], results[3], cut),
            swap_seq(wires, ins[2], results[2]),
        ]

    copies = 3 * (count * packs + count) + 4 * (count // 2) * cut
    small, mix, wide, block = talk("first_exchange", 1, ("dp", "seq"), (small, mix, wide, block), outs, plan, copies)
    return small, mix.reshape(-1, mix.shape[-1]), wide, block.reshape(-1, block.shape[-1])


def gather_seq(name, cid, block):
    count = lax.axis_size("seq")
    (got,) = talk(
        name, cid, ("seq",), (block,), [shape_of((count,) + block.shape, block.dtype)],
        lambda wires, ins, outs, _: [spread_seq(wires, ins[0], outs[0])], count,
    )
    return got


def scatter_with(name, cid, terms, over_dp, cut=2):
    count, packs = lax.axis_size("seq"), lax.axis_size("dp")
    rows, width = terms.shape[0] // count, terms.shape[1]
    box = pltpu.VMEM((count // 2, rows, width), terms.dtype)
    blocks = [array.reshape((packs, -1) + array.shape[1:]) for array in over_dp]
    outs = [shape_of((rows, width), jnp.float32)] + [shape_of(b.shape, b.dtype) for b in blocks]

    def plan(wires, ins, results, boxes):
        jobs = [swap_dp(wires, source, result) for source, result in zip(ins[1:], results[1:])]
        return jobs + [scatter_line(wires, ins[0], results[0], *boxes, cut)]

    got = talk(
        name, cid, ("line", "dp") if blocks else ("line",), (terms.reshape(count, rows, width), *blocks), outs, plan,
        3 * (count // 2) * cut + packs * len(blocks), in_vmem=(0,), out_vmem=(0,), scratch=(box,) * 5,
    )
    return got


def swap_places(name, cid, arrays):
    count = lax.axis_size("seq")
    return talk(
        name, cid, ("seq",), arrays, [shape_of(a.shape, a.dtype) for a in arrays],
        lambda wires, ins, outs, _: [swap_seq(wires, i, o) for i, o in zip(ins, outs)], count * len(arrays),
    )


def add_packs(array):
    return jnp.sum(array.astype(jnp.float32), axis=0)


def cross_rows(left_side, right_side):
    return lax.dot_general(left_side, right_side, (((0,), (0,)), ((), ())), preferred_element_type=jnp.float32)


def cross_cols(left_side, right_side):
    return lax.dot_general(left_side, right_side, (((1,), (1,)), ((), ())), preferred_element_type=jnp.float32)


def dot(left_side, right_side):
    return jnp.dot(left_side, right_side, preferred_element_type=jnp.float32)


def on_device(
    tokens,
    segments,
    norm_one,
    w_qkv,
    w_lr,
    lr_bias,
    w_gate,
    w_out,
    w_init,
    b_init,
    tnorm_w,
    tnorm_b,
    post_w,
    post_b,
    norm_two,
    w_gate_up,
    w_down,
    grad_out,
):
    floats = jnp.float32
    bf16 = jnp.bfloat16
    both = ("dp", "seq")
    packs, per_seq = lax.axis_size("dp"), lax.axis_size("seq")
    devices = packs * per_seq
    place = lax.axis_index("seq")
    span, width = tokens.shape[1], tokens.shape[2]
    rows = norm_one.shape[0]
    heads_all = lr_bias.shape[0]
    units = w_down.shape[0]
    length = span * per_seq
    blocks = length // MB
    heads = heads_all // per_seq
    aligned = rows % HD == 0
    outer = packs if aligned else 1
    inner = width // (outer * per_seq)
    mine = outer * inner

    def own_rows(array):
        cut = array.reshape((outer, per_seq, inner) + array.shape[1:])
        cut = lax.dynamic_index_in_dim(cut, place, 1, keepdims=False)
        return cut.reshape((mine,) + array.shape[1:])

    def put_rows(array):
        full = jnp.zeros((outer, per_seq, inner) + array.shape[1:], array.dtype)
        part = array.reshape((outer, 1, inner) + array.shape[1:])
        at = (0, place) + (0,) * (part.ndim - 2)
        return lax.dynamic_update_slice(full, part, at).reshape((width,) + array.shape[1:])

    def by_place(weight, parts, out, last):
        depth = weight.shape[0]
        cut = weight.reshape(depth, parts, out, per_seq, last).transpose(3, 0, 1, 2, 4)
        cut = cut.reshape(per_seq, depth, parts * out * last)
        return cut

    def columns_back(got, parts, out, last):
        depth = got.shape[1]
        got = got.reshape(per_seq, depth, parts, out, last).transpose(1, 2, 3, 0, 4)
        return got.reshape(depth, parts * out * per_seq * last)

    lanes = max(HD, heads_all)
    pad = lambda array: jnp.pad(array, ((0, 0), (0, lanes - array.shape[1])))
    tags = segments[0].reshape(span // MB, MB)[:, 0].astype(bf16)
    vectors = jnp.stack([norm_one, norm_two, b_init, tnorm_w, tnorm_b, post_w, post_b], axis=1)
    small = jnp.concatenate([pad(w_init), pad(w_lr), pad(vectors), pad(jnp.broadcast_to(tags[None], (8, span // MB)))], axis=0)
    small, w_mix, gu_part, rows_all = first_exchange(
        small,
        jnp.concatenate([by_place(w_qkv, 3, outer, inner), by_place(w_gate, 1, outer, inner)], axis=2),
        by_place(w_gate_up, 2, packs, units),
        tokens[0],
    )
    small = small.reshape((devices,) + small.shape[2:])
    init_all = small[:, :rows, :HD].reshape(width, HD)
    lr_all = small[:, rows : 2 * rows, :heads_all].reshape(width, heads_all)
    vec_all = small[:, 2 * rows : 3 * rows, :7].reshape(width, 7)
    pack_tags = lax.dynamic_index_in_dim(
        small[:, 3 * rows, : span // MB].reshape(packs, blocks), lax.axis_index("dp"), 0, keepdims=False
    )
    fresh = jnp.concatenate([jnp.ones((1,), jnp.int32), (pack_tags[1:] != pack_tags[:-1]).astype(jnp.int32)])
    gain_one, gain_two = vec_all[:, 0].astype(floats), vec_all[:, 1].astype(floats)
    vec_own = own_rows(vec_all).astype(floats)
    post_gain, post_shift = vec_own[:, 5], vec_own[:, 6]
    lr_cols = lr_all.reshape(width, outer, per_seq, heads // outer)
    lr_own = lax.dynamic_index_in_dim(lr_cols, place, 2, keepdims=False).reshape(width, heads)
    bias_own = lax.dynamic_index_in_dim(lr_bias.reshape(outer, per_seq, heads // outer), place, 1, keepdims=False)
    bias_own = bias_own.reshape(heads).astype(floats)

    w_gu = lax.all_gather(gu_part.reshape(-1, gu_part.shape[-1]), "dp", axis=0, tiled=True)
    if aligned:
        w_o = lax.all_gather(w_out, "dp", axis=0, tiled=True)
    else:
        w_o = own_rows(lax.all_gather(w_out, both, axis=0, tiled=True))
    w_d = lax.all_gather(w_down, "dp", axis=0, tiled=True)
    d_top = lax.all_gather(grad_out[0], "seq", axis=0, tiled=True)

    inputs = rows_all.astype(floats)
    scale_one = lax.rsqrt(jnp.mean(inputs * inputs, -1, keepdims=True) + EPSILON)
    normed_in = inputs * scale_one
    x_one = (normed_in * gain_one).astype(bf16)
    qkv = dot(x_one, w_mix[:, : 3 * mine])
    gate_pre = dot(x_one, w_mix[:, 3 * mine :])
    lr_sigm = jax.nn.sigmoid(dot(x_one, lr_own) + bias_own)
    e_rows = (lr_sigm * (1.0 / (HD * MB))).reshape(blocks, MB, heads).transpose(0, 2, 1).reshape(blocks, 1, heads * MB)

    def by_token(vector):
        return jnp.repeat(vector.reshape(heads, HD).T, MB, axis=1)

    init_w = own_rows(init_all).astype(floats).reshape(heads, HD, HD)
    init_w = (init_w - jnp.mean(init_w, -1, keepdims=True)).transpose(2, 0, 1).reshape(HD, heads * HD)
    init_b = vec_own[:, 2].reshape(heads, HD)
    init_b = (init_b - jnp.mean(init_b, -1, keepdims=True)).reshape(-1)
    gain_t, shift_t = by_token(vec_own[:, 3]), by_token(vec_own[:, 4])
    mixed, *saved = inner_forward(fresh, qkv, e_rows, init_w, by_token(init_b), gain_t, shift_t)

    mean_own = jnp.mean(mixed, -1)
    spread_own = jnp.sum((mixed - mean_own[:, None]) ** 2, -1)
    stats = gather_seq("share_moments", 2, jnp.stack([mean_own, spread_own]))
    mean_all = jnp.mean(stats[:, 0], 0)
    var_all = (jnp.sum(stats[:, 1], 0) + mine * jnp.sum((stats[:, 0] - mean_all) ** 2, 0)) * (1.0 / width)
    out_scale = lax.rsqrt(var_all + EPSILON)[:, None]
    out_hat = (mixed - mean_all[:, None]) * out_scale
    normed_out = out_hat * post_gain + post_shift
    gelu_gate, gelu_pull = jax.vjp(jax.nn.gelu, gate_pre)
    gated_unit = (gelu_gate * normed_out).astype(bf16)
    (branch,) = scatter_with("scatter_branch", 3, dot(gated_unit, w_o).astype(bf16), ())
    inputs = tokens[0].astype(floats)
    residual = inputs + branch
    scale_two = lax.rsqrt(jnp.mean(residual * residual, -1, keepdims=True) + EPSILON)
    normed_mid = residual * scale_two
    x_two = all_gather_line("gather_mid", 4, (normed_mid * gain_two).astype(bf16))
    hidden_units = packs * units
    gate_up = dot(x_two, w_gu)
    gate_part, up_part = gate_up[:, :hidden_units], gate_up[:, hidden_units:]
    silu_sig = jax.nn.sigmoid(gate_part)
    silu_val = gate_part * silu_sig
    hidden = (silu_val * up_part).astype(bf16)
    down = lax.psum_scatter(dot(hidden, w_d).astype(bf16), "seq", scatter_dimension=0, tiled=True)
    result = residual + down.astype(floats)

    g_down = cross_rows(hidden, d_top).astype(bf16)
    d_hidden = cross_cols(d_top, w_d)
    d_gate = d_hidden * up_part * silu_sig * (1.0 + gate_part * (1.0 - silu_sig))
    d_up = d_hidden * silu_val
    d_gate_up = jnp.concatenate([d_gate, d_up], axis=1).astype(bf16)
    d_xtwo, g_down = scatter_with("scatter_mid", 5, cross_cols(d_gate_up, w_gu).astype(bf16), (g_down,))
    g_down = add_packs(g_down)
    g_gate_up = lax.psum_scatter(cross_rows(x_two, d_gate_up).astype(bf16), "dp", scatter_dimension=0, tiled=True)
    g_two = jnp.sum(d_xtwo * normed_mid, axis=0)
    d_mid = d_xtwo * gain_two
    d_residual = grad_out[0].astype(floats) + scale_two * (
        d_mid - normed_mid * jnp.mean(d_mid * normed_mid, -1, keepdims=True)
    )
    d_branch = all_gather_line("gather_branch", 6, d_residual.astype(bf16))
    g_out = cross_rows(gated_unit, d_branch).astype(bf16)
    if aligned:
        g_out = lax.psum_scatter(g_out, "dp", scatter_dimension=0, tiled=True)
    else:
        g_out = lax.psum_scatter(put_rows(g_out), both, scatter_dimension=0, tiled=True)
    g_out = g_out.astype(floats)
    d_unit = cross_cols(d_branch, w_o)
    d_normed = d_unit * gelu_gate
    g_post_w = jnp.sum(d_normed * out_hat, axis=0)
    g_post_b = jnp.sum(d_normed, axis=0)
    d_hat = d_normed * post_gain
    sums = gather_seq("share_sums", 7, jnp.stack([jnp.sum(d_hat, -1), jnp.sum(d_hat * out_hat, -1)]))
    sums = jnp.sum(sums, 0) * (1.0 / width)
    d_mixed = out_scale * (d_hat - sums[0][:, None] - out_hat * sums[1][:, None])
    d_gate_pre = gelu_pull(d_unit * normed_out)[0].astype(bf16)
    d_qkv, d_rate, d_w0, d_c0, d_gain, d_shift = inner_backward(fresh, qkv, e_rows, d_mixed, saved, gain_t, shift_t)
    d_rate = d_rate.reshape(blocks, heads, MB).transpose(0, 2, 1).reshape(length, heads)
    d_logit = (d_rate * (1.0 / HD) * lr_sigm * (1.0 - lr_sigm)).astype(bf16)
    d_mix = jnp.concatenate([d_qkv, d_gate_pre], axis=1)
    g_mix = cross_rows(x_one, d_mix).astype(bf16)
    d_xone = cross_cols(d_mix, w_mix) + cross_cols(d_logit, lr_own)
    g_one = jnp.sum(d_xone * normed_in, axis=0)
    def from_token(array):
        return jnp.sum(array.reshape(HD, heads, MB), -1).T.reshape(mine)

    g_vec = jnp.stack(
        [d_c0.reshape(HD, heads, MB)[:, :, 0].T.reshape(mine), from_token(d_gain), from_token(d_shift), g_post_w, g_post_b],
        axis=1,
    )
    g_vec = jnp.concatenate([jnp.stack([g_one, g_two], axis=1), put_rows(g_vec)], axis=1)
    g_init = put_rows(d_w0.reshape(HD, heads, HD).transpose(1, 2, 0).reshape(mine, HD))
    g_lr = cross_rows(x_one, d_logit).reshape(width, outer, 1, heads // outer)
    g_lr = lax.dynamic_update_slice(
        jnp.zeros((width, outer, per_seq, heads // outer), floats), g_lr, (0, 0, place, 0)
    ).reshape(width, heads_all)
    g_bias = jnp.sum(d_logit.astype(floats), axis=0).reshape(outer, 1, heads // outer)
    g_bias = lax.dynamic_update_slice(
        jnp.zeros((outer, per_seq, heads // outer), floats), g_bias, (0, place, 0)
    ).reshape(heads_all)
    wide = HD + heads_all + 7
    g_small = jnp.concatenate([g_init, g_lr, g_vec], axis=1).reshape(devices, rows, wide)
    g_last = jnp.broadcast_to(jnp.pad(g_bias, (0, wide - heads_all)), (devices, 8, wide))
    g_small = jnp.concatenate([g_small, g_last], axis=1)
    d_xone, g_mix, g_small = scatter_with("scatter_first", 8, d_xone.astype(bf16), (g_mix, g_small))
    place_rows = lambda array: array.reshape((per_seq, -1) + array.shape[1:])
    g_gate_up, g_mix, g_small = swap_places(
        "return_columns",
        9,
        (place_rows(g_gate_up), place_rows(add_packs(g_mix).astype(bf16)), place_rows(add_packs(g_small))),
    )
    g_gate_up = columns_back(g_gate_up.astype(floats), 2, packs, units)
    g_mix = g_mix.astype(floats)
    g_qkv = columns_back(g_mix[:, :, : 3 * mine], 3, outer, inner)
    g_gate = columns_back(g_mix[:, :, 3 * mine :], 1, outer, inner)
    g_small = jnp.sum(g_small, 0).reshape(-1, wide)
    scale_one = lax.rsqrt(jnp.mean(inputs * inputs, -1, keepdims=True) + EPSILON)
    normed_in = inputs * scale_one
    d_inner = d_xone * gain_one
    d_tokens = d_residual + scale_one * (
        d_inner - normed_in * jnp.mean(d_inner * normed_in, -1, keepdims=True)
    )
    g_vec = g_small[:rows, HD + heads_all :]
    return (
        result.astype(bf16)[None],
        d_tokens.astype(bf16)[None],
        g_vec[:, 0],
        g_qkv,
        g_small[:rows, HD : HD + heads_all],
        g_small[rows, :heads_all],
        g_gate,
        g_out,
        g_small[:rows, :HD],
        g_vec[:, 2],
        g_vec[:, 3],
        g_vec[:, 4],
        g_vec[:, 5],
        g_vec[:, 6],
        g_vec[:, 1],
        g_gate_up,
        g_down,
    )


def solution(mesh):
    placed = (
        P("dp", "seq", None),
        P("dp", "seq"),
        P(("dp", "seq")),
        P(("dp", "seq"), None),
        P(("dp", "seq"), None),
        P(),
        P(("dp", "seq"), None),
        P(("dp", "seq"), None),
        P(("dp", "seq"), None),
        P(("dp", "seq")),
        P(("dp", "seq")),
        P(("dp", "seq")),
        P(("dp", "seq")),
        P(("dp", "seq")),
        P(("dp", "seq")),
        P(("dp", "seq"), None),
        P(("dp", "seq"), None),
        P("dp", "seq", None),
    )
    return jax.shard_map(
        on_device,
        mesh=mesh,
        in_specs=placed,
        out_specs=(
            P("dp", "seq", None),
            P("dp", "seq", None),
            P(("dp", "seq")),
            P(("dp", "seq"), None),
            P(("dp", "seq"), None),
            P(),
            P(("dp", "seq"), None),
            P(("dp", "seq"), None),
            P(("dp", "seq"), None),
            P(("dp", "seq")),
            P(("dp", "seq")),
            P(("dp", "seq")),
            P(("dp", "seq")),
            P(("dp", "seq")),
            P(("dp", "seq")),
            P(("dp", "seq"), None),
            P(("dp", "seq"), None),
        ),
        check_vma=False,
    )
```

```python
import functools
import jax
import jax.numpy as jnp
from jax import lax
from jax.experimental import pallas as pl
from jax.experimental.pallas import tpu as pltpu
from jax.sharding import PartitionSpec as P

HD = 64
MB = 16
PER = 8
EPSILON = 1e-06


def nn(left, right):
    return lax.dot_general(left, right, (((1,), (0,)), ((), ())), preferred_element_type=jnp.float32)


def nt(left, right):
    return lax.dot_general(left, right, (((1,), (1,)), ((), ())), preferred_element_type=jnp.float32)


def tn(left, right):
    return lax.dot_general(left, right, (((0,), (0,)), ((), ())), preferred_element_type=jnp.float32)


def halves(value):
    high = value.astype(jnp.bfloat16)
    return high, (value - high.astype(jnp.float32)).astype(jnp.bfloat16)


def head_masks(heads):
    ht, hi = heads * MB, heads * HD

    def iota(shape, axis):
        return lax.broadcasted_iota(jnp.int32, shape, axis)

    own = (iota((ht, hi), 0) // MB == iota((ht, hi), 1) // HD).astype(jnp.float32)
    unit = (iota((HD, hi), 0) == iota((HD, hi), 1) % HD).astype(jnp.bfloat16)
    row, col = iota((ht, ht), 0), iota((ht, ht), 1)
    same = (row // MB == col // MB).astype(jnp.bfloat16)
    ts, tt = row % MB, col % MB
    later = jnp.where((row // MB == col // MB) & (ts <= tt), MB / (tt + 1).astype(jnp.float32), 0.0)
    earlier = jnp.where((row // MB == col // MB) & (tt <= ts), MB / (ts + 1).astype(jnp.float32), 0.0)
    return own, unit, same, later, earlier


def spread(rows, own, heads):
    return (jnp.concatenate([rows] * heads, axis=0) * own).astype(jnp.bfloat16)


def fold(values, heads):
    total = values[:MB]
    for h in range(1, heads):
        total = total + values[h * MB : (h + 1) * MB]
    return total


def turned(rows, own, unit, heads):
    wide = jnp.concatenate([rows] * heads, axis=0) * own
    high, low = halves(wide)
    return nt(unit, high) + nt(unit, low)


def mean0(value):
    return jnp.sum(value, axis=0, keepdims=True) * (1.0 / HD)


def forward_kernel(heads, per, moved, fresh_ref, qkv_ref, e_ref, w0_ref, c0_ref, gain_ref, shift_ref, *refs):
    sources, refs = refs[:moved], refs[moved:]
    mixed_ref, wsave_ref, hat_ref, slope_ref, gap_ref, bar_ref, rows_ref = refs[:7]
    results, (w_ref, c_ref, send_sems, recv_sems) = refs[7 : 7 + moved], refs[7 + moved :]
    beside(("seq",), send_sems, recv_sems, lambda wires: [swap_seq(wires, a, b) for a, b in zip(sources, results)])
    hi = heads * HD
    own, unit, same, later, _ = head_masks(heads)
    gain, shift, w0, c0 = gain_ref[...], shift_ref[...], w0_ref[...], c0_ref[...]
    gain2 = gain * gain

    @pl.when(pl.program_id(0) == 0)
    def _():
        w_ref[...] = jnp.zeros_like(w_ref)
        c_ref[...] = jnp.zeros_like(c_ref)

    w, c = w_ref[...], c_ref[...]
    for b in range(per):
        is_fresh = fresh_ref[pl.program_id(0) * per + b] != 0
        lines = slice(b * MB, (b + 1) * MB)
        q, k, v = qkv_ref[lines, :hi], qkv_ref[lines, hi : 2 * hi], qkv_ref[lines, 2 * hi :]
        e = e_ref[b]
        kb, qb = spread(k, own, heads), spread(q, own, heads)
        gap = shift - turned(v - k, own, unit, heads)
        base = gain * gap
        w = jnp.where(is_fresh, w0, w)
        c = jnp.where(is_fresh, c0, c)
        wb = w.astype(jnp.bfloat16)
        wsave_ref[b] = wb
        z = nt(wb, kb) + c
        gz = gain2 * z
        s = lax.rsqrt(mean0(z * z) + EPSILON)
        mean_g = s * mean0(gz) + mean0(base)
        mean_gx = s * (s * mean0(gz * z) + mean0(base * z))
        hat = s * z
        slope = s * (gain2 * hat + base - mean_g - hat * mean_gx)
        eb = (e * slope).astype(jnp.bfloat16)
        mix = (later * (nt(kb, qb) + 1.0)).astype(jnp.bfloat16)
        zbar = nt(wb, qb) + c - nn(eb, mix)
        w = w - nn(eb, kb)
        c = c - nn(eb, same)
        sbar = lax.rsqrt(mean0(zbar * zbar) + EPSILON)
        bar = zbar * sbar
        high, low = halves(gain * bar + shift)
        mixed_ref[lines, :] = q + fold((tn(high, unit) + tn(low, unit)) * own, heads)
        hat_ref[b] = hat
        slope_ref[b] = slope
        gap_ref[b] = gap
        bar_ref[b] = bar
        rows_ref[b] = jnp.concatenate([s, sbar, mean_g, mean_gx], axis=0)
    w_ref[...] = w
    c_ref[...] = c


def inner_forward(cid, fresh, qkv, e_rows, w0, c0, gain, shift, arrays):
    tokens, heads = qkv.shape[0], qkv.shape[1] // (3 * HD)
    ht, hi = heads * MB, heads * HD
    blocks = tokens // MB
    per = PER
    f32 = jnp.float32
    whole = lambda shape: pl.BlockSpec(shape, lambda i: (0, 0))
    save = pl.BlockSpec((per, HD, ht), lambda i: (i, 0, 0))
    return pl.pallas_call(
        functools.partial(forward_kernel, heads, per, len(arrays)),
        grid=(blocks // per,),
        in_specs=[
            pl.BlockSpec(memory_space=pltpu.SMEM),
            pl.BlockSpec((per * MB, 3 * hi), lambda i: (i, 0)),
            pl.BlockSpec((per, 1, ht), lambda i: (i, 0, 0)),
            whole((HD, hi)), whole((HD, ht)), whole((HD, ht)), whole((HD, ht)),
        ] + [pl.BlockSpec(memory_space=pl.ANY)] * len(arrays),
        out_specs=[
            pl.BlockSpec((per * MB, hi), lambda i: (i, 0)),
            pl.BlockSpec((per, HD, hi), lambda i: (i, 0, 0)),
            save, save, save, save,
            pl.BlockSpec((per, 4, ht), lambda i: (i, 0, 0)),
        ] + [pl.BlockSpec(memory_space=pl.ANY)] * len(arrays),
        out_shape=[
            jax.ShapeDtypeStruct((tokens, hi), f32),
            jax.ShapeDtypeStruct((blocks, HD, hi), jnp.bfloat16),
        ] + [jax.ShapeDtypeStruct((blocks, HD, ht), f32)] * 4 + [jax.ShapeDtypeStruct((blocks, 4, ht), f32)]
        + [shape_of(a.shape, a.dtype) for a in arrays],
        scratch_shapes=[pltpu.VMEM((HD, hi), f32), pltpu.VMEM((HD, ht), f32)] + wire_sems(len(arrays) * lax.axis_size("seq")),
        compiler_params=pltpu.CompilerParams(
            vmem_limit_bytes=48 * 1024 * 1024, collective_id=cid, has_side_effects=True
        ),
        name="inner_forward",
    )(fresh, qkv, e_rows, w0, c0, gain, shift, *arrays)


def backward_kernel(heads, per, over_seq, over_dp, fresh_ref, qkv_ref, e_ref, dmix_ref, wsave_ref, hat_ref, slope_ref,
                    gap_ref, bar_ref, rows_ref, gain_ref, shift_ref, *refs):
    moved = over_seq + over_dp
    sources, refs = refs[:moved], refs[moved:]
    dqkv_ref, drate_ref, dw0_ref, dc0_ref, dgain_ref, dshift_ref = refs[:6]
    results, (a_ref, ac_ref, send_sems, recv_sems) = refs[6 : 6 + moved], refs[6 + moved :]
    swaps = [swap_seq] * over_seq + [swap_dp] * over_dp
    beside(
        ("seq", "dp"), send_sems, recv_sems,
        lambda wires: [swap(wires, a, b) for swap, a, b in zip(swaps, sources, results)],
    )
    hi, ht = heads * HD, heads * MB
    own, unit, same, later, earlier = head_masks(heads)
    gain = gain_ref[...]
    gain2 = gain * gain
    step = pl.program_id(0)

    @pl.when(step == 0)
    def _():
        for ref in (a_ref, ac_ref, dw0_ref, dc0_ref, dgain_ref, dshift_ref):
            ref[...] = jnp.zeros_like(ref)

    a, ac = a_ref[...], ac_ref[...]
    dw0, dc0, dgain, dshift = dw0_ref[...], dc0_ref[...], dgain_ref[...], dshift_ref[...]
    for b in reversed(range(per)):
        is_fresh = fresh_ref[(pl.num_programs(0) - 1 - step) * per + b] != 0
        lines = slice(b * MB, (b + 1) * MB)
        q, k = qkv_ref[lines, :hi], qkv_ref[lines, hi : 2 * hi]
        e = e_ref[b]
        wb, hat, slope, gap, bar = wsave_ref[b], hat_ref[b], slope_ref[b], gap_ref[b], bar_ref[b]
        s, sbar, mean_g, mean_gx = (rows_ref[b][i : i + 1] for i in range(4))
        kb, qb = spread(k, own, heads), spread(q, own, heads)
        dout = dmix_ref[lines, :]
        dturn = turned(dout, own, unit, heads)
        head = gain * dturn
        dbar = sbar * (head - mean0(head) - bar * mean0(head * bar))
        dbarb = dbar.astype(jnp.bfloat16)
        scores = nt(qb, kb) + 1.0
        mix = earlier * scores
        s2 = s * s
        gh = gain2 * hat
        alpha = s2 * (gain2 - mean_gx)
        kappa = s2 * (gain2 * hat + gap * gain + gh)
        kappa1 = mean_g + mean0(gh)
        kappa2 = 2.0 * mean_gx + mean0(gh * hat)
        ab = a.astype(jnp.bfloat16)
        ka = nt(ab, kb) + ac
        u = -e * (ka + nn(dbarb, mix.astype(jnp.bfloat16)))
        ug = gain2 * u
        r2 = mean0(u * hat)
        r3 = mean0(ug)
        r4 = mean0(ug * hat)
        r5 = mean0(u * slope)
        row1 = s2 * (r3 - r2 * kappa1)
        row2 = s2 * (r4 - r2 * kappa2) + s * r5
        dz = alpha * u - r2 * kappa - row1 - hat * row2
        dzb = dz.astype(jnp.bfloat16)
        dg = s * (u - hat * r2)
        a_next = a + nn(dbarb, qb) + nn(dzb, kb)
        ac_next = ac + nn(dbarb, same) + nn(dzb, same)
        dm = -tn(dbarb, slope.astype(jnp.bfloat16))
        ds = (earlier * e * dm).astype(jnp.bfloat16)
        drate_ref[b] = (jnp.sum(mix * dm, axis=0, keepdims=True) - jnp.sum(ka * slope, axis=0, keepdims=True)) * (1.0 / MB)
        dgb = (gain * dg)
        ndg = fold(tn(dgb.astype(jnp.bfloat16), unit) * own, heads)
        dq = dout + fold(tn(dbarb, wb) * own + nn(ds, kb), heads)
        dk = ndg + fold((tn(dzb, wb) - tn((e * slope).astype(jnp.bfloat16), ab)) * own + tn(ds, qb), heads)
        dqkv_ref[lines, :hi] = dq.astype(jnp.bfloat16)
        dqkv_ref[lines, hi : 2 * hi] = dk.astype(jnp.bfloat16)
        dqkv_ref[lines, 2 * hi :] = (-ndg).astype(jnp.bfloat16)
        dgain = dgain + dturn * bar + dg * (2.0 * gain * hat + gap)
        dshift = dshift + dturn + dgb
        dw0 = dw0 + jnp.where(is_fresh, a_next, 0.0)
        dc0 = dc0 + jnp.where(is_fresh, ac_next, 0.0)
        a = jnp.where(is_fresh, 0.0, a_next)
        ac = jnp.where(is_fresh, 0.0, ac_next)
    a_ref[...] = a
    ac_ref[...] = ac
    dw0_ref[...] = dw0
    dc0_ref[...] = dc0
    dgain_ref[...] = dgain
    dshift_ref[...] = dshift


def inner_backward(cid, fresh, qkv, e_rows, dmix, saved, gain, shift, seq_arrays, dp_arrays):
    arrays = tuple(seq_arrays) + tuple(dp_arrays)
    tokens, heads = qkv.shape[0], qkv.shape[1] // (3 * HD)
    ht, hi = heads * MB, heads * HD
    blocks = tokens // MB
    per = PER
    last = blocks // per - 1
    f32 = jnp.float32
    whole = lambda shape: pl.BlockSpec(shape, lambda i: (0, 0))
    three = lambda shape: pl.BlockSpec(shape, lambda i: (last - i, 0, 0))
    two = lambda shape: pl.BlockSpec(shape, lambda i: (last - i, 0))
    save = three((per, HD, ht))
    return pl.pallas_call(
        functools.partial(backward_kernel, heads, per, len(seq_arrays), len(dp_arrays)),
        grid=(blocks // per,),
        in_specs=[
            pl.BlockSpec(memory_space=pltpu.SMEM),
            two((per * MB, 3 * hi)), three((per, 1, ht)), two((per * MB, hi)),
            three((per, HD, hi)), save, save, save, save, three((per, 4, ht)),
            whole((HD, ht)), whole((HD, ht)),
        ] + [pl.BlockSpec(memory_space=pl.ANY)] * len(arrays),
        out_specs=[
            two((per * MB, 3 * hi)), three((per, 1, ht)),
            whole((HD, hi)), whole((HD, ht)), whole((HD, ht)), whole((HD, ht)),
        ] + [pl.BlockSpec(memory_space=pl.ANY)] * len(arrays),
        out_shape=[
            jax.ShapeDtypeStruct((tokens, 3 * hi), jnp.bfloat16),
            jax.ShapeDtypeStruct((blocks, 1, ht), f32),
            jax.ShapeDtypeStruct((HD, hi), f32),
        ] + [jax.ShapeDtypeStruct((HD, ht), f32)] * 3 + [shape_of(a.shape, a.dtype) for a in arrays],
        scratch_shapes=[pltpu.VMEM((HD, hi), f32), pltpu.VMEM((HD, ht), f32)]
        + wire_sems(len(seq_arrays) * lax.axis_size("seq") + len(dp_arrays) * lax.axis_size("dp")),
        compiler_params=pltpu.CompilerParams(
            vmem_limit_bytes=48 * 1024 * 1024, collective_id=cid, has_side_effects=True
        ),
        name="inner_backward",
    )(fresh, qkv, e_rows, dmix, *saved, gain, shift, *arrays)

MESH = pl.DeviceIdType.MESH


class Wires:
    def __init__(self, send_sems, recv_sems, started=False):
        self.send_sems, self.recv_sems, self.used, self.started = send_sems, recv_sems, 0, started

    def begin(self, copy):
        if not self.started:
            copy.start()
        return copy

    def copy(self, source, target, device):
        at = self.number()
        return self.numbered(at, source, target, device)

    def number(self):
        self.used += 1
        return self.used - 1

    def numbered(self, at, source, target, device):
        return pltpu.make_async_remote_copy(
            src_ref=source,
            dst_ref=target,
            send_sem=self.send_sems.at[at],
            recv_sem=self.recv_sems.at[at],
            device_id=device,
            device_id_type=MESH,
        )

    def keep(self, source, target):
        at = self.number()
        return pltpu.make_async_copy(source, target, self.send_sems.at[at])


def on_line(step):
    return {"seq": lax.axis_index("seq") + step}


def sibling():
    me = lax.axis_index("seq")
    return {"seq": me + 1 - 2 * lax.rem(me, 2)}


def pack_peer(step):
    packs = lax.axis_size("dp")
    return {"dp": lax.rem(lax.axis_index("dp") + step, packs)}


def seq_peer(step):
    count = lax.axis_size("seq")
    return {"seq": lax.rem(lax.axis_index("seq") + step, count)}


def meet(groups):
    barrier = pltpu.get_barrier_semaphore()
    me, count = lax.axis_index("seq"), lax.axis_size("seq")

    def greet(device):
        pl.semaphore_signal(barrier, inc=1, device_id=device, device_id_type=MESH)

    peers = 0
    if "dp" in groups:
        for step in range(1, lax.axis_size("dp")):
            greet(pack_peer(step))
        peers += lax.axis_size("dp") - 1
    if "seq" in groups:
        for step in range(1, count):
            greet(seq_peer(step))
        peers += count - 1
    elif "line" in groups:
        greet(sibling())

        @pl.when(me >= 2)
        def _():
            greet(on_line(-2))

        @pl.when(me < count - 2)
        def _():
            greet(on_line(2))

        peers += 1 + jnp.minimum(me // 2, 1) + jnp.minimum((count - 1 - me) // 2, 1)
    pl.semaphore_wait(barrier, peers)


def gather_line(wires, source, out, cut):
    me, count = lax.axis_index("seq"), lax.axis_size("seq")
    chips, chip = count // 2, me // 2
    step = source.shape[0] // cut
    other = me + 1 - 2 * lax.rem(me, 2)

    def piece(slot, part):
        return out.at[slot, pl.ds(part * step, step)]

    own = wires.keep(source, out.at[me])
    own.start()
    numbers = {(way, i, part): wires.number() for way in "rlRL" for i in range(chips) for part in range(cut)}

    def copy(way, i, part):
        slot = me - 2 * i if way in "rR" else me + 2 * i
        start = source.at[pl.ds(part * step, step)] if i == 0 else piece(slot, part)
        device = {"r": on_line(2), "l": on_line(-2), "R": sibling(), "L": sibling()}[way]
        return wires.numbered(numbers[way, i, part], start, piece(slot, part), device)

    def arrived(way, i, part):
        if way in "rl":
            slot = me - 2 * (i + 1) if way == "r" else me + 2 * (i + 1)
        else:
            slot = other - 2 * i if way == "R" else other + 2 * i
        there = piece(slot, part)
        wires.numbered(numbers[way, i, part], there, there, sibling()).wait_recv()

    @pl.when(chip < chips - 1)
    def _():
        for part in range(cut):
            copy("r", 0, part).start()

    @pl.when(chip > 0)
    def _():
        for part in range(cut):
            copy("l", 0, part).start()

    for part in range(cut):
        copy("R", 0, part).start()
    for i in range(1, chips):
        for part in range(cut):
            yield True

            @pl.when(chip >= i)
            def _():
                arrived("r", i - 1, part)

                @pl.when(chip < chips - 1)
                def _():
                    copy("r", i, part).start()

                copy("R", i, part).start()

            @pl.when(chip + i <= chips - 1)
            def _():
                arrived("l", i - 1, part)

                @pl.when(chip > 0)
                def _():
                    copy("l", i, part).start()

                copy("L", i, part).start()

    yield True
    own.wait()
    for i in range(chips):
        for part in range(cut):
            if i == 0:
                arrived("R", 0, part)
                copy("R", 0, part).wait_send()
            else:

                @pl.when(chip >= i)
                def _():
                    arrived("R", i, part)
                    copy("R", i, part).wait_send()

                @pl.when(chip + i <= chips - 1)
                def _():
                    arrived("L", i, part)
                    copy("L", i, part).wait_send()

            @pl.when((chip >= i) & (chip < chips - 1))
            def _():
                copy("r", i, part).wait_send()

            @pl.when((chip + i <= chips - 1) & (chip > 0))
            def _():
                copy("l", i, part).wait_send()


def add_into(out, parts, rows=16):
    def body(i, _):
        lines = pl.ds(pl.multiple_of(i * rows, rows), rows)
        total = parts[0][lines, :].astype(jnp.float32)
        for part in parts[1:]:
            total = total + part[lines, :].astype(jnp.float32)
        out[lines, :] = total.astype(out.dtype)
        return 0

    lax.fori_loop(0, out.shape[0] // rows, body, 0)


def scatter_line(wires, source, out, near, from_left, from_right, to_right, to_left, cut):
    me, count = lax.axis_index("seq"), lax.axis_size("seq")
    chips, chip, core = count // 2, me // 2, lax.rem(me, 2)
    step = source.shape[1] // cut

    def lines(part):
        return pl.ds(part * step, step)

    order = []
    for i in range(chips // 2):
        order += [chips - 1 - i, i]
    order += [chips // 2] if chips % 2 else []
    across = {}
    for dest in order:
        for part in range(cut):
            across[dest, part] = wires.copy(
                source.at[2 * dest + 1 - core, lines(part)], near.at[dest, lines(part)], sibling()
            )
            across[dest, part].start()
    right, left = {}, {}
    for dest in range(chips):
        for part in range(cut):
            right[dest, part] = wires.copy(to_right.at[dest, lines(part)], from_left.at[dest, lines(part)], on_line(2))
            left[dest, part] = wires.copy(to_left.at[dest, lines(part)], from_right.at[dest, lines(part)], on_line(-2))
    for i in range(chips - 1):
        for part in range(cut):
            yield True
            for dest, table, inbox, outbox, ahead, first in (
                (chips - 1 - i, right, from_left, to_right, chip < chips - 1 - i, chip == 0),
                (i, left, from_right, to_left, chip > i, chip == chips - 1),
            ):
                terms = [source.at[2 * dest + core, lines(part)], near.at[dest, lines(part)]]

                @pl.when(ahead)
                def _():
                    across[dest, part].wait_recv()

                    @pl.when(first)
                    def _():
                        add_into(outbox.at[dest, lines(part)], terms)

                    @pl.when(jnp.logical_not(first))
                    def _():
                        table[dest, part].wait_recv()
                        add_into(outbox.at[dest, lines(part)], terms + [inbox.at[dest, lines(part)]])

                    table[dest, part].start()

    for part in range(cut):
        yield True
        for dest in range(chips):

            @pl.when(chip == dest)
            def _():
                across[dest, part].wait_recv()
                terms = [source.at[2 * dest + core, lines(part)], near.at[dest, lines(part)]]
                if dest > 0:
                    right[dest, part].wait_recv()
                    terms = terms + [from_left.at[dest, lines(part)]]
                if dest < chips - 1:
                    left[dest, part].wait_recv()
                    terms = terms + [from_right.at[dest, lines(part)]]
                add_into(out.at[lines(part)], terms)

    for dest in range(chips):
        for part in range(cut):
            across[dest, part].wait_send()

            @pl.when(chip < dest)
            def _():
                right[dest, part].wait_send()

            @pl.when(chip > dest)
            def _():
                left[dest, part].wait_send()


def swap_seq(wires, source, out):
    me, count = lax.axis_index("seq"), lax.axis_size("seq")
    own = wires.keep(source.at[me], out.at[me])
    wires.begin(own)
    sent = []
    for step in range(1, count):
        peer = lax.rem(me + step, count)
        sent.append(wires.copy(source.at[peer], out.at[me], seq_peer(step)))
        wires.begin(sent[-1])
    yield True
    own.wait()
    for copy in sent:
        copy.wait()


def spread_seq(wires, source, out):
    me, count = lax.axis_index("seq"), lax.axis_size("seq")
    own = wires.keep(source, out.at[me])
    wires.begin(own)
    sent = []
    for step in range(1, count):
        sent.append(wires.copy(source, out.at[me], seq_peer(step)))
        wires.begin(sent[-1])
    yield True
    own.wait()
    for copy in sent:
        copy.wait()


def swap_dp(wires, source, out):
    me, count = lax.axis_index("dp"), lax.axis_size("dp")
    own = wires.keep(source.at[me], out.at[me])
    wires.begin(own)
    sent = []
    for step in range(1, count):
        sent.append(wires.copy(source.at[lax.rem(me + step, count)], out.at[me], pack_peer(step)))
        wires.begin(sent[-1])
    yield True
    own.wait()
    for copy in sent:
        copy.wait()


PIECES = 4
HALVES = 8 + 4 * PIECES


def halves_dp(wires, source, out):
    me, count = lax.axis_index("dp"), lax.axis_size("dp")
    rows, width = source.shape
    by_rows = rows % (16 * PIECES) == 0
    step = (rows if by_rows else width) // PIECES
    own = wires.keep(source, out.at[me])
    own.start()
    bit = lax.rem(me, 2)
    flip = {1: me + 1 - 2 * bit, 2: lax.rem(me + 2, 4)}
    part = lambda ref, i: ref.at[pl.ds(i * step, step)] if by_rows else ref.at[:, pl.ds(i * step, step)]
    first, then = {}, {}
    for i in list(range(PIECES // 2)):
        for way, j in ((1, i), (2, PIECES // 2 + i)):
            first[way, j] = wires.copy(part(source, j), part(out.at[me], j), {"dp": flip[way]})
            first[way, j].start()
    for i in list(range(PIECES // 2)):
        for way, j in ((2, i), (1, PIECES // 2 + i)):
            first[way, j] = wires.copy(part(source, j), part(out.at[me], j), {"dp": flip[way]})
            first[way, j].start()
    for i in range(PIECES // 2):
        for way, j in ((1, i), (2, PIECES // 2 + i)):
            yield True
            first[way, j].wait_recv()
            came = part(out.at[flip[way]], j)
            then[way, j] = wires.copy(came, came, {"dp": flip[3 - way]})
            then[way, j].start()
    yield True
    own.wait()
    for i in range(PIECES // 2):
        for way, j in ((2, i), (1, PIECES // 2 + i)):
            first[way, j].wait_recv()
    for copy in first.values():
        copy.wait_send()
    for copy in then.values():
        copy.wait()


def spread_dp(wires, source, out):
    me, count = lax.axis_index("dp"), lax.axis_size("dp")
    own = wires.keep(source, out.at[me])
    wires.begin(own)
    sent = []
    for step in range(1, count):
        sent.append(wires.copy(source, out.at[me], pack_peer(step)))
        wires.begin(sent[-1])
    yield True
    own.wait()
    for copy in sent:
        copy.wait()


def run_all(jobs, patient=()):
    jobs, patient = list(jobs), list(patient)
    for job in patient:
        next(job)
    while jobs:
        for job in list(jobs):
            if next(job, False) is False:
                jobs.remove(job)
    for job in patient:
        for _ in job:
            pass


def beside(groups, send_sems, recv_sems, plan):
    @pl.when(pl.program_id(0) == 0)
    def _():
        meet(groups)
        for job in plan(Wires(send_sems, recv_sems)):
            next(job)

    @pl.when(pl.program_id(0) == pl.num_programs(0) - 1)
    def _():
        for job in plan(Wires(send_sems, recv_sems, started=True)):
            for _ in job:
                pass


def wire_sems(copies):
    return [pltpu.SemaphoreType.DMA((copies,)), pltpu.SemaphoreType.DMA((copies,))]


def talk(name, cid, groups, operands, outs, plan, copies, in_vmem=(), out_vmem=(), scratch=()):
    n_in, n_out = len(operands), len(outs)

    def kernel(*refs):
        ins, results = refs[:n_in], refs[n_in : n_in + n_out]
        buffers, (send_sems, recv_sems) = refs[n_in + n_out : -2], refs[-2:]
        meet(groups)
        wires = Wires(send_sems, recv_sems)
        run_all(*plan(wires, ins, results, buffers))
        assert wires.used <= copies, wires.used

    def where(i, chosen):
        return pl.BlockSpec(memory_space=pltpu.VMEM if i in chosen else pl.ANY)

    return pl.pallas_call(
        kernel,
        out_shape=outs,
        in_specs=[where(i, in_vmem) for i in range(n_in)],
        out_specs=[where(i, out_vmem) for i in range(n_out)],
        scratch_shapes=list(scratch) + [pltpu.SemaphoreType.DMA((copies,)), pltpu.SemaphoreType.DMA((copies,))],
        compiler_params=pltpu.CompilerParams(
            collective_id=cid, has_side_effects=True, vmem_limit_bytes=48 * 1024 * 1024
        ),
        name=name,
    )(*operands)


def can_halve(array):
    rows, width = array.shape
    return lax.axis_size("dp") == 4 and (rows % (16 * PIECES) == 0 or width % (128 * PIECES) == 0)


def gather_jobs(wires, arrays, sources, results):
    jobs, patient = [], []
    for array, source, result in zip(arrays, sources, results):
        if can_halve(array):
            jobs.append(halves_dp(wires, source, result))
        else:
            patient.append(spread_dp(wires, source, result))
    return jobs, patient


def gather_with(name, cid, block, over_dp, cut=2):
    count, packs = lax.axis_size("seq"), lax.axis_size("dp")
    outs = [shape_of((count,) + block.shape, block.dtype)] + [shape_of((packs,) + a.shape, a.dtype) for a in over_dp]

    def plan(wires, ins, results, _):
        jobs, patient = gather_jobs(wires, over_dp, ins[1:], results[1:])
        return [gather_line(wires, ins[0], results[0], cut)] + jobs, patient

    got = talk(
        name, cid, ("line", "dp") if over_dp else ("line",), (block, *over_dp), outs, plan,
        1 + 4 * (count // 2) * cut + HALVES * len(over_dp),
    )
    return [g.reshape((-1,) + a.shape[1:]) for g, a in zip(got, (block, *over_dp))]


def columns_out(wires, source, out):
    mine, me, count, packs = lax.axis_index("dp"), lax.axis_index("seq"), lax.axis_size("seq"), lax.axis_size("dp")
    own = wires.keep(source.at[me], out.at[mine, me])
    own.start()
    sent, onward = [], []
    for step in range(1, count):
        sent.append(wires.copy(source.at[lax.rem(me + step, count)], out.at[mine, me], seq_peer(step)))
        sent[-1].start()
    for step in range(1, packs):
        onward.append(wires.copy(source.at[me], out.at[mine, me], pack_peer(step)))
        onward[-1].start()
    for step in range(1, count):
        yield True
        sent[step - 1].wait_recv()
        came = out.at[mine, lax.rem(me + count - step, count)]
        for other in range(1, packs):
            onward.append(wires.copy(came, came, pack_peer(other)))
            onward[-1].start()
    yield True
    own.wait()
    for copy in sent:
        copy.wait_send()
    for copy in onward:
        copy.wait()


def spread_all(wires, source, out):
    mine, me, count, packs = lax.axis_index("dp"), lax.axis_index("seq"), lax.axis_size("seq"), lax.axis_size("dp")
    own = wires.keep(source, out.at[mine, me])
    own.start()
    sent, onward = [], []
    for step in range(1, packs):
        sent.append(wires.copy(source, out.at[mine, me], pack_peer(step)))
        sent[-1].start()
    for step in range(1, count):
        onward.append(wires.copy(source, out.at[mine, me], seq_peer(step)))
        onward[-1].start()
    for other in range(1, packs):
        yield True
        sent[other - 1].wait_recv()
        came = out.at[lax.rem(mine + packs - other, packs), me]
        for step in range(1, count):
            onward.append(wires.copy(came, came, seq_peer(step)))
            onward[-1].start()
    yield True
    own.wait()
    for copy in sent:
        copy.wait_send()
    for copy in onward:
        copy.wait()


def shape_of(shape, dtype):
    return jax.ShapeDtypeStruct(tuple(shape), dtype)


def first_exchange(small, mix, block, over_dp):
    packs, count = lax.axis_size("dp"), lax.axis_size("seq")
    outs = [
        shape_of((packs, count) + small.shape, small.dtype),
        shape_of((packs,) + mix.shape, mix.dtype),
        shape_of((count,) + block.shape, block.dtype),
        shape_of((packs,) + over_dp.shape, over_dp.dtype),
    ]
    cut = 2

    def plan(wires, ins, results, _):
        return [
            spread_all(wires, ins[0], results[0]),
            columns_out(wires, ins[1], results[1]),
            gather_line(wires, ins[2], results[2], cut),
        ], [spread_dp(wires, ins[3], results[3])]

    copies = 3 * (count * packs + count) + 4 * (count // 2) * cut
    small, mix, block, over_dp = talk(
        "first_exchange", 1, ("dp", "seq"), (small, mix, block, over_dp), outs, plan, copies
    )
    flat = lambda array: array.reshape(-1, array.shape[-1])
    return small, flat(mix), flat(block), flat(over_dp)


def gather_seq(name, cid, block):
    count = lax.axis_size("seq")
    (got,) = talk(
        name, cid, ("seq",), (block,), [shape_of((count,) + block.shape, block.dtype)],
        lambda wires, ins, outs, _: ([spread_seq(wires, ins[0], outs[0])],), count,
    )
    return got


def scatter_with(name, cid, terms, swaps=(), gathers=(), cut=2):
    count, packs = lax.axis_size("seq"), lax.axis_size("dp")
    rows, width = terms.shape[0] // count, terms.shape[1]
    box = pltpu.VMEM((count // 2, rows, width), terms.dtype)
    blocks = [array.reshape((packs, -1) + array.shape[1:]) for array in swaps]
    outs = [shape_of((rows, width), jnp.float32)] + [shape_of(b.shape, b.dtype) for b in blocks]
    outs += [shape_of((packs,) + a.shape, a.dtype) for a in gathers]
    n = 1 + len(blocks)

    def plan(wires, ins, results, boxes):
        jobs, patient = gather_jobs(wires, gathers, ins[n:], results[n:])
        patient += [swap_dp(wires, a, b) for a, b in zip(ins[1:n], results[1:n])]
        return [scatter_line(wires, ins[0], results[0], *boxes, cut)] + jobs, patient

    got = talk(
        name, cid, ("line", "dp") if swaps or gathers else ("line",),
        (terms.reshape(count, rows, width), *blocks, *gathers), outs, plan,
        3 * (count // 2) * cut + packs * len(blocks) + HALVES * len(gathers),
        in_vmem=(0,), out_vmem=(0,), scratch=(box,) * 5,
    )
    return list(got[:n]) + [g.reshape((-1,) + a.shape[1:]) for g, a in zip(got[n:], gathers)]


def swap_places(name, cid, arrays):
    count = lax.axis_size("seq")
    return talk(
        name, cid, ("seq",), arrays, [shape_of(a.shape, a.dtype) for a in arrays],
        lambda wires, ins, outs, _: ([], [swap_seq(wires, i, o) for i, o in zip(ins, outs)]), count * len(arrays),
    )


def split_columns(arrays, pieces):
    rows = arrays[0].shape[0]
    width = sum(p[2] for p in pieces[0])
    tall = min(rows, 16)

    def kernel(*refs):
        for place, cuts in enumerate(pieces):
            refs[-1][place] = jnp.concatenate([refs[a][:, at : at + n] for a, at, n in cuts], axis=1)

    return pl.pallas_call(
        kernel,
        grid=(rows // tall,),
        in_specs=[pl.BlockSpec((tall, a.shape[1]), lambda i: (i, 0)) for a in arrays],
        out_specs=pl.BlockSpec((len(pieces), tall, width), lambda i: (0, i, 0)),
        out_shape=shape_of((len(pieces), rows, width), arrays[0].dtype),
        compiler_params=pltpu.CompilerParams(vmem_limit_bytes=48 * 1024 * 1024),
        name="split_columns",
    )(*arrays)


def join_columns(array, widths, pieces):
    places, rows, width = array.shape
    tall = min(rows, 16)

    def kernel(source, *outs):
        whole = [source[place].astype(jnp.float32) for place in range(places)]
        for which, out in enumerate(outs):
            found = []
            for place, cuts in enumerate(pieces):
                start = 0
                for a, at, n in cuts:
                    if a == which:
                        found.append((at, whole[place][:, start : start + n]))
                    start += n
            out[...] = jnp.concatenate([part for _, part in sorted(found, key=lambda f: f[0])], axis=1)

    return pl.pallas_call(
        kernel,
        grid=(rows // tall,),
        in_specs=[pl.BlockSpec((places, tall, width), lambda i: (0, i, 0))],
        out_specs=[pl.BlockSpec((tall, w), lambda i: (i, 0)) for w in widths],
        out_shape=[shape_of((rows, w), jnp.float32) for w in widths],
        compiler_params=pltpu.CompilerParams(vmem_limit_bytes=48 * 1024 * 1024),
        name="join_columns",
    )(array)


def add_packs(array):
    return jnp.sum(array.astype(jnp.float32), axis=0)


def cross_rows(left_side, right_side):
    return lax.dot_general(left_side, right_side, (((0,), (0,)), ((), ())), preferred_element_type=jnp.float32)


def cross_cols(left_side, right_side):
    return lax.dot_general(left_side, right_side, (((1,), (1,)), ((), ())), preferred_element_type=jnp.float32)


def dot(left_side, right_side):
    return jnp.dot(left_side, right_side, preferred_element_type=jnp.float32)


def on_device(
    tokens,
    segments,
    norm_one,
    w_qkv,
    w_lr,
    lr_bias,
    w_gate,
    w_out,
    w_init,
    b_init,
    tnorm_w,
    tnorm_b,
    post_w,
    post_b,
    norm_two,
    w_gate_up,
    w_down,
    grad_out,
):
    floats = jnp.float32
    bf16 = jnp.bfloat16
    both = ("dp", "seq")
    packs, per_seq = lax.axis_size("dp"), lax.axis_size("seq")
    devices = packs * per_seq
    place = lax.axis_index("seq")
    span, width = tokens.shape[1], tokens.shape[2]
    rows = norm_one.shape[0]
    heads_all = lr_bias.shape[0]
    units = w_down.shape[0]
    length = span * per_seq
    blocks = length // MB
    heads = heads_all // per_seq
    aligned = rows % HD == 0
    outer = packs if aligned else 1
    inner = width // (outer * per_seq)
    mine = outer * inner

    def own_rows(array):
        cut = array.reshape((outer, per_seq, inner) + array.shape[1:])
        cut = lax.dynamic_index_in_dim(cut, place, 1, keepdims=False)
        return cut.reshape((mine,) + array.shape[1:])

    def put_rows(array):
        full = jnp.zeros((outer, per_seq, inner) + array.shape[1:], array.dtype)
        part = array.reshape((outer, 1, inner) + array.shape[1:])
        at = (0, place) + (0,) * (part.ndim - 2)
        return lax.dynamic_update_slice(full, part, at).reshape((width,) + array.shape[1:])

    feature_cuts = [
        [(0, (part * outer + o) * per_seq * inner + s * inner, inner) for part in range(3) for o in range(outer)]
        + [(1, o * per_seq * inner + s * inner, inner) for o in range(outer)]
        for s in range(per_seq)
    ]
    unit_cuts = [
        [(0, (part * per_seq + s) * units, units) for part in range(2 * packs)] for s in range(per_seq)
    ]

    lanes = max(HD, heads_all)
    pad = lambda array: jnp.pad(array, ((0, 0), (0, lanes - array.shape[1])))
    tags = segments[0].reshape(span // MB, MB)[:, 0].astype(bf16)
    vectors = jnp.stack([norm_one, norm_two, b_init, tnorm_w, tnorm_b, post_w, post_b], axis=1)
    small = jnp.concatenate([pad(w_init), pad(w_lr), pad(vectors), pad(jnp.broadcast_to(tags[None], (8, span // MB)))], axis=0)
    small, w_mix, rows_all, w_o = first_exchange(
        small,
        split_columns((w_qkv, w_gate), feature_cuts),
        tokens[0],
        w_out,
    )
    small = small.reshape((devices,) + small.shape[2:])
    init_all = small[:, :rows, :HD].reshape(width, HD)
    lr_all = small[:, rows : 2 * rows, :heads_all].reshape(width, heads_all)
    vec_all = small[:, 2 * rows : 3 * rows, :7].reshape(width, 7)
    pack_tags = lax.dynamic_index_in_dim(
        small[:, 3 * rows, : span // MB].reshape(packs, blocks), lax.axis_index("dp"), 0, keepdims=False
    )
    fresh = jnp.concatenate([jnp.ones((1,), jnp.int32), (pack_tags[1:] != pack_tags[:-1]).astype(jnp.int32)])
    gain_one, gain_two = vec_all[:, 0].astype(floats), vec_all[:, 1].astype(floats)
    vec_own = own_rows(vec_all).astype(floats)
    post_gain, post_shift = vec_own[:, 5], vec_own[:, 6]
    lr_cols = lr_all.reshape(width, outer, per_seq, heads // outer)
    lr_own = lax.dynamic_index_in_dim(lr_cols, place, 2, keepdims=False).reshape(width, heads)
    bias_own = lax.dynamic_index_in_dim(lr_bias.reshape(outer, per_seq, heads // outer), place, 1, keepdims=False)
    bias_own = bias_own.reshape(heads).astype(floats)

    if not aligned:
        w_o = own_rows(lax.all_gather(w_out, both, axis=0, tiled=True))
    later_top, rows_all = lax.optimization_barrier((grad_out[0], rows_all))
    d_top = lax.all_gather(later_top, "seq", axis=0, tiled=True)
    gu_mine = split_columns((w_gate_up,), unit_cuts)

    inputs = rows_all.astype(floats)
    scale_one = lax.rsqrt(jnp.mean(inputs * inputs, -1, keepdims=True) + EPSILON)
    normed_in = inputs * scale_one
    x_one = (normed_in * gain_one).astype(bf16)
    qkv = dot(x_one, w_mix[:, : 3 * mine])
    gate_pre = dot(x_one, w_mix[:, 3 * mine :])
    lr_sigm = jax.nn.sigmoid(dot(x_one, lr_own) + bias_own)
    e_rows = (lr_sigm * (1.0 / (HD * MB))).reshape(blocks, MB, heads).transpose(0, 2, 1).reshape(blocks, 1, heads * MB)

    def by_token(vector):
        return jnp.repeat(vector.reshape(heads, HD).T, MB, axis=1)

    init_w = own_rows(init_all).astype(floats).reshape(heads, HD, HD)
    init_w = (init_w - jnp.mean(init_w, -1, keepdims=True)).transpose(2, 0, 1).reshape(HD, heads * HD)
    init_b = vec_own[:, 2].reshape(heads, HD)
    init_b = (init_b - jnp.mean(init_b, -1, keepdims=True)).reshape(-1)
    gain_t, shift_t = by_token(vec_own[:, 3]), by_token(vec_own[:, 4])
    *results, gu_part = inner_forward(
        10, fresh, qkv, e_rows, init_w, by_token(init_b), gain_t, shift_t, (gu_mine,)
    )
    mixed, *saved = results

    mean_own = jnp.mean(mixed, -1)
    spread_own = jnp.sum((mixed - mean_own[:, None]) ** 2, -1)
    stats = gather_seq("share_moments", 2, jnp.stack([mean_own, spread_own]))
    mean_all = jnp.mean(stats[:, 0], 0)
    var_all = (jnp.sum(stats[:, 1], 0) + mine * jnp.sum((stats[:, 0] - mean_all) ** 2, 0)) * (1.0 / width)
    out_scale = lax.rsqrt(var_all + EPSILON)[:, None]
    out_hat = (mixed - mean_all[:, None]) * out_scale
    normed_out = out_hat * post_gain + post_shift
    gelu_gate, gelu_pull = jax.vjp(jax.nn.gelu, gate_pre)
    gated_unit = (gelu_gate * normed_out).astype(bf16)
    branch_terms, d_top = lax.optimization_barrier((dot(gated_unit, w_o).astype(bf16), d_top))
    branch, w_gu = scatter_with("scatter_branch", 3, branch_terms, (), (gu_part.reshape(-1, gu_part.shape[-1]),))
    inputs = tokens[0].astype(floats)
    residual = inputs + branch
    scale_two = lax.rsqrt(jnp.mean(residual * residual, -1, keepdims=True) + EPSILON)
    normed_mid = residual * scale_two
    x_two, w_d = gather_with("gather_mid", 4, (normed_mid * gain_two).astype(bf16), (w_down,))
    hidden_units = packs * units
    gate_up = dot(x_two, w_gu)
    gate_part, up_part = gate_up[:, :hidden_units], gate_up[:, hidden_units:]
    silu_sig = jax.nn.sigmoid(gate_part)
    silu_val = gate_part * silu_sig
    hidden = (silu_val * up_part).astype(bf16)
    down = lax.psum_scatter(dot(hidden, w_d).astype(bf16), "seq", scatter_dimension=0, tiled=True)

    g_down = cross_rows(hidden, d_top).astype(bf16)
    d_hidden = cross_cols(d_top, w_d)
    d_gate = d_hidden * up_part * silu_sig * (1.0 + gate_part * (1.0 - silu_sig))
    d_up = d_hidden * silu_val
    d_gate_up = jnp.concatenate([d_gate, d_up], axis=1).astype(bf16)
    g_gate_up = cross_rows(x_two, d_gate_up).astype(bf16)
    mid_terms, down = lax.optimization_barrier((cross_cols(d_gate_up, w_gu).astype(bf16), down))
    d_xtwo, g_gate_up = scatter_with("scatter_mid", 5, mid_terms, (g_gate_up,))
    g_gate_up = add_packs(g_gate_up).astype(bf16)
    result = residual + down.astype(floats)
    g_two = jnp.sum(d_xtwo * normed_mid, axis=0)
    d_mid = d_xtwo * gain_two
    d_residual = grad_out[0].astype(floats) + scale_two * (
        d_mid - normed_mid * jnp.mean(d_mid * normed_mid, -1, keepdims=True)
    )
    (d_branch,) = gather_with("gather_branch", 6, d_residual.astype(bf16), ())
    g_out = cross_rows(gated_unit, d_branch).astype(bf16)
    d_unit = cross_cols(d_branch, w_o)
    d_normed = d_unit * gelu_gate
    g_post_w = jnp.sum(d_normed * out_hat, axis=0)
    g_post_b = jnp.sum(d_normed, axis=0)
    d_hat = d_normed * post_gain
    sums = gather_seq("share_sums", 7, jnp.stack([jnp.sum(d_hat, -1), jnp.sum(d_hat * out_hat, -1)]))
    sums = jnp.sum(sums, 0) * (1.0 / width)
    d_mixed = out_scale * (d_hat - sums[0][:, None] - out_hat * sums[1][:, None])
    d_gate_pre = gelu_pull(d_unit * normed_out)[0].astype(bf16)
    place_rows = lambda array: array.reshape((per_seq, -1) + array.shape[1:])
    pack_rows = lambda array: array.reshape((packs, -1) + array.shape[1:])
    d_qkv, d_rate, d_w0, d_c0, d_gain, d_shift, g_gate_up, g_down, *g_outs = inner_backward(
        11, fresh, qkv, e_rows, d_mixed, saved, gain_t, shift_t, (place_rows(g_gate_up),),
        (pack_rows(g_down), pack_rows(g_out)) if aligned else (pack_rows(g_down),),
    )
    (g_gate_up,) = join_columns(g_gate_up, (w_gate_up.shape[1],), unit_cuts)
    g_down = add_packs(g_down)
    if aligned:
        g_out = add_packs(g_outs[0])
    else:
        g_out = lax.psum_scatter(put_rows(g_out), both, scatter_dimension=0, tiled=True).astype(floats)
    d_rate = d_rate.reshape(blocks, heads, MB).transpose(0, 2, 1).reshape(length, heads)
    d_logit = (d_rate * (1.0 / HD) * lr_sigm * (1.0 - lr_sigm)).astype(bf16)
    d_mix = jnp.concatenate([d_qkv, d_gate_pre], axis=1)
    g_mix = cross_rows(x_one, d_mix).astype(bf16)
    d_xone = cross_cols(d_mix, w_mix) + cross_cols(d_logit, lr_own)
    g_one = jnp.sum(d_xone * normed_in, axis=0)
    def from_token(array):
        return jnp.sum(array.reshape(HD, heads, MB), -1).T.reshape(mine)

    g_vec = jnp.stack(
        [d_c0.reshape(HD, heads, MB)[:, :, 0].T.reshape(mine), from_token(d_gain), from_token(d_shift), g_post_w, g_post_b],
        axis=1,
    )
    g_vec = jnp.concatenate([jnp.stack([g_one, g_two], axis=1), put_rows(g_vec)], axis=1)
    g_init = put_rows(d_w0.reshape(HD, heads, HD).transpose(1, 2, 0).reshape(mine, HD))
    g_lr = cross_rows(x_one, d_logit).reshape(width, outer, 1, heads // outer)
    g_lr = lax.dynamic_update_slice(
        jnp.zeros((width, outer, per_seq, heads // outer), floats), g_lr, (0, 0, place, 0)
    ).reshape(width, heads_all)
    g_bias = jnp.sum(d_logit.astype(floats), axis=0).reshape(outer, 1, heads // outer)
    g_bias = lax.dynamic_update_slice(
        jnp.zeros((outer, per_seq, heads // outer), floats), g_bias, (0, place, 0)
    ).reshape(heads_all)
    wide = HD + heads_all + 7
    g_small = jnp.concatenate([g_init, g_lr, g_vec], axis=1).reshape(devices, rows, wide)
    g_last = jnp.broadcast_to(jnp.pad(g_bias, (0, wide - heads_all)), (devices, 8, wide))
    g_small = jnp.concatenate([g_small, g_last], axis=1)
    d_xone, g_mix, g_small = scatter_with("scatter_first", 8, d_xone.astype(bf16), (g_mix, g_small))
    g_mix, g_small = swap_places(
        "return_columns", 9, (place_rows(add_packs(g_mix).astype(bf16)), place_rows(add_packs(g_small)))
    )
    g_qkv, g_gate = join_columns(g_mix, (w_qkv.shape[1], w_gate.shape[1]), feature_cuts)
    g_small = jnp.sum(g_small, 0).reshape(-1, wide)
    scale_one = lax.rsqrt(jnp.mean(inputs * inputs, -1, keepdims=True) + EPSILON)
    normed_in = inputs * scale_one
    d_inner = d_xone * gain_one
    d_tokens = d_residual + scale_one * (
        d_inner - normed_in * jnp.mean(d_inner * normed_in, -1, keepdims=True)
    )
    g_vec = g_small[:rows, HD + heads_all :]
    return (
        result.astype(bf16)[None],
        d_tokens.astype(bf16)[None],
        g_vec[:, 0],
        g_qkv,
        g_small[:rows, HD : HD + heads_all],
        g_small[rows, :heads_all],
        g_gate,
        g_out,
        g_small[:rows, :HD],
        g_vec[:, 2],
        g_vec[:, 3],
        g_vec[:, 4],
        g_vec[:, 5],
        g_vec[:, 6],
        g_vec[:, 1],
        g_gate_up,
        g_down,
    )


def solution(mesh):
    placed = (
        P("dp", "seq", None),
        P("dp", "seq"),
        P(("dp", "seq")),
        P(("dp", "seq"), None),
        P(("dp", "seq"), None),
        P(),
        P(("dp", "seq"), None),
        P(("dp", "seq"), None),
        P(("dp", "seq"), None),
        P(("dp", "seq")),
        P(("dp", "seq")),
        P(("dp", "seq")),
        P(("dp", "seq")),
        P(("dp", "seq")),
        P(("dp", "seq")),
        P(("dp", "seq"), None),
        P(("dp", "seq"), None),
        P("dp", "seq", None),
    )
    return jax.shard_map(
        on_device,
        mesh=mesh,
        in_specs=placed,
        out_specs=(
            P("dp", "seq", None),
            P("dp", "seq", None),
            P(("dp", "seq")),
            P(("dp", "seq"), None),
            P(("dp", "seq"), None),
            P(),
            P(("dp", "seq"), None),
            P(("dp", "seq"), None),
            P(("dp", "seq"), None),
            P(("dp", "seq")),
            P(("dp", "seq")),
            P(("dp", "seq")),
            P(("dp", "seq")),
            P(("dp", "seq")),
            P(("dp", "seq")),
            P(("dp", "seq"), None),
            P(("dp", "seq"), None),
        ),
        check_vma=False,
    )
```

```python
import functools
import jax
import jax.numpy as jnp
from jax import lax
from jax.experimental import pallas as pl
from jax.experimental.pallas import tpu as pltpu
from jax.sharding import PartitionSpec as P

HD = 64
MB = 16
PER = 8
EPSILON = 1e-06


def nn(left, right):
    return lax.dot_general(left, right, (((1,), (0,)), ((), ())), preferred_element_type=jnp.float32)


def nt(left, right):
    return lax.dot_general(left, right, (((1,), (1,)), ((), ())), preferred_element_type=jnp.float32)


def tn(left, right):
    return lax.dot_general(left, right, (((0,), (0,)), ((), ())), preferred_element_type=jnp.float32)


def halves(value):
    high = value.astype(jnp.bfloat16)
    return high, (value - high.astype(jnp.float32)).astype(jnp.bfloat16)


def head_masks(heads):
    ht, hi = heads * MB, heads * HD

    def iota(shape, axis):
        return lax.broadcasted_iota(jnp.int32, shape, axis)

    own = (iota((ht, hi), 0) // MB == iota((ht, hi), 1) // HD).astype(jnp.float32)
    unit = (iota((HD, hi), 0) == iota((HD, hi), 1) % HD).astype(jnp.bfloat16)
    row, col = iota((ht, ht), 0), iota((ht, ht), 1)
    same = (row // MB == col // MB).astype(jnp.bfloat16)
    ts, tt = row % MB, col % MB
    later = jnp.where((row // MB == col // MB) & (ts <= tt), MB / (tt + 1).astype(jnp.float32), 0.0)
    earlier = jnp.where((row // MB == col // MB) & (tt <= ts), MB / (ts + 1).astype(jnp.float32), 0.0)
    return own, unit, same, later, earlier


def spread(rows, own, heads):
    return (jnp.concatenate([rows] * heads, axis=0) * own).astype(jnp.bfloat16)


def fold(values, heads):
    total = values[:MB]
    for h in range(1, heads):
        total = total + values[h * MB : (h + 1) * MB]
    return total


def turned(rows, own, unit, heads):
    wide = jnp.concatenate([rows] * heads, axis=0) * own
    high, low = halves(wide)
    return nt(unit, high) + nt(unit, low)


def mean0(value):
    return jnp.sum(value, axis=0, keepdims=True) * (1.0 / HD)


def forward_kernel(heads, per, over_seq, over_dp, fresh_ref, qkv_ref, e_ref, w0_ref, c0_ref, gain_ref, shift_ref, *refs):
    moved = over_seq + over_dp
    sources, refs = refs[:moved], refs[moved:]
    mixed_ref, wsave_ref, hat_ref, slope_ref, gap_ref, bar_ref, rows_ref = refs[:7]
    results, (w_ref, c_ref, send_sems, recv_sems) = refs[7 : 7 + moved], refs[7 + moved :]
    jobs = [swap_seq] * over_seq + [spread_dp] * over_dp
    beside(
        ("seq", "dp"), send_sems, recv_sems,
        lambda wires: [job(wires, a, b) for job, a, b in zip(jobs, sources, results)],
    )
    hi = heads * HD
    own, unit, same, later, _ = head_masks(heads)
    gain, shift, w0, c0 = gain_ref[...], shift_ref[...], w0_ref[...], c0_ref[...]
    gain2 = gain * gain

    @pl.when(pl.program_id(0) == 0)
    def _():
        w_ref[...] = jnp.zeros_like(w_ref)
        c_ref[...] = jnp.zeros_like(c_ref)

    w, c = w_ref[...], c_ref[...]
    for b in range(per):
        is_fresh = fresh_ref[pl.program_id(0) * per + b] != 0
        lines = slice(b * MB, (b + 1) * MB)
        q, k, v = qkv_ref[lines, :hi], qkv_ref[lines, hi : 2 * hi], qkv_ref[lines, 2 * hi :]
        e = e_ref[b]
        kb, qb = spread(k, own, heads), spread(q, own, heads)
        gap = shift - turned(v - k, own, unit, heads)
        base = gain * gap
        w = jnp.where(is_fresh, w0, w)
        c = jnp.where(is_fresh, c0, c)
        wb = w.astype(jnp.bfloat16)
        wsave_ref[b] = wb
        z = nt(wb, kb) + c
        gz = gain2 * z
        s = lax.rsqrt(mean0(z * z) + EPSILON)
        mean_g = s * mean0(gz) + mean0(base)
        mean_gx = s * (s * mean0(gz * z) + mean0(base * z))
        hat = s * z
        slope = s * (gain2 * hat + base - mean_g - hat * mean_gx)
        eb = (e * slope).astype(jnp.bfloat16)
        mix = (later * (nt(kb, qb) + 1.0)).astype(jnp.bfloat16)
        zbar = nt(wb, qb) + c - nn(eb, mix)
        w = w - nn(eb, kb)
        c = c - nn(eb, same)
        sbar = lax.rsqrt(mean0(zbar * zbar) + EPSILON)
        bar = zbar * sbar
        high, low = halves(gain * bar + shift)
        mixed_ref[lines, :] = q + fold((tn(high, unit) + tn(low, unit)) * own, heads)
        hat_ref[b] = hat
        slope_ref[b] = slope
        gap_ref[b] = gap
        bar_ref[b] = bar
        rows_ref[b] = jnp.concatenate([s, sbar, mean_g, mean_gx], axis=0)
    w_ref[...] = w
    c_ref[...] = c


def inner_forward(cid, fresh, qkv, e_rows, w0, c0, gain, shift, seq_arrays, dp_arrays):
    arrays = tuple(seq_arrays) + tuple(dp_arrays)
    packs = lax.axis_size("dp")
    tokens, heads = qkv.shape[0], qkv.shape[1] // (3 * HD)
    ht, hi = heads * MB, heads * HD
    blocks = tokens // MB
    per = PER
    f32 = jnp.float32
    whole = lambda shape: pl.BlockSpec(shape, lambda i: (0, 0))
    save = pl.BlockSpec((per, HD, ht), lambda i: (i, 0, 0))
    return pl.pallas_call(
        functools.partial(forward_kernel, heads, per, len(seq_arrays), len(dp_arrays)),
        grid=(blocks // per,),
        in_specs=[
            pl.BlockSpec(memory_space=pltpu.SMEM),
            pl.BlockSpec((per * MB, 3 * hi), lambda i: (i, 0)),
            pl.BlockSpec((per, 1, ht), lambda i: (i, 0, 0)),
            whole((HD, hi)), whole((HD, ht)), whole((HD, ht)), whole((HD, ht)),
        ] + [pl.BlockSpec(memory_space=pl.ANY)] * len(arrays),
        out_specs=[
            pl.BlockSpec((per * MB, hi), lambda i: (i, 0)),
            pl.BlockSpec((per, HD, hi), lambda i: (i, 0, 0)),
            save, save, save, save,
            pl.BlockSpec((per, 4, ht), lambda i: (i, 0, 0)),
        ] + [pl.BlockSpec(memory_space=pl.ANY)] * len(arrays),
        out_shape=[
            jax.ShapeDtypeStruct((tokens, hi), f32),
            jax.ShapeDtypeStruct((blocks, HD, hi), jnp.bfloat16),
        ] + [jax.ShapeDtypeStruct((blocks, HD, ht), f32)] * 4 + [jax.ShapeDtypeStruct((blocks, 4, ht), f32)]
        + [shape_of(a.shape, a.dtype) for a in seq_arrays]
        + [shape_of((packs,) + a.shape, a.dtype) for a in dp_arrays],
        scratch_shapes=[pltpu.VMEM((HD, hi), f32), pltpu.VMEM((HD, ht), f32)]
        + wire_sems(len(seq_arrays) * lax.axis_size("seq") + len(dp_arrays) * packs),
        compiler_params=pltpu.CompilerParams(
            vmem_limit_bytes=48 * 1024 * 1024, collective_id=cid, has_side_effects=True
        ),
        name="inner_forward",
    )(fresh, qkv, e_rows, w0, c0, gain, shift, *arrays)


def backward_kernel(heads, per, over_seq, items, fresh_ref, qkv_ref, e_ref, dmix_ref, wsave_ref, hat_ref, slope_ref,
                    gap_ref, bar_ref, rows_ref, gain_ref, shift_ref, *refs):
    moved = over_seq + len(items)
    sources, refs = refs[:moved], refs[moved:]
    sources = list(sources[:over_seq]) + [window(ref, item) for ref, item in zip(sources[over_seq:], items)]
    dqkv_ref, drate_ref, dw0_ref, dc0_ref, dgain_ref, dshift_ref = refs[:6]
    results, (a_ref, ac_ref, send_sems, recv_sems) = refs[6 : 6 + moved], refs[6 + moved :]
    swaps = [swap_seq] * over_seq + [swap_dp] * len(items)
    beside(
        ("seq", "dp"), send_sems, recv_sems,
        lambda wires: [swap(wires, a, b) for swap, a, b in zip(swaps, sources, results)],
    )
    hi, ht = heads * HD, heads * MB
    own, unit, same, later, earlier = head_masks(heads)
    gain = gain_ref[...]
    gain2 = gain * gain
    step = pl.program_id(0)

    @pl.when(step == 0)
    def _():
        for ref in (a_ref, ac_ref, dw0_ref, dc0_ref, dgain_ref, dshift_ref):
            ref[...] = jnp.zeros_like(ref)

    a, ac = a_ref[...], ac_ref[...]
    dw0, dc0, dgain, dshift = dw0_ref[...], dc0_ref[...], dgain_ref[...], dshift_ref[...]
    for b in reversed(range(per)):
        is_fresh = fresh_ref[(pl.num_programs(0) - 1 - step) * per + b] != 0
        lines = slice(b * MB, (b + 1) * MB)
        q, k = qkv_ref[lines, :hi], qkv_ref[lines, hi : 2 * hi]
        e = e_ref[b]
        wb, hat, slope, gap, bar = wsave_ref[b], hat_ref[b], slope_ref[b], gap_ref[b], bar_ref[b]
        s, sbar, mean_g, mean_gx = (rows_ref[b][i : i + 1] for i in range(4))
        kb, qb = spread(k, own, heads), spread(q, own, heads)
        dout = dmix_ref[lines, :]
        dturn = turned(dout, own, unit, heads)
        head = gain * dturn
        dbar = sbar * (head - mean0(head) - bar * mean0(head * bar))
        dbarb = dbar.astype(jnp.bfloat16)
        scores = nt(qb, kb) + 1.0
        mix = earlier * scores
        s2 = s * s
        gh = gain2 * hat
        alpha = s2 * (gain2 - mean_gx)
        kappa = s2 * (gain2 * hat + gap * gain + gh)
        kappa1 = mean_g + mean0(gh)
        kappa2 = 2.0 * mean_gx + mean0(gh * hat)
        ab = a.astype(jnp.bfloat16)
        ka = nt(ab, kb) + ac
        u = -e * (ka + nn(dbarb, mix.astype(jnp.bfloat16)))
        ug = gain2 * u
        r2 = mean0(u * hat)
        r3 = mean0(ug)
        r4 = mean0(ug * hat)
        r5 = mean0(u * slope)
        row1 = s2 * (r3 - r2 * kappa1)
        row2 = s2 * (r4 - r2 * kappa2) + s * r5
        dz = alpha * u - r2 * kappa - row1 - hat * row2
        dzb = dz.astype(jnp.bfloat16)
        dg = s * (u - hat * r2)
        a_next = a + nn(dbarb, qb) + nn(dzb, kb)
        ac_next = ac + nn(dbarb, same) + nn(dzb, same)
        dm = -tn(dbarb, slope.astype(jnp.bfloat16))
        ds = (earlier * e * dm).astype(jnp.bfloat16)
        drate_ref[b] = (jnp.sum(mix * dm, axis=0, keepdims=True) - jnp.sum(ka * slope, axis=0, keepdims=True)) * (1.0 / MB)
        dgb = (gain * dg)
        ndg = fold(tn(dgb.astype(jnp.bfloat16), unit) * own, heads)
        dq = dout + fold(tn(dbarb, wb) * own + nn(ds, kb), heads)
        dk = ndg + fold((tn(dzb, wb) - tn((e * slope).astype(jnp.bfloat16), ab)) * own + tn(ds, qb), heads)
        dqkv_ref[lines, :hi] = dq.astype(jnp.bfloat16)
        dqkv_ref[lines, hi : 2 * hi] = dk.astype(jnp.bfloat16)
        dqkv_ref[lines, 2 * hi :] = (-ndg).astype(jnp.bfloat16)
        dgain = dgain + dturn * bar + dg * (2.0 * gain * hat + gap)
        dshift = dshift + dturn + dgb
        dw0 = dw0 + jnp.where(is_fresh, a_next, 0.0)
        dc0 = dc0 + jnp.where(is_fresh, ac_next, 0.0)
        a = jnp.where(is_fresh, 0.0, a_next)
        ac = jnp.where(is_fresh, 0.0, ac_next)
    a_ref[...] = a
    ac_ref[...] = ac
    dw0_ref[...] = dw0
    dc0_ref[...] = dc0
    dgain_ref[...] = dgain
    dshift_ref[...] = dshift


def inner_backward(cid, fresh, qkv, e_rows, dmix, saved, gain, shift, seq_arrays, items):
    arrays = tuple(seq_arrays) + tuple(item[0] for item in items)
    tokens, heads = qkv.shape[0], qkv.shape[1] // (3 * HD)
    ht, hi = heads * MB, heads * HD
    blocks = tokens // MB
    per = PER
    last = blocks // per - 1
    f32 = jnp.float32
    whole = lambda shape: pl.BlockSpec(shape, lambda i: (0, 0))
    three = lambda shape: pl.BlockSpec(shape, lambda i: (last - i, 0, 0))
    two = lambda shape: pl.BlockSpec(shape, lambda i: (last - i, 0))
    save = three((per, HD, ht))
    return pl.pallas_call(
        functools.partial(backward_kernel, heads, per, len(seq_arrays), items),
        grid=(blocks // per,),
        in_specs=[
            pl.BlockSpec(memory_space=pltpu.SMEM),
            two((per * MB, 3 * hi)), three((per, 1, ht)), two((per * MB, hi)),
            three((per, HD, hi)), save, save, save, save, three((per, 4, ht)),
            whole((HD, ht)), whole((HD, ht)),
        ] + [pl.BlockSpec(memory_space=pl.ANY)] * len(arrays),
        out_specs=[
            two((per * MB, 3 * hi)), three((per, 1, ht)),
            whole((HD, hi)), whole((HD, ht)), whole((HD, ht)), whole((HD, ht)),
        ] + [pl.BlockSpec(memory_space=pl.ANY)] * len(arrays),
        out_shape=[
            jax.ShapeDtypeStruct((tokens, 3 * hi), jnp.bfloat16),
            jax.ShapeDtypeStruct((blocks, 1, ht), f32),
            jax.ShapeDtypeStruct((HD, hi), f32),
        ] + [jax.ShapeDtypeStruct((HD, ht), f32)] * 3 + [shape_of(a.shape, a.dtype) for a in seq_arrays]
        + [window_shape(item) for item in items],
        scratch_shapes=[pltpu.VMEM((HD, hi), f32), pltpu.VMEM((HD, ht), f32)]
        + wire_sems(len(seq_arrays) * lax.axis_size("seq") + len(items) * lax.axis_size("dp")),
        compiler_params=pltpu.CompilerParams(
            vmem_limit_bytes=48 * 1024 * 1024, collective_id=cid, has_side_effects=True
        ),
        name="inner_backward",
    )(fresh, qkv, e_rows, dmix, *saved, gain, shift, *arrays)

MESH = pl.DeviceIdType.MESH


class Wires:
    def __init__(self, send_sems, recv_sems, started=False):
        self.send_sems, self.recv_sems, self.used, self.started = send_sems, recv_sems, 0, started

    def begin(self, copy):
        if not self.started:
            copy.start()
        return copy

    def copy(self, source, target, device):
        at = self.number()
        return self.numbered(at, source, target, device)

    def number(self):
        self.used += 1
        return self.used - 1

    def numbered(self, at, source, target, device):
        return pltpu.make_async_remote_copy(
            src_ref=source,
            dst_ref=target,
            send_sem=self.send_sems.at[at],
            recv_sem=self.recv_sems.at[at],
            device_id=device,
            device_id_type=MESH,
        )

    def keep(self, source, target):
        at = self.number()
        return pltpu.make_async_copy(source, target, self.send_sems.at[at])


def on_line(step):
    return {"seq": lax.axis_index("seq") + step}


def sibling():
    me = lax.axis_index("seq")
    return {"seq": me + 1 - 2 * lax.rem(me, 2)}


def pack_peer(step):
    packs = lax.axis_size("dp")
    return {"dp": lax.rem(lax.axis_index("dp") + step, packs)}


def seq_peer(step):
    count = lax.axis_size("seq")
    return {"seq": lax.rem(lax.axis_index("seq") + step, count)}


def meet(groups):
    barrier = pltpu.get_barrier_semaphore()
    me, count = lax.axis_index("seq"), lax.axis_size("seq")

    def greet(device):
        pl.semaphore_signal(barrier, inc=1, device_id=device, device_id_type=MESH)

    peers = 0
    if "dp" in groups:
        for step in range(1, lax.axis_size("dp")):
            greet(pack_peer(step))
        peers += lax.axis_size("dp") - 1
    if "seq" in groups:
        for step in range(1, count):
            greet(seq_peer(step))
        peers += count - 1
    elif "line" in groups:
        greet(sibling())

        @pl.when(me >= 2)
        def _():
            greet(on_line(-2))

        @pl.when(me < count - 2)
        def _():
            greet(on_line(2))

        peers += 1 + jnp.minimum(me // 2, 1) + jnp.minimum((count - 1 - me) // 2, 1)
    pl.semaphore_wait(barrier, peers)


def gather_line(wires, source, out, cut):
    me, count = lax.axis_index("seq"), lax.axis_size("seq")
    chips, chip = count // 2, me // 2
    step = source.shape[0] // cut
    other = me + 1 - 2 * lax.rem(me, 2)

    def piece(slot, part):
        return out.at[slot, pl.ds(part * step, step)]

    own = wires.keep(source, out.at[me])
    own.start()
    numbers = {(way, i, part): wires.number() for way in "rlRL" for i in range(chips) for part in range(cut)}

    def copy(way, i, part):
        slot = me - 2 * i if way in "rR" else me + 2 * i
        start = source.at[pl.ds(part * step, step)] if i == 0 else piece(slot, part)
        device = {"r": on_line(2), "l": on_line(-2), "R": sibling(), "L": sibling()}[way]
        return wires.numbered(numbers[way, i, part], start, piece(slot, part), device)

    def arrived(way, i, part):
        if way in "rl":
            slot = me - 2 * (i + 1) if way == "r" else me + 2 * (i + 1)
        else:
            slot = other - 2 * i if way == "R" else other + 2 * i
        there = piece(slot, part)
        wires.numbered(numbers[way, i, part], there, there, sibling()).wait_recv()

    @pl.when(chip < chips - 1)
    def _():
        for part in range(cut):
            copy("r", 0, part).start()

    @pl.when(chip > 0)
    def _():
        for part in range(cut):
            copy("l", 0, part).start()

    for part in range(cut):
        copy("R", 0, part).start()
    for i in range(1, chips):
        for part in range(cut):
            yield True

            @pl.when(chip >= i)
            def _():
                arrived("r", i - 1, part)

                @pl.when(chip < chips - 1)
                def _():
                    copy("r", i, part).start()

                copy("R", i, part).start()

            @pl.when(chip + i <= chips - 1)
            def _():
                arrived("l", i - 1, part)

                @pl.when(chip > 0)
                def _():
                    copy("l", i, part).start()

                copy("L", i, part).start()

    yield True
    own.wait()
    for i in range(chips):
        for part in range(cut):
            if i == 0:
                arrived("R", 0, part)
                copy("R", 0, part).wait_send()
            else:

                @pl.when(chip >= i)
                def _():
                    arrived("R", i, part)
                    copy("R", i, part).wait_send()

                @pl.when(chip + i <= chips - 1)
                def _():
                    arrived("L", i, part)
                    copy("L", i, part).wait_send()

            @pl.when((chip >= i) & (chip < chips - 1))
            def _():
                copy("r", i, part).wait_send()

            @pl.when((chip + i <= chips - 1) & (chip > 0))
            def _():
                copy("l", i, part).wait_send()


def add_into(out, parts, rows=16):
    def body(i, _):
        lines = pl.ds(pl.multiple_of(i * rows, rows), rows)
        total = parts[0][lines, :].astype(jnp.float32)
        for part in parts[1:]:
            total = total + part[lines, :].astype(jnp.float32)
        out[lines, :] = total.astype(out.dtype)
        return 0

    lax.fori_loop(0, out.shape[0] // rows, body, 0)


def scatter_line(wires, source, out, near, from_left, from_right, to_right, to_left, cut):
    me, count = lax.axis_index("seq"), lax.axis_size("seq")
    chips, chip, core = count // 2, me // 2, lax.rem(me, 2)
    step = source.shape[1] // cut

    def lines(part):
        return pl.ds(part * step, step)

    order = []
    for i in range(chips // 2):
        order += [chips - 1 - i, i]
    order += [chips // 2] if chips % 2 else []
    across = {}
    for dest in order:
        for part in range(cut):
            across[dest, part] = wires.copy(
                source.at[2 * dest + 1 - core, lines(part)], near.at[dest, lines(part)], sibling()
            )
            across[dest, part].start()
    right, left = {}, {}
    for dest in range(chips):
        for part in range(cut):
            right[dest, part] = wires.copy(to_right.at[dest, lines(part)], from_left.at[dest, lines(part)], on_line(2))
            left[dest, part] = wires.copy(to_left.at[dest, lines(part)], from_right.at[dest, lines(part)], on_line(-2))
    for i in range(chips - 1):
        for part in range(cut):
            yield True
            for dest, table, inbox, outbox, ahead, first in (
                (chips - 1 - i, right, from_left, to_right, chip < chips - 1 - i, chip == 0),
                (i, left, from_right, to_left, chip > i, chip == chips - 1),
            ):
                terms = [source.at[2 * dest + core, lines(part)], near.at[dest, lines(part)]]

                @pl.when(ahead)
                def _():
                    across[dest, part].wait_recv()

                    @pl.when(first)
                    def _():
                        add_into(outbox.at[dest, lines(part)], terms)

                    @pl.when(jnp.logical_not(first))
                    def _():
                        table[dest, part].wait_recv()
                        add_into(outbox.at[dest, lines(part)], terms + [inbox.at[dest, lines(part)]])

                    table[dest, part].start()

    for part in range(cut):
        yield True
        for dest in range(chips):

            @pl.when(chip == dest)
            def _():
                across[dest, part].wait_recv()
                terms = [source.at[2 * dest + core, lines(part)], near.at[dest, lines(part)]]
                if dest > 0:
                    right[dest, part].wait_recv()
                    terms = terms + [from_left.at[dest, lines(part)]]
                if dest < chips - 1:
                    left[dest, part].wait_recv()
                    terms = terms + [from_right.at[dest, lines(part)]]
                add_into(out.at[lines(part)], terms)

    for dest in range(chips):
        for part in range(cut):
            across[dest, part].wait_send()

            @pl.when(chip < dest)
            def _():
                right[dest, part].wait_send()

            @pl.when(chip > dest)
            def _():
                left[dest, part].wait_send()


def swap_seq(wires, source, out):
    me, count = lax.axis_index("seq"), lax.axis_size("seq")
    own = wires.keep(source.at[me], out.at[me])
    wires.begin(own)
    sent = []
    for step in range(1, count):
        peer = lax.rem(me + step, count)
        sent.append(wires.copy(source.at[peer], out.at[me], seq_peer(step)))
        wires.begin(sent[-1])
    yield True
    own.wait()
    for copy in sent:
        copy.wait()


def spread_seq(wires, source, out):
    me, count = lax.axis_index("seq"), lax.axis_size("seq")
    own = wires.keep(source, out.at[me])
    wires.begin(own)
    sent = []
    for step in range(1, count):
        sent.append(wires.copy(source, out.at[me], seq_peer(step)))
        wires.begin(sent[-1])
    yield True
    own.wait()
    for copy in sent:
        copy.wait()


def swap_dp(wires, source, out):
    me, count = lax.axis_index("dp"), lax.axis_size("dp")
    own = wires.keep(source.at[me], out.at[me])
    wires.begin(own)
    sent = []
    for step in range(1, count):
        sent.append(wires.copy(source.at[lax.rem(me + step, count)], out.at[me], pack_peer(step)))
        wires.begin(sent[-1])
    yield True
    own.wait()
    for copy in sent:
        copy.wait()


PIECES = 4
HALVES = 8 + 4 * PIECES


def halves_dp(wires, source, out):
    me, count = lax.axis_index("dp"), lax.axis_size("dp")
    rows, width = source.shape
    by_rows = rows % (16 * PIECES) == 0
    step = (rows if by_rows else width) // PIECES
    own = wires.keep(source, out.at[me])
    own.start()
    bit = lax.rem(me, 2)
    flip = {1: me + 1 - 2 * bit, 2: lax.rem(me + 2, 4)}
    part = lambda ref, i: ref.at[pl.ds(i * step, step)] if by_rows else ref.at[:, pl.ds(i * step, step)]
    first, then = {}, {}

    def send(way, j):
        first[way, j] = wires.copy(part(source, j), part(out.at[me], j), {"dp": flip[way]})
        first[way, j].start()

    half = PIECES // 2
    for i in range(half):
        send(1, i)
        send(2, half + i)
    for i in range(half):
        for way, j in ((1, i), (2, half + i)):
            yield True
            first[way, j].wait_recv()
            came = part(out.at[flip[way]], j)
            then[way, j] = wires.copy(came, came, {"dp": flip[3 - way]})
            then[way, j].start()
            send(3 - way, j)
    yield True
    own.wait()
    for i in range(half):
        for way, j in ((2, i), (1, half + i)):
            first[way, j].wait_recv()
    for copy in first.values():
        copy.wait_send()
    for copy in then.values():
        copy.wait()


def spread_dp(wires, source, out):
    me, count = lax.axis_index("dp"), lax.axis_size("dp")
    own = wires.keep(source, out.at[me])
    wires.begin(own)
    sent = []
    for step in range(1, count):
        sent.append(wires.copy(source, out.at[me], pack_peer(step)))
        wires.begin(sent[-1])
    yield True
    own.wait()
    for copy in sent:
        copy.wait()


def run_all(jobs, patient=()):
    jobs, patient = list(jobs), list(patient)
    for job in patient:
        next(job)
    while jobs:
        for job in list(jobs):
            if next(job, False) is False:
                jobs.remove(job)
    for job in patient:
        for _ in job:
            pass


def beside(groups, send_sems, recv_sems, plan):
    @pl.when(pl.program_id(0) == 0)
    def _():
        meet(groups)
        for job in plan(Wires(send_sems, recv_sems)):
            next(job)

    @pl.when(pl.program_id(0) == pl.num_programs(0) - 1)
    def _():
        for job in plan(Wires(send_sems, recv_sems, started=True)):
            for _ in job:
                pass


def wire_sems(copies):
    return [pltpu.SemaphoreType.DMA((copies,)), pltpu.SemaphoreType.DMA((copies,))]


def talk(name, cid, groups, operands, outs, plan, copies, in_vmem=(), out_vmem=(), scratch=()):
    n_in, n_out = len(operands), len(outs)

    def kernel(*refs):
        ins, results = refs[:n_in], refs[n_in : n_in + n_out]
        buffers, (send_sems, recv_sems) = refs[n_in + n_out : -2], refs[-2:]
        meet(groups)
        wires = Wires(send_sems, recv_sems)
        run_all(*plan(wires, ins, results, buffers))
        assert wires.used <= copies, wires.used

    def where(i, chosen):
        return pl.BlockSpec(memory_space=pltpu.VMEM if i in chosen else pl.ANY)

    return pl.pallas_call(
        kernel,
        out_shape=outs,
        in_specs=[where(i, in_vmem) for i in range(n_in)],
        out_specs=[where(i, out_vmem) for i in range(n_out)],
        scratch_shapes=list(scratch) + [pltpu.SemaphoreType.DMA((copies,)), pltpu.SemaphoreType.DMA((copies,))],
        compiler_params=pltpu.CompilerParams(
            collective_id=cid, has_side_effects=True, vmem_limit_bytes=48 * 1024 * 1024
        ),
        name=name,
    )(*operands)


def can_halve(array):
    rows, width = array.shape
    return lax.axis_size("dp") == 4 and (rows % (16 * PIECES) == 0 or width % (128 * PIECES) == 0)


def gather_jobs(wires, arrays, sources, results):
    jobs, patient = [], []
    for array, source, result in zip(arrays, sources, results):
        if can_halve(array):
            jobs.append(halves_dp(wires, source, result))
        else:
            patient.append(spread_dp(wires, source, result))
    return jobs, patient


def window(ref, item):
    _, rows, columns = item
    if rows is None and columns is None:
        return ref
    lines = slice(None) if rows is None else pl.ds(rows[0], rows[1] - rows[0])
    lanes = slice(None) if columns is None else pl.ds(columns[0], columns[1] - columns[0])
    return ref.at[:, lines, lanes]


def window_shape(item):
    array, rows, columns = item
    shape = list(array.shape)
    if rows is not None:
        shape[1] = rows[1] - rows[0]
    if columns is not None:
        shape[2] = columns[1] - columns[0]
    return shape_of(shape, array.dtype)


def gather_with(name, cid, block, over_dp, swaps=(), cut=2):
    count, packs = lax.axis_size("seq"), lax.axis_size("dp")
    outs = [shape_of((count,) + block.shape, block.dtype)] + [shape_of((packs,) + a.shape, a.dtype) for a in over_dp]
    outs += [window_shape(item) for item in swaps]
    n = 1 + len(over_dp)

    def plan(wires, ins, results, _):
        jobs, patient = gather_jobs(wires, over_dp, ins[1:n], results[1:n])
        patient += [swap_dp(wires, window(a, item), b) for a, b, item in zip(ins[n:], results[n:], swaps)]
        return [gather_line(wires, ins[0], results[0], cut)] + jobs, patient

    got = talk(
        name, cid, ("line", "dp") if over_dp or swaps else ("line",), (block, *over_dp, *(i[0] for i in swaps)), outs, plan,
        1 + 4 * (count // 2) * cut + HALVES * len(over_dp) + packs * len(swaps),
    )
    return [g.reshape((-1,) + a.shape[1:]) for g, a in zip(got, (block, *over_dp))] + list(got[n:])


def columns_out(wires, source, out):
    mine, me, count, packs = lax.axis_index("dp"), lax.axis_index("seq"), lax.axis_size("seq"), lax.axis_size("dp")
    own = wires.keep(source.at[me], out.at[mine, me])
    own.start()
    sent, onward = [], []
    for step in range(1, count):
        sent.append(wires.copy(source.at[lax.rem(me + step, count)], out.at[mine, me], seq_peer(step)))
        sent[-1].start()
    for step in range(1, packs):
        onward.append(wires.copy(source.at[me], out.at[mine, me], pack_peer(step)))
        onward[-1].start()
    for step in range(1, count):
        yield True
        sent[step - 1].wait_recv()
        came = out.at[mine, lax.rem(me + count - step, count)]
        for other in range(1, packs):
            onward.append(wires.copy(came, came, pack_peer(other)))
            onward[-1].start()
    yield True
    own.wait()
    for copy in sent:
        copy.wait_send()
    for copy in onward:
        copy.wait()


def spread_all(wires, source, out):
    mine, me, count, packs = lax.axis_index("dp"), lax.axis_index("seq"), lax.axis_size("seq"), lax.axis_size("dp")
    own = wires.keep(source, out.at[mine, me])
    own.start()
    sent, onward = [], []
    for step in range(1, packs):
        sent.append(wires.copy(source, out.at[mine, me], pack_peer(step)))
        sent[-1].start()
    for step in range(1, count):
        onward.append(wires.copy(source, out.at[mine, me], seq_peer(step)))
        onward[-1].start()
    for other in range(1, packs):
        yield True
        sent[other - 1].wait_recv()
        came = out.at[lax.rem(mine + packs - other, packs), me]
        for step in range(1, count):
            onward.append(wires.copy(came, came, seq_peer(step)))
            onward[-1].start()
    yield True
    own.wait()
    for copy in sent:
        copy.wait_send()
    for copy in onward:
        copy.wait()


def shape_of(shape, dtype):
    return jax.ShapeDtypeStruct(tuple(shape), dtype)


def first_exchange(mix, block, over_dp):
    packs, count = lax.axis_size("dp"), lax.axis_size("seq")
    outs = [shape_of((packs,) + mix.shape, mix.dtype), shape_of((count,) + block.shape, block.dtype)]
    outs += [shape_of((packs,) + a.shape, a.dtype) for a in over_dp]
    cut = 2

    def plan(wires, ins, results, _):
        return [
            columns_out(wires, ins[0], results[0]),
            gather_line(wires, ins[1], results[1], cut),
        ], [spread_dp(wires, a, b) for a, b in zip(ins[2:], results[2:])]

    copies = count * packs + count + 4 * (count // 2) * cut + packs * len(over_dp) + 8
    got = talk("first_exchange", 1, ("dp", "seq"), (mix, block, *over_dp), outs, plan, copies)
    return [array.reshape(-1, array.shape[-1]) for array in got]


def gather_seq(name, cid, block):
    count = lax.axis_size("seq")
    (got,) = talk(
        name, cid, ("seq",), (block,), [shape_of((count,) + block.shape, block.dtype)],
        lambda wires, ins, outs, _: ([spread_seq(wires, ins[0], outs[0])],), count,
    )
    return got


def scatter_with(name, cid, terms, swaps=(), gathers=(), cut=2):
    count, packs = lax.axis_size("seq"), lax.axis_size("dp")
    rows, width = terms.shape[0] // count, terms.shape[1]
    box = pltpu.VMEM((count // 2, rows, width), terms.dtype)
    blocks = [item[0] for item in swaps]
    outs = [shape_of((rows, width), jnp.float32)] + [window_shape(item) for item in swaps]
    outs += [shape_of((packs,) + a.shape, a.dtype) for a in gathers]
    n = 1 + len(blocks)

    def plan(wires, ins, results, boxes):
        jobs, patient = gather_jobs(wires, gathers, ins[n:], results[n:])
        patient += [swap_dp(wires, window(a, item), b) for a, b, item in zip(ins[1:n], results[1:n], swaps)]
        return [scatter_line(wires, ins[0], results[0], *boxes, cut)] + jobs, patient

    got = talk(
        name, cid, ("line", "dp") if swaps or gathers else ("line",),
        (terms.reshape(count, rows, width), *blocks, *gathers), outs, plan,
        3 * (count // 2) * cut + packs * len(blocks) + HALVES * len(gathers),
        in_vmem=(0,), out_vmem=(0,), scratch=(box,) * 5,
    )
    return list(got[:n]) + [g.reshape((-1,) + a.shape[1:]) for g, a in zip(got[n:], gathers)]


def swap_places(name, cid, arrays):
    count = lax.axis_size("seq")
    return talk(
        name, cid, ("seq",), arrays, [shape_of(a.shape, a.dtype) for a in arrays],
        lambda wires, ins, outs, _: ([], [swap_seq(wires, i, o) for i, o in zip(ins, outs)]), count * len(arrays),
    )


def split_columns(arrays, pieces):
    rows = arrays[0].shape[0]
    width = sum(p[2] for p in pieces[0])
    tall = min(rows, 16)

    def kernel(*refs):
        for place, cuts in enumerate(pieces):
            refs[-1][place] = jnp.concatenate(
                [jnp.zeros((tall, n), refs[-1].dtype) if a is None else refs[a][:, at : at + n] for a, at, n in cuts], axis=1
            )

    return pl.pallas_call(
        kernel,
        grid=(rows // tall,),
        in_specs=[pl.BlockSpec((tall, a.shape[1]), lambda i: (i, 0)) for a in arrays],
        out_specs=pl.BlockSpec((len(pieces), tall, width), lambda i: (0, i, 0)),
        out_shape=shape_of((len(pieces), rows, width), arrays[0].dtype),
        compiler_params=pltpu.CompilerParams(vmem_limit_bytes=48 * 1024 * 1024),
        name="split_columns",
    )(*arrays)


def join_columns(array, widths, pieces):
    places, rows, width = array.shape
    tall = min(rows, 16)

    def kernel(source, *outs):
        whole = [source[place].astype(jnp.float32) for place in range(places)]
        for which, out in enumerate(outs):
            found = []
            for place, cuts in enumerate(pieces):
                start = 0
                for a, at, n in cuts:
                    if a == which:
                        found.append((at, whole[place][:, start : start + n]))
                    start += n
            out[...] = jnp.concatenate([part for _, part in sorted(found, key=lambda f: f[0])], axis=1)

    return pl.pallas_call(
        kernel,
        grid=(rows // tall,),
        in_specs=[pl.BlockSpec((places, tall, width), lambda i: (0, i, 0))],
        out_specs=[pl.BlockSpec((tall, w), lambda i: (i, 0)) for w in widths],
        out_shape=[shape_of((rows, w), jnp.float32) for w in widths],
        compiler_params=pltpu.CompilerParams(vmem_limit_bytes=48 * 1024 * 1024),
        name="join_columns",
    )(array)


def add_packs(array):
    return jnp.sum(array.astype(jnp.float32), axis=0)


def unit_groups(units):
    return [(at, min(128, units - at)) for at in range(0, units, 128)]


def feed_forward_kernel(
    cut, block_ref, top_ref, wgu_hbm, wd_hbm,
    x_out, hid_out, dgu_out, down_out, mid_out,
    wgu_ref, wd_ref, xbuf, topbuf, hidbuf, dgubuf, downbuf, terms, near, from_left, from_right, outbox,
    local_sems, line_send, line_recv, near_send, near_recv, sum_send, sum_recv, across_send, across_recv,
):
    me, count = lax.axis_index("seq"), lax.axis_size("seq")
    chips, chip, core = count // 2, me // 2, lax.rem(me, 2)
    other = me + 1 - 2 * core
    tall = block_ref.shape[0]
    step = tall // cut
    units = wd_ref.shape[0]
    width = wd_ref.shape[1]
    meet(("line",))

    def lines(part):
        return pl.ds(part * step, step)

    def along(sign, i, part, source=None):
        at = ((1 - sign) // 2 * chips + i) * cut + part
        slot = x_out.at[me + 2 * sign * i, lines(part)]
        return pltpu.make_async_remote_copy(
            slot if source is None else source.at[lines(part)], slot,
            line_send.at[at], line_recv.at[at], on_line(-2 * sign), MESH,
        )

    def over(sign, i, part, source=None):
        at = ((1 - sign) // 2 * chips + i) * cut + part
        slot = x_out.at[me + 2 * sign * i, lines(part)]
        return pltpu.make_async_remote_copy(
            slot if source is None else source.at[lines(part)], slot,
            near_send.at[at], near_recv.at[at], sibling(), MESH,
        )

    def along_came(sign, i, part):
        at = ((1 - sign) // 2 * chips + i - 1) * cut + part
        slot = x_out.at[me + 2 * sign * i, lines(part)]
        pltpu.make_async_remote_copy(slot, slot, line_send.at[at], line_recv.at[at], sibling(), MESH).wait_recv()

    def over_came(sign, i, part):
        at = ((1 - sign) // 2 * chips + i) * cut + part
        slot = x_out.at[other + 2 * sign * i, lines(part)]
        pltpu.make_async_remote_copy(slot, slot, near_send.at[at], near_recv.at[at], sibling(), MESH).wait_recv()

    def more(sign):
        return jnp.where(sign > 0, chip > 0, chip < chips - 1)

    def across(dest, part):
        at = dest * cut + part
        return pltpu.make_async_remote_copy(
            terms.at[2 * dest + 1 - core, lines(part)], near.at[dest, lines(part)],
            across_send.at[at], across_recv.at[at], sibling(), MESH,
        )

    def onward(right, dest, part):
        at = ((0 if right else chips) + dest) * cut + part
        inbox = from_left if right else from_right
        return pltpu.make_async_remote_copy(
            outbox.at[dest, lines(part)], inbox.at[dest, lines(part)],
            sum_send.at[at], sum_recv.at[at], on_line(2 if right else -2), MESH,
        )

    own = pltpu.make_async_copy(block_ref, x_out.at[me], local_sems.at[0])
    own.start()
    for part in range(cut):
        for sign in (1, -1):

            @pl.when(more(sign))
            def _():
                along(sign, 0, part, block_ref).start()

        over(1, 0, part, block_ref).start()
    weights = [
        pltpu.make_async_copy(wgu_hbm, wgu_ref, local_sems.at[1]),
        pltpu.make_async_copy(wd_hbm, wd_ref, local_sems.at[2]),
    ]
    for copy in weights:
        copy.start()
    own.wait()
    for copy in weights:
        copy.wait()

    def compute(dest):
        x = xbuf[...].reshape(2 * tall, width)
        top = topbuf[...].reshape(2 * tall, width)
        for at, n in unit_groups(units):
            both = nn(x, wgu_ref[:, 2 * at : 2 * at + 2 * n])
            gate, up = both[:, :n], both[:, n:]
            d_hidden = nt(top, wd_ref[at : at + n, :])
            sig = 1.0 / (1.0 + jnp.exp(-gate))
            silu = gate * sig
            hidbuf[:, :, at : at + n] = (silu * up).astype(jnp.bfloat16).reshape(2, tall, n)
            d_gate = d_hidden * up * sig * (1.0 + gate * (1.0 - sig))
            d_both = jnp.concatenate([d_gate, d_hidden * silu], axis=1)
            dgubuf[:, :, 2 * at : 2 * at + 2 * n] = d_both.astype(jnp.bfloat16).reshape(2, tall, 2 * n)
        hid = hidbuf[...].reshape(2 * tall, units)
        dgu = dgubuf[...].reshape(2 * tall, 2 * units)
        wide = 512
        for at in range(0, width, wide):
            mid = nt(dgu, wgu_ref[at : at + wide, :]).astype(jnp.bfloat16)
            terms[pl.ds(2 * dest, 2), :, at : at + wide] = mid.reshape(2, tall, wide)
        for part in range(cut):
            across(dest, part).start()
        for at in range(0, width, wide):
            downbuf[:, :, at : at + wide] = nn(hid, wd_ref[:, at : at + wide]).astype(jnp.bfloat16).reshape(2, tall, wide)

    def send_sum(right, dest, part, first, in_turn=True):
        mine = [terms.at[2 * dest + core, lines(part)], near.at[dest, lines(part)]]
        across_came(dest, part)
        if first:
            add_into(outbox.at[dest, lines(part)], mine)
        else:
            inbox = from_left if right else from_right
            sum_came(right, dest, part)
            add_into(outbox.at[dest, lines(part)], mine + [inbox.at[dest, lines(part)]])
        if in_turn and part > 0:
            onward(right, dest, part - 1).wait_send()
        onward(right, dest, part).start()

    def across_came(dest, part):
        at = dest * cut + part
        there = near.at[dest, lines(part)]
        pltpu.make_async_remote_copy(there, there, across_send.at[at], across_recv.at[at], sibling(), MESH).wait_recv()

    def sum_came(right, dest, part):
        at = ((0 if right else chips) + dest) * cut + part
        there = (from_left if right else from_right).at[dest, lines(part)]
        pltpu.make_async_remote_copy(there, there, sum_send.at[at], sum_recv.at[at], sibling(), MESH).wait_recv()

    def inside(dest):
        return (dest >= 0) & (dest < chips)

    def visit(i, j):
        sign = 1 - 2 * j
        dest = chip + sign * i

        @pl.when(inside(dest) & (i + 1 - j > 0))
        def _():
            top = pltpu.make_async_copy(top_ref.at[pl.ds(2 * dest, 2)], topbuf, local_sems.at[1])
            top.start()
            for part in range(cut):
                over_came(sign, i, part)
            x = pltpu.make_async_copy(x_out.at[pl.ds(2 * dest, 2)], xbuf, local_sems.at[0])
            x.start()
            top.wait()
            x.wait()
            compute(dest)
            saved = [
                pltpu.make_async_copy(hidbuf, hid_out.at[pl.ds(2 * dest, 2)], local_sems.at[0]),
                pltpu.make_async_copy(dgubuf, dgu_out.at[pl.ds(2 * dest, 2)], local_sems.at[1]),
                pltpu.make_async_copy(downbuf, down_out.at[pl.ds(2 * dest, 2)], local_sems.at[2]),
            ]
            for copy in saved:
                copy.start()

            @pl.when((chip == 0) & (dest > 0) & (dest < chips - 1))
            def _():
                for part in range(cut):
                    send_sum(True, dest, part, True, False)

            @pl.when((chip == chips - 1) & (dest < chips - 1) & (dest > 0))
            def _():
                for part in range(cut):
                    send_sum(False, dest, part, True, False)

            for copy in saved:
                copy.wait()

    def distance(i, _):
        for sign in (1, -1):

            @pl.when((i > 0) & inside(chip + sign * i))
            def _():
                for part in range(cut):
                    along_came(sign, i, part)

                    @pl.when(more(sign))
                    def _():
                        along(sign, i, part).start()

                    over(sign, i, part).start()

        def side(j, _):
            visit(i, j)
            return 0

        lax.fori_loop(0, 2, side, 0)
        return 0

    lax.fori_loop(0, chips, distance, 0)

    @pl.when(chip == 0)
    def _():
        for part in range(cut):
            send_sum(True, chips - 1, part, True)

    @pl.when(chip == chips - 1)
    def _():
        for part in range(cut):
            send_sum(False, 0, part, True)

    def rightward():
        for i in range(1, chips - 1):

            @pl.when((chip > 0) & (chip + i < chips))
            def _():
                for part in range(cut):
                    send_sum(True, chip + i, part, False)

    def leftward():
        for i in range(1, chips - 1):

            @pl.when((chip < chips - 1) & (chip - i >= 0))
            def _():
                for part in range(cut):
                    send_sum(False, chip - i, part, False)

    @pl.when(chip < chips // 2)
    def _():
        rightward()
        leftward()

    @pl.when(chip >= chips // 2)
    def _():
        leftward()
        rightward()

    for part in range(cut):
        across_came(chip, part)
        mine = [terms.at[2 * chip + core, lines(part)], near.at[chip, lines(part)]]
        left_in, right_in = from_left.at[chip, lines(part)], from_right.at[chip, lines(part)]

        @pl.when(chip == 0)
        def _():
            sum_came(False, chip, part)
            add_into(mid_out.at[lines(part)], mine + [right_in])

        @pl.when(chip == chips - 1)
        def _():
            sum_came(True, chip, part)
            add_into(mid_out.at[lines(part)], mine + [left_in])

        @pl.when((chip > 0) & (chip < chips - 1))
        def _():
            sum_came(True, chip, part)
            sum_came(False, chip, part)
            add_into(mid_out.at[lines(part)], mine + [left_in, right_in])

    for part in range(cut):
        for dest in range(chips):
            across(dest, part).wait_send()

            early_right = (chip == 0) & (dest < chips - 1) | (part == cut - 1)
            early_left = (chip == chips - 1) & (dest > 0) | (part == cut - 1)

            @pl.when((chip < dest) & early_right)
            def _():
                onward(True, dest, part).wait_send()

            @pl.when((chip > dest) & early_left)
            def _():
                onward(False, dest, part).wait_send()

        for i in range(chips):
            for sign in (1, -1):
                there = (chip + sign * i >= 0) & (chip + sign * i < chips)

                @pl.when(there & more(sign))
                def _():
                    along(sign, i, part).wait_send()

                if i > 0 or sign > 0:

                    @pl.when(there)
                    def _():
                        over(sign, i, part).wait_send()


def feed_forward(cid, block, top, w_gu, w_d, cut=2):
    count = lax.axis_size("seq")
    chips = count // 2
    tall, width = block.shape
    units = w_d.shape[0]
    bf16 = jnp.bfloat16
    outs = [
        shape_of((count, tall, width), bf16),
        shape_of((count, tall, units), bf16),
        shape_of((count, tall, 2 * units), bf16),
        shape_of((count, tall, width), bf16),
        shape_of((tall, width), jnp.float32),
    ]
    box = pltpu.VMEM((chips, tall, width), bf16)
    dma = lambda n: pltpu.SemaphoreType.DMA((n,))
    anywhere, vmem = pl.BlockSpec(memory_space=pl.ANY), pl.BlockSpec(memory_space=pltpu.VMEM)
    flops = 2 * 2 * count * tall * width * 3 * units
    got = pl.pallas_call(
        functools.partial(feed_forward_kernel, cut),
        out_shape=outs,
        in_specs=[anywhere] * 4,
        out_specs=[anywhere] * 4 + [vmem],
        scratch_shapes=[
            pltpu.VMEM(w_gu.shape, bf16),
            pltpu.VMEM(w_d.shape, bf16),
            pltpu.VMEM((2, tall, width), bf16),
            pltpu.VMEM((2, tall, width), bf16),
            pltpu.VMEM((2, tall, units), bf16),
            pltpu.VMEM((2, tall, 2 * units), bf16),
            pltpu.VMEM((2, tall, width), bf16),
            pltpu.VMEM((count, tall, width), bf16),
            box, box, box, box,
            dma(3),
        ] + [dma(2 * chips * cut)] * 6 + [dma(chips * cut)] * 2,
        compiler_params=pltpu.CompilerParams(
            collective_id=cid, has_side_effects=True, vmem_limit_bytes=56 * 1024 * 1024
        ),
        cost_estimate=pl.CostEstimate(flops=flops, bytes_accessed=20 << 20, transcendentals=0),
        name="feed_forward",
    )(block, top.reshape(count, tall, width), w_gu, w_d)
    flat = [g.reshape(-1, g.shape[-1]) for g in got]
    return flat


def cross_rows(left_side, right_side):
    return lax.dot_general(left_side, right_side, (((0,), (0,)), ((), ())), preferred_element_type=jnp.float32)


def cross_cols(left_side, right_side):
    return lax.dot_general(left_side, right_side, (((1,), (1,)), ((), ())), preferred_element_type=jnp.float32)


def dot(left_side, right_side):
    return jnp.dot(left_side, right_side, preferred_element_type=jnp.float32)


def on_device(
    tokens,
    segments,
    norm_one,
    w_qkv,
    w_lr,
    lr_bias,
    w_gate,
    w_out,
    w_init,
    b_init,
    tnorm_w,
    tnorm_b,
    post_w,
    post_b,
    norm_two,
    w_gate_up,
    w_down,
    grad_out,
):
    floats = jnp.float32
    bf16 = jnp.bfloat16
    both = ("dp", "seq")
    packs, per_seq = lax.axis_size("dp"), lax.axis_size("seq")
    devices = packs * per_seq
    place = lax.axis_index("seq")
    span, width = tokens.shape[1], tokens.shape[2]
    rows = norm_one.shape[0]
    heads_all = lr_bias.shape[0]
    units = w_down.shape[0]
    length = span * per_seq
    blocks = length // MB
    heads = heads_all // per_seq
    aligned = rows % HD == 0
    outer = packs if aligned else 1
    inner = width // (outer * per_seq)
    mine = outer * inner

    def own_rows(array):
        cut = array.reshape((outer, per_seq, inner) + array.shape[1:])
        cut = lax.dynamic_index_in_dim(cut, place, 1, keepdims=False)
        return cut.reshape((mine,) + array.shape[1:])

    def put_rows(array):
        full = jnp.zeros((outer, per_seq, inner) + array.shape[1:], array.dtype)
        part = array.reshape((outer, 1, inner) + array.shape[1:])
        at = (0, place) + (0,) * (part.ndim - 2)
        return lax.dynamic_update_slice(full, part, at).reshape((width,) + array.shape[1:])

    extra = 128
    feature_cuts = [
        [(0, (part * outer + o) * per_seq * inner + s * inner, inner) for part in range(3) for o in range(outer)]
        + [(1, o * per_seq * inner + s * inner, inner) for o in range(outer)]
        for s in range(per_seq)
    ]
    filled = -(-units // 16) * 16
    unit_cuts = []
    for s in range(per_seq):
        cuts = []
        for at, n in unit_groups(packs * filled):
            for part in range(2):
                u = at
                while u < at + n:
                    pack, i = divmod(u, filled)
                    run = min((units if i < units else filled) - i, at + n - u)
                    first = (part * packs * per_seq + pack * per_seq + s) * units + i
                    cuts.append((0, first, run) if i < units else (None, 0, run))
                    u += run
        unit_cuts.append(cuts)

    spans = span // MB
    lr_places = w_lr.reshape(rows, outer, per_seq, heads // outer).transpose(0, 2, 1, 3).reshape(rows, per_seq, heads)
    tags = segments[0].reshape(1, 1, spans, MB)[:, :, :, 0].astype(bf16)
    beside_cols = jnp.concatenate(
        [
            lr_places,
            jnp.broadcast_to(jnp.stack([norm_one, norm_two], axis=1)[:, None], (rows, per_seq, 2)),
            jnp.broadcast_to(tags, (rows, per_seq, spans)),
            jnp.zeros((rows, per_seq, extra - heads - 2 - spans), bf16),
        ],
        axis=2,
    ).reshape(rows, per_seq * extra)
    mix_cuts = [cuts + [(2, s * extra, extra)] for s, cuts in enumerate(feature_cuts)]
    vectors = jnp.stack([b_init, tnorm_w, tnorm_b, post_w, post_b], axis=1)
    head_rows = jnp.concatenate([w_init, vectors, jnp.zeros((rows, extra - HD - 5), bf16)], axis=1)
    over_dp = (w_out, head_rows) if aligned else ()
    w_mix, rows_all, *got = first_exchange(
        split_columns((w_qkv, w_gate, beside_cols), mix_cuts), tokens[0], over_dp
    )
    if aligned:
        w_o, head_rows = got
    else:
        w_o, head_rows = (own_rows(lax.all_gather(a, both, axis=0, tiled=True)) for a in (w_out, head_rows))
    w_extra = w_mix[:, 4 * mine :]
    gain_one, gain_two = w_extra[:, heads].astype(floats), w_extra[:, heads + 1].astype(floats)
    pack_tags = w_extra.reshape(packs, per_seq, rows, extra)[:, :, 0, heads + 2 : heads + 2 + spans]
    pack_tags = lax.dynamic_index_in_dim(pack_tags.reshape(packs, blocks), lax.axis_index("dp"), 0, keepdims=False)
    fresh = jnp.concatenate([jnp.ones((1,), jnp.int32), (pack_tags[1:] != pack_tags[:-1]).astype(jnp.int32)])
    vec_own = head_rows[:, HD : HD + 5].astype(floats)
    post_gain, post_shift = vec_own[:, 3], vec_own[:, 4]
    bias_own = lax.dynamic_index_in_dim(lr_bias.reshape(outer, per_seq, heads // outer), place, 1, keepdims=False)
    bias_own = bias_own.reshape(heads).astype(floats)

    later_top, rows_all = lax.optimization_barrier((grad_out[0], rows_all))
    d_top = lax.all_gather(later_top, "seq", axis=0, tiled=True)
    gu_mine = split_columns((w_gate_up,), unit_cuts)

    inputs = rows_all.astype(floats)
    scale_one = lax.rsqrt(jnp.mean(inputs * inputs, -1, keepdims=True) + EPSILON)
    normed_in = inputs * scale_one
    x_one = (normed_in * gain_one).astype(bf16)
    qkv = dot(x_one, w_mix[:, : 3 * mine])
    gate_pre = dot(x_one, w_mix[:, 3 * mine : 4 * mine])
    lr_sigm = jax.nn.sigmoid(dot(x_one, w_extra)[:, :heads] + bias_own)
    e_rows = (lr_sigm * (1.0 / (HD * MB))).reshape(blocks, MB, heads).transpose(0, 2, 1).reshape(blocks, 1, heads * MB)

    def by_token(vector):
        return jnp.repeat(vector.reshape(heads, HD).T, MB, axis=1)

    init_w = head_rows[:, :HD].astype(floats).reshape(heads, HD, HD)
    init_w = (init_w - jnp.mean(init_w, -1, keepdims=True)).transpose(2, 0, 1).reshape(HD, heads * HD)
    init_b = vec_own[:, 0].reshape(heads, HD)
    init_b = (init_b - jnp.mean(init_b, -1, keepdims=True)).reshape(-1)
    gain_t, shift_t = by_token(vec_own[:, 1]), by_token(vec_own[:, 2])
    *results, gu_part, w_d = inner_forward(
        10, fresh, qkv, e_rows, init_w, by_token(init_b), gain_t, shift_t, (gu_mine,),
        (jnp.pad(w_down, ((0, filled - units), (0, 0))),),
    )
    w_d = w_d.reshape(-1, w_d.shape[-1])
    mixed, *saved = results

    mean_own = jnp.mean(mixed, -1)
    spread_own = jnp.sum((mixed - mean_own[:, None]) ** 2, -1)
    stats = gather_seq("share_moments", 2, jnp.stack([mean_own, spread_own]))
    mean_all = jnp.mean(stats[:, 0], 0)
    var_all = (jnp.sum(stats[:, 1], 0) + mine * jnp.sum((stats[:, 0] - mean_all) ** 2, 0)) * (1.0 / width)
    out_scale = lax.rsqrt(var_all + EPSILON)[:, None]
    out_hat = (mixed - mean_all[:, None]) * out_scale
    normed_out = out_hat * post_gain + post_shift
    gelu_gate, gelu_pull = jax.vjp(jax.nn.gelu, gate_pre)
    gated_unit = (gelu_gate * normed_out).astype(bf16)
    branch_terms, d_top = lax.optimization_barrier((dot(gated_unit, w_o).astype(bf16), d_top))
    branch, w_gu = scatter_with("scatter_branch", 3, branch_terms, (), (gu_part.reshape(-1, gu_part.shape[-1]),))
    inputs = tokens[0].astype(floats)
    residual = inputs + branch
    scale_two = lax.rsqrt(jnp.mean(residual * residual, -1, keepdims=True) + EPSILON)
    normed_mid = residual * scale_two
    x_two, hidden, d_gate_up, down, d_xtwo = feed_forward(5, (normed_mid * gain_two).astype(bf16), d_top, w_gu, w_d)
    pack_rows = lambda array: array.reshape((packs, -1) + array.shape[1:])
    g_gate_up = pack_rows(cross_rows(x_two, d_gate_up).astype(bf16))
    g_down = pack_rows(cross_rows(hidden, d_top).astype(bf16))
    g_two = jnp.sum(d_xtwo * normed_mid, axis=0)
    d_mid = d_xtwo * gain_two
    d_residual = grad_out[0].astype(floats) + scale_two * (
        d_mid - normed_mid * jnp.mean(d_mid * normed_mid, -1, keepdims=True)
    )
    d_branch, g_gate_up = gather_with(
        "gather_branch", 6, d_residual.astype(bf16), (), [(g_gate_up, None, None)]
    )
    g_gate_up = add_packs(g_gate_up).astype(bf16)
    down, d_branch = lax.optimization_barrier((down, d_branch))
    down = lax.psum_scatter(down, "seq", scatter_dimension=0, tiled=True)
    result = residual + down.astype(floats)
    g_out = cross_rows(gated_unit, d_branch).astype(bf16)
    d_unit = cross_cols(d_branch, w_o)
    d_normed = d_unit * gelu_gate
    g_post_w = jnp.sum(d_normed * out_hat, axis=0)
    g_post_b = jnp.sum(d_normed, axis=0)
    d_hat = d_normed * post_gain
    sums = gather_seq("share_sums", 7, jnp.stack([jnp.sum(d_hat, -1), jnp.sum(d_hat * out_hat, -1)]))
    sums = jnp.sum(sums, 0) * (1.0 / width)
    d_mixed = out_scale * (d_hat - sums[0][:, None] - out_hat * sums[1][:, None])
    d_gate_pre = gelu_pull(d_unit * normed_out)[0].astype(bf16)
    place_rows = lambda array: array.reshape((per_seq, -1) + array.shape[1:])
    g_gate = pack_rows(cross_rows(x_one, d_gate_pre).astype(bf16))
    d_qkv, d_rate, d_w0, d_c0, d_gain, d_shift, g_gate_up, g_down, g_gate, *g_outs = inner_backward(
        11, fresh, qkv, e_rows, d_mixed, saved, gain_t, shift_t, (place_rows(g_gate_up),),
        [(g_down, None, None), (g_gate, None, None)] + [(pack_rows(g_out), None, None)] * aligned,
    )
    (g_gate_up,) = join_columns(g_gate_up, (w_gate_up.shape[1],), unit_cuts)
    g_down = add_packs(g_down)[:units]
    if aligned:
        g_out = add_packs(g_outs[0])
    else:
        g_out = lax.psum_scatter(put_rows(g_out), both, scatter_dimension=0, tiled=True).astype(floats)
    d_rate = d_rate.reshape(blocks, heads, MB).transpose(0, 2, 1).reshape(length, heads)
    d_logit = (d_rate * (1.0 / HD) * lr_sigm * (1.0 - lr_sigm)).astype(bf16)
    g_qkv = cross_rows(x_one, d_qkv).astype(bf16)
    d_logit_wide = jnp.pad(d_logit, ((0, 0), (0, extra - heads)))
    d_xone = cross_cols(jnp.concatenate([d_qkv, d_gate_pre, d_logit_wide], axis=1), w_mix)
    g_one = jnp.sum(d_xone * (lax.optimization_barrier(rows_all).astype(floats) * scale_one), axis=0)

    lane = jnp.arange(extra)[None, :]
    g_bias = jnp.pad(jnp.sum(d_logit.astype(floats), axis=0), (heads + 2, extra - 2 * heads - 2))
    g_beside = cross_rows(x_one, d_logit_wide) + jnp.where(lane == heads, g_one[:, None], 0.0)
    g_beside = (g_beside + jnp.where(lane == heads + 1, g_two[:, None], 0.0) + g_bias[None, :]).astype(bf16)

    def from_token(array):
        return jnp.sum(array.reshape(HD, heads, MB), -1).T.reshape(mine)

    g_vec = jnp.stack(
        [d_c0.reshape(HD, heads, MB)[:, :, 0].T.reshape(mine), from_token(d_gain), from_token(d_shift), g_post_w, g_post_b],
        axis=1,
    )
    g_heads = jnp.concatenate(
        [d_w0.reshape(HD, heads, HD).transpose(1, 2, 0).reshape(mine, HD), g_vec, jnp.zeros((mine, extra - HD - 5), floats)],
        axis=1,
    )
    swaps = [(pack_rows(g_beside), None, None), (pack_rows(g_qkv), None, None)]
    d_xone, *got = scatter_with(
        "scatter_first", 8, d_xone.astype(bf16), [(pack_rows(g_heads), None, None)] * aligned + swaps
    )
    if aligned:
        g_heads = add_packs(got[0])
    else:
        g_heads = lax.psum_scatter(put_rows(g_heads), both, scatter_dimension=0, tiled=True)
    g_mix = jnp.concatenate([add_packs(got[-1]), add_packs(g_gate), add_packs(got[-2])], axis=1).astype(bf16)
    (g_mix,) = swap_places("return_columns", 9, (place_rows(g_mix),))
    g_qkv, g_gate = join_columns(g_mix, (w_qkv.shape[1], w_gate.shape[1]), feature_cuts)
    g_beside = g_mix[:, :, 4 * mine :].astype(floats)
    g_norms = jnp.sum(g_beside[:, :, heads : heads + 2], 0)

    def by_head(part):
        part = part.reshape(part.shape[:-1] + (outer, heads // outer))
        return jnp.moveaxis(part, 0, -2).reshape(part.shape[1:-2] + (heads_all,))

    scale_one = lax.rsqrt(jnp.mean(inputs * inputs, -1, keepdims=True) + EPSILON)
    normed_in = inputs * scale_one
    d_inner = d_xone * gain_one
    d_tokens = d_residual + scale_one * (
        d_inner - normed_in * jnp.mean(d_inner * normed_in, -1, keepdims=True)
    )
    return (
        result.astype(bf16)[None],
        d_tokens.astype(bf16)[None],
        g_norms[:, 0],
        g_qkv,
        by_head(g_beside[:, :, :heads]),
        by_head(g_beside[:, 0, heads + 2 : 2 * heads + 2]),
        g_gate,
        g_out,
        g_heads[:, :HD],
        g_heads[:, HD],
        g_heads[:, HD + 1],
        g_heads[:, HD + 2],
        g_heads[:, HD + 3],
        g_heads[:, HD + 4],
        g_norms[:, 1],
        g_gate_up,
        g_down,
    )


def solution(mesh):
    placed = (
        P("dp", "seq", None),
        P("dp", "seq"),
        P(("dp", "seq")),
        P(("dp", "seq"), None),
        P(("dp", "seq"), None),
        P(),
        P(("dp", "seq"), None),
        P(("dp", "seq"), None),
        P(("dp", "seq"), None),
        P(("dp", "seq")),
        P(("dp", "seq")),
        P(("dp", "seq")),
        P(("dp", "seq")),
        P(("dp", "seq")),
        P(("dp", "seq")),
        P(("dp", "seq"), None),
        P(("dp", "seq"), None),
        P("dp", "seq", None),
    )
    return jax.shard_map(
        on_device,
        mesh=mesh,
        in_specs=placed,
        out_specs=(
            P("dp", "seq", None),
            P("dp", "seq", None),
            P(("dp", "seq")),
            P(("dp", "seq"), None),
            P(("dp", "seq"), None),
            P(),
            P(("dp", "seq"), None),
            P(("dp", "seq"), None),
            P(("dp", "seq"), None),
            P(("dp", "seq")),
            P(("dp", "seq")),
            P(("dp", "seq")),
            P(("dp", "seq")),
            P(("dp", "seq")),
            P(("dp", "seq")),
            P(("dp", "seq"), None),
            P(("dp", "seq"), None),
        ),
        check_vma=False,
    )
```

```python
import functools
import jax
import jax.numpy as jnp
from jax import lax
from jax.experimental import pallas as pl
from jax.experimental.pallas import tpu as pltpu
from jax.sharding import PartitionSpec as P

HD = 64
MB = 16
PER = 8
EPSILON = 1e-06


def nn(left, right):
    return lax.dot_general(left, right, (((1,), (0,)), ((), ())), preferred_element_type=jnp.float32)


def nt(left, right):
    return lax.dot_general(left, right, (((1,), (1,)), ((), ())), preferred_element_type=jnp.float32)


def tn(left, right):
    return lax.dot_general(left, right, (((0,), (0,)), ((), ())), preferred_element_type=jnp.float32)


def halves(value):
    high = value.astype(jnp.bfloat16)
    return high, (value - high.astype(jnp.float32)).astype(jnp.bfloat16)


def head_masks(heads):
    ht, hi = heads * MB, heads * HD

    def iota(shape, axis):
        return lax.broadcasted_iota(jnp.int32, shape, axis)

    own = (iota((ht, hi), 0) // MB == iota((ht, hi), 1) // HD).astype(jnp.float32)
    unit = (iota((HD, hi), 0) == iota((HD, hi), 1) % HD).astype(jnp.bfloat16)
    row, col = iota((ht, ht), 0), iota((ht, ht), 1)
    same = (row // MB == col // MB).astype(jnp.bfloat16)
    ts, tt = row % MB, col % MB
    later = jnp.where((row // MB == col // MB) & (ts <= tt), MB / (tt + 1).astype(jnp.float32), 0.0)
    earlier = jnp.where((row // MB == col // MB) & (tt <= ts), MB / (ts + 1).astype(jnp.float32), 0.0)
    return own, unit, same, later, earlier


def spread(rows, own, heads):
    return (jnp.concatenate([rows] * heads, axis=0) * own).astype(jnp.bfloat16)


def fold(values, heads):
    total = values[:MB]
    for h in range(1, heads):
        total = total + values[h * MB : (h + 1) * MB]
    return total


def turned(rows, own, unit, heads):
    wide = jnp.concatenate([rows] * heads, axis=0) * own
    high, low = halves(wide)
    return nt(unit, high) + nt(unit, low)


def mean0(value):
    return jnp.sum(value, axis=0, keepdims=True) * (1.0 / HD)


def forward_kernel(heads, per, over_seq, over_dp, fresh_ref, qkv_ref, e_ref, w0_ref, c0_ref, gain_ref, shift_ref, *refs):
    moved = over_seq + over_dp
    sources, refs = refs[:moved], refs[moved:]
    mixed_ref, wsave_ref, hat_ref, slope_ref, gap_ref, bar_ref, rows_ref = refs[:7]
    results, (w_ref, c_ref, send_sems, recv_sems, *rooms) = refs[7 : 7 + moved], refs[7 + moved :]
    jobs = [swap_seq] * over_seq + [spread_dp] * over_dp
    beside(
        ("seq", "dp"), send_sems, recv_sems, rooms,
        lambda wires: [job(wires, a, b) for job, a, b in zip(jobs, sources, results)],
    )
    hi = heads * HD
    own, unit, same, later, _ = head_masks(heads)
    gain, shift, w0, c0 = gain_ref[...], shift_ref[...], w0_ref[...], c0_ref[...]
    gain2 = gain * gain

    @pl.when(pl.program_id(0) == 0)
    def _():
        w_ref[...] = jnp.zeros_like(w_ref)
        c_ref[...] = jnp.zeros_like(c_ref)

    w, c = w_ref[...], c_ref[...]
    for b in range(per):
        is_fresh = fresh_ref[pl.program_id(0) * per + b] != 0
        lines = slice(b * MB, (b + 1) * MB)
        q, k, v = qkv_ref[lines, :hi], qkv_ref[lines, hi : 2 * hi], qkv_ref[lines, 2 * hi :]
        e = e_ref[b]
        kb, qb = spread(k, own, heads), spread(q, own, heads)
        gap = shift - turned(v - k, own, unit, heads)
        base = gain * gap
        w = jnp.where(is_fresh, w0, w)
        c = jnp.where(is_fresh, c0, c)
        wb = w.astype(jnp.bfloat16)
        wsave_ref[b] = wb
        z = nt(wb, kb) + c
        gz = gain2 * z
        s = lax.rsqrt(mean0(z * z) + EPSILON)
        mean_g = s * mean0(gz) + mean0(base)
        mean_gx = s * (s * mean0(gz * z) + mean0(base * z))
        hat = s * z
        slope = s * (gain2 * hat + base - mean_g - hat * mean_gx)
        eb = (e * slope).astype(jnp.bfloat16)
        mix = (later * (nt(kb, qb) + 1.0)).astype(jnp.bfloat16)
        zbar = nt(wb, qb) + c - nn(eb, mix)
        w = w - nn(eb, kb)
        c = c - nn(eb, same)
        sbar = lax.rsqrt(mean0(zbar * zbar) + EPSILON)
        bar = zbar * sbar
        high, low = halves(gain * bar + shift)
        mixed_ref[lines, :] = q + fold((tn(high, unit) + tn(low, unit)) * own, heads)
        hat_ref[b] = hat
        slope_ref[b] = slope
        gap_ref[b] = gap
        bar_ref[b] = bar
        rows_ref[b] = jnp.concatenate([s, sbar, mean_g, mean_gx], axis=0)
    w_ref[...] = w
    c_ref[...] = c


def inner_forward(cid, fresh, qkv, e_rows, w0, c0, gain, shift, seq_arrays, dp_arrays):
    arrays = tuple(seq_arrays) + tuple(dp_arrays)
    packs = lax.axis_size("dp")
    tokens, heads = qkv.shape[0], qkv.shape[1] // (3 * HD)
    ht, hi = heads * MB, heads * HD
    blocks = tokens // MB
    per = PER
    f32 = jnp.float32
    whole = lambda shape: pl.BlockSpec(shape, lambda i: (0, 0))
    save = pl.BlockSpec((per, HD, ht), lambda i: (i, 0, 0))
    return pl.pallas_call(
        functools.partial(forward_kernel, heads, per, len(seq_arrays), len(dp_arrays)),
        grid=(blocks // per,),
        in_specs=[
            pl.BlockSpec(memory_space=pltpu.SMEM),
            pl.BlockSpec((per * MB, 3 * hi), lambda i: (i, 0)),
            pl.BlockSpec((per, 1, ht), lambda i: (i, 0, 0)),
            whole((HD, hi)), whole((HD, ht)), whole((HD, ht)), whole((HD, ht)),
        ] + [pl.BlockSpec(memory_space=pl.ANY)] * len(arrays),
        out_specs=[
            pl.BlockSpec((per * MB, hi), lambda i: (i, 0)),
            pl.BlockSpec((per, HD, hi), lambda i: (i, 0, 0)),
            save, save, save, save,
            pl.BlockSpec((per, 4, ht), lambda i: (i, 0, 0)),
        ] + [pl.BlockSpec(memory_space=pl.ANY)] * len(arrays),
        out_shape=[
            jax.ShapeDtypeStruct((tokens, hi), f32),
            jax.ShapeDtypeStruct((blocks, HD, hi), jnp.bfloat16),
        ] + [jax.ShapeDtypeStruct((blocks, HD, ht), f32)] * 4 + [jax.ShapeDtypeStruct((blocks, 4, ht), f32)]
        + [shape_of(a.shape, a.dtype) for a in seq_arrays]
        + [shape_of((packs,) + a.shape, a.dtype) for a in dp_arrays],
        scratch_shapes=[pltpu.VMEM((HD, hi), f32), pltpu.VMEM((HD, ht), f32)]
        + wire_sems(len(seq_arrays) * lax.axis_size("seq") + len(dp_arrays) * packs)
        + [room(a.shape[1:], a.dtype) for a in seq_arrays] + [room(a.shape, a.dtype) for a in dp_arrays],
        compiler_params=pltpu.CompilerParams(
            vmem_limit_bytes=48 * 1024 * 1024, collective_id=cid, has_side_effects=True
        ),
        name="inner_forward",
    )(fresh, qkv, e_rows, w0, c0, gain, shift, *arrays)


def backward_kernel(heads, per, over_seq, items, fresh_ref, qkv_ref, e_ref, dmix_ref, wsave_ref, hat_ref, slope_ref,
                    gap_ref, bar_ref, rows_ref, gain_ref, shift_ref, *refs):
    moved = over_seq + len(items)
    sources, refs = refs[:moved], refs[moved:]
    sources = list(sources[:over_seq]) + [window(ref, item) for ref, item in zip(sources[over_seq:], items)]
    dqkv_ref, drate_ref, dw0_ref, dc0_ref, dgain_ref, dshift_ref = refs[:6]
    results, (a_ref, ac_ref, send_sems, recv_sems, *rooms) = refs[6 : 6 + moved], refs[6 + moved :]
    swaps = [swap_seq] * over_seq + [swap_dp] * len(items)
    beside(
        ("seq", "dp"), send_sems, recv_sems, rooms,
        lambda wires: [swap(wires, a, b) for swap, a, b in zip(swaps, sources, results)],
    )
    hi, ht = heads * HD, heads * MB
    own, unit, same, later, earlier = head_masks(heads)
    gain = gain_ref[...]
    gain2 = gain * gain
    step = pl.program_id(0)

    @pl.when(step == 0)
    def _():
        for ref in (a_ref, ac_ref, dw0_ref, dc0_ref, dgain_ref, dshift_ref):
            ref[...] = jnp.zeros_like(ref)

    a, ac = a_ref[...], ac_ref[...]
    dw0, dc0, dgain, dshift = dw0_ref[...], dc0_ref[...], dgain_ref[...], dshift_ref[...]
    for b in reversed(range(per)):
        is_fresh = fresh_ref[(pl.num_programs(0) - 1 - step) * per + b] != 0
        lines = slice(b * MB, (b + 1) * MB)
        q, k = qkv_ref[lines, :hi], qkv_ref[lines, hi : 2 * hi]
        e = e_ref[b]
        wb, hat, slope, gap, bar = wsave_ref[b], hat_ref[b], slope_ref[b], gap_ref[b], bar_ref[b]
        s, sbar, mean_g, mean_gx = (rows_ref[b][i : i + 1] for i in range(4))
        kb, qb = spread(k, own, heads), spread(q, own, heads)
        dout = dmix_ref[lines, :]
        dturn = turned(dout, own, unit, heads)
        head = gain * dturn
        dbar = sbar * (head - mean0(head) - bar * mean0(head * bar))
        dbarb = dbar.astype(jnp.bfloat16)
        scores = nt(qb, kb) + 1.0
        mix = earlier * scores
        s2 = s * s
        gh = gain2 * hat
        alpha = s2 * (gain2 - mean_gx)
        kappa = s2 * (gain2 * hat + gap * gain + gh)
        kappa1 = mean_g + mean0(gh)
        kappa2 = 2.0 * mean_gx + mean0(gh * hat)
        ab = a.astype(jnp.bfloat16)
        ka = nt(ab, kb) + ac
        u = -e * (ka + nn(dbarb, mix.astype(jnp.bfloat16)))
        ug = gain2 * u
        r2 = mean0(u * hat)
        r3 = mean0(ug)
        r4 = mean0(ug * hat)
        r5 = mean0(u * slope)
        row1 = s2 * (r3 - r2 * kappa1)
        row2 = s2 * (r4 - r2 * kappa2) + s * r5
        dz = alpha * u - r2 * kappa - row1 - hat * row2
        dzb = dz.astype(jnp.bfloat16)
        dg = s * (u - hat * r2)
        a_next = a + nn(dbarb, qb) + nn(dzb, kb)
        ac_next = ac + nn(dbarb, same) + nn(dzb, same)
        dm = -tn(dbarb, slope.astype(jnp.bfloat16))
        ds = (earlier * e * dm).astype(jnp.bfloat16)
        drate_ref[b] = (jnp.sum(mix * dm, axis=0, keepdims=True) - jnp.sum(ka * slope, axis=0, keepdims=True)) * (1.0 / MB)
        dgb = (gain * dg)
        ndg = fold(tn(dgb.astype(jnp.bfloat16), unit) * own, heads)
        dq = dout + fold(tn(dbarb, wb) * own + nn(ds, kb), heads)
        dk = ndg + fold((tn(dzb, wb) - tn((e * slope).astype(jnp.bfloat16), ab)) * own + tn(ds, qb), heads)
        dqkv_ref[lines, :hi] = dq.astype(jnp.bfloat16)
        dqkv_ref[lines, hi : 2 * hi] = dk.astype(jnp.bfloat16)
        dqkv_ref[lines, 2 * hi :] = (-ndg).astype(jnp.bfloat16)
        dgain = dgain + dturn * bar + dg * (2.0 * gain * hat + gap)
        dshift = dshift + dturn + dgb
        dw0 = dw0 + jnp.where(is_fresh, a_next, 0.0)
        dc0 = dc0 + jnp.where(is_fresh, ac_next, 0.0)
        a = jnp.where(is_fresh, 0.0, a_next)
        ac = jnp.where(is_fresh, 0.0, ac_next)
    a_ref[...] = a
    ac_ref[...] = ac
    dw0_ref[...] = dw0
    dc0_ref[...] = dc0
    dgain_ref[...] = dgain
    dshift_ref[...] = dshift


def inner_backward(cid, fresh, qkv, e_rows, dmix, saved, gain, shift, seq_arrays, items):
    arrays = tuple(seq_arrays) + tuple(item[0] for item in items)
    tokens, heads = qkv.shape[0], qkv.shape[1] // (3 * HD)
    ht, hi = heads * MB, heads * HD
    blocks = tokens // MB
    per = PER
    last = blocks // per - 1
    f32 = jnp.float32
    whole = lambda shape: pl.BlockSpec(shape, lambda i: (0, 0))
    three = lambda shape: pl.BlockSpec(shape, lambda i: (last - i, 0, 0))
    two = lambda shape: pl.BlockSpec(shape, lambda i: (last - i, 0))
    save = three((per, HD, ht))
    return pl.pallas_call(
        functools.partial(backward_kernel, heads, per, len(seq_arrays), items),
        grid=(blocks // per,),
        in_specs=[
            pl.BlockSpec(memory_space=pltpu.SMEM),
            two((per * MB, 3 * hi)), three((per, 1, ht)), two((per * MB, hi)),
            three((per, HD, hi)), save, save, save, save, three((per, 4, ht)),
            whole((HD, ht)), whole((HD, ht)),
        ] + [pl.BlockSpec(memory_space=pl.ANY)] * len(arrays),
        out_specs=[
            two((per * MB, 3 * hi)), three((per, 1, ht)),
            whole((HD, hi)), whole((HD, ht)), whole((HD, ht)), whole((HD, ht)),
        ] + [pl.BlockSpec(memory_space=pl.ANY)] * len(arrays),
        out_shape=[
            jax.ShapeDtypeStruct((tokens, 3 * hi), jnp.bfloat16),
            jax.ShapeDtypeStruct((blocks, 1, ht), f32),
            jax.ShapeDtypeStruct((HD, hi), f32),
        ] + [jax.ShapeDtypeStruct((HD, ht), f32)] * 3 + [shape_of(a.shape, a.dtype) for a in seq_arrays]
        + [window_shape(item) for item in items],
        scratch_shapes=[pltpu.VMEM((HD, hi), f32), pltpu.VMEM((HD, ht), f32)]
        + wire_sems(len(seq_arrays) * lax.axis_size("seq") + len(items) * lax.axis_size("dp"))
        + [room(a.shape[1:], a.dtype) for a in seq_arrays]
        + [room(window_shape(item).shape[1:], item[0].dtype) for item in items],
        compiler_params=pltpu.CompilerParams(
            vmem_limit_bytes=48 * 1024 * 1024, collective_id=cid, has_side_effects=True
        ),
        name="inner_backward",
    )(fresh, qkv, e_rows, dmix, *saved, gain, shift, *arrays)

MESH = pl.DeviceIdType.MESH


class Kept:
    def __init__(self, source, target, room, sem):
        self.bring = pltpu.make_async_copy(source, room, sem)
        self.leave = pltpu.make_async_copy(room, target, sem)

    def start(self):
        self.bring.start()
        self.bring.wait()
        self.leave.start()

    def wait(self):
        self.leave.wait()


class Wires:
    def __init__(self, send_sems, recv_sems, rooms=(), started=False):
        self.send_sems, self.recv_sems, self.used, self.started = send_sems, recv_sems, 0, started
        self.rooms = list(rooms)

    def begin(self, copy):
        if not self.started:
            copy.start()
        return copy

    def copy(self, source, target, device):
        at = self.number()
        return self.numbered(at, source, target, device)

    def number(self):
        self.used += 1
        return self.used - 1

    def numbered(self, at, source, target, device):
        return pltpu.make_async_remote_copy(
            src_ref=source,
            dst_ref=target,
            send_sem=self.send_sems.at[at],
            recv_sem=self.recv_sems.at[at],
            device_id=device,
            device_id_type=MESH,
        )

    def load(self, source, target):
        return pltpu.make_async_copy(source, target, self.send_sems.at[self.number()])

    def keep(self, source, target):
        return Kept(source, target, self.rooms.pop(0), self.send_sems.at[self.number()])


def on_line(step):
    return {"seq": lax.axis_index("seq") + step}


def sibling():
    me = lax.axis_index("seq")
    return {"seq": me + 1 - 2 * lax.rem(me, 2)}


def pack_peer(step):
    packs = lax.axis_size("dp")
    return {"dp": lax.rem(lax.axis_index("dp") + step, packs)}


def seq_peer(step):
    count = lax.axis_size("seq")
    return {"seq": lax.rem(lax.axis_index("seq") + step, count)}


def meet(groups):
    barrier = pltpu.get_barrier_semaphore()
    me, count = lax.axis_index("seq"), lax.axis_size("seq")

    def greet(device):
        pl.semaphore_signal(barrier, inc=1, device_id=device, device_id_type=MESH)

    peers = 0
    if "dp" in groups:
        for step in range(1, lax.axis_size("dp")):
            greet(pack_peer(step))
        peers += lax.axis_size("dp") - 1
    if "seq" in groups:
        for step in range(1, count):
            greet(seq_peer(step))
        peers += count - 1
    elif "line" in groups:
        greet(sibling())

        @pl.when(me >= 2)
        def _():
            greet(on_line(-2))

        @pl.when(me < count - 2)
        def _():
            greet(on_line(2))

        peers += 1 + jnp.minimum(me // 2, 1) + jnp.minimum((count - 1 - me) // 2, 1)
    pl.semaphore_wait(barrier, peers)


def gather_line(wires, source, out, cut):
    me, count = lax.axis_index("seq"), lax.axis_size("seq")
    chips, chip = count // 2, me // 2
    step = source.shape[0] // cut
    other = me + 1 - 2 * lax.rem(me, 2)

    def piece(slot, part):
        return out.at[slot, pl.ds(part * step, step)]

    own = wires.keep(source, out.at[me])
    numbers = {(way, i, part): wires.number() for way in "rlRL" for i in range(chips) for part in range(cut)}

    def copy(way, i, part):
        slot = me - 2 * i if way in "rR" else me + 2 * i
        start = source.at[pl.ds(part * step, step)] if i == 0 else piece(slot, part)
        device = {"r": on_line(2), "l": on_line(-2), "R": sibling(), "L": sibling()}[way]
        return wires.numbered(numbers[way, i, part], start, piece(slot, part), device)

    def arrived(way, i, part):
        if way in "rl":
            slot = me - 2 * (i + 1) if way == "r" else me + 2 * (i + 1)
        else:
            slot = other - 2 * i if way == "R" else other + 2 * i
        there = piece(slot, part)
        wires.numbered(numbers[way, i, part], there, there, sibling()).wait_recv()

    @pl.when(chip < chips - 1)
    def _():
        for part in range(cut):
            copy("r", 0, part).start()

    @pl.when(chip > 0)
    def _():
        for part in range(cut):
            copy("l", 0, part).start()

    for part in range(cut):
        copy("R", 0, part).start()
    own.start()
    for i in range(1, chips):
        for part in range(cut):
            yield True

            @pl.when(chip >= i)
            def _():
                arrived("r", i - 1, part)

                @pl.when(chip < chips - 1)
                def _():
                    copy("r", i, part).start()

                copy("R", i, part).start()

            @pl.when(chip + i <= chips - 1)
            def _():
                arrived("l", i - 1, part)

                @pl.when(chip > 0)
                def _():
                    copy("l", i, part).start()

                copy("L", i, part).start()

    yield True
    own.wait()
    for i in range(chips):
        for part in range(cut):
            if i == 0:
                arrived("R", 0, part)
                copy("R", 0, part).wait_send()
            else:

                @pl.when(chip >= i)
                def _():
                    arrived("R", i, part)
                    copy("R", i, part).wait_send()

                @pl.when(chip + i <= chips - 1)
                def _():
                    arrived("L", i, part)
                    copy("L", i, part).wait_send()

            @pl.when((chip >= i) & (chip < chips - 1))
            def _():
                copy("r", i, part).wait_send()

            @pl.when((chip + i <= chips - 1) & (chip > 0))
            def _():
                copy("l", i, part).wait_send()


def add_into(out, parts, rows=16):
    def body(i, _):
        lines = pl.ds(pl.multiple_of(i * rows, rows), rows)
        total = parts[0][lines, :].astype(jnp.float32)
        for part in parts[1:]:
            total = total + part[lines, :].astype(jnp.float32)
        out[lines, :] = total.astype(out.dtype)
        return 0

    lax.fori_loop(0, out.shape[0] // rows, body, 0)


def scatter_line(wires, produce, source, out, near, from_left, from_right, outbox, cut):
    me, count = lax.axis_index("seq"), lax.axis_size("seq")
    chips, chip, core = count // 2, me // 2, lax.rem(me, 2)
    step = source.shape[1] // cut

    def lines(part):
        return pl.ds(part * step, step)

    order = []
    for i in range(chips // 2):
        order += [chips - 1 - i, i]
    order += [chips // 2] if chips % 2 else []
    across = {}
    for dest in order:
        for part in range(cut):
            across[dest, part] = wires.copy(
                source.at[2 * dest + 1 - core, lines(part)], near.at[dest, lines(part)], sibling()
            )

    def begin(dests):
        for dest in dests:
            produce(dest)
            for part in range(cut):
                across[dest, part].start()

    right, left = {}, {}
    for dest in range(chips):
        for part in range(cut):
            right[dest, part] = wires.copy(outbox.at[dest, lines(part)], from_left.at[dest, lines(part)], on_line(2))
            left[dest, part] = wires.copy(outbox.at[dest, lines(part)], from_right.at[dest, lines(part)], on_line(-2))
    def handle(part, ahead, turn, dest, table, inbox, first):
        terms = [source.at[2 * dest + core, lines(part)], near.at[dest, lines(part)]]

        @pl.when(ahead & turn)
        def _():
            across[dest, part].wait_recv()

            @pl.when(first)
            def _():
                add_into(outbox.at[dest, lines(part)], terms)

            @pl.when(jnp.logical_not(first))
            def _():
                table[dest, part].wait_recv()
                add_into(outbox.at[dest, lines(part)], terms + [inbox.at[dest, lines(part)]])

            table[dest, part].start()

    for i in range(chips - 1):
        begin(order[2 * i : 2 * i + 2])
        for part in range(cut):
            yield True
            rightward, leftward = (chips - 1 - i, right, from_left, chip == 0), (i, left, from_right, chip == chips - 1)
            handle(part, chip < chips - 1 - i, chip < chips // 2, *rightward)
            handle(part, chip > i, True, *leftward)
            handle(part, chip < chips - 1 - i, chip >= chips // 2, *rightward)

    for part in range(cut):
        yield True
        for dest in range(chips):

            @pl.when(chip == dest)
            def _():
                across[dest, part].wait_recv()
                terms = [source.at[2 * dest + core, lines(part)], near.at[dest, lines(part)]]
                if dest > 0:
                    right[dest, part].wait_recv()
                    terms = terms + [from_left.at[dest, lines(part)]]
                if dest < chips - 1:
                    left[dest, part].wait_recv()
                    terms = terms + [from_right.at[dest, lines(part)]]
                add_into(out.at[lines(part)], terms)

    for dest in range(chips):
        for part in range(cut):
            across[dest, part].wait_send()

            @pl.when(chip < dest)
            def _():
                right[dest, part].wait_send()

            @pl.when(chip > dest)
            def _():
                left[dest, part].wait_send()


def swap_seq(wires, source, out):
    me, count = lax.axis_index("seq"), lax.axis_size("seq")
    own = wires.keep(source.at[me], out.at[me])
    sent = []
    for step in range(1, count):
        peer = lax.rem(me + step, count)
        sent.append(wires.copy(source.at[peer], out.at[me], seq_peer(step)))
        wires.begin(sent[-1])
    wires.begin(own)
    yield True
    own.wait()
    for copy in sent:
        copy.wait()


def spread_seq(wires, source, out):
    me, count = lax.axis_index("seq"), lax.axis_size("seq")
    own = wires.keep(source, out.at[me])
    sent = []
    for step in range(1, count):
        sent.append(wires.copy(source, out.at[me], seq_peer(step)))
        wires.begin(sent[-1])
    wires.begin(own)
    yield True
    own.wait()
    for copy in sent:
        copy.wait()


def swap_dp(wires, source, out):
    me, count = lax.axis_index("dp"), lax.axis_size("dp")
    own = wires.keep(source.at[me], out.at[me])
    sent = []
    for step in range(1, count):
        sent.append(wires.copy(source.at[lax.rem(me + step, count)], out.at[me], pack_peer(step)))
        wires.begin(sent[-1])
    wires.begin(own)
    yield True
    own.wait()
    for copy in sent:
        copy.wait()


PIECES = 4
HALVES = 8 + 4 * PIECES


def halves_dp(wires, source, out, idle=1):
    me, count = lax.axis_index("dp"), lax.axis_size("dp")
    rows, width = source.shape
    by_rows = rows % (16 * PIECES) == 0
    step = (rows if by_rows else width) // PIECES
    own = wires.keep(source, out.at[me])
    bit = lax.rem(me, 2)
    flip = {1: me + 1 - 2 * bit, 2: lax.rem(me + 2, 4)}
    part = lambda ref, i: ref.at[pl.ds(i * step, step)] if by_rows else ref.at[:, pl.ds(i * step, step)]
    first, then = {}, {}

    def send(way, j):
        first[way, j] = wires.copy(part(source, j), part(out.at[me], j), {"dp": flip[way]})
        first[way, j].start()

    half = PIECES // 2
    for i in range(half):
        send(1, i)
        send(2, half + i)
    own.start()
    for _ in range(idle):
        yield True
    for i in range(half):
        for way, j in ((1, i), (2, half + i)):
            yield True
            first[way, j].wait_recv()
            came = part(out.at[flip[way]], j)
            then[way, j] = wires.copy(came, came, {"dp": flip[3 - way]})
            then[way, j].start()
            send(3 - way, j)
    yield PATIENT
    own.wait()
    for i in range(half):
        for way, j in ((2, i), (1, half + i)):
            first[way, j].wait_recv()
    for copy in first.values():
        copy.wait_send()
    for copy in then.values():
        copy.wait()


def spread_dp(wires, source, out):
    me, count = lax.axis_index("dp"), lax.axis_size("dp")
    own = wires.keep(source, out.at[me])
    sent = []
    for step in range(1, count):
        sent.append(wires.copy(source, out.at[me], pack_peer(step)))
        wires.begin(sent[-1])
    wires.begin(own)
    yield True
    own.wait()
    for copy in sent:
        copy.wait()


PATIENT = None


def run_all(jobs, patient=()):
    jobs, patient = list(jobs), list(patient)
    for job in patient:
        next(job)
    while jobs:
        for job in list(jobs):
            state = next(job, False)
            if state is not True:
                jobs.remove(job)
            if state is PATIENT:
                patient.append(job)
    for job in patient:
        for _ in job:
            pass


def beside(groups, send_sems, recv_sems, rooms, plan):
    @pl.when(pl.program_id(0) == 0)
    def _():
        meet(groups)
        for job in plan(Wires(send_sems, recv_sems, rooms)):
            next(job)

    @pl.when(pl.program_id(0) == pl.num_programs(0) - 1)
    def _():
        for job in plan(Wires(send_sems, recv_sems, rooms, started=True)):
            for _ in job:
                pass


def wire_sems(copies):
    return [pltpu.SemaphoreType.DMA((copies,)), pltpu.SemaphoreType.DMA((copies,))]


def room(shape, dtype):
    return pltpu.VMEM(tuple(shape), dtype)


def talk(name, cid, groups, operands, outs, plan, copies, in_vmem=(), out_vmem=(), scratch=(), rooms=()):
    n_in, n_out, n_rooms = len(operands), len(outs), len(rooms)

    def kernel(*refs):
        ins, results = refs[:n_in], refs[n_in : n_in + n_out]
        held = refs[n_in + n_out : n_in + n_out + n_rooms]
        buffers, (send_sems, recv_sems) = refs[n_in + n_out + n_rooms : -2], refs[-2:]
        meet(groups)
        wires = Wires(send_sems, recv_sems, held)
        run_all(*plan(wires, ins, results, buffers))
        assert wires.used <= copies, wires.used

    def where(i, chosen):
        return pl.BlockSpec(memory_space=pltpu.VMEM if i in chosen else pl.ANY)

    return pl.pallas_call(
        kernel,
        out_shape=outs,
        in_specs=[where(i, in_vmem) for i in range(n_in)],
        out_specs=[where(i, out_vmem) for i in range(n_out)],
        scratch_shapes=list(rooms) + list(scratch) + [pltpu.SemaphoreType.DMA((copies,)), pltpu.SemaphoreType.DMA((copies,))],
        compiler_params=pltpu.CompilerParams(
            collective_id=cid, has_side_effects=True, vmem_limit_bytes=60 * 1024 * 1024
        ),
        name=name,
    )(*operands)


def can_halve(array):
    rows, width = array.shape
    return lax.axis_size("dp") == 4 and (rows % (16 * PIECES) == 0 or width % (128 * PIECES) == 0)


def gather_jobs(wires, arrays, sources, results):
    jobs, patient = [], []
    for array, source, result in zip(arrays, sources, results):
        if can_halve(array):
            jobs.append(halves_dp(wires, source, result))
        else:
            patient.append(spread_dp(wires, source, result))
    return jobs, patient


def window(ref, item):
    _, rows, columns = item
    if rows is None and columns is None:
        return ref
    lines = slice(None) if rows is None else pl.ds(rows[0], rows[1] - rows[0])
    lanes = slice(None) if columns is None else pl.ds(columns[0], columns[1] - columns[0])
    return ref.at[:, lines, lanes]


def window_shape(item):
    array, rows, columns = item
    shape = list(array.shape)
    if rows is not None:
        shape[1] = rows[1] - rows[0]
    if columns is not None:
        shape[2] = columns[1] - columns[0]
    return shape_of(shape, array.dtype)


def gather_with(name, cid, block, beside, cut=2):
    count = lax.axis_size("seq")
    outs = [shape_of((count,) + block.shape, block.dtype)] + beside.outs

    def plan(wires, ins, results, scratch):
        jobs, patient = beside.jobs(wires, ins[1:], results[1:], scratch)
        return [gather_line(wires, ins[0], results[0], cut)] + jobs, patient

    got = talk(
        name, cid, ("line", "dp") if beside.arrays else ("line",), (block, *beside.arrays), outs, plan,
        1 + 4 * (count // 2) * cut + beside.copies, out_vmem=[1 + i for i in beside.in_vmem_outs], scratch=beside.scratch,
        rooms=beside.patient_rooms + [room(block.shape, block.dtype)] + beside.job_rooms,
    )
    return [got[0].reshape((-1,) + block.shape[1:])] + beside.finish(got[1:])


def columns_out(wires, source, out):
    mine, me, count, packs = lax.axis_index("dp"), lax.axis_index("seq"), lax.axis_size("seq"), lax.axis_size("dp")
    own = wires.keep(source.at[me], out.at[mine, me])
    sent, onward = [], []
    for step in range(1, count):
        sent.append(wires.copy(source.at[lax.rem(me + step, count)], out.at[mine, me], seq_peer(step)))
        sent[-1].start()
    for step in range(1, packs):
        onward.append(wires.copy(source.at[me], out.at[mine, me], pack_peer(step)))
        onward[-1].start()
    own.start()
    for step in range(1, count):
        yield True
        sent[step - 1].wait_recv()
        came = out.at[mine, lax.rem(me + count - step, count)]
        for other in range(1, packs):
            onward.append(wires.copy(came, came, pack_peer(other)))
            onward[-1].start()
    yield True
    own.wait()
    for copy in sent:
        copy.wait_send()
    for copy in onward:
        copy.wait()


def spread_all(wires, source, out):
    mine, me, count, packs = lax.axis_index("dp"), lax.axis_index("seq"), lax.axis_size("seq"), lax.axis_size("dp")
    own = wires.keep(source, out.at[mine, me])
    sent, onward = [], []
    for step in range(1, packs):
        sent.append(wires.copy(source, out.at[mine, me], pack_peer(step)))
        sent[-1].start()
    for step in range(1, count):
        onward.append(wires.copy(source, out.at[mine, me], seq_peer(step)))
        onward[-1].start()
    own.start()
    for other in range(1, packs):
        yield True
        sent[other - 1].wait_recv()
        came = out.at[lax.rem(mine + packs - other, packs), me]
        for step in range(1, count):
            onward.append(wires.copy(came, came, seq_peer(step)))
            onward[-1].start()
    yield True
    own.wait()
    for copy in sent:
        copy.wait_send()
    for copy in onward:
        copy.wait()


def shape_of(shape, dtype):
    return jax.ShapeDtypeStruct(tuple(shape), dtype)


def first_exchange(mix, block, over_dp):
    packs, count = lax.axis_size("dp"), lax.axis_size("seq")
    outs = [shape_of((packs,) + mix.shape, mix.dtype), shape_of((count,) + block.shape, block.dtype)]
    outs += [shape_of((packs,) + a.shape, a.dtype) for a in over_dp]
    cut = 2

    def plan(wires, ins, results, _):
        return [
            columns_out(wires, ins[0], results[0]),
            gather_line(wires, ins[1], results[1], cut),
        ], [spread_dp(wires, a, b) for a, b in zip(ins[2:], results[2:])]

    copies = count * packs + count + 4 * (count // 2) * cut + packs * len(over_dp) + 8
    rooms = [room(a.shape, a.dtype) for a in over_dp] + [room(mix.shape[1:], mix.dtype), room(block.shape, block.dtype)]
    got = talk("first_exchange", 1, ("dp", "seq"), (mix, block, *over_dp), outs, plan, copies, rooms=rooms)
    return [array.reshape(-1, array.shape[-1]) for array in got]


def gather_seq(name, cid, block):
    count = lax.axis_size("seq")
    (got,) = talk(
        name, cid, ("seq",), (block,), [shape_of((count,) + block.shape, block.dtype)],
        lambda wires, ins, outs, _: ([spread_seq(wires, ins[0], outs[0])],), count,
        rooms=[room(block.shape, block.dtype)],
    )
    return got


def fold_dp(wires, source, out, boxes, here, sums, idle=2):
    me = lax.axis_index("dp")
    half = source.shape[1] // 2
    bit = lax.rem(me, 2)
    flip = {1: me + 1 - 2 * bit, 2: lax.rem(me + 2, 4)}
    corner = lax.rem(flip[1] + 2, 4)
    rows = {1: pl.ds(0, half), 2: pl.ds(half, half)}
    load = [wires.load(source.at[me], here.at[0])]
    passing, direct, second = {}, {}, {}
    for way in (1, 2):
        passing[way] = wires.copy(source.at[corner, rows[way]], boxes.at[1 + way], {"dp": flip[way]})
        passing[way].start()
        load.append(wires.load(source.at[flip[3 - way], rows[way]], here.at[1, rows[way]]))
    for copy in load:
        copy.start()
    for _ in range(idle):
        yield True
    for way in (1, 2):
        yield True
        load[way].wait()
        passing[way].wait_recv()
        add_into(sums.at[way - 1], [here.at[1, rows[way]], boxes.at[1 + way]])
        second[way] = wires.copy(sums.at[way - 1], boxes.at[3 + way], {"dp": flip[3 - way]})
        second[way].start()
        direct[way] = wires.copy(source.at[flip[way], rows[way]], boxes.at[way - 1], {"dp": flip[way]})
        direct[way].start()
    load[0].wait()
    yield PATIENT
    for way in (1, 2):
        direct[way].wait_recv()
        second[way].wait_recv()
        add_into(out.at[rows[way]], [here.at[0, rows[way]], boxes.at[way - 1], boxes.at[3 + way]])
    for way in (1, 2):
        passing[way].wait_send()
        direct[way].wait_send()
        second[way].wait_send()


def can_fold(array):
    return lax.axis_size("dp") == 4 and array.shape[1] % 32 == 0


def fold_scratch(array):
    _, rows, columns = array.shape
    return [
        pltpu.VMEM((6, rows // 2, columns), array.dtype),
        pltpu.VMEM((2, rows, columns), array.dtype),
        pltpu.VMEM((2, rows // 2, columns), array.dtype),
    ]


class Beside:
    def __init__(self, gathers=(), swaps=(), sums=()):
        self.gathers, self.swaps, self.sums = list(gathers), list(swaps), list(sums)
        self.arrays = self.gathers + self.swaps + self.sums
        packs = lax.axis_size("dp")
        self.outs = [shape_of((packs,) + a.shape, a.dtype) for a in self.gathers]
        self.outs += [shape_of(a.shape, a.dtype) for a in self.swaps]
        self.scratch = []
        for a in self.sums:
            fold = can_fold(a)
            self.outs.append(shape_of(a.shape[1:] if fold else a.shape, a.dtype))
            self.scratch += fold_scratch(a) if fold else []
        self.copies = HALVES * len(self.gathers) + packs * len(self.swaps) + 16 * len(self.sums)
        self.job_rooms = [room(a.shape, a.dtype) for a in self.gathers if can_halve(a)]
        self.patient_rooms = [room(a.shape, a.dtype) for a in self.gathers if not can_halve(a)]
        self.patient_rooms += [room(a.shape[1:], a.dtype) for a in self.swaps]
        self.patient_rooms += [room(a.shape[1:], a.dtype) for a in self.sums if not can_fold(a)]
        self.in_vmem_outs = [len(self.gathers) + len(self.swaps) + i for i, a in enumerate(self.sums) if can_fold(a)]

    def jobs(self, wires, ins, results, scratch):
        g, s = len(self.gathers), len(self.gathers) + len(self.swaps)
        jobs, patient = gather_jobs(wires, self.gathers, ins[:g], results[:g])
        patient += [swap_dp(wires, a, b) for a, b in zip(ins[g:s], results[g:s])]
        scratch = list(scratch)
        for array, a, b in zip(self.sums, ins[s:], results[s:]):
            if can_fold(array):
                jobs.append(fold_dp(wires, a, b, *scratch[:3]))
                scratch = scratch[3:]
            else:
                patient.append(swap_dp(wires, a, b))
        return jobs, patient

    def finish(self, got):
        g, s = len(self.gathers), len(self.gathers) + len(self.swaps)
        got = list(got)
        done = [r.reshape((-1,) + a.shape[1:]) for r, a in zip(got[:g], self.gathers)] + got[g:s]
        return done + [r if can_fold(a) else add_packs(r).astype(r.dtype) for r, a in zip(got[s:], self.sums)]


def scatter_with(name, cid, out_shape, factors, product, beside, cut=2):
    count = lax.axis_size("seq")
    rows, width = out_shape
    box = pltpu.VMEM((count // 2, rows, width), jnp.bfloat16)
    made = [pltpu.VMEM((count, rows, width), jnp.bfloat16)] if product else []
    if not product:
        factors = (factors[0].reshape(count, rows, width),)
    n_f, n_b = len(factors), len(beside.arrays)
    outs = [shape_of((rows, width), jnp.float32)] + beside.outs

    def plan(wires, ins, results, scratch):
        terms = scratch[0] if product else ins[0]
        boxes, rest = scratch[len(made) : len(made) + 4], scratch[len(made) + 4 :]
        jobs, patient = beside.jobs(wires, ins[n_f:], results[1:], rest)

        def produce(dest):
            if product:
                product(dest, ins[:n_f], terms)

        return jobs + [scatter_line(wires, produce, terms, results[0], *boxes, cut)], patient

    got = talk(
        name, cid, ("line", "dp") if n_b else ("line",), (*factors, *beside.arrays), outs, plan,
        3 * (count // 2) * cut + beside.copies,
        in_vmem=range(n_f), out_vmem=[0] + [1 + i for i in beside.in_vmem_outs], scratch=made + [box] * 4 + beside.scratch,
        rooms=beside.patient_rooms + beside.job_rooms,
    )
    return [got[0]] + beside.finish(got[1:])


def swap_places(name, cid, arrays):
    count = lax.axis_size("seq")
    return talk(
        name, cid, ("seq",), arrays, [shape_of(a.shape, a.dtype) for a in arrays],
        lambda wires, ins, outs, _: ([], [swap_seq(wires, i, o) for i, o in zip(ins, outs)]), count * len(arrays),
        rooms=[room(a.shape[1:], a.dtype) for a in arrays],
    )


def split_columns(arrays, pieces):
    rows = arrays[0].shape[0]
    width = sum(p[2] for p in pieces[0])
    tall = min(rows, 16)

    def kernel(*refs):
        for place, cuts in enumerate(pieces):
            refs[-1][place] = jnp.concatenate(
                [jnp.zeros((tall, n), refs[-1].dtype) if a is None else refs[a][:, at : at + n] for a, at, n in cuts], axis=1
            )

    return pl.pallas_call(
        kernel,
        grid=(rows // tall,),
        in_specs=[pl.BlockSpec((tall, a.shape[1]), lambda i: (i, 0)) for a in arrays],
        out_specs=pl.BlockSpec((len(pieces), tall, width), lambda i: (0, i, 0)),
        out_shape=shape_of((len(pieces), rows, width), arrays[0].dtype),
        compiler_params=pltpu.CompilerParams(vmem_limit_bytes=48 * 1024 * 1024),
        name="split_columns",
    )(*arrays)


def join_columns(array, widths, pieces):
    places, rows, width = array.shape
    tall = min(rows, 16)

    def kernel(source, *outs):
        whole = [source[place].astype(jnp.float32) for place in range(places)]
        for which, out in enumerate(outs):
            found = []
            for place, cuts in enumerate(pieces):
                start = 0
                for a, at, n in cuts:
                    if a == which:
                        found.append((at, whole[place][:, start : start + n]))
                    start += n
            out[...] = jnp.concatenate([part for _, part in sorted(found, key=lambda f: f[0])], axis=1)

    return pl.pallas_call(
        kernel,
        grid=(rows // tall,),
        in_specs=[pl.BlockSpec((places, tall, width), lambda i: (0, i, 0))],
        out_specs=[pl.BlockSpec((tall, w), lambda i: (i, 0)) for w in widths],
        out_shape=[shape_of((rows, w), jnp.float32) for w in widths],
        compiler_params=pltpu.CompilerParams(vmem_limit_bytes=48 * 1024 * 1024),
        name="join_columns",
    )(array)


def add_packs(array):
    return jnp.sum(array.astype(jnp.float32), axis=0)


def unit_groups(units):
    return [(at, min(128, units - at)) for at in range(0, units, 128)]


def feed_forward_kernel(
    cut, block_ref, top_first, top_second, wgu_hbm, wd_hbm,
    x_out, down_out, g_gu_out, g_down_out, mid_out,
    wgu_ref, wd_ref, xbuf, topbuf, hidbuf, dgubuf, downbuf, g_gu, g_down, g_gu_low, g_down_low,
    terms, near, from_left, from_right, outbox,
    local_sems, pack_send, pack_recv, line_send, line_recv, near_send, near_recv, sum_send, sum_recv, across_send, across_recv,
):
    me, count = lax.axis_index("seq"), lax.axis_size("seq")
    chips, chip, core = count // 2, me // 2, lax.rem(me, 2)
    other = me + 1 - 2 * core
    tall = block_ref.shape[0]
    step = tall // cut
    units = wd_ref.shape[0]
    packs = lax.axis_size("dp")
    pack = lax.axis_index("dp")
    share = units // packs
    width = wd_ref.shape[1]
    meet(("line", "dp"))

    def lines(part):
        return pl.ds(part * step, step)

    def along(sign, i, part, source=None):
        at = ((1 - sign) // 2 * chips + i) * cut + part
        slot = x_out.at[me + 2 * sign * i, lines(part)]
        return pltpu.make_async_remote_copy(
            slot if source is None else source.at[lines(part)], slot,
            line_send.at[at], line_recv.at[at], on_line(-2 * sign), MESH,
        )

    def over(sign, i, part, source=None):
        at = ((1 - sign) // 2 * chips + i) * cut + part
        slot = x_out.at[me + 2 * sign * i, lines(part)]
        return pltpu.make_async_remote_copy(
            slot if source is None else source.at[lines(part)], slot,
            near_send.at[at], near_recv.at[at], sibling(), MESH,
        )

    def along_came(sign, i, part):
        at = ((1 - sign) // 2 * chips + i - 1) * cut + part
        slot = x_out.at[me + 2 * sign * i, lines(part)]
        pltpu.make_async_remote_copy(slot, slot, line_send.at[at], line_recv.at[at], sibling(), MESH).wait_recv()

    def over_came(sign, i, part):
        at = ((1 - sign) // 2 * chips + i) * cut + part
        slot = x_out.at[other + 2 * sign * i, lines(part)]
        pltpu.make_async_remote_copy(slot, slot, near_send.at[at], near_recv.at[at], sibling(), MESH).wait_recv()

    def more(sign):
        return jnp.where(sign > 0, chip > 0, chip < chips - 1)

    def across(dest, part):
        at = dest * cut + part
        return pltpu.make_async_remote_copy(
            terms.at[2 * dest + 1 - core, lines(part)], near.at[dest, lines(part)],
            across_send.at[at], across_recv.at[at], sibling(), MESH,
        )

    def onward(right, dest, part):
        at = ((0 if right else chips) + dest) * cut + part
        inbox = from_left if right else from_right
        return pltpu.make_async_remote_copy(
            outbox.at[dest, lines(part)], inbox.at[dest, lines(part)],
            sum_send.at[at], sum_recv.at[at], on_line(2 if right else -2), MESH,
        )

    own = Kept(block_ref, x_out.at[me], xbuf.at[0], local_sems.at[0])
    for part in range(cut):
        for sign in (1, -1):

            @pl.when(more(sign))
            def _():
                along(sign, 0, part, block_ref).start()

        over(1, 0, part, block_ref).start()
    weights = [
        pltpu.make_async_copy(wgu_hbm, wgu_ref, local_sems.at[1]),
        pltpu.make_async_copy(wd_hbm, wd_ref, local_sems.at[2]),
    ]
    own.start()
    for copy in weights:
        copy.start()
    own.wait()
    for copy in weights:
        copy.wait()

    def compute(dest):
        x = xbuf[...].reshape(2 * tall, width)
        top = topbuf[...].reshape(2 * tall, width)
        for at, n in unit_groups(units):
            both = nn(x, wgu_ref[:, 2 * at : 2 * at + 2 * n])
            gate, up = both[:, :n], both[:, n:]
            d_hidden = nt(top, wd_ref[at : at + n, :])
            sig = 1.0 / (1.0 + jnp.exp(-gate))
            silu = gate * sig
            hidbuf[:, :, at : at + n] = (silu * up).astype(jnp.bfloat16).reshape(2, tall, n)
            d_gate = d_hidden * up * sig * (1.0 + gate * (1.0 - sig))
            d_both = jnp.concatenate([d_gate, d_hidden * silu], axis=1)
            dgubuf[:, :, 2 * at : 2 * at + 2 * n] = d_both.astype(jnp.bfloat16).reshape(2, tall, 2 * n)
        hid = hidbuf[...].reshape(2 * tall, units)
        dgu = dgubuf[...].reshape(2 * tall, 2 * units)
        wide = 512
        for at in range(0, width, wide):
            mid = nt(dgu, wgu_ref[at : at + wide, :]).astype(jnp.bfloat16)
            terms[pl.ds(2 * dest, 2), :, at : at + wide] = mid.reshape(2, tall, wide)
        for part in range(cut):
            across(dest, part).start()

    def compute_rest():
        x = xbuf[...].reshape(2 * tall, width)
        top = topbuf[...].reshape(2 * tall, width)
        hid = hidbuf[...].reshape(2 * tall, units)
        dgu = dgubuf[...].reshape(2 * tall, 2 * units)
        wide = 512
        for at in range(0, width, wide):
            downbuf[:, :, at : at + wide] = nn(hid, wd_ref[:, at : at + wide]).astype(jnp.bfloat16).reshape(2, tall, wide)
        for at in range(0, units, 128):
            n = min(128, units - at)
            g_down[at : at + n, :] += tn(hid[:, at : at + n], top)
        for at in range(0, width, 256):
            g_gu[at : at + 256, :] += tn(x[:, at : at + 256], dgu)

    def send_sum(right, dest, part, first, in_turn=True):
        mine = [terms.at[2 * dest + core, lines(part)], near.at[dest, lines(part)]]
        across_came(dest, part)
        if first:
            add_into(outbox.at[dest, lines(part)], mine)
        else:
            inbox = from_left if right else from_right
            sum_came(right, dest, part)
            add_into(outbox.at[dest, lines(part)], mine + [inbox.at[dest, lines(part)]])
        if in_turn and part > 0:
            onward(right, dest, part - 1).wait_send()
        onward(right, dest, part).start()

    def across_came(dest, part):
        at = dest * cut + part
        there = near.at[dest, lines(part)]
        pltpu.make_async_remote_copy(there, there, across_send.at[at], across_recv.at[at], sibling(), MESH).wait_recv()

    def sum_came(right, dest, part):
        at = ((0 if right else chips) + dest) * cut + part
        there = (from_left if right else from_right).at[dest, lines(part)]
        pltpu.make_async_remote_copy(there, there, sum_send.at[at], sum_recv.at[at], sibling(), MESH).wait_recv()

    def inside(dest):
        return (dest >= 0) & (dest < chips)

    def visit(i, j):
        sign = 1 - 2 * j
        dest = chip + sign * i

        @pl.when(inside(dest) & (i + 1 - j > 0))
        def _():
            half = tall // 2
            tops = [
                pltpu.make_async_copy(
                    ref.at[pl.ds(2 * dest, 2)], topbuf.at[:, pl.ds(at, half)], local_sems.at[1 + at // half]
                )
                for ref, at in ((top_first, 0), (top_second, half))
            ]
            for top in tops:
                top.start()
            for part in range(cut):
                over_came(sign, i, part)
            x = pltpu.make_async_copy(x_out.at[pl.ds(2 * dest, 2)], xbuf, local_sems.at[0])
            x.start()
            for top in tops:
                top.wait()
            x.wait()
            compute(dest)
            @pl.when((chip == 0) & (dest > 0) & (dest < chips - 1))
            def _():
                for part in range(cut):
                    send_sum(True, dest, part, True, False)

            @pl.when((chip == chips - 1) & (dest < chips - 1) & (dest > 0))
            def _():
                for part in range(cut):
                    send_sum(False, dest, part, True, False)

            compute_rest()
            saved = pltpu.make_async_copy(downbuf, down_out.at[pl.ds(2 * dest, 2)], local_sems.at[2])
            saved.start()
            saved.wait()

    def forward(i):
        for sign in (1, -1):

            @pl.when((i > 0) & (i < chips) & inside(chip + sign * i))
            def _():
                for part in range(cut):
                    along_came(sign, i, part)

                    @pl.when(more(sign))
                    def _():
                        along(sign, i, part).start()

                    over(sign, i, part).start()

    def distance(i, _):
        def side(j, _):
            visit(i, j)

            @pl.when((j == 0) & (i > 0) | (j == 1) & (i == 0))
            def _():
                forward(i + 1)

            return 0

        lax.fori_loop(0, 2, side, 0)
        return 0

    g_gu[...] = jnp.zeros_like(g_gu)
    g_down[...] = jnp.zeros_like(g_down)
    lax.fori_loop(0, chips, distance, 0)

    def lower(i, _):
        lines = pl.ds(pl.multiple_of(i * 16, 16), 16)
        g_down_low[lines, :] = g_down[lines, :].astype(jnp.bfloat16)
        return 0

    lax.fori_loop(0, units // 16, lower, 0)
    kept = pltpu.make_async_copy(g_down_low.at[pl.ds(pack * share, share)], g_down_out.at[pack], local_sems.at[2])
    kept.start()

    def swap(step):
        peer = lax.rem(pack + step, packs)
        return pltpu.make_async_remote_copy(
            g_down_low.at[pl.ds(peer * share, share)], g_down_out.at[pack],
            pack_send.at[step], pack_recv.at[step], pack_peer(step), MESH,
        )

    for turn in range(1, packs):
        swap(turn).start()

    @pl.when(chip == 0)
    def _():
        for part in range(cut):
            send_sum(True, chips - 1, part, True)

    @pl.when(chip == chips - 1)
    def _():
        for part in range(cut):
            send_sum(False, 0, part, True)

    def rightward():
        for i in range(1, chips - 1):

            @pl.when((chip > 0) & (chip + i < chips))
            def _():
                for part in range(cut):
                    send_sum(True, chip + i, part, False)

    def leftward():
        for i in range(1, chips - 1):

            @pl.when((chip < chips - 1) & (chip - i >= 0))
            def _():
                for part in range(cut):
                    send_sum(False, chip - i, part, False)

    @pl.when(chip < chips // 2)
    def _():
        rightward()
        leftward()

    @pl.when(chip >= chips // 2)
    def _():
        leftward()
        rightward()

    for part in range(cut):
        across_came(chip, part)
        mine = [terms.at[2 * chip + core, lines(part)], near.at[chip, lines(part)]]
        left_in, right_in = from_left.at[chip, lines(part)], from_right.at[chip, lines(part)]

        @pl.when(chip == 0)
        def _():
            sum_came(False, chip, part)
            add_into(mid_out.at[lines(part)], mine + [right_in])

        @pl.when(chip == chips - 1)
        def _():
            sum_came(True, chip, part)
            add_into(mid_out.at[lines(part)], mine + [left_in])

        @pl.when((chip > 0) & (chip < chips - 1))
        def _():
            sum_came(True, chip, part)
            sum_came(False, chip, part)
            add_into(mid_out.at[lines(part)], mine + [left_in, right_in])

    def lower_gu(i, _):
        lines = pl.ds(pl.multiple_of(i * 16, 16), 16)
        g_gu_low[lines, :] = g_gu[lines, :].astype(jnp.bfloat16)
        return 0

    lax.fori_loop(0, width // 16, lower_gu, 0)
    gu_kept = pltpu.make_async_copy(g_gu_low, g_gu_out, local_sems.at[1])
    gu_kept.start()
    for turn in range(1, packs):
        swap(turn).wait()
    kept.wait()
    gu_kept.wait()
    for part in range(cut):
        for dest in range(chips):
            across(dest, part).wait_send()

            early_right = (chip == 0) & (dest < chips - 1) | (part == cut - 1)
            early_left = (chip == chips - 1) & (dest > 0) | (part == cut - 1)

            @pl.when((chip < dest) & early_right)
            def _():
                onward(True, dest, part).wait_send()

            @pl.when((chip > dest) & early_left)
            def _():
                onward(False, dest, part).wait_send()

        for i in range(chips):
            for sign in (1, -1):
                there = (chip + sign * i >= 0) & (chip + sign * i < chips)

                @pl.when(there & more(sign))
                def _():
                    along(sign, i, part).wait_send()

                if i > 0 or sign > 0:

                    @pl.when(there)
                    def _():
                        over(sign, i, part).wait_send()


def feed_forward(cid, block, tops, w_gu, w_d, cut=2):
    count = lax.axis_size("seq")
    chips = count // 2
    tall, width = block.shape
    units = w_d.shape[0]
    packs = lax.axis_size("dp")
    bf16 = jnp.bfloat16
    outs = [
        shape_of((count, tall, width), bf16),
        shape_of((count, tall, width), bf16),
        shape_of((width, 2 * units), bf16),
        shape_of((packs, units // packs, width), bf16),
        shape_of((tall, width), jnp.float32),
    ]
    box = pltpu.VMEM((chips, tall, width), bf16)
    dma = lambda n: pltpu.SemaphoreType.DMA((n,))
    anywhere, vmem = pl.BlockSpec(memory_space=pl.ANY), pl.BlockSpec(memory_space=pltpu.VMEM)
    flops = 2 * 2 * count * tall * width * 3 * units
    got = pl.pallas_call(
        functools.partial(feed_forward_kernel, cut),
        out_shape=outs,
        in_specs=[anywhere] * 5,
        out_specs=[anywhere] * 4 + [vmem],
        scratch_shapes=[
            pltpu.VMEM(w_gu.shape, bf16),
            pltpu.VMEM(w_d.shape, bf16),
            pltpu.VMEM((2, tall, width), bf16),
            pltpu.VMEM((2, tall, width), bf16),
            pltpu.VMEM((2, tall, units), bf16),
            pltpu.VMEM((2, tall, 2 * units), bf16),
            pltpu.VMEM((2, tall, width), bf16),
            pltpu.VMEM((width, 2 * units), jnp.float32),
            pltpu.VMEM((units, width), jnp.float32),
            pltpu.VMEM((width, 2 * units), bf16),
            pltpu.VMEM((units, width), bf16),
            pltpu.VMEM((count, tall, width), bf16),
            box, box, box, box,
            dma(3), dma(packs), dma(packs),
        ] + [dma(2 * chips * cut)] * 6 + [dma(chips * cut)] * 2,
        compiler_params=pltpu.CompilerParams(
            collective_id=cid, has_side_effects=True, vmem_limit_bytes=62 * 1024 * 1024
        ),
        cost_estimate=pl.CostEstimate(flops=flops, bytes_accessed=20 << 20, transcendentals=0),
        name="feed_forward",
    )(block, *tops, w_gu, w_d)
    return got


def cross_rows(left_side, right_side):
    return lax.dot_general(left_side, right_side, (((0,), (0,)), ((), ())), preferred_element_type=jnp.float32)


def cross_cols(left_side, right_side):
    return lax.dot_general(left_side, right_side, (((1,), (1,)), ((), ())), preferred_element_type=jnp.float32)


def dot(left_side, right_side):
    return jnp.dot(left_side, right_side, preferred_element_type=jnp.float32)


def on_device(
    tokens,
    segments,
    norm_one,
    w_qkv,
    w_lr,
    lr_bias,
    w_gate,
    w_out,
    w_init,
    b_init,
    tnorm_w,
    tnorm_b,
    post_w,
    post_b,
    norm_two,
    w_gate_up,
    w_down,
    grad_out,
):
    floats = jnp.float32
    bf16 = jnp.bfloat16
    both = ("dp", "seq")
    packs, per_seq = lax.axis_size("dp"), lax.axis_size("seq")
    devices = packs * per_seq
    place = lax.axis_index("seq")
    span, width = tokens.shape[1], tokens.shape[2]
    rows = norm_one.shape[0]
    heads_all = lr_bias.shape[0]
    units = w_down.shape[0]
    length = span * per_seq
    blocks = length // MB
    heads = heads_all // per_seq
    aligned = rows % HD == 0
    outer = packs if aligned else 1
    inner = width // (outer * per_seq)
    mine = outer * inner

    def own_rows(array):
        cut = array.reshape((outer, per_seq, inner) + array.shape[1:])
        cut = lax.dynamic_index_in_dim(cut, place, 1, keepdims=False)
        return cut.reshape((mine,) + array.shape[1:])

    def put_rows(array):
        full = jnp.zeros((outer, per_seq, inner) + array.shape[1:], array.dtype)
        part = array.reshape((outer, 1, inner) + array.shape[1:])
        at = (0, place) + (0,) * (part.ndim - 2)
        return lax.dynamic_update_slice(full, part, at).reshape((width,) + array.shape[1:])

    extra = 128
    feature_cuts = [
        [(0, (part * outer + o) * per_seq * inner + s * inner, inner) for part in range(3) for o in range(outer)]
        + [(1, o * per_seq * inner + s * inner, inner) for o in range(outer)]
        for s in range(per_seq)
    ]
    filled = -(-units // 16) * 16
    unit_cuts = []
    for s in range(per_seq):
        cuts = []
        for at, n in unit_groups(packs * filled):
            for part in range(2):
                u = at
                while u < at + n:
                    pack, i = divmod(u, filled)
                    run = min((units if i < units else filled) - i, at + n - u)
                    first = (part * packs * per_seq + pack * per_seq + s) * units + i
                    cuts.append((0, first, run) if i < units else (None, 0, run))
                    u += run
        unit_cuts.append(cuts)

    spans = span // MB
    lr_places = w_lr.reshape(rows, outer, per_seq, heads // outer).transpose(0, 2, 1, 3).reshape(rows, per_seq, heads)
    tags = segments[0].reshape(1, 1, spans, MB)[:, :, :, 0].astype(bf16)
    beside_cols = jnp.concatenate(
        [
            lr_places,
            jnp.broadcast_to(jnp.stack([norm_one, norm_two], axis=1)[:, None], (rows, per_seq, 2)),
            jnp.broadcast_to(tags, (rows, per_seq, spans)),
            jnp.zeros((rows, per_seq, extra - heads - 2 - spans), bf16),
        ],
        axis=2,
    ).reshape(rows, per_seq * extra)
    mix_cuts = [cuts + [(2, s * extra, extra)] for s, cuts in enumerate(feature_cuts)]
    vectors = jnp.stack([b_init, tnorm_w, tnorm_b, post_w, post_b], axis=1)
    head_rows = jnp.concatenate([w_init, vectors, jnp.zeros((rows, extra - HD - 5), bf16)], axis=1)
    over_dp = (w_out, head_rows) if aligned else ()
    w_mix, rows_all, *got = first_exchange(
        split_columns((w_qkv, w_gate, beside_cols), mix_cuts), tokens[0], over_dp
    )
    if aligned:
        w_o, head_rows = got
    else:
        w_o, head_rows = (own_rows(lax.all_gather(a, both, axis=0, tiled=True)) for a in (w_out, head_rows))
    w_extra = w_mix[:, 4 * mine :]
    gain_one, gain_two = w_extra[:, heads].astype(floats), w_extra[:, heads + 1].astype(floats)
    pack_tags = w_extra.reshape(packs, per_seq, rows, extra)[:, :, 0, heads + 2 : heads + 2 + spans]
    pack_tags = lax.dynamic_index_in_dim(pack_tags.reshape(packs, blocks), lax.axis_index("dp"), 0, keepdims=False)
    fresh = jnp.concatenate([jnp.ones((1,), jnp.int32), (pack_tags[1:] != pack_tags[:-1]).astype(jnp.int32)])
    vec_own = head_rows[:, HD : HD + 5].astype(floats)
    post_gain, post_shift = vec_own[:, 3], vec_own[:, 4]
    bias_own = lax.dynamic_index_in_dim(lr_bias.reshape(outer, per_seq, heads // outer), place, 1, keepdims=False)
    bias_own = bias_own.reshape(heads).astype(floats)

    half = span // 2
    later_top, rows_all = lax.optimization_barrier((grad_out[0, :half], rows_all))
    top_first = lax.all_gather(later_top, "seq", axis=0)
    gu_mine = split_columns((w_gate_up,), unit_cuts)

    inputs = rows_all.astype(floats)
    scale_one = lax.rsqrt(jnp.mean(inputs * inputs, -1, keepdims=True) + EPSILON)
    normed_in = inputs * scale_one
    x_one = (normed_in * gain_one).astype(bf16)
    qkv = dot(x_one, w_mix[:, : 3 * mine])
    gate_pre = dot(x_one, w_mix[:, 3 * mine : 4 * mine])
    lr_sigm = jax.nn.sigmoid(dot(x_one, w_extra)[:, :heads] + bias_own)
    e_rows = (lr_sigm * (1.0 / (HD * MB))).reshape(blocks, MB, heads).transpose(0, 2, 1).reshape(blocks, 1, heads * MB)

    def by_token(vector):
        return jnp.repeat(vector.reshape(heads, HD).T, MB, axis=1)

    init_w = head_rows[:, :HD].astype(floats).reshape(heads, HD, HD)
    init_w = (init_w - jnp.mean(init_w, -1, keepdims=True)).transpose(2, 0, 1).reshape(HD, heads * HD)
    init_b = vec_own[:, 0].reshape(heads, HD)
    init_b = (init_b - jnp.mean(init_b, -1, keepdims=True)).reshape(-1)
    gain_t, shift_t = by_token(vec_own[:, 1]), by_token(vec_own[:, 2])
    *results, gu_part, w_d = inner_forward(
        10, fresh, qkv, e_rows, init_w, by_token(init_b), gain_t, shift_t, (gu_mine,),
        (jnp.pad(w_down, ((0, filled - units), (0, 0))),),
    )
    w_d = w_d.reshape(-1, w_d.shape[-1])
    mixed, *saved = results
    later_top, mixed = lax.optimization_barrier((grad_out[0, half:], mixed))
    top_second = lax.all_gather(later_top, "seq", axis=0)

    mean_own = jnp.mean(mixed, -1)
    spread_own = jnp.sum((mixed - mean_own[:, None]) ** 2, -1)
    stats = gather_seq("share_moments", 2, jnp.stack([mean_own, spread_own]))
    mean_all = jnp.mean(stats[:, 0], 0)
    var_all = (jnp.sum(stats[:, 1], 0) + mine * jnp.sum((stats[:, 0] - mean_all) ** 2, 0)) * (1.0 / width)
    out_scale = lax.rsqrt(var_all + EPSILON)[:, None]
    out_hat = (mixed - mean_all[:, None]) * out_scale
    normed_out = out_hat * post_gain + post_shift
    gelu_gate, gelu_pull = jax.vjp(jax.nn.gelu, gate_pre)
    gated_unit = (gelu_gate * normed_out).astype(bf16)
    pair = 2 * span
    wide = 512

    def branch_terms(dest, factors, terms):
        unit = factors[0][dest * pair : (dest + 1) * pair, :]
        for at in range(0, width, wide):
            part = nn(unit, factors[1][:, at : at + wide]).astype(bf16)
            terms[2 * dest : 2 * dest + 2, :, at : at + wide] = part.reshape(2, span, wide)

    branch, w_gu = scatter_with(
        "scatter_branch", 3, (span, width), (gated_unit, w_o), branch_terms,
        Beside(gathers=(gu_part.reshape(-1, gu_part.shape[-1]),)),
    )
    inputs = tokens[0].astype(floats)
    residual = inputs + branch
    scale_two = lax.rsqrt(jnp.mean(residual * residual, -1, keepdims=True) + EPSILON)
    normed_mid = residual * scale_two
    _, down, g_gate_up, g_down, d_xtwo = feed_forward(
        5, (normed_mid * gain_two).astype(bf16), (top_first, top_second), w_gu, w_d
    )
    down = down.reshape(-1, width)
    pack_rows = lambda array: array.reshape((packs, -1) + array.shape[1:])
    g_gate_up = pack_rows(g_gate_up)
    g_down = add_packs(g_down)[:units]
    g_two = jnp.sum(d_xtwo * normed_mid, axis=0)
    d_mid = d_xtwo * gain_two
    d_residual = grad_out[0].astype(floats) + scale_two * (
        d_mid - normed_mid * jnp.mean(d_mid * normed_mid, -1, keepdims=True)
    )
    d_branch, g_gate_up = gather_with("gather_branch", 6, d_residual.astype(bf16), Beside(sums=(g_gate_up,)))
    down_first, d_branch = lax.optimization_barrier((down[:, : width // 2], d_branch))
    down_first = lax.psum_scatter(down_first, "seq", scatter_dimension=0, tiled=True)
    g_out = cross_rows(gated_unit, d_branch).astype(bf16)
    d_unit = cross_cols(d_branch, w_o)
    d_normed = d_unit * gelu_gate
    g_post_w = jnp.sum(d_normed * out_hat, axis=0)
    g_post_b = jnp.sum(d_normed, axis=0)
    d_hat = d_normed * post_gain
    sums = gather_seq("share_sums", 7, jnp.stack([jnp.sum(d_hat, -1), jnp.sum(d_hat * out_hat, -1)]))
    sums = jnp.sum(sums, 0) * (1.0 / width)
    d_mixed = out_scale * (d_hat - sums[0][:, None] - out_hat * sums[1][:, None])
    d_gate_pre = gelu_pull(d_unit * normed_out)[0].astype(bf16)
    place_rows = lambda array: array.reshape((per_seq, -1) + array.shape[1:])
    g_gate = pack_rows(cross_rows(x_one, d_gate_pre).astype(bf16))
    d_qkv, d_rate, d_w0, d_c0, d_gain, d_shift, g_gate_up, g_gate, *g_outs = inner_backward(
        11, fresh, qkv, e_rows, d_mixed, saved, gain_t, shift_t, (place_rows(g_gate_up),),
        [(g_gate, None, None)] + [(pack_rows(g_out), None, None)] * aligned,
    )
    (g_gate_up,) = join_columns(g_gate_up, (w_gate_up.shape[1],), unit_cuts)
    if aligned:
        g_out = add_packs(g_outs[0])
    else:
        g_out = lax.psum_scatter(put_rows(g_out), both, scatter_dimension=0, tiled=True).astype(floats)
    down_second, d_qkv = lax.optimization_barrier((down[:, width // 2 :], d_qkv))
    down_second = lax.psum_scatter(down_second, "seq", scatter_dimension=0, tiled=True)
    result = residual + jnp.concatenate([down_first, down_second], axis=1).astype(floats)
    d_rate = d_rate.reshape(blocks, heads, MB).transpose(0, 2, 1).reshape(length, heads)
    d_logit = (d_rate * (1.0 / HD) * lr_sigm * (1.0 - lr_sigm)).astype(bf16)
    g_qkv = cross_rows(x_one, d_qkv).astype(bf16)
    d_logit_wide = jnp.pad(d_logit, ((0, 0), (0, extra - heads)))
    d_xone = cross_cols(jnp.concatenate([d_qkv, d_gate_pre, d_logit_wide], axis=1), w_mix)
    g_one = jnp.sum(d_xone * (lax.optimization_barrier(rows_all).astype(floats) * scale_one), axis=0)

    lane = jnp.arange(extra)[None, :]
    g_bias = jnp.pad(jnp.sum(d_logit.astype(floats), axis=0), (heads + 2, extra - 2 * heads - 2))
    g_beside = cross_rows(x_one, d_logit_wide) + jnp.where(lane == heads, g_one[:, None], 0.0)
    g_beside = (g_beside + jnp.where(lane == heads + 1, g_two[:, None], 0.0) + g_bias[None, :]).astype(bf16)

    def from_token(array):
        return jnp.sum(array.reshape(HD, heads, MB), -1).T.reshape(mine)

    g_vec = jnp.stack(
        [d_c0.reshape(HD, heads, MB)[:, :, 0].T.reshape(mine), from_token(d_gain), from_token(d_shift), g_post_w, g_post_b],
        axis=1,
    )
    g_heads = jnp.concatenate(
        [d_w0.reshape(HD, heads, HD).transpose(1, 2, 0).reshape(mine, HD), g_vec, jnp.zeros((mine, extra - HD - 5), floats)],
        axis=1,
    )

    swaps = [pack_rows(g_heads)] * aligned + [pack_rows(g_beside), pack_rows(g_qkv)]
    d_xone, *got = scatter_with("scatter_first", 8, (span, width), (d_xone.astype(bf16),), None, Beside(swaps=swaps))
    if aligned:
        g_heads = add_packs(got[0])
    else:
        g_heads = lax.psum_scatter(put_rows(g_heads), both, scatter_dimension=0, tiled=True)
    g_mix = jnp.concatenate([add_packs(got[-1]), add_packs(g_gate), add_packs(got[-2])], axis=1).astype(bf16)
    (g_mix,) = swap_places("return_columns", 9, (place_rows(g_mix),))
    g_qkv, g_gate = join_columns(g_mix, (w_qkv.shape[1], w_gate.shape[1]), feature_cuts)
    g_beside = g_mix[:, :, 4 * mine :].astype(floats)
    g_norms = jnp.sum(g_beside[:, :, heads : heads + 2], 0)

    def by_head(part):
        part = part.reshape(part.shape[:-1] + (outer, heads // outer))
        return jnp.moveaxis(part, 0, -2).reshape(part.shape[1:-2] + (heads_all,))

    scale_one = lax.rsqrt(jnp.mean(inputs * inputs, -1, keepdims=True) + EPSILON)
    normed_in = inputs * scale_one
    d_inner = d_xone * gain_one
    d_tokens = d_residual + scale_one * (
        d_inner - normed_in * jnp.mean(d_inner * normed_in, -1, keepdims=True)
    )
    return (
        result.astype(bf16)[None],
        d_tokens.astype(bf16)[None],
        g_norms[:, 0],
        g_qkv,
        by_head(g_beside[:, :, :heads]),
        by_head(g_beside[:, 0, heads + 2 : 2 * heads + 2]),
        g_gate,
        g_out,
        g_heads[:, :HD],
        g_heads[:, HD],
        g_heads[:, HD + 1],
        g_heads[:, HD + 2],
        g_heads[:, HD + 3],
        g_heads[:, HD + 4],
        g_norms[:, 1],
        g_gate_up,
        g_down,
    )


def solution(mesh):
    placed = (
        P("dp", "seq", None),
        P("dp", "seq"),
        P(("dp", "seq")),
        P(("dp", "seq"), None),
        P(("dp", "seq"), None),
        P(),
        P(("dp", "seq"), None),
        P(("dp", "seq"), None),
        P(("dp", "seq"), None),
        P(("dp", "seq")),
        P(("dp", "seq")),
        P(("dp", "seq")),
        P(("dp", "seq")),
        P(("dp", "seq")),
        P(("dp", "seq")),
        P(("dp", "seq"), None),
        P(("dp", "seq"), None),
        P("dp", "seq", None),
    )
    return jax.shard_map(
        on_device,
        mesh=mesh,
        in_specs=placed,
        out_specs=(
            P("dp", "seq", None),
            P("dp", "seq", None),
            P(("dp", "seq")),
            P(("dp", "seq"), None),
            P(("dp", "seq"), None),
            P(),
            P(("dp", "seq"), None),
            P(("dp", "seq"), None),
            P(("dp", "seq"), None),
            P(("dp", "seq")),
            P(("dp", "seq")),
            P(("dp", "seq")),
            P(("dp", "seq")),
            P(("dp", "seq")),
            P(("dp", "seq")),
            P(("dp", "seq"), None),
            P(("dp", "seq"), None),
        ),
        check_vma=False,
    )
```

```python
import functools
import jax
import jax.numpy as jnp
from jax import lax
from jax.experimental import pallas as pl
from jax.experimental.pallas import tpu as pltpu
from jax.sharding import PartitionSpec as P

HD = 64
MB = 16
PER = 8
EPSILON = 1e-06


def nn(left, right):
    return lax.dot_general(left, right, (((1,), (0,)), ((), ())), preferred_element_type=jnp.float32)


def nt(left, right):
    return lax.dot_general(left, right, (((1,), (1,)), ((), ())), preferred_element_type=jnp.float32)


def tn(left, right):
    return lax.dot_general(left, right, (((0,), (0,)), ((), ())), preferred_element_type=jnp.float32)


def halves(value):
    high = value.astype(jnp.bfloat16)
    return high, (value - high.astype(jnp.float32)).astype(jnp.bfloat16)


def head_masks(heads):
    ht, hi = heads * MB, heads * HD

    def iota(shape, axis):
        return lax.broadcasted_iota(jnp.int32, shape, axis)

    own = (iota((ht, hi), 0) // MB == iota((ht, hi), 1) // HD).astype(jnp.float32)
    unit = (iota((HD, hi), 0) == iota((HD, hi), 1) % HD).astype(jnp.bfloat16)
    row, col = iota((ht, ht), 0), iota((ht, ht), 1)
    same = (row // MB == col // MB).astype(jnp.bfloat16)
    ts, tt = row % MB, col % MB
    later = jnp.where((row // MB == col // MB) & (ts <= tt), MB / (tt + 1).astype(jnp.float32), 0.0)
    earlier = jnp.where((row // MB == col // MB) & (tt <= ts), MB / (ts + 1).astype(jnp.float32), 0.0)
    return own, unit, same, later, earlier


def spread(rows, own, heads):
    return (jnp.concatenate([rows] * heads, axis=0) * own).astype(jnp.bfloat16)


def fold(values, heads):
    total = values[:MB]
    for h in range(1, heads):
        total = total + values[h * MB : (h + 1) * MB]
    return total


def turned(rows, own, unit, heads):
    wide = jnp.concatenate([rows] * heads, axis=0) * own
    high, low = halves(wide)
    return nt(unit, high) + nt(unit, low)


def mean0(value):
    return jnp.sum(value, axis=0, keepdims=True) * (1.0 / HD)


def forward_kernel(heads, per, over_seq, over_dp, fresh_ref, qkv_ref, e_ref, w0_ref, c0_ref, gain_ref, shift_ref, *refs):
    moved = over_seq + over_dp
    sources, refs = refs[:moved], refs[moved:]
    mixed_ref, wsave_ref, hat_ref, slope_ref, gap_ref, bar_ref, rows_ref = refs[:7]
    results, (w_ref, c_ref, send_sems, recv_sems, *rooms) = refs[7 : 7 + moved], refs[7 + moved :]
    jobs = [swap_seq] * over_seq + [spread_dp] * over_dp
    beside(
        ("seq", "dp"), send_sems, recv_sems, rooms,
        lambda wires: [job(wires, a, b) for job, a, b in zip(jobs, sources, results)],
    )
    hi = heads * HD
    own, unit, same, later, _ = head_masks(heads)
    gain, shift, w0, c0 = gain_ref[...], shift_ref[...], w0_ref[...], c0_ref[...]
    gain2 = gain * gain

    @pl.when(pl.program_id(0) == 0)
    def _():
        w_ref[...] = jnp.zeros_like(w_ref)
        c_ref[...] = jnp.zeros_like(c_ref)

    w, c = w_ref[...], c_ref[...]
    for b in range(per):
        is_fresh = fresh_ref[pl.program_id(0) * per + b] != 0
        lines = slice(b * MB, (b + 1) * MB)
        q, k, v = qkv_ref[lines, :hi], qkv_ref[lines, hi : 2 * hi], qkv_ref[lines, 2 * hi :]
        e = e_ref[b]
        kb, qb = spread(k, own, heads), spread(q, own, heads)
        gap = shift - turned(v - k, own, unit, heads)
        base = gain * gap
        w = jnp.where(is_fresh, w0, w)
        c = jnp.where(is_fresh, c0, c)
        wb = w.astype(jnp.bfloat16)
        wsave_ref[b] = wb
        z = nt(wb, kb) + c
        gz = gain2 * z
        s = lax.rsqrt(mean0(z * z) + EPSILON)
        mean_g = s * mean0(gz) + mean0(base)
        mean_gx = s * (s * mean0(gz * z) + mean0(base * z))
        hat = s * z
        slope = s * (gain2 * hat + base - mean_g - hat * mean_gx)
        eb = (e * slope).astype(jnp.bfloat16)
        mix = (later * (nt(kb, qb) + 1.0)).astype(jnp.bfloat16)
        zbar = nt(wb, qb) + c - nn(eb, mix)
        w = w - nn(eb, kb)
        c = c - nn(eb, same)
        sbar = lax.rsqrt(mean0(zbar * zbar) + EPSILON)
        bar = zbar * sbar
        high, low = halves(gain * bar + shift)
        mixed_ref[lines, :] = q + fold((tn(high, unit) + tn(low, unit)) * own, heads)
        hat_ref[b] = hat
        slope_ref[b] = slope
        gap_ref[b] = gap
        bar_ref[b] = bar
        rows_ref[b] = jnp.concatenate([s, sbar, mean_g, mean_gx], axis=0)
    w_ref[...] = w
    c_ref[...] = c


def inner_forward(cid, fresh, qkv, e_rows, w0, c0, gain, shift, seq_arrays, dp_arrays):
    arrays = tuple(seq_arrays) + tuple(dp_arrays)
    packs = lax.axis_size("dp")
    tokens, heads = qkv.shape[0], qkv.shape[1] // (3 * HD)
    ht, hi = heads * MB, heads * HD
    blocks = tokens // MB
    per = PER
    f32 = jnp.float32
    whole = lambda shape: pl.BlockSpec(shape, lambda i: (0, 0))
    save = pl.BlockSpec((per, HD, ht), lambda i: (i, 0, 0))
    return pl.pallas_call(
        functools.partial(forward_kernel, heads, per, len(seq_arrays), len(dp_arrays)),
        grid=(blocks // per,),
        in_specs=[
            pl.BlockSpec(memory_space=pltpu.SMEM),
            pl.BlockSpec((per * MB, 3 * hi), lambda i: (i, 0)),
            pl.BlockSpec((per, 1, ht), lambda i: (i, 0, 0)),
            whole((HD, hi)), whole((HD, ht)), whole((HD, ht)), whole((HD, ht)),
        ] + [pl.BlockSpec(memory_space=pl.ANY)] * len(arrays),
        out_specs=[
            pl.BlockSpec((per * MB, hi), lambda i: (i, 0)),
            pl.BlockSpec((per, HD, hi), lambda i: (i, 0, 0)),
            save, save, save, save,
            pl.BlockSpec((per, 4, ht), lambda i: (i, 0, 0)),
        ] + [pl.BlockSpec(memory_space=pl.ANY)] * len(arrays),
        out_shape=[
            jax.ShapeDtypeStruct((tokens, hi), f32),
            jax.ShapeDtypeStruct((blocks, HD, hi), jnp.bfloat16),
        ] + [jax.ShapeDtypeStruct((blocks, HD, ht), f32)] * 4 + [jax.ShapeDtypeStruct((blocks, 4, ht), f32)]
        + [shape_of(a.shape, a.dtype) for a in seq_arrays]
        + [shape_of((packs,) + a.shape, a.dtype) for a in dp_arrays],
        scratch_shapes=[pltpu.VMEM((HD, hi), f32), pltpu.VMEM((HD, ht), f32)]
        + wire_sems(len(seq_arrays) * lax.axis_size("seq") + len(dp_arrays) * packs)
        + [room(a.shape[1:], a.dtype) for a in seq_arrays] + [room(a.shape, a.dtype) for a in dp_arrays],
        compiler_params=pltpu.CompilerParams(
            vmem_limit_bytes=48 * 1024 * 1024, collective_id=cid, has_side_effects=True
        ),
        name="inner_forward",
    )(fresh, qkv, e_rows, w0, c0, gain, shift, *arrays)


def backward_kernel(heads, per, over_seq, items, fresh_ref, qkv_ref, e_ref, dmix_ref, wsave_ref, hat_ref, slope_ref,
                    gap_ref, bar_ref, rows_ref, gain_ref, shift_ref, *refs):
    moved = over_seq + len(items)
    sources, refs = refs[:moved], refs[moved:]
    sources = list(sources[:over_seq]) + [window(ref, item) for ref, item in zip(sources[over_seq:], items)]
    dqkv_ref, drate_ref, dw0_ref, dc0_ref, dgain_ref, dshift_ref = refs[:6]
    results, (a_ref, ac_ref, send_sems, recv_sems, *rooms) = refs[6 : 6 + moved], refs[6 + moved :]
    swaps = [swap_seq] * over_seq + [swap_dp] * len(items)
    beside(
        ("seq", "dp"), send_sems, recv_sems, rooms,
        lambda wires: [swap(wires, a, b) for swap, a, b in zip(swaps, sources, results)],
    )
    hi, ht = heads * HD, heads * MB
    own, unit, same, later, earlier = head_masks(heads)
    gain = gain_ref[...]
    gain2 = gain * gain
    step = pl.program_id(0)

    @pl.when(step == 0)
    def _():
        for ref in (a_ref, ac_ref, dw0_ref, dc0_ref, dgain_ref, dshift_ref):
            ref[...] = jnp.zeros_like(ref)

    a, ac = a_ref[...], ac_ref[...]
    dw0, dc0, dgain, dshift = dw0_ref[...], dc0_ref[...], dgain_ref[...], dshift_ref[...]
    for b in reversed(range(per)):
        is_fresh = fresh_ref[(pl.num_programs(0) - 1 - step) * per + b] != 0
        lines = slice(b * MB, (b + 1) * MB)
        q, k = qkv_ref[lines, :hi], qkv_ref[lines, hi : 2 * hi]
        e = e_ref[b]
        wb, hat, slope, gap, bar = wsave_ref[b], hat_ref[b], slope_ref[b], gap_ref[b], bar_ref[b]
        s, sbar, mean_g, mean_gx = (rows_ref[b][i : i + 1] for i in range(4))
        kb, qb = spread(k, own, heads), spread(q, own, heads)
        dout = dmix_ref[lines, :]
        dturn = turned(dout, own, unit, heads)
        head = gain * dturn
        dbar = sbar * (head - mean0(head) - bar * mean0(head * bar))
        dbarb = dbar.astype(jnp.bfloat16)
        scores = nt(qb, kb) + 1.0
        mix = earlier * scores
        s2 = s * s
        gh = gain2 * hat
        alpha = s2 * (gain2 - mean_gx)
        kappa = s2 * (gain2 * hat + gap * gain + gh)
        kappa1 = mean_g + mean0(gh)
        kappa2 = 2.0 * mean_gx + mean0(gh * hat)
        ab = a.astype(jnp.bfloat16)
        ka = nt(ab, kb) + ac
        u = -e * (ka + nn(dbarb, mix.astype(jnp.bfloat16)))
        ug = gain2 * u
        r2 = mean0(u * hat)
        r3 = mean0(ug)
        r4 = mean0(ug * hat)
        r5 = mean0(u * slope)
        row1 = s2 * (r3 - r2 * kappa1)
        row2 = s2 * (r4 - r2 * kappa2) + s * r5
        dz = alpha * u - r2 * kappa - row1 - hat * row2
        dzb = dz.astype(jnp.bfloat16)
        dg = s * (u - hat * r2)
        a_next = a + nn(dbarb, qb) + nn(dzb, kb)
        ac_next = ac + nn(dbarb, same) + nn(dzb, same)
        dm = -tn(dbarb, slope.astype(jnp.bfloat16))
        ds = (earlier * e * dm).astype(jnp.bfloat16)
        drate_ref[b] = (jnp.sum(mix * dm, axis=0, keepdims=True) - jnp.sum(ka * slope, axis=0, keepdims=True)) * (1.0 / MB)
        dgb = (gain * dg)
        ndg = fold(tn(dgb.astype(jnp.bfloat16), unit) * own, heads)
        dq = dout + fold(tn(dbarb, wb) * own + nn(ds, kb), heads)
        dk = ndg + fold((tn(dzb, wb) - tn((e * slope).astype(jnp.bfloat16), ab)) * own + tn(ds, qb), heads)
        dqkv_ref[lines, :hi] = dq.astype(jnp.bfloat16)
        dqkv_ref[lines, hi : 2 * hi] = dk.astype(jnp.bfloat16)
        dqkv_ref[lines, 2 * hi :] = (-ndg).astype(jnp.bfloat16)
        dgain = dgain + dturn * bar + dg * (2.0 * gain * hat + gap)
        dshift = dshift + dturn + dgb
        dw0 = dw0 + jnp.where(is_fresh, a_next, 0.0)
        dc0 = dc0 + jnp.where(is_fresh, ac_next, 0.0)
        a = jnp.where(is_fresh, 0.0, a_next)
        ac = jnp.where(is_fresh, 0.0, ac_next)
    a_ref[...] = a
    ac_ref[...] = ac
    dw0_ref[...] = dw0
    dc0_ref[...] = dc0
    dgain_ref[...] = dgain
    dshift_ref[...] = dshift


def inner_backward(cid, fresh, qkv, e_rows, dmix, saved, gain, shift, seq_arrays, items):
    arrays = tuple(seq_arrays) + tuple(item[0] for item in items)
    tokens, heads = qkv.shape[0], qkv.shape[1] // (3 * HD)
    ht, hi = heads * MB, heads * HD
    blocks = tokens // MB
    per = PER
    last = blocks // per - 1
    f32 = jnp.float32
    whole = lambda shape: pl.BlockSpec(shape, lambda i: (0, 0))
    three = lambda shape: pl.BlockSpec(shape, lambda i: (last - i, 0, 0))
    two = lambda shape: pl.BlockSpec(shape, lambda i: (last - i, 0))
    save = three((per, HD, ht))
    return pl.pallas_call(
        functools.partial(backward_kernel, heads, per, len(seq_arrays), items),
        grid=(blocks // per,),
        in_specs=[
            pl.BlockSpec(memory_space=pltpu.SMEM),
            two((per * MB, 3 * hi)), three((per, 1, ht)), two((per * MB, hi)),
            three((per, HD, hi)), save, save, save, save, three((per, 4, ht)),
            whole((HD, ht)), whole((HD, ht)),
        ] + [pl.BlockSpec(memory_space=pl.ANY)] * len(arrays),
        out_specs=[
            two((per * MB, 3 * hi)), three((per, 1, ht)),
            whole((HD, hi)), whole((HD, ht)), whole((HD, ht)), whole((HD, ht)),
        ] + [pl.BlockSpec(memory_space=pl.ANY)] * len(arrays),
        out_shape=[
            jax.ShapeDtypeStruct((tokens, 3 * hi), jnp.bfloat16),
            jax.ShapeDtypeStruct((blocks, 1, ht), f32),
            jax.ShapeDtypeStruct((HD, hi), f32),
        ] + [jax.ShapeDtypeStruct((HD, ht), f32)] * 3 + [shape_of(a.shape, a.dtype) for a in seq_arrays]
        + [window_shape(item) for item in items],
        scratch_shapes=[pltpu.VMEM((HD, hi), f32), pltpu.VMEM((HD, ht), f32)]
        + wire_sems(len(seq_arrays) * lax.axis_size("seq") + len(items) * lax.axis_size("dp"))
        + [room(a.shape[1:], a.dtype) for a in seq_arrays]
        + [room(window_shape(item).shape[1:], item[0].dtype) for item in items],
        compiler_params=pltpu.CompilerParams(
            vmem_limit_bytes=48 * 1024 * 1024, collective_id=cid, has_side_effects=True
        ),
        name="inner_backward",
    )(fresh, qkv, e_rows, dmix, *saved, gain, shift, *arrays)

MESH = pl.DeviceIdType.MESH


class Kept:
    def __init__(self, source, target, room, sem):
        self.bring = pltpu.make_async_copy(source, room, sem)
        self.leave = pltpu.make_async_copy(room, target, sem)

    def start(self):
        self.bring.start()
        self.bring.wait()
        self.leave.start()

    def wait(self):
        self.leave.wait()


class Wires:
    def __init__(self, send_sems, recv_sems, rooms=(), started=False):
        self.send_sems, self.recv_sems, self.used, self.started = send_sems, recv_sems, 0, started
        self.rooms = list(rooms)

    def begin(self, copy):
        if not self.started:
            copy.start()
        return copy

    def copy(self, source, target, device):
        at = self.number()
        return self.numbered(at, source, target, device)

    def number(self):
        self.used += 1
        return self.used - 1

    def numbered(self, at, source, target, device):
        return pltpu.make_async_remote_copy(
            src_ref=source,
            dst_ref=target,
            send_sem=self.send_sems.at[at],
            recv_sem=self.recv_sems.at[at],
            device_id=device,
            device_id_type=MESH,
        )

    def load(self, source, target):
        return pltpu.make_async_copy(source, target, self.send_sems.at[self.number()])

    def keep(self, source, target):
        return Kept(source, target, self.rooms.pop(0), self.send_sems.at[self.number()])


def on_line(step):
    return {"seq": lax.axis_index("seq") + step}


def sibling():
    me = lax.axis_index("seq")
    return {"seq": me + 1 - 2 * lax.rem(me, 2)}


def pack_peer(step):
    packs = lax.axis_size("dp")
    return {"dp": lax.rem(lax.axis_index("dp") + step, packs)}


def seq_peer(step):
    count = lax.axis_size("seq")
    return {"seq": lax.rem(lax.axis_index("seq") + step, count)}


def meet(groups):
    barrier = pltpu.get_barrier_semaphore()
    me, count = lax.axis_index("seq"), lax.axis_size("seq")

    def greet(device):
        pl.semaphore_signal(barrier, inc=1, device_id=device, device_id_type=MESH)

    peers = 0
    if "dp" in groups:
        for step in range(1, lax.axis_size("dp")):
            greet(pack_peer(step))
        peers += lax.axis_size("dp") - 1
    if "seq" in groups:
        for step in range(1, count):
            greet(seq_peer(step))
        peers += count - 1
    elif "line" in groups:
        greet(sibling())

        @pl.when(me >= 2)
        def _():
            greet(on_line(-2))

        @pl.when(me < count - 2)
        def _():
            greet(on_line(2))

        peers += 1 + jnp.minimum(me // 2, 1) + jnp.minimum((count - 1 - me) // 2, 1)
    pl.semaphore_wait(barrier, peers)


def gather_line(wires, source, out, cut):
    me, count = lax.axis_index("seq"), lax.axis_size("seq")
    chips, chip = count // 2, me // 2
    step = source.shape[0] // cut
    other = me + 1 - 2 * lax.rem(me, 2)

    def piece(slot, part):
        return out.at[slot, pl.ds(part * step, step)]

    own = wires.keep(source, out.at[me])
    numbers = {(way, i, part): wires.number() for way in "rlRL" for i in range(chips) for part in range(cut)}

    def copy(way, i, part):
        slot = me - 2 * i if way in "rR" else me + 2 * i
        start = source.at[pl.ds(part * step, step)] if i == 0 else piece(slot, part)
        device = {"r": on_line(2), "l": on_line(-2), "R": sibling(), "L": sibling()}[way]
        return wires.numbered(numbers[way, i, part], start, piece(slot, part), device)

    def arrived(way, i, part):
        if way in "rl":
            slot = me - 2 * (i + 1) if way == "r" else me + 2 * (i + 1)
        else:
            slot = other - 2 * i if way == "R" else other + 2 * i
        there = piece(slot, part)
        wires.numbered(numbers[way, i, part], there, there, sibling()).wait_recv()

    @pl.when(chip < chips - 1)
    def _():
        for part in range(cut):
            copy("r", 0, part).start()

    @pl.when(chip > 0)
    def _():
        for part in range(cut):
            copy("l", 0, part).start()

    for part in range(cut):
        copy("R", 0, part).start()
    own.start()
    for i in range(1, chips):
        for part in range(cut):
            yield True

            @pl.when(chip >= i)
            def _():
                arrived("r", i - 1, part)

                @pl.when(chip < chips - 1)
                def _():
                    copy("r", i, part).start()

                copy("R", i, part).start()

            @pl.when(chip + i <= chips - 1)
            def _():
                arrived("l", i - 1, part)

                @pl.when(chip > 0)
                def _():
                    copy("l", i, part).start()

                copy("L", i, part).start()

    yield True
    own.wait()
    for i in range(chips):
        for part in range(cut):
            if i == 0:
                arrived("R", 0, part)
                copy("R", 0, part).wait_send()
            else:

                @pl.when(chip >= i)
                def _():
                    arrived("R", i, part)
                    copy("R", i, part).wait_send()

                @pl.when(chip + i <= chips - 1)
                def _():
                    arrived("L", i, part)
                    copy("L", i, part).wait_send()

            @pl.when((chip >= i) & (chip < chips - 1))
            def _():
                copy("r", i, part).wait_send()

            @pl.when((chip + i <= chips - 1) & (chip > 0))
            def _():
                copy("l", i, part).wait_send()


def add_into(out, parts, rows=16):
    def body(i, _):
        lines = pl.ds(pl.multiple_of(i * rows, rows), rows)
        total = parts[0][lines, :].astype(jnp.float32)
        for part in parts[1:]:
            total = total + part[lines, :].astype(jnp.float32)
        out[lines, :] = total.astype(out.dtype)
        return 0

    lax.fori_loop(0, out.shape[0] // rows, body, 0)


def scatter_line(wires, produce, source, out, near, from_left, from_right, outbox, cut):
    me, count = lax.axis_index("seq"), lax.axis_size("seq")
    chips, chip, core = count // 2, me // 2, lax.rem(me, 2)
    step = source.shape[1] // cut

    def lines(part):
        return pl.ds(part * step, step)

    order = []
    for i in range(chips // 2):
        order += [chips - 1 - i, i]
    order += [chips // 2] if chips % 2 else []
    across = {}
    for dest in order:
        for part in range(cut):
            across[dest, part] = wires.copy(
                source.at[2 * dest + 1 - core, lines(part)], near.at[dest, lines(part)], sibling()
            )

    def begin(dests):
        for dest in dests:
            produce(dest)
            for part in range(cut):
                across[dest, part].start()

    right, left = {}, {}
    for dest in range(chips):
        for part in range(cut):
            right[dest, part] = wires.copy(outbox.at[dest, lines(part)], from_left.at[dest, lines(part)], on_line(2))
            left[dest, part] = wires.copy(outbox.at[dest, lines(part)], from_right.at[dest, lines(part)], on_line(-2))
    def handle(part, ahead, turn, dest, table, inbox, first):
        terms = [source.at[2 * dest + core, lines(part)], near.at[dest, lines(part)]]

        @pl.when(ahead & turn)
        def _():
            across[dest, part].wait_recv()

            @pl.when(first)
            def _():
                add_into(outbox.at[dest, lines(part)], terms)

            @pl.when(jnp.logical_not(first))
            def _():
                table[dest, part].wait_recv()
                add_into(outbox.at[dest, lines(part)], terms + [inbox.at[dest, lines(part)]])

            table[dest, part].start()

    for i in range(chips - 1):
        begin(order[2 * i : 2 * i + 2])
        for part in range(cut):
            yield True
            rightward, leftward = (chips - 1 - i, right, from_left, chip == 0), (i, left, from_right, chip == chips - 1)
            handle(part, chip < chips - 1 - i, chip < chips // 2, *rightward)
            handle(part, chip > i, True, *leftward)
            handle(part, chip < chips - 1 - i, chip >= chips // 2, *rightward)

    for part in range(cut):
        yield True
        for dest in range(chips):

            @pl.when(chip == dest)
            def _():
                across[dest, part].wait_recv()
                terms = [source.at[2 * dest + core, lines(part)], near.at[dest, lines(part)]]
                if dest > 0:
                    right[dest, part].wait_recv()
                    terms = terms + [from_left.at[dest, lines(part)]]
                if dest < chips - 1:
                    left[dest, part].wait_recv()
                    terms = terms + [from_right.at[dest, lines(part)]]
                add_into(out.at[lines(part)], terms)

    for dest in range(chips):
        for part in range(cut):
            across[dest, part].wait_send()

            @pl.when(chip < dest)
            def _():
                right[dest, part].wait_send()

            @pl.when(chip > dest)
            def _():
                left[dest, part].wait_send()


def swap_seq(wires, source, out):
    me, count = lax.axis_index("seq"), lax.axis_size("seq")
    own = wires.keep(source.at[me], out.at[me])
    sent = []
    for step in range(1, count):
        peer = lax.rem(me + step, count)
        sent.append(wires.copy(source.at[peer], out.at[me], seq_peer(step)))
        wires.begin(sent[-1])
    wires.begin(own)
    yield True
    own.wait()
    for copy in sent:
        copy.wait()


def spread_seq(wires, source, out):
    me, count = lax.axis_index("seq"), lax.axis_size("seq")
    own = wires.keep(source, out.at[me])
    sent = []
    for step in range(1, count):
        sent.append(wires.copy(source, out.at[me], seq_peer(step)))
        wires.begin(sent[-1])
    wires.begin(own)
    yield True
    own.wait()
    for copy in sent:
        copy.wait()


def swap_dp(wires, source, out):
    me, count = lax.axis_index("dp"), lax.axis_size("dp")
    own = wires.keep(source.at[me], out.at[me])
    sent = []
    for step in range(1, count):
        sent.append(wires.copy(source.at[lax.rem(me + step, count)], out.at[me], pack_peer(step)))
        wires.begin(sent[-1])
    wires.begin(own)
    yield True
    own.wait()
    for copy in sent:
        copy.wait()


PIECES = 4
HALVES = 8 + 4 * PIECES


def halves_dp(wires, source, out, idle=1):
    me, count = lax.axis_index("dp"), lax.axis_size("dp")
    rows, width = source.shape
    by_rows = rows % (16 * PIECES) == 0
    step = (rows if by_rows else width) // PIECES
    own = wires.keep(source, out.at[me])
    bit = lax.rem(me, 2)
    flip = {1: me + 1 - 2 * bit, 2: lax.rem(me + 2, 4)}
    part = lambda ref, i: ref.at[pl.ds(i * step, step)] if by_rows else ref.at[:, pl.ds(i * step, step)]
    first, then = {}, {}

    def send(way, j):
        first[way, j] = wires.copy(part(source, j), part(out.at[me], j), {"dp": flip[way]})
        first[way, j].start()

    half = PIECES // 2
    for i in range(half):
        send(1, i)
        send(2, half + i)
    own.start()
    for _ in range(idle):
        yield True
    for i in range(half):
        for way, j in ((1, i), (2, half + i)):
            yield True
            first[way, j].wait_recv()
            came = part(out.at[flip[way]], j)
            then[way, j] = wires.copy(came, came, {"dp": flip[3 - way]})
            then[way, j].start()
            send(3 - way, j)
    yield PATIENT
    own.wait()
    for i in range(half):
        for way, j in ((2, i), (1, half + i)):
            first[way, j].wait_recv()
    for copy in first.values():
        copy.wait_send()
    for copy in then.values():
        copy.wait()


def spread_dp(wires, source, out):
    me, count = lax.axis_index("dp"), lax.axis_size("dp")
    own = wires.keep(source, out.at[me])
    sent = []
    for step in range(1, count):
        sent.append(wires.copy(source, out.at[me], pack_peer(step)))
        wires.begin(sent[-1])
    wires.begin(own)
    yield True
    own.wait()
    for copy in sent:
        copy.wait()


PATIENT = None


def run_all(jobs, patient=()):
    jobs, patient = list(jobs), list(patient)
    for job in patient:
        next(job)
    while jobs:
        for job in list(jobs):
            state = next(job, False)
            if state is not True:
                jobs.remove(job)
            if state is PATIENT:
                patient.append(job)
    for job in patient:
        for _ in job:
            pass


def beside(groups, send_sems, recv_sems, rooms, plan):
    @pl.when(pl.program_id(0) == 0)
    def _():
        meet(groups)
        for job in plan(Wires(send_sems, recv_sems, rooms)):
            next(job)

    @pl.when(pl.program_id(0) == pl.num_programs(0) - 1)
    def _():
        for job in plan(Wires(send_sems, recv_sems, rooms, started=True)):
            for _ in job:
                pass


def wire_sems(copies):
    return [pltpu.SemaphoreType.DMA((copies,)), pltpu.SemaphoreType.DMA((copies,))]


def room(shape, dtype):
    return pltpu.VMEM(tuple(shape), dtype)


def talk(name, cid, groups, operands, outs, plan, copies, in_vmem=(), out_vmem=(), scratch=(), rooms=()):
    n_in, n_out, n_rooms = len(operands), len(outs), len(rooms)

    def kernel(*refs):
        ins, results = refs[:n_in], refs[n_in : n_in + n_out]
        held = refs[n_in + n_out : n_in + n_out + n_rooms]
        buffers, (send_sems, recv_sems) = refs[n_in + n_out + n_rooms : -2], refs[-2:]
        meet(groups)
        wires = Wires(send_sems, recv_sems, held)
        run_all(*plan(wires, ins, results, buffers))
        assert wires.used <= copies, wires.used

    def where(i, chosen):
        return pl.BlockSpec(memory_space=pltpu.VMEM if i in chosen else pl.ANY)

    return pl.pallas_call(
        kernel,
        out_shape=outs,
        in_specs=[where(i, in_vmem) for i in range(n_in)],
        out_specs=[where(i, out_vmem) for i in range(n_out)],
        scratch_shapes=list(rooms) + list(scratch) + [pltpu.SemaphoreType.DMA((copies,)), pltpu.SemaphoreType.DMA((copies,))],
        compiler_params=pltpu.CompilerParams(
            collective_id=cid, has_side_effects=True, vmem_limit_bytes=60 * 1024 * 1024
        ),
        name=name,
    )(*operands)


def can_halve(array):
    rows, width = array.shape
    return lax.axis_size("dp") == 4 and (rows % (16 * PIECES) == 0 or width % (128 * PIECES) == 0)


def gather_jobs(wires, arrays, sources, results):
    jobs, patient = [], []
    for array, source, result in zip(arrays, sources, results):
        if can_halve(array):
            jobs.append(halves_dp(wires, source, result))
        else:
            patient.append(spread_dp(wires, source, result))
    return jobs, patient


def window(ref, item):
    _, rows, columns = item
    if rows is None and columns is None:
        return ref
    lines = slice(None) if rows is None else pl.ds(rows[0], rows[1] - rows[0])
    lanes = slice(None) if columns is None else pl.ds(columns[0], columns[1] - columns[0])
    return ref.at[:, lines, lanes]


def window_shape(item):
    array, rows, columns = item
    shape = list(array.shape)
    if rows is not None:
        shape[1] = rows[1] - rows[0]
    if columns is not None:
        shape[2] = columns[1] - columns[0]
    return shape_of(shape, array.dtype)


def gather_with(name, cid, block, beside, cut=2):
    count = lax.axis_size("seq")
    outs = [shape_of((count,) + block.shape, block.dtype)] + beside.outs

    def plan(wires, ins, results, scratch):
        jobs, patient = beside.jobs(wires, ins[1:], results[1:], scratch)
        return [gather_line(wires, ins[0], results[0], cut)] + jobs, patient

    got = talk(
        name, cid, ("line", "dp") if beside.arrays else ("line",), (block, *beside.arrays), outs, plan,
        1 + 4 * (count // 2) * cut + beside.copies, out_vmem=[1 + i for i in beside.in_vmem_outs], scratch=beside.scratch,
        rooms=beside.patient_rooms + [room(block.shape, block.dtype)] + beside.job_rooms,
    )
    return [got[0].reshape((-1,) + block.shape[1:])] + beside.finish(got[1:])


def columns_out(wires, source, out):
    mine, me, count, packs = lax.axis_index("dp"), lax.axis_index("seq"), lax.axis_size("seq"), lax.axis_size("dp")
    own = wires.keep(source.at[me], out.at[mine, me])
    square = packs == 4
    bit = lax.rem(mine, 2)
    flip = {1: mine + 1 - 2 * bit, 2: lax.rem(mine + 2, 4)}
    sent, onward, turned_on = [], {}, []
    for step in range(1, count):
        sent.append(wires.copy(source.at[lax.rem(me + step, count)], out.at[mine, me], seq_peer(step)))
        sent[-1].start()

    def pass_on(k):
        slot = lax.rem(me + count - k, count)
        came = source.at[me] if k == 0 else out.at[mine, slot]
        for way in (1, 2) if square else range(1, packs):
            device = {"dp": flip[way]} if square else pack_peer(way)
            onward[k, way] = wires.copy(came, out.at[mine, slot], device)
            onward[k, way].start()

    def turn(k):
        way = 1 + k % 2
        onward[k, way].wait_recv()
        came = out.at[flip[way], lax.rem(me + count - k, count)]
        turned_on.append(wires.copy(came, came, {"dp": flip[3 - way]}))
        turned_on[-1].start()

    pass_on(0)
    own.start()
    for k in range(1, count):
        yield True
        sent[k - 1].wait_recv()
        pass_on(k)
        if square:
            turn(k - 1)
    yield True
    if square:
        turn(count - 1)
    yield PATIENT
    own.wait()
    for copy in sent:
        copy.wait_send()
    for (k, way), copy in onward.items():
        copy.wait_send()
        if not square or way != 1 + k % 2:
            copy.wait_recv()
    for copy in turned_on:
        copy.wait()


def spread_all(wires, source, out):
    mine, me, count, packs = lax.axis_index("dp"), lax.axis_index("seq"), lax.axis_size("seq"), lax.axis_size("dp")
    own = wires.keep(source, out.at[mine, me])
    sent, onward = [], []
    for step in range(1, packs):
        sent.append(wires.copy(source, out.at[mine, me], pack_peer(step)))
        sent[-1].start()
    for step in range(1, count):
        onward.append(wires.copy(source, out.at[mine, me], seq_peer(step)))
        onward[-1].start()
    own.start()
    for other in range(1, packs):
        yield True
        sent[other - 1].wait_recv()
        came = out.at[lax.rem(mine + packs - other, packs), me]
        for step in range(1, count):
            onward.append(wires.copy(came, came, seq_peer(step)))
            onward[-1].start()
    yield True
    own.wait()
    for copy in sent:
        copy.wait_send()
    for copy in onward:
        copy.wait()


def shape_of(shape, dtype):
    return jax.ShapeDtypeStruct(tuple(shape), dtype)


def first_exchange(mix, block, over_dp):
    packs, count = lax.axis_size("dp"), lax.axis_size("seq")
    outs = [shape_of((packs,) + mix.shape, mix.dtype), shape_of((count,) + block.shape, block.dtype)]
    outs += [shape_of((packs,) + a.shape, a.dtype) for a in over_dp]
    cut = 2

    def plan(wires, ins, results, _):
        return [
            columns_out(wires, ins[0], results[0]),
            gather_line(wires, ins[1], results[1], cut),
        ], [spread_dp(wires, a, b) for a, b in zip(ins[2:], results[2:])]

    copies = count * packs + count + 4 * (count // 2) * cut + packs * len(over_dp) + 8
    rooms = [room(a.shape, a.dtype) for a in over_dp] + [room(mix.shape[1:], mix.dtype), room(block.shape, block.dtype)]
    got = talk("first_exchange", 1, ("dp", "seq"), (mix, block, *over_dp), outs, plan, copies, rooms=rooms)
    return [array.reshape(-1, array.shape[-1]) for array in got]


def gather_seq(name, cid, block):
    count = lax.axis_size("seq")
    (got,) = talk(
        name, cid, ("seq",), (block,), [shape_of((count,) + block.shape, block.dtype)],
        lambda wires, ins, outs, _: ([spread_seq(wires, ins[0], outs[0])],), count,
        rooms=[room(block.shape, block.dtype)],
    )
    return got


def fold_dp(wires, source, out, boxes, here, sums, idle=2):
    me = lax.axis_index("dp")
    half = source.shape[1] // 2
    bit = lax.rem(me, 2)
    flip = {1: me + 1 - 2 * bit, 2: lax.rem(me + 2, 4)}
    corner = lax.rem(flip[1] + 2, 4)
    rows = {1: pl.ds(0, half), 2: pl.ds(half, half)}
    load = [wires.load(source.at[me], here.at[0])]
    passing, direct, second = {}, {}, {}
    for way in (1, 2):
        passing[way] = wires.copy(source.at[corner, rows[way]], boxes.at[1 + way], {"dp": flip[way]})
        passing[way].start()
        load.append(wires.load(source.at[flip[3 - way], rows[way]], here.at[1, rows[way]]))
    for copy in load:
        copy.start()
    for _ in range(idle):
        yield True
    for way in (1, 2):
        yield True
        load[way].wait()
        passing[way].wait_recv()
        add_into(sums.at[way - 1], [here.at[1, rows[way]], boxes.at[1 + way]])
        second[way] = wires.copy(sums.at[way - 1], boxes.at[3 + way], {"dp": flip[3 - way]})
        second[way].start()
        direct[way] = wires.copy(source.at[flip[way], rows[way]], boxes.at[way - 1], {"dp": flip[way]})
        direct[way].start()
    load[0].wait()
    yield PATIENT
    for way in (1, 2):
        direct[way].wait_recv()
        second[way].wait_recv()
        add_into(out.at[rows[way]], [here.at[0, rows[way]], boxes.at[way - 1], boxes.at[3 + way]])
    for way in (1, 2):
        passing[way].wait_send()
        direct[way].wait_send()
        second[way].wait_send()


def can_fold(array):
    return lax.axis_size("dp") == 4 and array.shape[1] % 32 == 0


def fold_scratch(array):
    _, rows, columns = array.shape
    return [
        pltpu.VMEM((6, rows // 2, columns), array.dtype),
        pltpu.VMEM((2, rows, columns), array.dtype),
        pltpu.VMEM((2, rows // 2, columns), array.dtype),
    ]


class Beside:
    def __init__(self, gathers=(), swaps=(), sums=()):
        self.gathers, self.swaps, self.sums = list(gathers), list(swaps), list(sums)
        self.arrays = self.gathers + self.swaps + self.sums
        packs = lax.axis_size("dp")
        self.outs = [shape_of((packs,) + a.shape, a.dtype) for a in self.gathers]
        self.outs += [shape_of(a.shape, a.dtype) for a in self.swaps]
        self.scratch = []
        for a in self.sums:
            fold = can_fold(a)
            self.outs.append(shape_of(a.shape[1:] if fold else a.shape, a.dtype))
            self.scratch += fold_scratch(a) if fold else []
        self.copies = HALVES * len(self.gathers) + packs * len(self.swaps) + 16 * len(self.sums)
        self.job_rooms = [room(a.shape, a.dtype) for a in self.gathers if can_halve(a)]
        self.patient_rooms = [room(a.shape, a.dtype) for a in self.gathers if not can_halve(a)]
        self.patient_rooms += [room(a.shape[1:], a.dtype) for a in self.swaps]
        self.patient_rooms += [room(a.shape[1:], a.dtype) for a in self.sums if not can_fold(a)]
        self.in_vmem_outs = [len(self.gathers) + len(self.swaps) + i for i, a in enumerate(self.sums) if can_fold(a)]

    def jobs(self, wires, ins, results, scratch):
        g, s = len(self.gathers), len(self.gathers) + len(self.swaps)
        jobs, patient = gather_jobs(wires, self.gathers, ins[:g], results[:g])
        patient += [swap_dp(wires, a, b) for a, b in zip(ins[g:s], results[g:s])]
        scratch = list(scratch)
        for array, a, b in zip(self.sums, ins[s:], results[s:]):
            if can_fold(array):
                jobs.append(fold_dp(wires, a, b, *scratch[:3]))
                scratch = scratch[3:]
            else:
                patient.append(swap_dp(wires, a, b))
        return jobs, patient

    def finish(self, got):
        g, s = len(self.gathers), len(self.gathers) + len(self.swaps)
        got = list(got)
        done = [r.reshape((-1,) + a.shape[1:]) for r, a in zip(got[:g], self.gathers)] + got[g:s]
        return done + [r if can_fold(a) else add_packs(r).astype(r.dtype) for r, a in zip(got[s:], self.sums)]


def scatter_with(name, cid, out_shape, factors, product, beside, cut=2):
    count = lax.axis_size("seq")
    rows, width = out_shape
    box = pltpu.VMEM((count // 2, rows, width), jnp.bfloat16)
    made = [pltpu.VMEM((count, rows, width), jnp.bfloat16)] if product else []
    if not product:
        factors = (factors[0].reshape(count, rows, width),)
    n_f, n_b = len(factors), len(beside.arrays)
    outs = [shape_of((rows, width), jnp.float32)] + beside.outs

    def plan(wires, ins, results, scratch):
        terms = scratch[0] if product else ins[0]
        boxes, rest = scratch[len(made) : len(made) + 4], scratch[len(made) + 4 :]
        jobs, patient = beside.jobs(wires, ins[n_f:], results[1:], rest)

        def produce(dest):
            if product:
                product(dest, ins[:n_f], terms)

        return jobs + [scatter_line(wires, produce, terms, results[0], *boxes, cut)], patient

    got = talk(
        name, cid, ("line", "dp") if n_b else ("line",), (*factors, *beside.arrays), outs, plan,
        3 * (count // 2) * cut + beside.copies,
        in_vmem=range(n_f), out_vmem=[0] + [1 + i for i in beside.in_vmem_outs], scratch=made + [box] * 4 + beside.scratch,
        rooms=beside.patient_rooms + beside.job_rooms,
    )
    return [got[0]] + beside.finish(got[1:])


def swap_places(name, cid, arrays):
    count = lax.axis_size("seq")
    return talk(
        name, cid, ("seq",), arrays, [shape_of(a.shape, a.dtype) for a in arrays],
        lambda wires, ins, outs, _: ([], [swap_seq(wires, i, o) for i, o in zip(ins, outs)]), count * len(arrays),
        rooms=[room(a.shape[1:], a.dtype) for a in arrays],
    )


def split_columns(arrays, pieces):
    rows = arrays[0].shape[0]
    width = sum(p[2] for p in pieces[0])
    tall = min(rows, 16)

    def kernel(*refs):
        for place, cuts in enumerate(pieces):
            refs[-1][place] = jnp.concatenate(
                [jnp.zeros((tall, n), refs[-1].dtype) if a is None else refs[a][:, at : at + n] for a, at, n in cuts], axis=1
            )

    return pl.pallas_call(
        kernel,
        grid=(rows // tall,),
        in_specs=[pl.BlockSpec((tall, a.shape[1]), lambda i: (i, 0)) for a in arrays],
        out_specs=pl.BlockSpec((len(pieces), tall, width), lambda i: (0, i, 0)),
        out_shape=shape_of((len(pieces), rows, width), arrays[0].dtype),
        compiler_params=pltpu.CompilerParams(vmem_limit_bytes=48 * 1024 * 1024),
        name="split_columns",
    )(*arrays)


def join_columns(array, widths, pieces):
    places, rows, width = array.shape
    tall = min(rows, 16)

    def kernel(source, *outs):
        whole = [source[place].astype(jnp.float32) for place in range(places)]
        for which, out in enumerate(outs):
            found = []
            for place, cuts in enumerate(pieces):
                start = 0
                for a, at, n in cuts:
                    if a == which:
                        found.append((at, whole[place][:, start : start + n]))
                    start += n
            out[...] = jnp.concatenate([part for _, part in sorted(found, key=lambda f: f[0])], axis=1)

    return pl.pallas_call(
        kernel,
        grid=(rows // tall,),
        in_specs=[pl.BlockSpec((places, tall, width), lambda i: (0, i, 0))],
        out_specs=[pl.BlockSpec((tall, w), lambda i: (i, 0)) for w in widths],
        out_shape=[shape_of((rows, w), jnp.float32) for w in widths],
        compiler_params=pltpu.CompilerParams(vmem_limit_bytes=48 * 1024 * 1024),
        name="join_columns",
    )(array)


def add_packs(array):
    return jnp.sum(array.astype(jnp.float32), axis=0)


def unit_groups(units):
    return [(at, min(128, units - at)) for at in range(0, units, 128)]


def feed_forward_kernel(
    cut, block_ref, top_first, top_second, wgu_hbm, wd_hbm,
    down_out, g_gu_out, g_down_out, mid_out,
    wgu_ref, wd_ref, x_out, tops, hidbuf, dgubuf, downbuf, g_gu, g_down, g_gu_low, g_down_low,
    terms, near, from_left, from_right, outbox,
    local_sems, pack_send, pack_recv, line_send, line_recv, near_send, near_recv, sum_send, sum_recv, across_send, across_recv,
):
    me, count = lax.axis_index("seq"), lax.axis_size("seq")
    chips, chip, core = count // 2, me // 2, lax.rem(me, 2)
    other = me + 1 - 2 * core
    tall = block_ref.shape[0]
    step = tall // cut
    units = wd_ref.shape[0]
    packs = lax.axis_size("dp")
    pack = lax.axis_index("dp")
    share = units // packs
    width = wd_ref.shape[1]
    meet(("line", "dp"))

    def lines(part):
        return pl.ds(part * step, step)

    def along(sign, i, part, source=None):
        at = ((1 - sign) // 2 * chips + i) * cut + part
        slot = x_out.at[me + 2 * sign * i, lines(part)]
        return pltpu.make_async_remote_copy(
            slot if source is None else source.at[lines(part)], slot,
            line_send.at[at], line_recv.at[at], on_line(-2 * sign), MESH,
        )

    def over(sign, i, part, source=None):
        at = ((1 - sign) // 2 * chips + i) * cut + part
        slot = x_out.at[me + 2 * sign * i, lines(part)]
        return pltpu.make_async_remote_copy(
            slot if source is None else source.at[lines(part)], slot,
            near_send.at[at], near_recv.at[at], sibling(), MESH,
        )

    def along_came(sign, i, part):
        at = ((1 - sign) // 2 * chips + i - 1) * cut + part
        slot = x_out.at[me + 2 * sign * i, lines(part)]
        pltpu.make_async_remote_copy(slot, slot, line_send.at[at], line_recv.at[at], sibling(), MESH).wait_recv()

    def over_came(sign, i, part):
        at = ((1 - sign) // 2 * chips + i) * cut + part
        slot = x_out.at[other + 2 * sign * i, lines(part)]
        pltpu.make_async_remote_copy(slot, slot, near_send.at[at], near_recv.at[at], sibling(), MESH).wait_recv()

    def more(sign):
        return jnp.where(sign > 0, chip > 0, chip < chips - 1)

    def across(dest, part):
        at = dest * cut + part
        return pltpu.make_async_remote_copy(
            terms.at[2 * dest + 1 - core, lines(part)], near.at[dest, lines(part)],
            across_send.at[at], across_recv.at[at], sibling(), MESH,
        )

    def onward(right, dest, part):
        at = ((0 if right else chips) + dest) * cut + part
        inbox = from_left if right else from_right
        return pltpu.make_async_remote_copy(
            outbox.at[dest, lines(part)], inbox.at[dest, lines(part)],
            sum_send.at[at], sum_recv.at[at], on_line(2 if right else -2), MESH,
        )

    own = pltpu.make_async_copy(block_ref, x_out.at[me], local_sems.at[0])
    for part in range(cut):
        for sign in (1, -1):

            @pl.when(more(sign))
            def _():
                along(sign, 0, part, block_ref).start()

        over(1, 0, part, block_ref).start()
    half = tall // 2
    weights = [
        pltpu.make_async_copy(top_first, tops.at[:, pl.ds(0, half)], local_sems.at[3]),
        pltpu.make_async_copy(top_second, tops.at[:, pl.ds(half, half)], local_sems.at[4]),
        pltpu.make_async_copy(wgu_hbm, wgu_ref, local_sems.at[1]),
        pltpu.make_async_copy(wd_hbm, wd_ref, local_sems.at[2]),
    ]
    own.start()
    for copy in weights:
        copy.start()
    own.wait()
    for copy in weights:
        copy.wait()

    def compute(dest):
        x = x_out[pl.ds(2 * dest, 2)].reshape(2 * tall, width)
        top = tops[pl.ds(2 * dest, 2)].reshape(2 * tall, width)
        for at, n in unit_groups(units):
            both = nn(x, wgu_ref[:, 2 * at : 2 * at + 2 * n])
            gate, up = both[:, :n], both[:, n:]
            d_hidden = nt(top, wd_ref[at : at + n, :])
            sig = 1.0 / (1.0 + jnp.exp(-gate))
            silu = gate * sig
            hidbuf[:, :, at : at + n] = (silu * up).astype(jnp.bfloat16).reshape(2, tall, n)
            d_gate = d_hidden * up * sig * (1.0 + gate * (1.0 - sig))
            d_both = jnp.concatenate([d_gate, d_hidden * silu], axis=1)
            dgubuf[:, :, 2 * at : 2 * at + 2 * n] = d_both.astype(jnp.bfloat16).reshape(2, tall, 2 * n)
        hid = hidbuf[...].reshape(2 * tall, units)
        dgu = dgubuf[...].reshape(2 * tall, 2 * units)
        wide = 512
        for at in range(0, width, wide):
            mid = nt(dgu, wgu_ref[at : at + wide, :]).astype(jnp.bfloat16)
            terms[pl.ds(2 * dest, 2), :, at : at + wide] = mid.reshape(2, tall, wide)
        for part in range(cut):
            across(dest, part).start()

    def compute_rest(dest):
        x = x_out[pl.ds(2 * dest, 2)].reshape(2 * tall, width)
        top = tops[pl.ds(2 * dest, 2)].reshape(2 * tall, width)
        hid = hidbuf[...].reshape(2 * tall, units)
        dgu = dgubuf[...].reshape(2 * tall, 2 * units)
        wide = 512
        for at in range(0, width, wide):
            downbuf[:, :, at : at + wide] = nn(hid, wd_ref[:, at : at + wide]).astype(jnp.bfloat16).reshape(2, tall, wide)
        for at in range(0, units, 128):
            n = min(128, units - at)
            g_down[at : at + n, :] += tn(hid[:, at : at + n], top)
        for at in range(0, width, 256):
            g_gu[at : at + 256, :] += tn(x[:, at : at + 256], dgu)

    def send_sum(right, dest, part, first, in_turn=True):
        mine = [terms.at[2 * dest + core, lines(part)], near.at[dest, lines(part)]]
        across_came(dest, part)
        if first:
            add_into(outbox.at[dest, lines(part)], mine)
        else:
            inbox = from_left if right else from_right
            sum_came(right, dest, part)
            add_into(outbox.at[dest, lines(part)], mine + [inbox.at[dest, lines(part)]])
        if in_turn and part > 0:
            onward(right, dest, part - 1).wait_send()
        onward(right, dest, part).start()

    def across_came(dest, part):
        at = dest * cut + part
        there = near.at[dest, lines(part)]
        pltpu.make_async_remote_copy(there, there, across_send.at[at], across_recv.at[at], sibling(), MESH).wait_recv()

    def sum_came(right, dest, part):
        at = ((0 if right else chips) + dest) * cut + part
        there = (from_left if right else from_right).at[dest, lines(part)]
        pltpu.make_async_remote_copy(there, there, sum_send.at[at], sum_recv.at[at], sibling(), MESH).wait_recv()

    def saved(dest):
        return pltpu.make_async_copy(downbuf, down_out.at[pl.ds(2 * dest, 2)], local_sems.at[2])

    def inside(dest):
        return (dest >= 0) & (dest < chips)

    def visit(i, j):
        sign = 1 - 2 * j
        dest = chip + sign * i

        @pl.when(inside(dest) & (i + 1 - j > 0))
        def _():
            for part in range(cut):
                over_came(sign, i, part)
            compute(dest)
            @pl.when((chip == 0) & (dest > 0) & (dest < chips - 1))
            def _():
                for part in range(cut):
                    send_sum(True, dest, part, True, False)

            @pl.when((chip == chips - 1) & (dest < chips - 1) & (dest > 0))
            def _():
                for part in range(cut):
                    send_sum(False, dest, part, True, False)

            @pl.when(i + j > 0)
            def _():
                saved(dest).wait()

            compute_rest(dest)
            saved(dest).start()

    def forward(i):
        for sign in (1, -1):

            @pl.when((i > 0) & (i < chips) & inside(chip + sign * i))
            def _():
                for part in range(cut):
                    along_came(sign, i, part)

                    @pl.when(more(sign))
                    def _():
                        along(sign, i, part).start()

                    over(sign, i, part).start()

    def distance(i, _):
        def side(j, _):
            visit(i, j)

            @pl.when((j == 0) & (i > 0) | (j == 1) & (i == 0))
            def _():
                forward(i + 1)

            return 0

        lax.fori_loop(0, 2, side, 0)
        return 0

    g_gu[...] = jnp.zeros_like(g_gu)
    g_down[...] = jnp.zeros_like(g_down)
    lax.fori_loop(0, chips, distance, 0)
    saved(chip).wait()

    def lower(i, _):
        lines = pl.ds(pl.multiple_of(i * 16, 16), 16)
        g_down_low[lines, :] = g_down[lines, :].astype(jnp.bfloat16)
        return 0

    lax.fori_loop(0, units // 16, lower, 0)
    kept = pltpu.make_async_copy(g_down_low.at[pl.ds(pack * share, share)], g_down_out.at[pack], local_sems.at[2])
    kept.start()

    def swap(step):
        peer = lax.rem(pack + step, packs)
        return pltpu.make_async_remote_copy(
            g_down_low.at[pl.ds(peer * share, share)], g_down_out.at[pack],
            pack_send.at[step], pack_recv.at[step], pack_peer(step), MESH,
        )

    for turn in range(1, packs):
        swap(turn).start()

    @pl.when(chip == 0)
    def _():
        for part in range(cut):
            send_sum(True, chips - 1, part, True)

    @pl.when(chip == chips - 1)
    def _():
        for part in range(cut):
            send_sum(False, 0, part, True)

    def rightward():
        for i in range(1, chips - 1):

            @pl.when((chip > 0) & (chip + i < chips))
            def _():
                for part in range(cut):
                    send_sum(True, chip + i, part, False)

    def leftward():
        for i in range(1, chips - 1):

            @pl.when((chip < chips - 1) & (chip - i >= 0))
            def _():
                for part in range(cut):
                    send_sum(False, chip - i, part, False)

    @pl.when(chip < chips // 2)
    def _():
        rightward()
        leftward()

    @pl.when(chip >= chips // 2)
    def _():
        leftward()
        rightward()

    for part in range(cut):
        across_came(chip, part)
        mine = [terms.at[2 * chip + core, lines(part)], near.at[chip, lines(part)]]
        left_in, right_in = from_left.at[chip, lines(part)], from_right.at[chip, lines(part)]

        @pl.when(chip == 0)
        def _():
            sum_came(False, chip, part)
            add_into(mid_out.at[lines(part)], mine + [right_in])

        @pl.when(chip == chips - 1)
        def _():
            sum_came(True, chip, part)
            add_into(mid_out.at[lines(part)], mine + [left_in])

        @pl.when((chip > 0) & (chip < chips - 1))
        def _():
            sum_came(True, chip, part)
            sum_came(False, chip, part)
            add_into(mid_out.at[lines(part)], mine + [left_in, right_in])

    chunk = g_gu_low.shape[1]

    def gu_copy(at):
        slot = lax.rem(at, 2)
        return pltpu.make_async_copy(
            g_gu_low.at[slot], g_gu_out.at[pl.ds(at * chunk, chunk)], local_sems.at[3 + slot]
        )

    def lower_gu(at, _):
        @pl.when(at > 1)
        def _():
            gu_copy(at - 2).wait()

        slot = lax.rem(at, 2)

        def some(i, _):
            there = pl.ds(pl.multiple_of(i * 16, 16), 16)
            came = pl.ds(pl.multiple_of(at * chunk + i * 16, 16), 16)
            g_gu_low[slot, there, :] = g_gu[came, :].astype(jnp.bfloat16)
            return 0

        lax.fori_loop(0, chunk // 16, some, 0)
        gu_copy(at).start()
        return 0

    chunks = width // chunk
    lax.fori_loop(0, chunks, lower_gu, 0)
    for at in range(max(chunks - 2, 0), chunks):
        gu_copy(at).wait()
    for turn in range(1, packs):
        swap(turn).wait()
    kept.wait()
    for part in range(cut):
        for dest in range(chips):
            across(dest, part).wait_send()

            early_right = (chip == 0) & (dest < chips - 1) | (part == cut - 1)
            early_left = (chip == chips - 1) & (dest > 0) | (part == cut - 1)

            @pl.when((chip < dest) & early_right)
            def _():
                onward(True, dest, part).wait_send()

            @pl.when((chip > dest) & early_left)
            def _():
                onward(False, dest, part).wait_send()

        for i in range(chips):
            for sign in (1, -1):
                there = (chip + sign * i >= 0) & (chip + sign * i < chips)

                @pl.when(there & more(sign))
                def _():
                    along(sign, i, part).wait_send()

                if i > 0 or sign > 0:

                    @pl.when(there)
                    def _():
                        over(sign, i, part).wait_send()


def feed_forward(cid, block, tops, w_gu, w_d, cut=2):
    count = lax.axis_size("seq")
    chips = count // 2
    tall, width = block.shape
    units = w_d.shape[0]
    packs = lax.axis_size("dp")
    bf16 = jnp.bfloat16
    outs = [
        shape_of((count, tall, width), bf16),
        shape_of((width, 2 * units), bf16),
        shape_of((packs, units // packs, width), bf16),
        shape_of((tall, width), jnp.float32),
    ]
    box = pltpu.VMEM((chips, tall, width), bf16)
    dma = lambda n: pltpu.SemaphoreType.DMA((n,))
    anywhere, vmem = pl.BlockSpec(memory_space=pl.ANY), pl.BlockSpec(memory_space=pltpu.VMEM)
    flops = 2 * 2 * count * tall * width * 3 * units
    got = pl.pallas_call(
        functools.partial(feed_forward_kernel, cut),
        out_shape=outs,
        in_specs=[anywhere] * 5,
        out_specs=[anywhere] * 3 + [vmem],
        scratch_shapes=[
            pltpu.VMEM(w_gu.shape, bf16),
            pltpu.VMEM(w_d.shape, bf16),
            pltpu.VMEM((count, tall, width), bf16),
            pltpu.VMEM((count, tall, width), bf16),
            pltpu.VMEM((2, tall, units), bf16),
            pltpu.VMEM((2, tall, 2 * units), bf16),
            pltpu.VMEM((2, tall, width), bf16),
            pltpu.VMEM((width, 2 * units), jnp.float32),
            pltpu.VMEM((units, width), jnp.float32),
            pltpu.VMEM((2, 256, 2 * units), bf16),
            pltpu.VMEM((units, width), bf16),
            pltpu.VMEM((count, tall, width), bf16),
            box, box, box, box,
            dma(5), dma(packs), dma(packs),
        ] + [dma(2 * chips * cut)] * 6 + [dma(chips * cut)] * 2,
        compiler_params=pltpu.CompilerParams(
            collective_id=cid, has_side_effects=True, vmem_limit_bytes=62 * 1024 * 1024
        ),
        cost_estimate=pl.CostEstimate(flops=flops, bytes_accessed=20 << 20, transcendentals=0),
        name="feed_forward",
    )(block, *tops, w_gu, w_d)
    return got


def cross_rows(left_side, right_side):
    return lax.dot_general(left_side, right_side, (((0,), (0,)), ((), ())), preferred_element_type=jnp.float32)


def cross_cols(left_side, right_side):
    return lax.dot_general(left_side, right_side, (((1,), (1,)), ((), ())), preferred_element_type=jnp.float32)


def dot(left_side, right_side):
    return jnp.dot(left_side, right_side, preferred_element_type=jnp.float32)


def on_device(
    tokens,
    segments,
    norm_one,
    w_qkv,
    w_lr,
    lr_bias,
    w_gate,
    w_out,
    w_init,
    b_init,
    tnorm_w,
    tnorm_b,
    post_w,
    post_b,
    norm_two,
    w_gate_up,
    w_down,
    grad_out,
):
    floats = jnp.float32
    bf16 = jnp.bfloat16
    both = ("dp", "seq")
    packs, per_seq = lax.axis_size("dp"), lax.axis_size("seq")
    devices = packs * per_seq
    place = lax.axis_index("seq")
    span, width = tokens.shape[1], tokens.shape[2]
    rows = norm_one.shape[0]
    heads_all = lr_bias.shape[0]
    units = w_down.shape[0]
    length = span * per_seq
    blocks = length // MB
    heads = heads_all // per_seq
    aligned = rows % HD == 0
    outer = packs if aligned else 1
    inner = width // (outer * per_seq)
    mine = outer * inner

    def own_rows(array):
        cut = array.reshape((outer, per_seq, inner) + array.shape[1:])
        cut = lax.dynamic_index_in_dim(cut, place, 1, keepdims=False)
        return cut.reshape((mine,) + array.shape[1:])

    def put_rows(array):
        full = jnp.zeros((outer, per_seq, inner) + array.shape[1:], array.dtype)
        part = array.reshape((outer, 1, inner) + array.shape[1:])
        at = (0, place) + (0,) * (part.ndim - 2)
        return lax.dynamic_update_slice(full, part, at).reshape((width,) + array.shape[1:])

    extra = 128
    feature_cuts = [
        [(0, (part * outer + o) * per_seq * inner + s * inner, inner) for part in range(3) for o in range(outer)]
        + [(1, o * per_seq * inner + s * inner, inner) for o in range(outer)]
        for s in range(per_seq)
    ]
    filled = -(-units // 16) * 16
    unit_cuts = []
    for s in range(per_seq):
        cuts = []
        for at, n in unit_groups(packs * filled):
            for part in range(2):
                u = at
                while u < at + n:
                    pack, i = divmod(u, filled)
                    run = min((units if i < units else filled) - i, at + n - u)
                    first = (part * packs * per_seq + pack * per_seq + s) * units + i
                    cuts.append((0, first, run) if i < units else (None, 0, run))
                    u += run
        unit_cuts.append(cuts)

    spans = span // MB
    lr_places = w_lr.reshape(rows, outer, per_seq, heads // outer).transpose(0, 2, 1, 3).reshape(rows, per_seq, heads)
    tags = segments[0].reshape(1, 1, spans, MB)[:, :, :, 0].astype(bf16)
    beside_cols = jnp.concatenate(
        [
            lr_places,
            jnp.broadcast_to(jnp.stack([norm_one, norm_two], axis=1)[:, None], (rows, per_seq, 2)),
            jnp.broadcast_to(tags, (rows, per_seq, spans)),
            jnp.zeros((rows, per_seq, extra - heads - 2 - spans), bf16),
        ],
        axis=2,
    ).reshape(rows, per_seq * extra)
    mix_cuts = [cuts + [(2, s * extra, extra)] for s, cuts in enumerate(feature_cuts)]
    vectors = jnp.stack([b_init, tnorm_w, tnorm_b, post_w, post_b], axis=1)
    head_rows = jnp.concatenate([w_init, vectors, jnp.zeros((rows, extra - HD - 5), bf16)], axis=1)
    over_dp = (w_out, head_rows) if aligned else ()
    w_mix, rows_all, *got = first_exchange(
        split_columns((w_qkv, w_gate, beside_cols), mix_cuts), tokens[0], over_dp
    )
    if aligned:
        w_o, head_rows = got
    else:
        w_o, head_rows = (own_rows(lax.all_gather(a, both, axis=0, tiled=True)) for a in (w_out, head_rows))
    w_extra = w_mix[:, 4 * mine :]
    gain_one, gain_two = w_extra[:, heads].astype(floats), w_extra[:, heads + 1].astype(floats)
    pack_tags = w_extra.reshape(packs, per_seq, rows, extra)[:, :, 0, heads + 2 : heads + 2 + spans]
    pack_tags = lax.dynamic_index_in_dim(pack_tags.reshape(packs, blocks), lax.axis_index("dp"), 0, keepdims=False)
    fresh = jnp.concatenate([jnp.ones((1,), jnp.int32), (pack_tags[1:] != pack_tags[:-1]).astype(jnp.int32)])
    vec_own = head_rows[:, HD : HD + 5].astype(floats)
    post_gain, post_shift = vec_own[:, 3], vec_own[:, 4]
    bias_own = lax.dynamic_index_in_dim(lr_bias.reshape(outer, per_seq, heads // outer), place, 1, keepdims=False)
    bias_own = bias_own.reshape(heads).astype(floats)

    half = span // 2
    later_top, rows_all = lax.optimization_barrier((grad_out[0, :half], rows_all))
    top_first = lax.all_gather(later_top, "seq", axis=0)
    gu_mine = split_columns((w_gate_up,), unit_cuts)

    inputs = rows_all.astype(floats)
    scale_one = lax.rsqrt(jnp.mean(inputs * inputs, -1, keepdims=True) + EPSILON)
    normed_in = inputs * scale_one
    x_one = (normed_in * gain_one).astype(bf16)
    qkv = dot(x_one, w_mix[:, : 3 * mine])
    gate_pre = dot(x_one, w_mix[:, 3 * mine : 4 * mine])
    lr_sigm = jax.nn.sigmoid(dot(x_one, w_extra)[:, :heads] + bias_own)
    e_rows = (lr_sigm * (1.0 / (HD * MB))).reshape(blocks, MB, heads).transpose(0, 2, 1).reshape(blocks, 1, heads * MB)

    def by_token(vector):
        return jnp.repeat(vector.reshape(heads, HD).T, MB, axis=1)

    init_w = head_rows[:, :HD].astype(floats).reshape(heads, HD, HD)
    init_w = (init_w - jnp.mean(init_w, -1, keepdims=True)).transpose(2, 0, 1).reshape(HD, heads * HD)
    init_b = vec_own[:, 0].reshape(heads, HD)
    init_b = (init_b - jnp.mean(init_b, -1, keepdims=True)).reshape(-1)
    gain_t, shift_t = by_token(vec_own[:, 1]), by_token(vec_own[:, 2])
    *results, gu_part, w_d = inner_forward(
        10, fresh, qkv, e_rows, init_w, by_token(init_b), gain_t, shift_t, (gu_mine,),
        (jnp.pad(w_down, ((0, filled - units), (0, 0))),),
    )
    w_d = w_d.reshape(-1, w_d.shape[-1])
    mixed, *saved = results
    later_top, mixed = lax.optimization_barrier((grad_out[0, half:], mixed))
    top_second = lax.all_gather(later_top, "seq", axis=0)

    mean_own = jnp.mean(mixed, -1)
    spread_own = jnp.sum((mixed - mean_own[:, None]) ** 2, -1)
    stats = gather_seq("share_moments", 2, jnp.stack([mean_own, spread_own]))
    mean_all = jnp.mean(stats[:, 0], 0)
    var_all = (jnp.sum(stats[:, 1], 0) + mine * jnp.sum((stats[:, 0] - mean_all) ** 2, 0)) * (1.0 / width)
    out_scale = lax.rsqrt(var_all + EPSILON)[:, None]
    out_hat = (mixed - mean_all[:, None]) * out_scale
    normed_out = out_hat * post_gain + post_shift
    gelu_gate, gelu_pull = jax.vjp(jax.nn.gelu, gate_pre)
    gated_unit = (gelu_gate * normed_out).astype(bf16)
    pair = 2 * span
    wide = 512

    def branch_terms(dest, factors, terms):
        unit = factors[0][dest * pair : (dest + 1) * pair, :]
        for at in range(0, width, wide):
            part = nn(unit, factors[1][:, at : at + wide]).astype(bf16)
            terms[2 * dest : 2 * dest + 2, :, at : at + wide] = part.reshape(2, span, wide)

    branch, w_gu = scatter_with(
        "scatter_branch", 3, (span, width), (gated_unit, w_o), branch_terms,
        Beside(gathers=(gu_part.reshape(-1, gu_part.shape[-1]),)),
    )
    inputs = tokens[0].astype(floats)
    residual = inputs + branch
    scale_two = lax.rsqrt(jnp.mean(residual * residual, -1, keepdims=True) + EPSILON)
    normed_mid = residual * scale_two
    down, g_gate_up, g_down, d_xtwo = feed_forward(
        5, (normed_mid * gain_two).astype(bf16), (top_first, top_second), w_gu, w_d
    )
    down = down.reshape(-1, width)
    pack_rows = lambda array: array.reshape((packs, -1) + array.shape[1:])
    g_gate_up = pack_rows(g_gate_up)
    g_down = add_packs(g_down)[:units]
    g_two = jnp.sum(d_xtwo * normed_mid, axis=0)
    d_mid = d_xtwo * gain_two
    d_residual = grad_out[0].astype(floats) + scale_two * (
        d_mid - normed_mid * jnp.mean(d_mid * normed_mid, -1, keepdims=True)
    )
    d_branch, g_gate_up = gather_with("gather_branch", 6, d_residual.astype(bf16), Beside(sums=(g_gate_up,)))
    down_first, d_branch = lax.optimization_barrier((down[:, : width // 2], d_branch))
    down_first = lax.psum_scatter(down_first, "seq", scatter_dimension=0, tiled=True)
    g_out = cross_rows(gated_unit, d_branch).astype(bf16)
    d_unit = cross_cols(d_branch, w_o)
    d_normed = d_unit * gelu_gate
    g_post_w = jnp.sum(d_normed * out_hat, axis=0)
    g_post_b = jnp.sum(d_normed, axis=0)
    d_hat = d_normed * post_gain
    sums = gather_seq("share_sums", 7, jnp.stack([jnp.sum(d_hat, -1), jnp.sum(d_hat * out_hat, -1)]))
    sums = jnp.sum(sums, 0) * (1.0 / width)
    d_mixed = out_scale * (d_hat - sums[0][:, None] - out_hat * sums[1][:, None])
    d_gate_pre = gelu_pull(d_unit * normed_out)[0].astype(bf16)
    place_rows = lambda array: array.reshape((per_seq, -1) + array.shape[1:])
    g_gate = pack_rows(cross_rows(x_one, d_gate_pre).astype(bf16))
    d_qkv, d_rate, d_w0, d_c0, d_gain, d_shift, g_gate_up, g_gate, *g_outs = inner_backward(
        11, fresh, qkv, e_rows, d_mixed, saved, gain_t, shift_t, (place_rows(g_gate_up),),
        [(g_gate, None, None)] + [(pack_rows(g_out), None, None)] * aligned,
    )
    (g_gate_up,) = join_columns(g_gate_up, (w_gate_up.shape[1],), unit_cuts)
    if aligned:
        g_out = add_packs(g_outs[0])
    else:
        g_out = lax.psum_scatter(put_rows(g_out), both, scatter_dimension=0, tiled=True).astype(floats)
    down_second, d_qkv = lax.optimization_barrier((down[:, width // 2 :], d_qkv))
    down_second = lax.psum_scatter(down_second, "seq", scatter_dimension=0, tiled=True)
    result = residual + jnp.concatenate([down_first, down_second], axis=1).astype(floats)
    d_rate = d_rate.reshape(blocks, heads, MB).transpose(0, 2, 1).reshape(length, heads)
    d_logit = (d_rate * (1.0 / HD) * lr_sigm * (1.0 - lr_sigm)).astype(bf16)
    g_qkv = cross_rows(x_one, d_qkv).astype(bf16)
    d_logit_wide = jnp.pad(d_logit, ((0, 0), (0, extra - heads)))
    d_xone = cross_cols(jnp.concatenate([d_qkv, d_gate_pre, d_logit_wide], axis=1), w_mix)
    g_one = jnp.sum(d_xone * (lax.optimization_barrier(rows_all).astype(floats) * scale_one), axis=0)

    lane = jnp.arange(extra)[None, :]
    g_bias = jnp.pad(jnp.sum(d_logit.astype(floats), axis=0), (heads + 2, extra - 2 * heads - 2))
    g_beside = cross_rows(x_one, d_logit_wide) + jnp.where(lane == heads, g_one[:, None], 0.0)
    g_beside = (g_beside + jnp.where(lane == heads + 1, g_two[:, None], 0.0) + g_bias[None, :]).astype(bf16)

    def from_token(array):
        return jnp.sum(array.reshape(HD, heads, MB), -1).T.reshape(mine)

    g_vec = jnp.stack(
        [d_c0.reshape(HD, heads, MB)[:, :, 0].T.reshape(mine), from_token(d_gain), from_token(d_shift), g_post_w, g_post_b],
        axis=1,
    )
    g_heads = jnp.concatenate(
        [d_w0.reshape(HD, heads, HD).transpose(1, 2, 0).reshape(mine, HD), g_vec, jnp.zeros((mine, extra - HD - 5), floats)],
        axis=1,
    )

    swaps = [pack_rows(g_heads)] * aligned + [pack_rows(g_beside), pack_rows(g_qkv)]
    d_xone, *got = scatter_with("scatter_first", 8, (span, width), (d_xone.astype(bf16),), None, Beside(swaps=swaps))
    if aligned:
        g_heads = add_packs(got[0])
    else:
        g_heads = lax.psum_scatter(put_rows(g_heads), both, scatter_dimension=0, tiled=True)
    g_mix = jnp.concatenate([add_packs(got[-1]), add_packs(g_gate), add_packs(got[-2])], axis=1).astype(bf16)
    (g_mix,) = swap_places("return_columns", 9, (place_rows(g_mix),))
    g_qkv, g_gate = join_columns(g_mix, (w_qkv.shape[1], w_gate.shape[1]), feature_cuts)
    g_beside = g_mix[:, :, 4 * mine :].astype(floats)
    g_norms = jnp.sum(g_beside[:, :, heads : heads + 2], 0)

    def by_head(part):
        part = part.reshape(part.shape[:-1] + (outer, heads // outer))
        return jnp.moveaxis(part, 0, -2).reshape(part.shape[1:-2] + (heads_all,))

    scale_one = lax.rsqrt(jnp.mean(inputs * inputs, -1, keepdims=True) + EPSILON)
    normed_in = inputs * scale_one
    d_inner = d_xone * gain_one
    d_tokens = d_residual + scale_one * (
        d_inner - normed_in * jnp.mean(d_inner * normed_in, -1, keepdims=True)
    )
    return (
        result.astype(bf16)[None],
        d_tokens.astype(bf16)[None],
        g_norms[:, 0],
        g_qkv,
        by_head(g_beside[:, :, :heads]),
        by_head(g_beside[:, 0, heads + 2 : 2 * heads + 2]),
        g_gate,
        g_out,
        g_heads[:, :HD],
        g_heads[:, HD],
        g_heads[:, HD + 1],
        g_heads[:, HD + 2],
        g_heads[:, HD + 3],
        g_heads[:, HD + 4],
        g_norms[:, 1],
        g_gate_up,
        g_down,
    )


def solution(mesh):
    placed = (
        P("dp", "seq", None),
        P("dp", "seq"),
        P(("dp", "seq")),
        P(("dp", "seq"), None),
        P(("dp", "seq"), None),
        P(),
        P(("dp", "seq"), None),
        P(("dp", "seq"), None),
        P(("dp", "seq"), None),
        P(("dp", "seq")),
        P(("dp", "seq")),
        P(("dp", "seq")),
        P(("dp", "seq")),
        P(("dp", "seq")),
        P(("dp", "seq")),
        P(("dp", "seq"), None),
        P(("dp", "seq"), None),
        P("dp", "seq", None),
    )
    return jax.shard_map(
        on_device,
        mesh=mesh,
        in_specs=placed,
        out_specs=(
            P("dp", "seq", None),
            P("dp", "seq", None),
            P(("dp", "seq")),
            P(("dp", "seq"), None),
            P(("dp", "seq"), None),
            P(),
            P(("dp", "seq"), None),
            P(("dp", "seq"), None),
            P(("dp", "seq"), None),
            P(("dp", "seq")),
            P(("dp", "seq")),
            P(("dp", "seq")),
            P(("dp", "seq")),
            P(("dp", "seq")),
            P(("dp", "seq")),
            P(("dp", "seq"), None),
            P(("dp", "seq"), None),
        ),
        check_vma=False,
    )
```

```python
import functools
import jax
import jax.numpy as jnp
from jax import lax
from jax.experimental import pallas as pl
from jax.experimental.pallas import tpu as pltpu
from jax.sharding import PartitionSpec as P

HD = 64
MB = 16
PER = 8
EPSILON = 1e-06


def nn(left, right):
    return lax.dot_general(left, right, (((1,), (0,)), ((), ())), preferred_element_type=jnp.float32)


def nt(left, right):
    return lax.dot_general(left, right, (((1,), (1,)), ((), ())), preferred_element_type=jnp.float32)


def tn(left, right):
    return lax.dot_general(left, right, (((0,), (0,)), ((), ())), preferred_element_type=jnp.float32)


def halves(value):
    high = value.astype(jnp.bfloat16)
    return high, (value - high.astype(jnp.float32)).astype(jnp.bfloat16)


def head_masks(heads):
    ht, hi = heads * MB, heads * HD

    def iota(shape, axis):
        return lax.broadcasted_iota(jnp.int32, shape, axis)

    own = (iota((ht, hi), 0) // MB == iota((ht, hi), 1) // HD).astype(jnp.float32)
    unit = (iota((HD, hi), 0) == iota((HD, hi), 1) % HD).astype(jnp.bfloat16)
    row, col = iota((ht, ht), 0), iota((ht, ht), 1)
    same = (row // MB == col // MB).astype(jnp.bfloat16)
    ts, tt = row % MB, col % MB
    later = jnp.where((row // MB == col // MB) & (ts <= tt), MB / (tt + 1).astype(jnp.float32), 0.0)
    earlier = jnp.where((row // MB == col // MB) & (tt <= ts), MB / (ts + 1).astype(jnp.float32), 0.0)
    return own, unit, same, later, earlier


def spread(rows, own, heads):
    return (jnp.concatenate([rows] * heads, axis=0) * own).astype(jnp.bfloat16)


def fold(values, heads):
    total = values[:MB]
    for h in range(1, heads):
        total = total + values[h * MB : (h + 1) * MB]
    return total


def turned(rows, own, unit, heads):
    wide = jnp.concatenate([rows] * heads, axis=0) * own
    high, low = halves(wide)
    return nt(unit, high) + nt(unit, low)


def mean0(value):
    return jnp.sum(value, axis=0, keepdims=True) * (1.0 / HD)


def forward_kernel(heads, per, over_seq, over_dp, fresh_ref, qkv_ref, e_ref, w0_ref, c0_ref, gain_ref, shift_ref, *refs):
    moved = over_seq + over_dp
    sources, refs = refs[:moved], refs[moved:]
    near_out, refs = refs[7 + moved], refs[: 7 + moved] + refs[8 + moved :]
    mixed_ref, wsave_ref, hat_ref, slope_ref, gap_ref, bar_ref, rows_ref = refs[:7]
    results, (w_ref, c_ref, send_sems, recv_sems, *rooms) = refs[7 : 7 + moved], refs[7 + moved :]
    jobs = [swap_seq] * over_seq + [spread_dp] * over_dp
    beside(
        ("seq", "dp", "cross"), send_sems, recv_sems, rooms,
        lambda wires: [job(wires, a, b) for job, a, b in zip(jobs, sources, results)]
        + [near_pieces(wires, sources[0], near_out)],
    )
    hi = heads * HD
    own, unit, same, later, _ = head_masks(heads)
    gain, shift, w0, c0 = gain_ref[...], shift_ref[...], w0_ref[...], c0_ref[...]
    gain2 = gain * gain

    @pl.when(pl.program_id(0) == 0)
    def _():
        w_ref[...] = jnp.zeros_like(w_ref)
        c_ref[...] = jnp.zeros_like(c_ref)

    w, c = w_ref[...], c_ref[...]
    for b in range(per):
        is_fresh = fresh_ref[pl.program_id(0) * per + b] != 0
        lines = slice(b * MB, (b + 1) * MB)
        q, k, v = qkv_ref[lines, :hi], qkv_ref[lines, hi : 2 * hi], qkv_ref[lines, 2 * hi :]
        e = e_ref[b]
        kb, qb = spread(k, own, heads), spread(q, own, heads)
        gap = shift - turned(v - k, own, unit, heads)
        base = gain * gap
        w = jnp.where(is_fresh, w0, w)
        c = jnp.where(is_fresh, c0, c)
        wb = w.astype(jnp.bfloat16)
        wsave_ref[b] = wb
        z = nt(wb, kb) + c
        gz = gain2 * z
        s = lax.rsqrt(mean0(z * z) + EPSILON)
        mean_g = s * mean0(gz) + mean0(base)
        mean_gx = s * (s * mean0(gz * z) + mean0(base * z))
        hat = s * z
        slope = s * (gain2 * hat + base - mean_g - hat * mean_gx)
        eb = (e * slope).astype(jnp.bfloat16)
        mix = (later * (nt(kb, qb) + 1.0)).astype(jnp.bfloat16)
        zbar = nt(wb, qb) + c - nn(eb, mix)
        w = w - nn(eb, kb)
        c = c - nn(eb, same)
        sbar = lax.rsqrt(mean0(zbar * zbar) + EPSILON)
        bar = zbar * sbar
        high, low = halves(gain * bar + shift)
        mixed_ref[lines, :] = q + fold((tn(high, unit) + tn(low, unit)) * own, heads)
        hat_ref[b] = hat
        slope_ref[b] = slope
        gap_ref[b] = gap
        bar_ref[b] = bar
        rows_ref[b] = jnp.concatenate([s, sbar, mean_g, mean_gx], axis=0)
    w_ref[...] = w
    c_ref[...] = c


def inner_forward(cid, fresh, qkv, e_rows, w0, c0, gain, shift, seq_arrays, dp_arrays):
    arrays = tuple(seq_arrays) + tuple(dp_arrays)
    packs = lax.axis_size("dp")
    tokens, heads = qkv.shape[0], qkv.shape[1] // (3 * HD)
    ht, hi = heads * MB, heads * HD
    blocks = tokens // MB
    per = PER
    f32 = jnp.float32
    whole = lambda shape: pl.BlockSpec(shape, lambda i: (0, 0))
    save = pl.BlockSpec((per, HD, ht), lambda i: (i, 0, 0))
    return pl.pallas_call(
        functools.partial(forward_kernel, heads, per, len(seq_arrays), len(dp_arrays)),
        grid=(blocks // per,),
        in_specs=[
            pl.BlockSpec(memory_space=pltpu.SMEM),
            pl.BlockSpec((per * MB, 3 * hi), lambda i: (i, 0)),
            pl.BlockSpec((per, 1, ht), lambda i: (i, 0, 0)),
            whole((HD, hi)), whole((HD, ht)), whole((HD, ht)), whole((HD, ht)),
        ] + [pl.BlockSpec(memory_space=pl.ANY)] * len(arrays),
        out_specs=[
            pl.BlockSpec((per * MB, hi), lambda i: (i, 0)),
            pl.BlockSpec((per, HD, hi), lambda i: (i, 0, 0)),
            save, save, save, save,
            pl.BlockSpec((per, 4, ht), lambda i: (i, 0, 0)),
        ] + [pl.BlockSpec(memory_space=pl.ANY)] * (len(arrays) + 1),
        out_shape=[
            jax.ShapeDtypeStruct((tokens, hi), f32),
            jax.ShapeDtypeStruct((blocks, HD, hi), jnp.bfloat16),
        ] + [jax.ShapeDtypeStruct((blocks, HD, ht), f32)] * 4 + [jax.ShapeDtypeStruct((blocks, 4, ht), f32)]
        + [shape_of(a.shape, a.dtype) for a in seq_arrays]
        + [shape_of((packs,) + a.shape, a.dtype) for a in dp_arrays]
        + [shape_of((packs,) + arrays[0].shape, arrays[0].dtype)],
        scratch_shapes=[pltpu.VMEM((HD, hi), f32), pltpu.VMEM((HD, ht), f32)]
        + wire_sems(len(seq_arrays) * lax.axis_size("seq") + len(dp_arrays) * packs + 2 * packs)
        + [room(a.shape[1:], a.dtype) for a in seq_arrays] + [room(a.shape, a.dtype) for a in dp_arrays],
        compiler_params=pltpu.CompilerParams(
            vmem_limit_bytes=48 * 1024 * 1024, collective_id=cid, has_side_effects=True
        ),
        name="inner_forward",
    )(fresh, qkv, e_rows, w0, c0, gain, shift, *arrays)


def backward_kernel(heads, per, over_seq, items, fresh_ref, qkv_ref, e_ref, dmix_ref, wsave_ref, hat_ref, slope_ref,
                    gap_ref, bar_ref, rows_ref, gain_ref, shift_ref, *refs):
    moved = over_seq + len(items)
    sources, refs = refs[:moved], refs[moved:]
    sources = list(sources[:over_seq]) + [window(ref, item) for ref, item in zip(sources[over_seq:], items)]
    dqkv_ref, drate_ref, dw0_ref, dc0_ref, dgain_ref, dshift_ref = refs[:6]
    results, (a_ref, ac_ref, send_sems, recv_sems, *rooms) = refs[6 : 6 + moved], refs[6 + moved :]
    swaps = [swap_seq] * over_seq + [swap_dp] * len(items)
    beside(
        ("seq", "dp"), send_sems, recv_sems, rooms,
        lambda wires: [swap(wires, a, b) for swap, a, b in zip(swaps, sources, results)],
    )
    hi, ht = heads * HD, heads * MB
    own, unit, same, later, earlier = head_masks(heads)
    gain = gain_ref[...]
    gain2 = gain * gain
    step = pl.program_id(0)

    @pl.when(step == 0)
    def _():
        for ref in (a_ref, ac_ref, dw0_ref, dc0_ref, dgain_ref, dshift_ref):
            ref[...] = jnp.zeros_like(ref)

    a, ac = a_ref[...], ac_ref[...]
    dw0, dc0, dgain, dshift = dw0_ref[...], dc0_ref[...], dgain_ref[...], dshift_ref[...]
    for b in reversed(range(per)):
        is_fresh = fresh_ref[(pl.num_programs(0) - 1 - step) * per + b] != 0
        lines = slice(b * MB, (b + 1) * MB)
        q, k = qkv_ref[lines, :hi], qkv_ref[lines, hi : 2 * hi]
        e = e_ref[b]
        wb, hat, slope, gap, bar = wsave_ref[b], hat_ref[b], slope_ref[b], gap_ref[b], bar_ref[b]
        s, sbar, mean_g, mean_gx = (rows_ref[b][i : i + 1] for i in range(4))
        kb, qb = spread(k, own, heads), spread(q, own, heads)
        dout = dmix_ref[lines, :]
        dturn = turned(dout, own, unit, heads)
        head = gain * dturn
        dbar = sbar * (head - mean0(head) - bar * mean0(head * bar))
        dbarb = dbar.astype(jnp.bfloat16)
        scores = nt(qb, kb) + 1.0
        mix = earlier * scores
        s2 = s * s
        gh = gain2 * hat
        alpha = s2 * (gain2 - mean_gx)
        kappa = s2 * (gain2 * hat + gap * gain + gh)
        kappa1 = mean_g + mean0(gh)
        kappa2 = 2.0 * mean_gx + mean0(gh * hat)
        ab = a.astype(jnp.bfloat16)
        ka = nt(ab, kb) + ac
        u = -e * (ka + nn(dbarb, mix.astype(jnp.bfloat16)))
        ug = gain2 * u
        r2 = mean0(u * hat)
        r3 = mean0(ug)
        r4 = mean0(ug * hat)
        r5 = mean0(u * slope)
        row1 = s2 * (r3 - r2 * kappa1)
        row2 = s2 * (r4 - r2 * kappa2) + s * r5
        dz = alpha * u - r2 * kappa - row1 - hat * row2
        dzb = dz.astype(jnp.bfloat16)
        dg = s * (u - hat * r2)
        a_next = a + nn(dbarb, qb) + nn(dzb, kb)
        ac_next = ac + nn(dbarb, same) + nn(dzb, same)
        dm = -tn(dbarb, slope.astype(jnp.bfloat16))
        ds = (earlier * e * dm).astype(jnp.bfloat16)
        drate_ref[b] = (jnp.sum(mix * dm, axis=0, keepdims=True) - jnp.sum(ka * slope, axis=0, keepdims=True)) * (1.0 / MB)
        dgb = (gain * dg)
        ndg = fold(tn(dgb.astype(jnp.bfloat16), unit) * own, heads)
        dq = dout + fold(tn(dbarb, wb) * own + nn(ds, kb), heads)
        dk = ndg + fold((tn(dzb, wb) - tn((e * slope).astype(jnp.bfloat16), ab)) * own + tn(ds, qb), heads)
        dqkv_ref[lines, :hi] = dq.astype(jnp.bfloat16)
        dqkv_ref[lines, hi : 2 * hi] = dk.astype(jnp.bfloat16)
        dqkv_ref[lines, 2 * hi :] = (-ndg).astype(jnp.bfloat16)
        dgain = dgain + dturn * bar + dg * (2.0 * gain * hat + gap)
        dshift = dshift + dturn + dgb
        dw0 = dw0 + jnp.where(is_fresh, a_next, 0.0)
        dc0 = dc0 + jnp.where(is_fresh, ac_next, 0.0)
        a = jnp.where(is_fresh, 0.0, a_next)
        ac = jnp.where(is_fresh, 0.0, ac_next)
    a_ref[...] = a
    ac_ref[...] = ac
    dw0_ref[...] = dw0
    dc0_ref[...] = dc0
    dgain_ref[...] = dgain
    dshift_ref[...] = dshift


def inner_backward(cid, fresh, qkv, e_rows, dmix, saved, gain, shift, seq_arrays, items):
    arrays = tuple(seq_arrays) + tuple(item[0] for item in items)
    tokens, heads = qkv.shape[0], qkv.shape[1] // (3 * HD)
    ht, hi = heads * MB, heads * HD
    blocks = tokens // MB
    per = PER
    last = blocks // per - 1
    f32 = jnp.float32
    whole = lambda shape: pl.BlockSpec(shape, lambda i: (0, 0))
    three = lambda shape: pl.BlockSpec(shape, lambda i: (last - i, 0, 0))
    two = lambda shape: pl.BlockSpec(shape, lambda i: (last - i, 0))
    save = three((per, HD, ht))
    return pl.pallas_call(
        functools.partial(backward_kernel, heads, per, len(seq_arrays), items),
        grid=(blocks // per,),
        in_specs=[
            pl.BlockSpec(memory_space=pltpu.SMEM),
            two((per * MB, 3 * hi)), three((per, 1, ht)), two((per * MB, hi)),
            three((per, HD, hi)), save, save, save, save, three((per, 4, ht)),
            whole((HD, ht)), whole((HD, ht)),
        ] + [pl.BlockSpec(memory_space=pl.ANY)] * len(arrays),
        out_specs=[
            two((per * MB, 3 * hi)), three((per, 1, ht)),
            whole((HD, hi)), whole((HD, ht)), whole((HD, ht)), whole((HD, ht)),
        ] + [pl.BlockSpec(memory_space=pl.ANY)] * len(arrays),
        out_shape=[
            jax.ShapeDtypeStruct((tokens, 3 * hi), jnp.bfloat16),
            jax.ShapeDtypeStruct((blocks, 1, ht), f32),
            jax.ShapeDtypeStruct((HD, hi), f32),
        ] + [jax.ShapeDtypeStruct((HD, ht), f32)] * 3 + [shape_of(a.shape, a.dtype) for a in seq_arrays]
        + [window_shape(item) for item in items],
        scratch_shapes=[pltpu.VMEM((HD, hi), f32), pltpu.VMEM((HD, ht), f32)]
        + wire_sems(len(seq_arrays) * lax.axis_size("seq") + len(items) * lax.axis_size("dp"))
        + [room(a.shape[1:], a.dtype) for a in seq_arrays]
        + [room(window_shape(item).shape[1:], item[0].dtype) for item in items],
        compiler_params=pltpu.CompilerParams(
            vmem_limit_bytes=48 * 1024 * 1024, collective_id=cid, has_side_effects=True
        ),
        name="inner_backward",
    )(fresh, qkv, e_rows, dmix, *saved, gain, shift, *arrays)

MESH = pl.DeviceIdType.MESH


class Kept:
    def __init__(self, source, target, room, sem):
        self.bring = pltpu.make_async_copy(source, room, sem)
        self.leave = pltpu.make_async_copy(room, target, sem)

    def start(self):
        self.bring.start()
        self.bring.wait()
        self.leave.start()

    def wait(self):
        self.leave.wait()


class Wires:
    def __init__(self, send_sems, recv_sems, rooms=(), started=False):
        self.send_sems, self.recv_sems, self.used, self.started = send_sems, recv_sems, 0, started
        self.rooms = list(rooms)

    def begin(self, copy):
        if not self.started:
            copy.start()
        return copy

    def copy(self, source, target, device):
        at = self.number()
        return self.numbered(at, source, target, device)

    def number(self):
        self.used += 1
        return self.used - 1

    def numbered(self, at, source, target, device):
        return pltpu.make_async_remote_copy(
            src_ref=source,
            dst_ref=target,
            send_sem=self.send_sems.at[at],
            recv_sem=self.recv_sems.at[at],
            device_id=device,
            device_id_type=MESH,
        )

    def load(self, source, target):
        return pltpu.make_async_copy(source, target, self.send_sems.at[self.number()])

    def keep(self, source, target):
        return Kept(source, target, self.rooms.pop(0), self.send_sems.at[self.number()])


def on_line(step):
    return {"seq": lax.axis_index("seq") + step}


def sibling():
    me = lax.axis_index("seq")
    return {"seq": me + 1 - 2 * lax.rem(me, 2)}


def pack_peer(step):
    packs = lax.axis_size("dp")
    return {"dp": lax.rem(lax.axis_index("dp") + step, packs)}


def seq_peer(step):
    count = lax.axis_size("seq")
    return {"seq": lax.rem(lax.axis_index("seq") + step, count)}


def meet(groups):
    barrier = pltpu.get_barrier_semaphore()
    me, count = lax.axis_index("seq"), lax.axis_size("seq")

    def greet(device):
        pl.semaphore_signal(barrier, inc=1, device_id=device, device_id_type=MESH)

    peers = 0
    if "dp" in groups:
        for step in range(1, lax.axis_size("dp")):
            greet(pack_peer(step))
        peers += lax.axis_size("dp") - 1
    if "cross" in groups:
        for step in range(1, lax.axis_size("dp")):
            greet({**pack_peer(step), **sibling()})
        peers += lax.axis_size("dp") - 1
    if "seq" in groups:
        for step in range(1, count):
            greet(seq_peer(step))
        peers += count - 1
    elif "line" in groups:
        greet(sibling())

        @pl.when(me >= 2)
        def _():
            greet(on_line(-2))

        @pl.when(me < count - 2)
        def _():
            greet(on_line(2))

        peers += 1 + jnp.minimum(me // 2, 1) + jnp.minimum((count - 1 - me) // 2, 1)
    pl.semaphore_wait(barrier, peers)


def gather_line(wires, source, out, cut):
    me, count = lax.axis_index("seq"), lax.axis_size("seq")
    chips, chip = count // 2, me // 2
    step = source.shape[0] // cut
    other = me + 1 - 2 * lax.rem(me, 2)

    def piece(slot, part):
        return out.at[slot, pl.ds(part * step, step)]

    own = wires.keep(source, out.at[me])
    numbers = {(way, i, part): wires.number() for way in "rlRL" for i in range(chips) for part in range(cut)}

    def copy(way, i, part):
        slot = me - 2 * i if way in "rR" else me + 2 * i
        start = source.at[pl.ds(part * step, step)] if i == 0 else piece(slot, part)
        device = {"r": on_line(2), "l": on_line(-2), "R": sibling(), "L": sibling()}[way]
        return wires.numbered(numbers[way, i, part], start, piece(slot, part), device)

    def arrived(way, i, part):
        if way in "rl":
            slot = me - 2 * (i + 1) if way == "r" else me + 2 * (i + 1)
        else:
            slot = other - 2 * i if way == "R" else other + 2 * i
        there = piece(slot, part)
        wires.numbered(numbers[way, i, part], there, there, sibling()).wait_recv()

    @pl.when(chip < chips - 1)
    def _():
        for part in range(cut):
            copy("r", 0, part).start()

    @pl.when(chip > 0)
    def _():
        for part in range(cut):
            copy("l", 0, part).start()

    for part in range(cut):
        copy("R", 0, part).start()
    own.start()
    for i in range(1, chips):
        for part in range(cut):
            yield True

            @pl.when(chip >= i)
            def _():
                arrived("r", i - 1, part)

                @pl.when(chip < chips - 1)
                def _():
                    copy("r", i, part).start()

                copy("R", i, part).start()

            @pl.when(chip + i <= chips - 1)
            def _():
                arrived("l", i - 1, part)

                @pl.when(chip > 0)
                def _():
                    copy("l", i, part).start()

                copy("L", i, part).start()

    yield True
    own.wait()
    for i in range(chips):
        for part in range(cut):
            if i == 0:
                arrived("R", 0, part)
                copy("R", 0, part).wait_send()
            else:

                @pl.when(chip >= i)
                def _():
                    arrived("R", i, part)
                    copy("R", i, part).wait_send()

                @pl.when(chip + i <= chips - 1)
                def _():
                    arrived("L", i, part)
                    copy("L", i, part).wait_send()

            @pl.when((chip >= i) & (chip < chips - 1))
            def _():
                copy("r", i, part).wait_send()

            @pl.when((chip + i <= chips - 1) & (chip > 0))
            def _():
                copy("l", i, part).wait_send()


def add_into(out, parts, rows=16):
    def body(i, _):
        lines = pl.ds(pl.multiple_of(i * rows, rows), rows)
        total = parts[0][lines, :].astype(jnp.float32)
        for part in parts[1:]:
            total = total + part[lines, :].astype(jnp.float32)
        out[lines, :] = total.astype(out.dtype)
        return 0

    lax.fori_loop(0, out.shape[0] // rows, body, 0)


def scatter_line(wires, produce, source, out, near, from_left, from_right, outbox, cut):
    me, count = lax.axis_index("seq"), lax.axis_size("seq")
    chips, chip, core = count // 2, me // 2, lax.rem(me, 2)
    step = source.shape[1] // cut

    def lines(part):
        return pl.ds(part * step, step)

    order = []
    for i in range(chips // 2):
        order += [chips - 1 - i, i]
    order += [chips // 2] if chips % 2 else []
    across = {}
    for dest in order:
        for part in range(cut):
            across[dest, part] = wires.copy(
                source.at[2 * dest + 1 - core, lines(part)], near.at[dest, lines(part)], sibling()
            )

    def begin(dests):
        for dest in dests:
            produce(dest)
            for part in range(cut):
                across[dest, part].start()

    right, left = {}, {}
    for dest in range(chips):
        for part in range(cut):
            right[dest, part] = wires.copy(outbox.at[dest, lines(part)], from_left.at[dest, lines(part)], on_line(2))
            left[dest, part] = wires.copy(outbox.at[dest, lines(part)], from_right.at[dest, lines(part)], on_line(-2))
    def handle(part, ahead, turn, dest, table, inbox, first):
        terms = [source.at[2 * dest + core, lines(part)], near.at[dest, lines(part)]]

        @pl.when(ahead & turn)
        def _():
            across[dest, part].wait_recv()

            @pl.when(first)
            def _():
                add_into(outbox.at[dest, lines(part)], terms)

            @pl.when(jnp.logical_not(first))
            def _():
                table[dest, part].wait_recv()
                add_into(outbox.at[dest, lines(part)], terms + [inbox.at[dest, lines(part)]])

            table[dest, part].start()

    for i in range(chips - 1):
        begin(order[2 * i : 2 * i + 2])
        for part in range(cut):
            yield True
            rightward, leftward = (chips - 1 - i, right, from_left, chip == 0), (i, left, from_right, chip == chips - 1)
            handle(part, chip < chips - 1 - i, chip < chips // 2, *rightward)
            handle(part, chip > i, True, *leftward)
            handle(part, chip < chips - 1 - i, chip >= chips // 2, *rightward)

    for part in range(cut):
        yield True
        for dest in range(chips):

            @pl.when(chip == dest)
            def _():
                across[dest, part].wait_recv()
                terms = [source.at[2 * dest + core, lines(part)], near.at[dest, lines(part)]]
                if dest > 0:
                    right[dest, part].wait_recv()
                    terms = terms + [from_left.at[dest, lines(part)]]
                if dest < chips - 1:
                    left[dest, part].wait_recv()
                    terms = terms + [from_right.at[dest, lines(part)]]
                add_into(out.at[lines(part)], terms)

    for dest in range(chips):
        for part in range(cut):
            across[dest, part].wait_send()

            @pl.when(chip < dest)
            def _():
                right[dest, part].wait_send()

            @pl.when(chip > dest)
            def _():
                left[dest, part].wait_send()


def swap_seq(wires, source, out):
    me, count = lax.axis_index("seq"), lax.axis_size("seq")
    own = wires.keep(source.at[me], out.at[me])
    sent = []
    for step in range(1, count):
        peer = lax.rem(me + step, count)
        sent.append(wires.copy(source.at[peer], out.at[me], seq_peer(step)))
        wires.begin(sent[-1])
    wires.begin(own)
    yield True
    own.wait()
    for copy in sent:
        copy.wait()


def spread_seq(wires, source, out):
    me, count = lax.axis_index("seq"), lax.axis_size("seq")
    own = wires.keep(source, out.at[me])
    sent = []
    for step in range(1, count):
        sent.append(wires.copy(source, out.at[me], seq_peer(step)))
        wires.begin(sent[-1])
    wires.begin(own)
    yield True
    own.wait()
    for copy in sent:
        copy.wait()


def swap_dp(wires, source, out):
    me, count = lax.axis_index("dp"), lax.axis_size("dp")
    own = wires.keep(source.at[me], out.at[me])
    sent = []
    for step in range(1, count):
        sent.append(wires.copy(source.at[lax.rem(me + step, count)], out.at[me], pack_peer(step)))
        wires.begin(sent[-1])
    wires.begin(own)
    yield True
    own.wait()
    for copy in sent:
        copy.wait()


PIECES = 4
HALVES = 8 + 4 * PIECES


def halves_dp(wires, source, out, idle=1):
    me, count = lax.axis_index("dp"), lax.axis_size("dp")
    rows, width = source.shape
    by_rows = rows % (16 * PIECES) == 0
    step = (rows if by_rows else width) // PIECES
    own = wires.keep(source, out.at[me])
    bit = lax.rem(me, 2)
    flip = {1: me + 1 - 2 * bit, 2: lax.rem(me + 2, 4)}
    part = lambda ref, i: ref.at[pl.ds(i * step, step)] if by_rows else ref.at[:, pl.ds(i * step, step)]
    first, then = {}, {}

    def send(way, j):
        first[way, j] = wires.copy(part(source, j), part(out.at[me], j), {"dp": flip[way]})
        first[way, j].start()

    half = PIECES // 2
    for i in range(half):
        send(1, i)
        send(2, half + i)
    own.start()
    for _ in range(idle):
        yield True
    for i in range(half):
        for way, j in ((1, i), (2, half + i)):
            yield True
            first[way, j].wait_recv()
            came = part(out.at[flip[way]], j)
            then[way, j] = wires.copy(came, came, {"dp": flip[3 - way]})
            then[way, j].start()
            send(3 - way, j)
    yield PATIENT
    own.wait()
    for i in range(half):
        for way, j in ((2, i), (1, half + i)):
            first[way, j].wait_recv()
    for copy in first.values():
        copy.wait_send()
    for copy in then.values():
        copy.wait()


def spread_dp(wires, source, out):
    me, count = lax.axis_index("dp"), lax.axis_size("dp")
    own = wires.keep(source, out.at[me])
    sent = []
    for step in range(1, count):
        sent.append(wires.copy(source, out.at[me], pack_peer(step)))
        wires.begin(sent[-1])
    wires.begin(own)
    yield True
    own.wait()
    for copy in sent:
        copy.wait()


PATIENT = None


def run_all(jobs, patient=()):
    jobs, patient = list(jobs), list(patient)
    for job in patient:
        next(job)
    while jobs:
        for job in list(jobs):
            state = next(job, False)
            if state is not True:
                jobs.remove(job)
            if state is PATIENT:
                patient.append(job)
    for job in patient:
        for _ in job:
            pass


def beside(groups, send_sems, recv_sems, rooms, plan):
    @pl.when(pl.program_id(0) == 0)
    def _():
        meet(groups)
        for job in plan(Wires(send_sems, recv_sems, rooms)):
            next(job)

    @pl.when(pl.program_id(0) == pl.num_programs(0) - 1)
    def _():
        for job in plan(Wires(send_sems, recv_sems, rooms, started=True)):
            for _ in job:
                pass


def wire_sems(copies):
    return [pltpu.SemaphoreType.DMA((copies,)), pltpu.SemaphoreType.DMA((copies,))]


def room(shape, dtype):
    return pltpu.VMEM(tuple(shape), dtype)


def talk(name, cid, groups, operands, outs, plan, copies, in_vmem=(), out_vmem=(), scratch=(), rooms=()):
    n_in, n_out, n_rooms = len(operands), len(outs), len(rooms)

    def kernel(*refs):
        ins, results = refs[:n_in], refs[n_in : n_in + n_out]
        held = refs[n_in + n_out : n_in + n_out + n_rooms]
        buffers, (send_sems, recv_sems) = refs[n_in + n_out + n_rooms : -2], refs[-2:]
        meet(groups)
        wires = Wires(send_sems, recv_sems, held)
        run_all(*plan(wires, ins, results, buffers))
        assert wires.used <= copies, wires.used

    def where(i, chosen):
        return pl.BlockSpec(memory_space=pltpu.VMEM if i in chosen else pl.ANY)

    return pl.pallas_call(
        kernel,
        out_shape=outs,
        in_specs=[where(i, in_vmem) for i in range(n_in)],
        out_specs=[where(i, out_vmem) for i in range(n_out)],
        scratch_shapes=list(rooms) + list(scratch) + [pltpu.SemaphoreType.DMA((copies,)), pltpu.SemaphoreType.DMA((copies,))],
        compiler_params=pltpu.CompilerParams(
            collective_id=cid, has_side_effects=True, vmem_limit_bytes=60 * 1024 * 1024
        ),
        name=name,
    )(*operands)


def can_halve(array):
    rows, width = array.shape
    return lax.axis_size("dp") == 4 and (rows % (16 * PIECES) == 0 or width % (128 * PIECES) == 0)


def gather_jobs(wires, arrays, sources, results):
    jobs, patient = [], []
    for array, source, result in zip(arrays, sources, results):
        if can_halve(array):
            jobs.append(halves_dp(wires, source, result))
        else:
            patient.append(spread_dp(wires, source, result))
    return jobs, patient


def window(ref, item):
    _, rows, columns = item
    if rows is None and columns is None:
        return ref
    lines = slice(None) if rows is None else pl.ds(rows[0], rows[1] - rows[0])
    lanes = slice(None) if columns is None else pl.ds(columns[0], columns[1] - columns[0])
    return ref.at[:, lines, lanes]


def window_shape(item):
    array, rows, columns = item
    shape = list(array.shape)
    if rows is not None:
        shape[1] = rows[1] - rows[0]
    if columns is not None:
        shape[2] = columns[1] - columns[0]
    return shape_of(shape, array.dtype)


def gather_with(name, cid, block, beside, cut=2):
    count = lax.axis_size("seq")
    outs = [shape_of((count,) + block.shape, block.dtype)] + beside.outs

    def plan(wires, ins, results, scratch):
        jobs, patient = beside.jobs(wires, ins[1:], results[1:], scratch)
        return [gather_line(wires, ins[0], results[0], cut)] + jobs, patient

    got = talk(
        name, cid, ("line", "dp") if beside.arrays else ("line",), (block, *beside.arrays), outs, plan,
        1 + 4 * (count // 2) * cut + beside.copies, out_vmem=[1 + i for i in beside.in_vmem_outs], scratch=beside.scratch,
        rooms=beside.patient_rooms + [room(block.shape, block.dtype)] + beside.job_rooms,
    )
    return [got[0].reshape((-1,) + block.shape[1:])] + beside.finish(got[1:])


def columns_out(wires, source, out):
    mine, me, count, packs = lax.axis_index("dp"), lax.axis_index("seq"), lax.axis_size("seq"), lax.axis_size("dp")
    own = wires.keep(source.at[me], out.at[mine, me])
    square = packs == 4
    bit = lax.rem(mine, 2)
    flip = {1: mine + 1 - 2 * bit, 2: lax.rem(mine + 2, 4)}
    sent, onward, turned_on = [], {}, []
    for step in range(1, count):
        sent.append(wires.copy(source.at[lax.rem(me + step, count)], out.at[mine, me], seq_peer(step)))
        sent[-1].start()

    def pass_on(k):
        slot = lax.rem(me + count - k, count)
        came = source.at[me] if k == 0 else out.at[mine, slot]
        for way in (1, 2) if square else range(1, packs):
            device = {"dp": flip[way]} if square else pack_peer(way)
            onward[k, way] = wires.copy(came, out.at[mine, slot], device)
            onward[k, way].start()

    def turn(k):
        way = 1 + k % 2
        onward[k, way].wait_recv()
        came = out.at[flip[way], lax.rem(me + count - k, count)]
        turned_on.append(wires.copy(came, came, {"dp": flip[3 - way]}))
        turned_on[-1].start()

    pass_on(0)
    own.start()
    for k in range(1, count):
        yield True
        sent[k - 1].wait_recv()
        pass_on(k)
        if square:
            turn(k - 1)
    yield True
    if square:
        turn(count - 1)
    yield PATIENT
    own.wait()
    for copy in sent:
        copy.wait_send()
    for (k, way), copy in onward.items():
        copy.wait_send()
        if not square or way != 1 + k % 2:
            copy.wait_recv()
    for copy in turned_on:
        copy.wait()


def near_pieces(wires, source, out):
    mine, me, packs = lax.axis_index("dp"), lax.axis_index("seq"), lax.axis_size("dp")
    other = sibling()["seq"]
    sent = []
    for step in range(1, packs):
        peer = pack_peer(step)
        sent.append(wires.begin(wires.copy(source.at[me], out.at[mine, me], peer)))
        sent.append(wires.begin(wires.copy(source.at[other], out.at[mine, me], {**peer, **sibling()})))
    yield True
    for copy in sent:
        copy.wait()


def far_pieces(wires, source, out, idle=1):
    mine, me, count, packs = lax.axis_index("dp"), lax.axis_index("seq"), lax.axis_size("seq"), lax.axis_size("dp")
    bit = lax.rem(mine, 2)
    flip = {1: mine + 1 - 2 * bit, 2: lax.rem(mine + 2, 4)}
    sent, turned = {}, []

    def slot(j):
        return lax.rem(me // 2 * 2 + 2 + j, count)

    def send(j, way, device):
        sent[j, way] = wires.copy(source.at[slot(j)], out.at[mine, slot(j)], device)
        sent[j, way].start()

    if packs != 4:
        for j in range(count - 2):
            for step in range(1, packs):
                send(j, step, pack_peer(step))
        yield PATIENT
        for copy in sent.values():
            copy.wait()
        return
    for j in range(count - 2):
        send(j, 1 + j % 2, {"dp": flip[1 + j % 2]})
    for _ in range(idle):
        yield True
    for j in range(count - 2):
        way = 1 + j % 2
        if j % 2 == 0:
            yield True
        sent[j, way].wait_recv()
        came = out.at[flip[way], slot(j)]
        turned.append(wires.copy(came, came, {"dp": flip[3 - way]}))
        turned[-1].start()
        send(j, 3 - way, {"dp": flip[3 - way]})
    yield PATIENT
    for (j, way), copy in sent.items():
        copy.wait_send()
        if way != 1 + j % 2:
            copy.wait_recv()
    for copy in turned:
        copy.wait()


def spread_all(wires, source, out):
    mine, me, count, packs = lax.axis_index("dp"), lax.axis_index("seq"), lax.axis_size("seq"), lax.axis_size("dp")
    own = wires.keep(source, out.at[mine, me])
    sent, onward = [], []
    for step in range(1, packs):
        sent.append(wires.copy(source, out.at[mine, me], pack_peer(step)))
        sent[-1].start()
    for step in range(1, count):
        onward.append(wires.copy(source, out.at[mine, me], seq_peer(step)))
        onward[-1].start()
    own.start()
    for other in range(1, packs):
        yield True
        sent[other - 1].wait_recv()
        came = out.at[lax.rem(mine + packs - other, packs), me]
        for step in range(1, count):
            onward.append(wires.copy(came, came, seq_peer(step)))
            onward[-1].start()
    yield True
    own.wait()
    for copy in sent:
        copy.wait_send()
    for copy in onward:
        copy.wait()


def shape_of(shape, dtype):
    return jax.ShapeDtypeStruct(tuple(shape), dtype)


def first_exchange(mix, block, over_dp):
    packs, count = lax.axis_size("dp"), lax.axis_size("seq")
    outs = [shape_of((packs,) + mix.shape, mix.dtype), shape_of((count,) + block.shape, block.dtype)]
    outs += [shape_of((packs,) + a.shape, a.dtype) for a in over_dp]
    cut = 2

    def plan(wires, ins, results, _):
        return [
            columns_out(wires, ins[0], results[0]),
            gather_line(wires, ins[1], results[1], cut),
        ], [spread_dp(wires, a, b) for a, b in zip(ins[2:], results[2:])]

    copies = count * packs + count + 4 * (count // 2) * cut + packs * len(over_dp) + 8
    rooms = [room(a.shape, a.dtype) for a in over_dp] + [room(mix.shape[1:], mix.dtype), room(block.shape, block.dtype)]
    got = talk("first_exchange", 1, ("dp", "seq"), (mix, block, *over_dp), outs, plan, copies, rooms=rooms)
    return [array.reshape(-1, array.shape[-1]) for array in got]


def gather_seq(name, cid, block):
    count = lax.axis_size("seq")
    (got,) = talk(
        name, cid, ("seq",), (block,), [shape_of((count,) + block.shape, block.dtype)],
        lambda wires, ins, outs, _: ([spread_seq(wires, ins[0], outs[0])],), count,
        rooms=[room(block.shape, block.dtype)],
    )
    return got


def fold_dp(wires, source, out, boxes, here, sums, idle=2):
    me = lax.axis_index("dp")
    half = source.shape[1] // 2
    bit = lax.rem(me, 2)
    flip = {1: me + 1 - 2 * bit, 2: lax.rem(me + 2, 4)}
    corner = lax.rem(flip[1] + 2, 4)
    rows = {1: pl.ds(0, half), 2: pl.ds(half, half)}
    load = [wires.load(source.at[me], here.at[0])]
    passing, direct, second = {}, {}, {}
    for way in (1, 2):
        passing[way] = wires.copy(source.at[corner, rows[way]], boxes.at[1 + way], {"dp": flip[way]})
        passing[way].start()
        load.append(wires.load(source.at[flip[3 - way], rows[way]], here.at[1, rows[way]]))
    for copy in load:
        copy.start()
    for _ in range(idle):
        yield True
    for way in (1, 2):
        yield True
        load[way].wait()
        passing[way].wait_recv()
        add_into(sums.at[way - 1], [here.at[1, rows[way]], boxes.at[1 + way]])
        second[way] = wires.copy(sums.at[way - 1], boxes.at[3 + way], {"dp": flip[3 - way]})
        second[way].start()
        direct[way] = wires.copy(source.at[flip[way], rows[way]], boxes.at[way - 1], {"dp": flip[way]})
        direct[way].start()
    load[0].wait()
    yield PATIENT
    for way in (1, 2):
        direct[way].wait_recv()
        second[way].wait_recv()
        add_into(out.at[rows[way]], [here.at[0, rows[way]], boxes.at[way - 1], boxes.at[3 + way]])
    for way in (1, 2):
        passing[way].wait_send()
        direct[way].wait_send()
        second[way].wait_send()


def can_fold(array):
    return lax.axis_size("dp") == 4 and array.shape[1] % 32 == 0


def fold_scratch(array):
    _, rows, columns = array.shape
    return [
        pltpu.VMEM((6, rows // 2, columns), array.dtype),
        pltpu.VMEM((2, rows, columns), array.dtype),
        pltpu.VMEM((2, rows // 2, columns), array.dtype),
    ]


class Beside:
    def __init__(self, gathers=(), swaps=(), sums=(), pieces=()):
        self.gathers, self.swaps, self.sums, self.pieces = list(gathers), list(swaps), list(sums), list(pieces)
        self.arrays = self.gathers + self.swaps + self.sums + self.pieces
        packs = lax.axis_size("dp")
        self.outs = [shape_of((packs,) + a.shape, a.dtype) for a in self.gathers]
        self.outs += [shape_of(a.shape, a.dtype) for a in self.swaps]
        self.scratch = []
        for a in self.sums:
            fold = can_fold(a)
            self.outs.append(shape_of(a.shape[1:] if fold else a.shape, a.dtype))
            self.scratch += fold_scratch(a) if fold else []
        self.outs += [shape_of((packs,) + a.shape, a.dtype) for a in self.pieces]
        self.copies = len(self.pieces) * packs * lax.axis_size("seq") + HALVES * len(self.gathers) + packs * len(self.swaps) + 16 * len(self.sums)
        self.job_rooms = [room(a.shape, a.dtype) for a in self.gathers if can_halve(a)]
        self.patient_rooms = [room(a.shape, a.dtype) for a in self.gathers if not can_halve(a)]
        self.patient_rooms += [room(a.shape[1:], a.dtype) for a in self.swaps]
        self.patient_rooms += [room(a.shape[1:], a.dtype) for a in self.sums if not can_fold(a)]
        self.in_vmem_outs = [len(self.gathers) + len(self.swaps) + i for i, a in enumerate(self.sums) if can_fold(a)]

    def jobs(self, wires, ins, results, scratch):
        g, s = len(self.gathers), len(self.gathers) + len(self.swaps)
        jobs, patient = gather_jobs(wires, self.gathers, ins[:g], results[:g])
        patient += [swap_dp(wires, a, b) for a, b in zip(ins[g:s], results[g:s])]
        scratch = list(scratch)
        for array, a, b in zip(self.sums, ins[s:], results[s:]):
            if can_fold(array):
                jobs.append(fold_dp(wires, a, b, *scratch[:3]))
                scratch = scratch[3:]
            else:
                patient.append(swap_dp(wires, a, b))
        p = s + len(self.sums)
        jobs += [far_pieces(wires, a, b) for a, b in zip(ins[p:], results[p:])]
        return jobs, patient

    def finish(self, got):
        g, s = len(self.gathers), len(self.gathers) + len(self.swaps)
        got = list(got)
        done = [r.reshape((-1,) + a.shape[1:]) for r, a in zip(got[:g], self.gathers)] + got[g:s]
        done += [r if can_fold(a) else add_packs(r).astype(r.dtype) for r, a in zip(got[s:], self.sums)]
        return done + got[s + len(self.sums) :]


def scatter_with(name, cid, out_shape, factors, product, beside, cut=2):
    count = lax.axis_size("seq")
    rows, width = out_shape
    box = pltpu.VMEM((count // 2, rows, width), jnp.bfloat16)
    made = [pltpu.VMEM((count, rows, width), jnp.bfloat16)] if product else []
    if not product:
        factors = (factors[0].reshape(count, rows, width),)
    n_f, n_b = len(factors), len(beside.arrays)
    outs = [shape_of((rows, width), jnp.float32)] + beside.outs

    def plan(wires, ins, results, scratch):
        terms = scratch[0] if product else ins[0]
        boxes, rest = scratch[len(made) : len(made) + 4], scratch[len(made) + 4 :]
        jobs, patient = beside.jobs(wires, ins[n_f:], results[1:], rest)

        def produce(dest):
            if product:
                product(dest, ins[:n_f], terms)

        return jobs + [scatter_line(wires, produce, terms, results[0], *boxes, cut)], patient

    got = talk(
        name, cid, ("line", "dp") if n_b else ("line",), (*factors, *beside.arrays), outs, plan,
        3 * (count // 2) * cut + beside.copies,
        in_vmem=range(n_f), out_vmem=[0] + [1 + i for i in beside.in_vmem_outs], scratch=made + [box] * 4 + beside.scratch,
        rooms=beside.patient_rooms + beside.job_rooms,
    )
    return [got[0]] + beside.finish(got[1:])


def swap_places(name, cid, arrays):
    count = lax.axis_size("seq")
    return talk(
        name, cid, ("seq",), arrays, [shape_of(a.shape, a.dtype) for a in arrays],
        lambda wires, ins, outs, _: ([], [swap_seq(wires, i, o) for i, o in zip(ins, outs)]), count * len(arrays),
        rooms=[room(a.shape[1:], a.dtype) for a in arrays],
    )


def split_columns(arrays, pieces):
    rows = arrays[0].shape[0]
    width = sum(p[2] for p in pieces[0])
    tall = min(rows, 16)

    def kernel(*refs):
        for place, cuts in enumerate(pieces):
            refs[-1][place] = jnp.concatenate(
                [jnp.zeros((tall, n), refs[-1].dtype) if a is None else refs[a][:, at : at + n] for a, at, n in cuts], axis=1
            )

    return pl.pallas_call(
        kernel,
        grid=(rows // tall,),
        in_specs=[pl.BlockSpec((tall, a.shape[1]), lambda i: (i, 0)) for a in arrays],
        out_specs=pl.BlockSpec((len(pieces), tall, width), lambda i: (0, i, 0)),
        out_shape=shape_of((len(pieces), rows, width), arrays[0].dtype),
        compiler_params=pltpu.CompilerParams(vmem_limit_bytes=48 * 1024 * 1024),
        name="split_columns",
    )(*arrays)


def join_columns(array, widths, pieces):
    places, rows, width = array.shape
    tall = min(rows, 16)

    def kernel(source, *outs):
        whole = [source[place].astype(jnp.float32) for place in range(places)]
        for which, out in enumerate(outs):
            found = []
            for place, cuts in enumerate(pieces):
                start = 0
                for a, at, n in cuts:
                    if a == which:
                        found.append((at, whole[place][:, start : start + n]))
                    start += n
            out[...] = jnp.concatenate([part for _, part in sorted(found, key=lambda f: f[0])], axis=1)

    return pl.pallas_call(
        kernel,
        grid=(rows // tall,),
        in_specs=[pl.BlockSpec((places, tall, width), lambda i: (0, i, 0))],
        out_specs=[pl.BlockSpec((tall, w), lambda i: (i, 0)) for w in widths],
        out_shape=[shape_of((rows, w), jnp.float32) for w in widths],
        compiler_params=pltpu.CompilerParams(vmem_limit_bytes=48 * 1024 * 1024),
        name="join_columns",
    )(array)


def add_packs(array):
    return jnp.sum(array.astype(jnp.float32), axis=0)


def unit_groups(units):
    return [(at, min(128, units - at)) for at in range(0, units, 128)]


def feed_forward_kernel(
    cut, block_ref, top_first, top_second, own_cols, near_cols, far_cols, wd_first, wd_second,
    down_out, g_gu_out, g_down_out, mid_out,
    wgu_ref, wd_ref, x_out, tops, hidbuf, dgubuf, downbuf, g_gu, g_down, g_gu_low, g_down_low,
    terms, near, from_left, from_right, outbox,
    local_sems, pack_send, pack_recv, line_send, line_recv, near_send, near_recv, sum_send, sum_recv, across_send, across_recv,
):
    me, count = lax.axis_index("seq"), lax.axis_size("seq")
    chips, chip, core = count // 2, me // 2, lax.rem(me, 2)
    other = me + 1 - 2 * core
    tall = block_ref.shape[0]
    step = tall // cut
    units = wd_ref.shape[0]
    packs = lax.axis_size("dp")
    pack = lax.axis_index("dp")
    share = units // packs
    width = wd_ref.shape[1]
    meet(("line", "dp"))

    def lines(part):
        return pl.ds(part * step, step)

    def along(sign, i, part, source=None):
        at = ((1 - sign) // 2 * chips + i) * cut + part
        slot = x_out.at[me + 2 * sign * i, lines(part)]
        return pltpu.make_async_remote_copy(
            slot if source is None else source.at[lines(part)], slot,
            line_send.at[at], line_recv.at[at], on_line(-2 * sign), MESH,
        )

    def over(sign, i, part, source=None):
        at = ((1 - sign) // 2 * chips + i) * cut + part
        slot = x_out.at[me + 2 * sign * i, lines(part)]
        return pltpu.make_async_remote_copy(
            slot if source is None else source.at[lines(part)], slot,
            near_send.at[at], near_recv.at[at], sibling(), MESH,
        )

    def along_came(sign, i, part):
        at = ((1 - sign) // 2 * chips + i - 1) * cut + part
        slot = x_out.at[me + 2 * sign * i, lines(part)]
        pltpu.make_async_remote_copy(slot, slot, line_send.at[at], line_recv.at[at], sibling(), MESH).wait_recv()

    def over_came(sign, i, part):
        at = ((1 - sign) // 2 * chips + i) * cut + part
        slot = x_out.at[other + 2 * sign * i, lines(part)]
        pltpu.make_async_remote_copy(slot, slot, near_send.at[at], near_recv.at[at], sibling(), MESH).wait_recv()

    def more(sign):
        return jnp.where(sign > 0, chip > 0, chip < chips - 1)

    def across(dest, part):
        at = dest * cut + part
        return pltpu.make_async_remote_copy(
            terms.at[2 * dest + 1 - core, lines(part)], near.at[dest, lines(part)],
            across_send.at[at], across_recv.at[at], sibling(), MESH,
        )

    def onward(right, dest, part):
        at = ((0 if right else chips) + dest) * cut + part
        inbox = from_left if right else from_right
        return pltpu.make_async_remote_copy(
            outbox.at[dest, lines(part)], inbox.at[dest, lines(part)],
            sum_send.at[at], sum_recv.at[at], on_line(2 if right else -2), MESH,
        )

    own = pltpu.make_async_copy(block_ref, x_out.at[me], local_sems.at[0])
    for part in range(cut):
        for sign in (1, -1):

            @pl.when(more(sign))
            def _():
                along(sign, 0, part, block_ref).start()

        over(1, 0, part, block_ref).start()
    half = tall // 2
    weights = [
        pltpu.make_async_copy(top_first, tops.at[:, pl.ds(0, half)], local_sems.at[3]),
        pltpu.make_async_copy(top_second, tops.at[:, pl.ds(half, half)], local_sems.at[4]),
        pltpu.make_async_copy(wd_first, wd_ref.at[:, pl.ds(0, width // 2)], local_sems.at[2]),
        pltpu.make_async_copy(wd_second, wd_ref.at[:, pl.ds(width // 2, width // 2)], local_sems.at[5]),
    ]
    own.start()
    for copy in weights:
        copy.start()
    deep = own_cols.shape[1]

    def fetch(at, _):
        from_pack, place = at // count, lax.rem(at, count)
        there = wgu_ref.at[pl.ds(pl.multiple_of(at * deep, deep), deep)]

        @pl.when(from_pack == pack)
        def _():
            pltpu.make_async_copy(own_cols.at[place], there, local_sems.at[1]).start()

        @pl.when((from_pack != pack) & (place // 2 == chip))
        def _():
            pltpu.make_async_copy(near_cols.at[from_pack, place], there, local_sems.at[1]).start()

        @pl.when((from_pack != pack) & (place // 2 != chip))
        def _():
            pltpu.make_async_copy(far_cols.at[from_pack, place], there, local_sems.at[1]).start()

        return 0

    lax.fori_loop(0, packs * count, fetch, 0)
    own.wait()
    pltpu.make_async_copy(wgu_ref, wgu_ref, local_sems.at[1]).wait()
    for copy in weights:
        copy.wait()

    def compute(dest):
        x = x_out[pl.ds(2 * dest, 2)].reshape(2 * tall, width)
        top = tops[pl.ds(2 * dest, 2)].reshape(2 * tall, width)
        for at, n in unit_groups(units):
            both = nn(x, wgu_ref[:, 2 * at : 2 * at + 2 * n])
            gate, up = both[:, :n], both[:, n:]
            d_hidden = nt(top, wd_ref[at : at + n, :])
            sig = 1.0 / (1.0 + jnp.exp(-gate))
            silu = gate * sig
            hidbuf[:, :, at : at + n] = (silu * up).astype(jnp.bfloat16).reshape(2, tall, n)
            d_gate = d_hidden * up * sig * (1.0 + gate * (1.0 - sig))
            d_both = jnp.concatenate([d_gate, d_hidden * silu], axis=1)
            dgubuf[:, :, 2 * at : 2 * at + 2 * n] = d_both.astype(jnp.bfloat16).reshape(2, tall, 2 * n)
        hid = hidbuf[...].reshape(2 * tall, units)
        dgu = dgubuf[...].reshape(2 * tall, 2 * units)
        wide = 512
        for at in range(0, width, wide):
            mid = nt(dgu, wgu_ref[at : at + wide, :]).astype(jnp.bfloat16)
            terms[pl.ds(2 * dest, 2), :, at : at + wide] = mid.reshape(2, tall, wide)
        for part in range(cut):
            across(dest, part).start()

    def compute_rest(dest):
        x = x_out[pl.ds(2 * dest, 2)].reshape(2 * tall, width)
        top = tops[pl.ds(2 * dest, 2)].reshape(2 * tall, width)
        hid = hidbuf[...].reshape(2 * tall, units)
        dgu = dgubuf[...].reshape(2 * tall, 2 * units)
        wide = 512
        for at in range(0, width, wide):
            downbuf[:, :, at : at + wide] = nn(hid, wd_ref[:, at : at + wide]).astype(jnp.bfloat16).reshape(2, tall, wide)
        for at in range(0, units, 128):
            n = min(128, units - at)
            g_down[at : at + n, :] += tn(hid[:, at : at + n], top)
        for at in range(0, width, 256):
            g_gu[at : at + 256, :] += tn(x[:, at : at + 256], dgu)

    def send_sum(right, dest, part, first, in_turn=True):
        mine = [terms.at[2 * dest + core, lines(part)], near.at[dest, lines(part)]]
        across_came(dest, part)
        if first:
            add_into(outbox.at[dest, lines(part)], mine)
        else:
            inbox = from_left if right else from_right
            sum_came(right, dest, part)
            add_into(outbox.at[dest, lines(part)], mine + [inbox.at[dest, lines(part)]])
        if in_turn and part > 0:
            onward(right, dest, part - 1).wait_send()
        onward(right, dest, part).start()

    def across_came(dest, part):
        at = dest * cut + part
        there = near.at[dest, lines(part)]
        pltpu.make_async_remote_copy(there, there, across_send.at[at], across_recv.at[at], sibling(), MESH).wait_recv()

    def sum_came(right, dest, part):
        at = ((0 if right else chips) + dest) * cut + part
        there = (from_left if right else from_right).at[dest, lines(part)]
        pltpu.make_async_remote_copy(there, there, sum_send.at[at], sum_recv.at[at], sibling(), MESH).wait_recv()

    def saved(dest):
        return pltpu.make_async_copy(downbuf, down_out.at[pl.ds(2 * dest, 2)], local_sems.at[2])

    def inside(dest):
        return (dest >= 0) & (dest < chips)

    def visit(i, j):
        sign = 1 - 2 * j
        dest = chip + sign * i

        @pl.when(inside(dest) & (i + 1 - j > 0))
        def _():
            for part in range(cut):
                over_came(sign, i, part)
            compute(dest)
            @pl.when((chip == 0) & (dest > 0) & (dest < chips - 1))
            def _():
                for part in range(cut):
                    send_sum(True, dest, part, True, False)

            @pl.when((chip == chips - 1) & (dest < chips - 1) & (dest > 0))
            def _():
                for part in range(cut):
                    send_sum(False, dest, part, True, False)

            @pl.when(i + j > 0)
            def _():
                saved(dest).wait()

            compute_rest(dest)
            saved(dest).start()

    def forward(i):
        for sign in (1, -1):

            @pl.when((i > 0) & (i < chips) & inside(chip + sign * i))
            def _():
                for part in range(cut):
                    along_came(sign, i, part)

                    @pl.when(more(sign))
                    def _():
                        along(sign, i, part).start()

                    over(sign, i, part).start()

    def distance(i, _):
        def side(j, _):
            visit(i, j)

            @pl.when((j == 0) & (i > 0) | (j == 1) & (i == 0))
            def _():
                forward(i + 1)

            return 0

        lax.fori_loop(0, 2, side, 0)
        return 0

    g_gu[...] = jnp.zeros_like(g_gu)
    g_down[...] = jnp.zeros_like(g_down)
    lax.fori_loop(0, chips, distance, 0)
    saved(chip).wait()

    def lower(i, _):
        lines = pl.ds(pl.multiple_of(i * 16, 16), 16)
        g_down_low[lines, :] = g_down[lines, :].astype(jnp.bfloat16)
        return 0

    lax.fori_loop(0, units // 16, lower, 0)
    kept = pltpu.make_async_copy(g_down_low.at[pl.ds(pack * share, share)], g_down_out.at[pack], local_sems.at[2])
    kept.start()

    def swap(step):
        peer = lax.rem(pack + step, packs)
        return pltpu.make_async_remote_copy(
            g_down_low.at[pl.ds(peer * share, share)], g_down_out.at[pack],
            pack_send.at[step], pack_recv.at[step], pack_peer(step), MESH,
        )

    for turn in range(1, packs):
        swap(turn).start()

    @pl.when(chip == 0)
    def _():
        for part in range(cut):
            send_sum(True, chips - 1, part, True)

    @pl.when(chip == chips - 1)
    def _():
        for part in range(cut):
            send_sum(False, 0, part, True)

    def rightward():
        for i in range(1, chips - 1):

            @pl.when((chip > 0) & (chip + i < chips))
            def _():
                for part in range(cut):
                    send_sum(True, chip + i, part, False)

    def leftward():
        for i in range(1, chips - 1):

            @pl.when((chip < chips - 1) & (chip - i >= 0))
            def _():
                for part in range(cut):
                    send_sum(False, chip - i, part, False)

    @pl.when(chip < chips // 2)
    def _():
        rightward()
        leftward()

    @pl.when(chip >= chips // 2)
    def _():
        leftward()
        rightward()

    for part in range(cut):
        across_came(chip, part)
        mine = [terms.at[2 * chip + core, lines(part)], near.at[chip, lines(part)]]
        left_in, right_in = from_left.at[chip, lines(part)], from_right.at[chip, lines(part)]

        @pl.when(chip == 0)
        def _():
            sum_came(False, chip, part)
            add_into(mid_out.at[lines(part)], mine + [right_in])

        @pl.when(chip == chips - 1)
        def _():
            sum_came(True, chip, part)
            add_into(mid_out.at[lines(part)], mine + [left_in])

        @pl.when((chip > 0) & (chip < chips - 1))
        def _():
            sum_came(True, chip, part)
            sum_came(False, chip, part)
            add_into(mid_out.at[lines(part)], mine + [left_in, right_in])

    chunk = g_gu_low.shape[1]

    def gu_copy(at):
        slot = lax.rem(at, 2)
        return pltpu.make_async_copy(
            g_gu_low.at[slot], g_gu_out.at[pl.ds(at * chunk, chunk)], local_sems.at[3 + slot]
        )

    def lower_gu(at, _):
        @pl.when(at > 1)
        def _():
            gu_copy(at - 2).wait()

        slot = lax.rem(at, 2)

        def some(i, _):
            there = pl.ds(pl.multiple_of(i * 16, 16), 16)
            came = pl.ds(pl.multiple_of(at * chunk + i * 16, 16), 16)
            g_gu_low[slot, there, :] = g_gu[came, :].astype(jnp.bfloat16)
            return 0

        lax.fori_loop(0, chunk // 16, some, 0)
        gu_copy(at).start()
        return 0

    chunks = width // chunk
    lax.fori_loop(0, chunks, lower_gu, 0)
    for at in range(max(chunks - 2, 0), chunks):
        gu_copy(at).wait()
    for turn in range(1, packs):
        swap(turn).wait()
    kept.wait()
    for part in range(cut):
        for dest in range(chips):
            across(dest, part).wait_send()

            early_right = (chip == 0) & (dest < chips - 1) | (part == cut - 1)
            early_left = (chip == chips - 1) & (dest > 0) | (part == cut - 1)

            @pl.when((chip < dest) & early_right)
            def _():
                onward(True, dest, part).wait_send()

            @pl.when((chip > dest) & early_left)
            def _():
                onward(False, dest, part).wait_send()

        for i in range(chips):
            for sign in (1, -1):
                there = (chip + sign * i >= 0) & (chip + sign * i < chips)

                @pl.when(there & more(sign))
                def _():
                    along(sign, i, part).wait_send()

                if i > 0 or sign > 0:

                    @pl.when(there)
                    def _():
                        over(sign, i, part).wait_send()


def feed_forward(cid, block, tops, columns, downs, cut=2):
    count = lax.axis_size("seq")
    chips = count // 2
    tall, width = block.shape
    units = downs[0].shape[0]
    packs = lax.axis_size("dp")
    bf16 = jnp.bfloat16
    outs = [
        shape_of((count, tall, width), bf16),
        shape_of((width, 2 * units), bf16),
        shape_of((packs, units // packs, width), bf16),
        shape_of((tall, width), jnp.float32),
    ]
    box = pltpu.VMEM((chips, tall, width), bf16)
    dma = lambda n: pltpu.SemaphoreType.DMA((n,))
    anywhere, vmem = pl.BlockSpec(memory_space=pl.ANY), pl.BlockSpec(memory_space=pltpu.VMEM)
    flops = 2 * 2 * count * tall * width * 3 * units
    got = pl.pallas_call(
        functools.partial(feed_forward_kernel, cut),
        out_shape=outs,
        in_specs=[anywhere] * 8,
        out_specs=[anywhere] * 3 + [vmem],
        scratch_shapes=[
            pltpu.VMEM((width, 2 * units), bf16),
            pltpu.VMEM((units, width), bf16),
            pltpu.VMEM((count, tall, width), bf16),
            pltpu.VMEM((count, tall, width), bf16),
            pltpu.VMEM((2, tall, units), bf16),
            pltpu.VMEM((2, tall, 2 * units), bf16),
            pltpu.VMEM((2, tall, width), bf16),
            pltpu.VMEM((width, 2 * units), jnp.float32),
            pltpu.VMEM((units, width), jnp.float32),
            pltpu.VMEM((2, 256, 2 * units), bf16),
            pltpu.VMEM((units, width), bf16),
            pltpu.VMEM((count, tall, width), bf16),
            box, box, box, box,
            dma(6), dma(packs), dma(packs),
        ] + [dma(2 * chips * cut)] * 6 + [dma(chips * cut)] * 2,
        compiler_params=pltpu.CompilerParams(
            collective_id=cid, has_side_effects=True, vmem_limit_bytes=62 * 1024 * 1024
        ),
        cost_estimate=pl.CostEstimate(flops=flops, bytes_accessed=20 << 20, transcendentals=0),
        name="feed_forward",
    )(block, *tops, *columns, *downs)
    return got


def cross_rows(left_side, right_side):
    return lax.dot_general(left_side, right_side, (((0,), (0,)), ((), ())), preferred_element_type=jnp.float32)


def cross_cols(left_side, right_side):
    return lax.dot_general(left_side, right_side, (((1,), (1,)), ((), ())), preferred_element_type=jnp.float32)


def dot(left_side, right_side):
    return jnp.dot(left_side, right_side, preferred_element_type=jnp.float32)


def on_device(
    tokens,
    segments,
    norm_one,
    w_qkv,
    w_lr,
    lr_bias,
    w_gate,
    w_out,
    w_init,
    b_init,
    tnorm_w,
    tnorm_b,
    post_w,
    post_b,
    norm_two,
    w_gate_up,
    w_down,
    grad_out,
):
    floats = jnp.float32
    bf16 = jnp.bfloat16
    both = ("dp", "seq")
    packs, per_seq = lax.axis_size("dp"), lax.axis_size("seq")
    devices = packs * per_seq
    place = lax.axis_index("seq")
    span, width = tokens.shape[1], tokens.shape[2]
    rows = norm_one.shape[0]
    heads_all = lr_bias.shape[0]
    units = w_down.shape[0]
    length = span * per_seq
    blocks = length // MB
    heads = heads_all // per_seq
    aligned = rows % HD == 0
    outer = packs if aligned else 1
    inner = width // (outer * per_seq)
    mine = outer * inner

    def own_rows(array):
        cut = array.reshape((outer, per_seq, inner) + array.shape[1:])
        cut = lax.dynamic_index_in_dim(cut, place, 1, keepdims=False)
        return cut.reshape((mine,) + array.shape[1:])

    def put_rows(array):
        full = jnp.zeros((outer, per_seq, inner) + array.shape[1:], array.dtype)
        part = array.reshape((outer, 1, inner) + array.shape[1:])
        at = (0, place) + (0,) * (part.ndim - 2)
        return lax.dynamic_update_slice(full, part, at).reshape((width,) + array.shape[1:])

    extra = 128
    feature_cuts = [
        [(0, (part * outer + o) * per_seq * inner + s * inner, inner) for part in range(3) for o in range(outer)]
        + [(1, o * per_seq * inner + s * inner, inner) for o in range(outer)]
        for s in range(per_seq)
    ]
    filled = -(-units // 16) * 16
    unit_cuts = []
    for s in range(per_seq):
        cuts = []
        for at, n in unit_groups(packs * filled):
            for part in range(2):
                u = at
                while u < at + n:
                    pack, i = divmod(u, filled)
                    run = min((units if i < units else filled) - i, at + n - u)
                    first = (part * packs * per_seq + pack * per_seq + s) * units + i
                    cuts.append((0, first, run) if i < units else (None, 0, run))
                    u += run
        unit_cuts.append(cuts)

    spans = span // MB
    lr_places = w_lr.reshape(rows, outer, per_seq, heads // outer).transpose(0, 2, 1, 3).reshape(rows, per_seq, heads)
    tags = segments[0].reshape(1, 1, spans, MB)[:, :, :, 0].astype(bf16)
    beside_cols = jnp.concatenate(
        [
            lr_places,
            jnp.broadcast_to(jnp.stack([norm_one, norm_two], axis=1)[:, None], (rows, per_seq, 2)),
            jnp.broadcast_to(tags, (rows, per_seq, spans)),
            jnp.zeros((rows, per_seq, extra - heads - 2 - spans), bf16),
        ],
        axis=2,
    ).reshape(rows, per_seq * extra)
    mix_cuts = [cuts + [(2, s * extra, extra)] for s, cuts in enumerate(feature_cuts)]
    vectors = jnp.stack([b_init, tnorm_w, tnorm_b, post_w, post_b], axis=1)
    head_rows = jnp.concatenate([w_init, vectors, jnp.zeros((rows, extra - HD - 5), bf16)], axis=1)
    over_dp = (w_out, head_rows) if aligned else ()
    down_rows = jnp.pad(w_down, ((0, filled - units), (0, 0)))
    w_mix, rows_all, *got = first_exchange(
        split_columns((w_qkv, w_gate, beside_cols), mix_cuts), tokens[0], over_dp + (down_rows[:, : width // 2],)
    )
    *got, w_d_first = got
    if aligned:
        w_o, head_rows = got
    else:
        w_o, head_rows = (own_rows(lax.all_gather(a, both, axis=0, tiled=True)) for a in (w_out, head_rows))
    w_extra = w_mix[:, 4 * mine :]
    gain_one, gain_two = w_extra[:, heads].astype(floats), w_extra[:, heads + 1].astype(floats)
    pack_tags = w_extra.reshape(packs, per_seq, rows, extra)[:, :, 0, heads + 2 : heads + 2 + spans]
    pack_tags = lax.dynamic_index_in_dim(pack_tags.reshape(packs, blocks), lax.axis_index("dp"), 0, keepdims=False)
    fresh = jnp.concatenate([jnp.ones((1,), jnp.int32), (pack_tags[1:] != pack_tags[:-1]).astype(jnp.int32)])
    vec_own = head_rows[:, HD : HD + 5].astype(floats)
    post_gain, post_shift = vec_own[:, 3], vec_own[:, 4]
    bias_own = lax.dynamic_index_in_dim(lr_bias.reshape(outer, per_seq, heads // outer), place, 1, keepdims=False)
    bias_own = bias_own.reshape(heads).astype(floats)

    half = span // 2
    later_top, rows_all = lax.optimization_barrier((grad_out[0, :half], rows_all))
    top_first = lax.all_gather(later_top, "seq", axis=0)
    gu_mine = split_columns((w_gate_up,), unit_cuts)

    inputs = rows_all.astype(floats)
    scale_one = lax.rsqrt(jnp.mean(inputs * inputs, -1, keepdims=True) + EPSILON)
    normed_in = inputs * scale_one
    x_one = (normed_in * gain_one).astype(bf16)
    qkv = dot(x_one, w_mix[:, : 3 * mine])
    gate_pre = dot(x_one, w_mix[:, 3 * mine : 4 * mine])
    lr_sigm = jax.nn.sigmoid(dot(x_one, w_extra)[:, :heads] + bias_own)
    e_rows = (lr_sigm * (1.0 / (HD * MB))).reshape(blocks, MB, heads).transpose(0, 2, 1).reshape(blocks, 1, heads * MB)

    def by_token(vector):
        return jnp.repeat(vector.reshape(heads, HD).T, MB, axis=1)

    init_w = head_rows[:, :HD].astype(floats).reshape(heads, HD, HD)
    init_w = (init_w - jnp.mean(init_w, -1, keepdims=True)).transpose(2, 0, 1).reshape(HD, heads * HD)
    init_b = vec_own[:, 0].reshape(heads, HD)
    init_b = (init_b - jnp.mean(init_b, -1, keepdims=True)).reshape(-1)
    gain_t, shift_t = by_token(vec_own[:, 1]), by_token(vec_own[:, 2])
    *results, gu_part, w_d_second, gu_near = inner_forward(
        10, fresh, qkv, e_rows, init_w, by_token(init_b), gain_t, shift_t, (gu_mine,),
        (down_rows[:, width // 2 :],),
    )
    w_d_second = w_d_second.reshape(-1, width // 2)
    mixed, *saved = results
    later_top, mixed = lax.optimization_barrier((grad_out[0, half:], mixed))
    top_second = lax.all_gather(later_top, "seq", axis=0)

    mean_own = jnp.mean(mixed, -1)
    spread_own = jnp.sum((mixed - mean_own[:, None]) ** 2, -1)
    stats = gather_seq("share_moments", 2, jnp.stack([mean_own, spread_own]))
    mean_all = jnp.mean(stats[:, 0], 0)
    var_all = (jnp.sum(stats[:, 1], 0) + mine * jnp.sum((stats[:, 0] - mean_all) ** 2, 0)) * (1.0 / width)
    out_scale = lax.rsqrt(var_all + EPSILON)[:, None]
    out_hat = (mixed - mean_all[:, None]) * out_scale
    normed_out = out_hat * post_gain + post_shift
    gelu_gate, gelu_pull = jax.vjp(jax.nn.gelu, gate_pre)
    gated_unit = (gelu_gate * normed_out).astype(bf16)
    pair = 2 * span
    wide = 512

    def branch_terms(dest, factors, terms):
        unit = factors[0][dest * pair : (dest + 1) * pair, :]
        for at in range(0, width, wide):
            part = nn(unit, factors[1][:, at : at + wide]).astype(bf16)
            terms[2 * dest : 2 * dest + 2, :, at : at + wide] = part.reshape(2, span, wide)

    branch, gu_far = scatter_with(
        "scatter_branch", 3, (span, width), (gated_unit, w_o), branch_terms,
        Beside(pieces=(gu_part,)),
    )
    inputs = tokens[0].astype(floats)
    residual = inputs + branch
    scale_two = lax.rsqrt(jnp.mean(residual * residual, -1, keepdims=True) + EPSILON)
    normed_mid = residual * scale_two
    down, g_gate_up, g_down, d_xtwo = feed_forward(
        5, (normed_mid * gain_two).astype(bf16), (top_first, top_second), (gu_part, gu_near, gu_far), (w_d_first, w_d_second)
    )
    down = down.reshape(-1, width)
    pack_rows = lambda array: array.reshape((packs, -1) + array.shape[1:])
    g_gate_up = pack_rows(g_gate_up)
    g_down = add_packs(g_down)[:units]
    g_two = jnp.sum(d_xtwo * normed_mid, axis=0)
    d_mid = d_xtwo * gain_two
    d_residual = grad_out[0].astype(floats) + scale_two * (
        d_mid - normed_mid * jnp.mean(d_mid * normed_mid, -1, keepdims=True)
    )
    d_branch, g_gate_up = gather_with("gather_branch", 6, d_residual.astype(bf16), Beside(sums=(g_gate_up,)))
    down_first, d_branch = lax.optimization_barrier((down[:, : width // 2], d_branch))
    down_first = lax.psum_scatter(down_first, "seq", scatter_dimension=0, tiled=True)
    g_out = cross_rows(gated_unit, d_branch).astype(bf16)
    d_unit = cross_cols(d_branch, w_o)
    d_normed = d_unit * gelu_gate
    g_post_w = jnp.sum(d_normed * out_hat, axis=0)
    g_post_b = jnp.sum(d_normed, axis=0)
    d_hat = d_normed * post_gain
    sums = gather_seq("share_sums", 7, jnp.stack([jnp.sum(d_hat, -1), jnp.sum(d_hat * out_hat, -1)]))
    sums = jnp.sum(sums, 0) * (1.0 / width)
    d_mixed = out_scale * (d_hat - sums[0][:, None] - out_hat * sums[1][:, None])
    d_gate_pre = gelu_pull(d_unit * normed_out)[0].astype(bf16)
    place_rows = lambda array: array.reshape((per_seq, -1) + array.shape[1:])
    g_gate = pack_rows(cross_rows(x_one, d_gate_pre).astype(bf16))
    d_qkv, d_rate, d_w0, d_c0, d_gain, d_shift, g_gate_up, g_gate, *g_outs = inner_backward(
        11, fresh, qkv, e_rows, d_mixed, saved, gain_t, shift_t, (place_rows(g_gate_up),),
        [(g_gate, None, None)] + [(pack_rows(g_out), None, None)] * aligned,
    )
    (g_gate_up,) = join_columns(g_gate_up, (w_gate_up.shape[1],), unit_cuts)
    if aligned:
        g_out = add_packs(g_outs[0])
    else:
        g_out = lax.psum_scatter(put_rows(g_out), both, scatter_dimension=0, tiled=True).astype(floats)
    down_second, d_qkv = lax.optimization_barrier((down[:, width // 2 :], d_qkv))
    down_second = lax.psum_scatter(down_second, "seq", scatter_dimension=0, tiled=True)
    result = residual + jnp.concatenate([down_first, down_second], axis=1).astype(floats)
    d_rate = d_rate.reshape(blocks, heads, MB).transpose(0, 2, 1).reshape(length, heads)
    d_logit = (d_rate * (1.0 / HD) * lr_sigm * (1.0 - lr_sigm)).astype(bf16)
    g_qkv = cross_rows(x_one, d_qkv).astype(bf16)
    d_logit_wide = jnp.pad(d_logit, ((0, 0), (0, extra - heads)))
    d_xone = cross_cols(jnp.concatenate([d_qkv, d_gate_pre, d_logit_wide], axis=1), w_mix)
    g_one = jnp.sum(d_xone * (lax.optimization_barrier(rows_all).astype(floats) * scale_one), axis=0)

    lane = jnp.arange(extra)[None, :]
    g_bias = jnp.pad(jnp.sum(d_logit.astype(floats), axis=0), (heads + 2, extra - 2 * heads - 2))
    g_beside = cross_rows(x_one, d_logit_wide) + jnp.where(lane == heads, g_one[:, None], 0.0)
    g_beside = (g_beside + jnp.where(lane == heads + 1, g_two[:, None], 0.0) + g_bias[None, :]).astype(bf16)

    def from_token(array):
        return jnp.sum(array.reshape(HD, heads, MB), -1).T.reshape(mine)

    g_vec = jnp.stack(
        [d_c0.reshape(HD, heads, MB)[:, :, 0].T.reshape(mine), from_token(d_gain), from_token(d_shift), g_post_w, g_post_b],
        axis=1,
    )
    g_heads = jnp.concatenate(
        [d_w0.reshape(HD, heads, HD).transpose(1, 2, 0).reshape(mine, HD), g_vec, jnp.zeros((mine, extra - HD - 5), floats)],
        axis=1,
    )

    swaps = [pack_rows(g_heads)] * aligned + [pack_rows(g_beside), pack_rows(g_qkv)]
    d_xone, *got = scatter_with("scatter_first", 8, (span, width), (d_xone.astype(bf16),), None, Beside(swaps=swaps))
    if aligned:
        g_heads = add_packs(got[0])
    else:
        g_heads = lax.psum_scatter(put_rows(g_heads), both, scatter_dimension=0, tiled=True)
    g_mix = jnp.concatenate([add_packs(got[-1]), add_packs(g_gate), add_packs(got[-2])], axis=1).astype(bf16)
    (g_mix,) = swap_places("return_columns", 9, (place_rows(g_mix),))
    g_qkv, g_gate = join_columns(g_mix, (w_qkv.shape[1], w_gate.shape[1]), feature_cuts)
    g_beside = g_mix[:, :, 4 * mine :].astype(floats)
    g_norms = jnp.sum(g_beside[:, :, heads : heads + 2], 0)

    def by_head(part):
        part = part.reshape(part.shape[:-1] + (outer, heads // outer))
        return jnp.moveaxis(part, 0, -2).reshape(part.shape[1:-2] + (heads_all,))

    scale_one = lax.rsqrt(jnp.mean(inputs * inputs, -1, keepdims=True) + EPSILON)
    normed_in = inputs * scale_one
    d_inner = d_xone * gain_one
    d_tokens = d_residual + scale_one * (
        d_inner - normed_in * jnp.mean(d_inner * normed_in, -1, keepdims=True)
    )
    return (
        result.astype(bf16)[None],
        d_tokens.astype(bf16)[None],
        g_norms[:, 0],
        g_qkv,
        by_head(g_beside[:, :, :heads]),
        by_head(g_beside[:, 0, heads + 2 : 2 * heads + 2]),
        g_gate,
        g_out,
        g_heads[:, :HD],
        g_heads[:, HD],
        g_heads[:, HD + 1],
        g_heads[:, HD + 2],
        g_heads[:, HD + 3],
        g_heads[:, HD + 4],
        g_norms[:, 1],
        g_gate_up,
        g_down,
    )


def solution(mesh):
    placed = (
        P("dp", "seq", None),
        P("dp", "seq"),
        P(("dp", "seq")),
        P(("dp", "seq"), None),
        P(("dp", "seq"), None),
        P(),
        P(("dp", "seq"), None),
        P(("dp", "seq"), None),
        P(("dp", "seq"), None),
        P(("dp", "seq")),
        P(("dp", "seq")),
        P(("dp", "seq")),
        P(("dp", "seq")),
        P(("dp", "seq")),
        P(("dp", "seq")),
        P(("dp", "seq"), None),
        P(("dp", "seq"), None),
        P("dp", "seq", None),
    )
    return jax.shard_map(
        on_device,
        mesh=mesh,
        in_specs=placed,
        out_specs=(
            P("dp", "seq", None),
            P("dp", "seq", None),
            P(("dp", "seq")),
            P(("dp", "seq"), None),
            P(("dp", "seq"), None),
            P(),
            P(("dp", "seq"), None),
            P(("dp", "seq"), None),
            P(("dp", "seq"), None),
            P(("dp", "seq")),
            P(("dp", "seq")),
            P(("dp", "seq")),
            P(("dp", "seq")),
            P(("dp", "seq")),
            P(("dp", "seq")),
            P(("dp", "seq"), None),
            P(("dp", "seq"), None),
        ),
        check_vma=False,
    )
```
